32 devices in a mesh: section: 4 (over y, core), dp: 8 (over z, x).
Axes of the slice: x: 2, y: 2, z: 4, core: 2. Of those that a mesh axis runs over, the one named last changes fastest.
Arguments:
- ids: int32 [32768, 26], P(('section', 'dp')), may hold values from 0 to 8191, as said below
- dense: bfloat16 [32768, 13], P(('section', 'dp')), may hold values from -6 to 6
- labels: int32 [32768], P(('section', 'dp')), may hold values from 0 to 1
- table: bfloat16 [26, 8192, 39], P(None, 'dp'), may hold values from -6 to 6
- cross_weight: bfloat16 [3, 1027, 1027], replicated, may hold values from -0.125 to 0.125
- cross_bias: float32 [3, 1027], replicated, may hold values from -3 to 3
- tower_in: bfloat16 [1027, 1024], replicated, may hold values from -0.1875 to 0.1875
- tower_in_bias: float32 [1024], replicated, may hold values from -3 to 3
- tower_out: bfloat16 [1024, 1024], replicated, may hold values from -0.25 to 0.25
- tower_out_bias: float32 [1024], replicated, may hold values from -3 to 3
- head_weight: float32 [2051], replicated, may hold values from -0.125 to 0.125
- head_bias: float32 [1], replicated, may hold values from -3 to 3
Outputs:
- probs: float32 [32768], P(('section', 'dp'))
- loss: float32 [1], replicated
- dense_grad: float32 [32768, 13], P(('section', 'dp'))
- table_grad: float32 [26, 8192, 39], P(None, 'dp')
- cross_weight_grad: float32 [3, 1027, 1027], replicated
- cross_bias_grad: float32 [3, 1027], replicated
- tower_in_grad: float32 [1027, 1024], P(None, ('section', 'dp'))
- tower_in_bias_grad: float32 [1024], P(('section', 'dp'))
- tower_out_grad: float32 [1024, 1024], P(None, ('section', 'dp'))
- tower_out_bias_grad: float32 [1024], P(('section', 'dp'))
- head_weight_grad: float32 [2051], replicated
- head_bias_grad: float32 [1], replicated
The draws below stay inside these ranges and needn't reach their ends.
Inputs may be any that keep to these rules, and one draw needn't show every extreme that they name: Row ids of every field are split over dp in blocks of 1024: id // 1024 is the dp index that owns the row. For each field, among the ids of the 1024 examples of one device, exactly 128 name rows of each dp index.
All inputs are finite; a program needn't handle non-finite values.
Results may differ from the reference program's by a relative error of at most 0.0059.
Values may be sent and summed in bfloat16 or wider, within the bound.
A program may use at most 384 MiB of HBM per device.

```python
import jax
import jax.numpy as jnp
from jax import lax

FIELDS = 26
EDIM = 39
DENSE = 13
HID = 1024
LAYERS = 3
MB = 1024
ROWS_DEV = 1024
D = 1027
EXAMPLES = 32768
ROWS = 8192


def draw_ids(key, part):
    key = jax.random.fold_in(key, 17)
    key_owner, key_ceiling, key_row, key_shuffle = jax.random.split(key, 4)
    per_block = MB
    block_count = EXAMPLES // per_block
    group_count = ROWS // ROWS_DEV
    owner_cycle = jnp.arange(per_block, dtype=jnp.int32) % group_count

    def shuffle_block(block_key):
        return jax.random.permutation(block_key, owner_cycle)
    owner_of = jax.vmap(shuffle_block)(jax.random.split(key_owner, block_count * FIELDS))
    owner_of = owner_of.reshape(block_count, FIELDS, per_block)
    ceilings = jax.random.randint(key_ceiling, (block_count, FIELDS, per_block), 1, ROWS_DEV + 1)
    local_rows = jax.random.randint(key_row, (block_count, FIELDS, per_block), 0, ceilings)
    shuffled = jax.random.permutation(key_shuffle, ROWS_DEV)
    local_rows = shuffled[local_rows]
    top_owner = owner_of == group_count - 1
    first_top = top_owner & (jnp.cumsum(top_owner.astype(jnp.int32), axis=2) == 1)
    bottom_owner = owner_of == 0
    first_bottom = bottom_owner & (jnp.cumsum(bottom_owner.astype(jnp.int32), axis=2) == 1)
    local_rows = jnp.where(first_top, ROWS_DEV - 1, jnp.where(first_bottom, 0, local_rows))
    full_ids = owner_of * ROWS_DEV + local_rows
    return jnp.transpose(full_ids, (0, 2, 1)).reshape(EXAMPLES, FIELDS).astype(jnp.int32)


def touch_ends(result, own_key, smallest, top_value):
    longest = result.shape.index(max(result.shape))
    spots = []
    for shift in (0, 1):
        where = [jax.random.randint(jax.random.fold_in(own_key, axis), (), 0, length) for axis, length in enumerate(result.shape)]
        where[longest] = (where[longest] + shift) % result.shape[longest]
        spots.append(tuple(where))
    return result.at[spots[0]].set(smallest).at[spots[1]].set(top_value)


def block_levels(stream_key, shape, cuts, low, top_value):
    level, own = 1.0, jax.random.fold_in(stream_key, 6)
    for dim, parts in cuts:
        steps = jnp.exp(jax.random.uniform(jax.random.fold_in(own, dim), (parts,), jnp.float32, low / len(cuts), top_value / len(cuts)))
        level = level * jnp.repeat(steps, shape[dim] // parts).reshape([-1 if axis == dim else 1 for axis in range(len(shape))])
    return level


def normal_values(own_key, extent, scale, most, shards=(), kind=jnp.bfloat16):
    gain = block_levels(own_key, extent, shards, -0.22, 0.18) if shards else 1.0
    result = jax.random.normal(own_key, extent, jnp.float32) * scale * gain
    return jnp.minimum(jnp.maximum(result, -most), most).astype(kind)


def setup_inputs(seed: int = 0) -> dict:
    streams_of = jax.random.split(jax.random.key(seed), 13)
    return {
        "ids": draw_ids(jax.random.fold_in(streams_of[12], 71), 0),
        "dense": normal_values(streams_of[1], (EXAMPLES, DENSE), 1.0, 6.0, ((0, 32),)),
        "labels": touch_ends(jax.random.randint(streams_of[2], (EXAMPLES,), 0, 2), jax.random.fold_in(streams_of[2], 1), 0, 1).astype(jnp.int32),
        "table": normal_values(streams_of[3], (FIELDS, ROWS, EDIM), 1.0, 6.0, ((1, 8),)),
        "cross_weight": normal_values(streams_of[4], (LAYERS, D, D), (2 * D) ** -0.5, 0.125),
        "cross_bias": normal_values(streams_of[5], (LAYERS, D), 0.4, 3.0, (), jnp.float32),
        "tower_in": normal_values(streams_of[6], (D, HID), D ** -0.5, 0.1875),
        "tower_in_bias": normal_values(streams_of[7], (HID,), 0.5, 3.0, (), jnp.float32),
        "tower_out": normal_values(streams_of[8], (HID, HID), (HID // 2) ** -0.5, 0.25),
        "tower_out_bias": normal_values(streams_of[9], (HID,), 0.5, 3.0, (), jnp.float32),
        "head_weight": normal_values(streams_of[10], (D + HID,), (D + HID) ** -0.5, 0.125, (), jnp.float32),
        "head_bias": normal_values(streams_of[11], (1,), 1.0, 3.0, (), jnp.float32),
    }


@jax.custom_vjp
def low(v):
    return lax.optimization_barrier(v.astype(jnp.bfloat16)).astype(jnp.float32)

@jax.custom_vjp
def low_back(v):
    return v

def low_keep(v):
    return (low(v), None)

def low_pass(kept, grad):
    return (grad,)

def back_keep(v):
    return (v, None)

def back_low(kept, grad):
    return (low(grad),)
low.defvjp(low_keep, low_pass)
low_back.defvjp(back_keep, back_low)

def reference(ids, dense, labels, table, cross_weight, cross_bias, tower_in, tower_in_bias, tower_out, tower_out_bias, head_weight, head_bias):
    highest = lax.Precision.HIGHEST
    field_index = jnp.arange(FIELDS).astype(jnp.int32)[None, :]

    def forward_sum(table_wide, dense_wide, cross_w, cross_b, inner_w, inner_b, outer_w, outer_b, head_w, head_b):

        def one_block(running, block_data):
            id_block, label_block, dense_block = block_data
            embedded = table_wide[field_index, id_block.astype(jnp.int32)].reshape(MB, FIELDS * EDIM)
            base_rows = jnp.concatenate([embedded, dense_block], axis=1)
            current = base_rows
            for layer_index in range(LAYERS):
                mixed = low_back(jnp.dot(current, cross_w[layer_index], precision=highest) + cross_b[layer_index])
                current = low_back(low(base_rows * mixed + current))
            inner_pre = low_back(jnp.dot(base_rows, inner_w, precision=highest) + inner_b)
            inner_act = low(jax.nn.gelu(inner_pre))
            outer_pre = low_back(jnp.dot(inner_act, outer_w, precision=highest) + outer_b)
            outer_act = jax.nn.gelu(outer_pre)
            logits = jnp.dot(current, head_w[:D], precision=highest) + jnp.dot(outer_act, head_w[D:], precision=highest) + head_b[0]
            targets = label_block.astype(jnp.float32)
            loss_part = jnp.sum(jnp.logaddexp(0.0, logits) - targets * logits)
            return (running + loss_part, jax.nn.sigmoid(logits))
        block_data = (ids.reshape(-1, MB, FIELDS), labels.reshape(-1, MB), dense_wide.reshape(-1, MB, DENSE))
        loss_total, probabilities = lax.scan(jax.checkpoint(one_block), jnp.zeros((), jnp.float32), block_data)
        return (loss_total, probabilities.reshape(-1))
    params = (table.astype(jnp.float32), dense.astype(jnp.float32), cross_weight.astype(jnp.float32), cross_bias, tower_in.astype(jnp.float32), tower_in_bias, tower_out.astype(jnp.float32), tower_out_bias, head_weight, head_bias)
    (loss_total, probabilities), pullback = jax.vjp(forward_sum, *params)
    gradients = pullback((jnp.ones((), jnp.float32), jnp.zeros_like(probabilities)))
    table_g, dense_g, cross_w_g, cross_b_g, inner_w_g, inner_b_g, outer_w_g, outer_b_g, head_w_g, head_b_g = gradients
    return (probabilities, (loss_total / EXAMPLES).reshape(1), dense_g, table_g, cross_w_g, cross_b_g, inner_w_g, inner_b_g, outer_w_g, outer_b_g, head_w_g, head_b_g)
```

```python
import jax
import jax.numpy as jnp
from jax import lax
from jax.sharding import PartitionSpec as P

BF = jnp.bfloat16
F32 = jnp.float32


def mm(left, right, contract):
    return lax.dot_general(
        left, right, ((contract[:1], contract[1:]), ((), ())), preferred_element_type=F32
    )


def gelu_parts(pre):
    act, back = jax.vjp(jax.nn.gelu, pre)
    return act, back(jnp.ones_like(pre))[0]


def body(
    ids,
    dense,
    labels,
    table,
    cross_weight,
    cross_bias,
    tower_in,
    tower_in_bias,
    tower_out,
    tower_out_bias,
    head_weight,
    head_bias,
):
    groups = lax.axis_size("dp")
    sections = lax.axis_size("section")
    device_count = groups * sections
    examples, fields = ids.shape
    table_rows, edim = table.shape[1:]
    layers, width = cross_weight.shape[:2]
    hidden = tower_out.shape[0]
    capacity = examples // groups
    sparse = fields * edim
    me = lax.axis_index("section") * groups + lax.axis_index("dp")

    idt = ids.T
    owner = idt // table_rows
    local = idt % table_rows
    owner_hot = owner[:, None, :] == jnp.arange(groups, dtype=jnp.int32)[None, :, None]
    lane = jnp.arange(examples, dtype=jnp.int32)
    before = (lane[:, None] < lane[None, :]).astype(BF)
    counts = mm(owner_hot.reshape(fields * groups, examples).astype(BF), before, (1, 0))
    rank = jnp.sum(jnp.where(owner_hot, counts.reshape(fields, groups, examples), 0.0), axis=1)
    slot = owner * capacity + rank.astype(jnp.int32)
    slot_hot = (slot[:, None, :] == lane[None, :, None]).astype(BF)
    halves = jnp.stack([local // 32, local % 32], axis=1).astype(BF)
    sent = lax.dot_general(
        halves, slot_hot, (((2,), (2,)), ((0,), (0,))), preferred_element_type=F32
    )
    requests = (sent[:, 0] * 32 + sent[:, 1]).astype(jnp.int32)
    requests = requests.reshape(fields, groups, capacity).transpose(1, 0, 2)
    arrived = lax.all_to_all(requests, "dp", 0, 0, tiled=True)
    arrived = arrived.transpose(1, 0, 2).reshape(fields, examples)
    row_hot = (
        arrived[:, None, :] == jnp.arange(table_rows, dtype=jnp.int32)[None, :, None]
    ).astype(BF)
    table_t = table.transpose(0, 2, 1)
    found = lax.dot_general(
        table_t, row_hot, (((2,), (1,)), ((0,), (0,))), preferred_element_type=F32
    ).astype(BF)
    found = found.reshape(sparse, groups, capacity).transpose(1, 0, 2)
    replies = lax.all_to_all(found, "dp", 0, 0, tiled=True)
    replies = replies.transpose(1, 0, 2).reshape(fields, edim, examples)
    embedded = lax.dot_general(
        replies, slot_hot, (((2,), (1,)), ((0,), (0,))), preferred_element_type=F32
    ).astype(BF)
    x0 = jnp.concatenate([embedded.reshape(sparse, examples), dense.T], axis=0)

    x0w = x0.astype(F32)
    xs, us = [x0], []
    for layer in range(layers):
        u = mm(cross_weight[layer], xs[-1], (0, 0)) + cross_bias[layer][:, None]
        us.append(u)
        xs.append((x0w * u + xs[-1].astype(F32)).astype(BF))
    p1 = mm(tower_in, x0, (0, 0)) + tower_in_bias[:, None]
    a1, d1 = gelu_parts(p1)
    h1 = a1.astype(BF)
    p2 = mm(tower_out, h1, (0, 0)) + tower_out_bias[:, None]
    h2, d2 = gelu_parts(p2)
    head_cross, head_tower = head_weight[:width], head_weight[width:]
    last = xs[-1].astype(F32)
    z = (
        jnp.sum(last * head_cross[:, None], axis=0)
        + jnp.sum(h2 * head_tower[:, None], axis=0)
        + head_bias[0]
    )
    probs = jax.nn.sigmoid(z)
    target = labels.astype(F32)
    loss = jnp.sum(jnp.logaddexp(0.0, z) - target * z)
    s = probs - target
    head_grad = jnp.concatenate([jnp.sum(s * last, axis=1), jnp.sum(s * h2, axis=1)])

    q2 = (s[None, :] * head_tower[:, None] * d2).astype(BF)
    tower_out_g = mm(q2, h1, (1, 1))
    q1 = (mm(tower_out, q2, (1, 0)) * d1).astype(BF)
    tower_in_g = mm(q1, x0, (1, 1))
    tower_biases = [jnp.sum(q1.astype(F32), axis=1), jnp.sum(q2.astype(F32), axis=1)]
    dx0 = mm(tower_in, q1, (1, 0))
    g = (s[None, :] * head_cross[:, None]).astype(BF)
    cross_g, cross_b = [None] * layers, [None] * layers
    for layer in reversed(range(layers)):
        gw = g.astype(F32)
        v = (gw * x0w).astype(BF)
        cross_g[layer] = mm(xs[layer], v, (1, 1))
        cross_b[layer] = jnp.sum(v.astype(F32), axis=1)
        dx0 = dx0 + gw * us[layer]
        g = gw + mm(cross_weight[layer], v, (1, 0))
        if layer:
            g = g.astype(BF)
    dx0 = dx0 + g

    packed = lax.dot_general(
        dx0[:sparse].astype(BF).reshape(fields, edim, examples),
        slot_hot,
        (((2,), (2,)), ((0,), (0,))),
        preferred_element_type=F32,
    ).astype(BF)
    packed = packed.reshape(sparse, groups, capacity).transpose(1, 0, 2)
    delivered = lax.all_to_all(packed, "dp", 0, 0, tiled=True)
    delivered = delivered.transpose(1, 0, 2).reshape(fields, edim, examples)
    table_g = lax.dot_general(
        delivered, row_hot, (((2,), (2,)), ((0,), (0,))), preferred_element_type=F32
    )
    table_g = lax.psum(table_g.astype(BF), "section").astype(F32).transpose(0, 2, 1)

    small = jnp.concatenate(
        cross_b + [head_grad, jnp.sum(s).reshape(1), loss.reshape(1)] + tower_biases
    )
    small = lax.psum(small, ("section", "dp"))
    sizes = [layers * width, width + hidden, 1, 1, hidden, hidden]
    ends = [sum(sizes[: i + 1]) for i in range(len(sizes))]
    pieces = [small[e - n : e] for e, n in zip(ends, sizes)]
    cross_b_out = pieces[0].reshape(layers, width)
    share = hidden // device_count
    bias_in, bias_out = (lax.dynamic_slice(p, (me * share,), (share,)) for p in pieces[4:])
    cross_out = lax.psum(jnp.stack(cross_g).astype(BF), ("section", "dp")).astype(F32)
    tower_in_out = lax.psum_scatter(
        tower_in_g, ("section", "dp"), scatter_dimension=0, tiled=True
    )
    tower_out_out = lax.psum_scatter(
        tower_out_g, ("section", "dp"), scatter_dimension=0, tiled=True
    )
    return (
        probs,
        pieces[3] / (examples * device_count),
        dx0[sparse:].T,
        table_g,
        cross_out,
        cross_b_out,
        tower_in_out.astype(F32).T,
        bias_in,
        tower_out_out.astype(F32).T,
        bias_out,
        pieces[1],
        pieces[2],
    )


def solution(mesh):
    both = ("section", "dp")
    return jax.shard_map(
        body,
        mesh=mesh,
        in_specs=(P(both, None), P(both, None), P(both), P(None, "dp", None)) + (P(),) * 8,
        out_specs=(
            P(both),
            P(),
            P(both, None),
            P(None, "dp", None),
            P(),
            P(),
            P(None, both),
            P(both),
            P(None, both),
            P(both),
            P(),
            P(),
        ),
        check_vma=False,
    )
```

```python
import jax
import jax.numpy as jnp
from jax import lax
from jax.experimental import pallas as pl
from jax.experimental.pallas import tpu as pltpu
from jax.sharding import PartitionSpec as P

BF = jnp.bfloat16
F32 = jnp.float32


def mm(left, right, contract):
    return lax.dot_general(
        left, right, ((contract[:1], contract[1:]), ((), ())), preferred_element_type=F32
    )


def gelu_parts(pre):
    act, back = jax.vjp(jax.nn.gelu, pre)
    return act, back(jnp.ones_like(pre))[0]


VIEW = (2, 2, 4, 2)


def reduce_kernel(
    units, gathered, *refs
):
    grads = refs[:units]
    table_ref, small_ref = refs[units : units + 2]
    whole, pieces, table_out, small_out = refs[units + 2 : units + 6]
    (rc, sa1, ra1, sb1, rb1, sa2, ra2, sb2, rb2, sz, rz, rtc, st, rt, sm, rm, rmz, send, recv) = refs[units + 6 :]
    section, dp = lax.axis_index("section"), lax.axis_index("dp")
    y, c = section // 2, section % 2
    z, x = dp // 2, dp % 2
    core_peer = (y * 2 + 1 - c, dp)
    y_peer = ((1 - y) * 2 + c, dp)
    x_peer = (section, z * 2 + 1 - x)
    half = 512
    lo, hi = pl.ds(0, half), pl.ds(half, half)

    def z_peer(j):
        return (section, lax.rem(z + j, 4) * 2 + x)

    peers = [core_peer, y_peer, x_peer] + [z_peer(j) for j in (1, 2, 3)]
    barrier = pltpu.get_barrier_semaphore()
    for peer in peers:
        pl.semaphore_signal(barrier, inc=1, device_id=peer, device_id_type=pl.DeviceIdType.MESH)
    pl.semaphore_wait(barrier, len(peers))

    flying = []

    def start(src, dst, m, k, peer):
        copy = pltpu.make_async_remote_copy(
            src_ref=src,
            dst_ref=dst,
            send_sem=send.at[m, k],
            recv_sem=recv.at[m, k],
            device_id=peer,
            device_id_type=pl.DeviceIdType.MESH,
        )
        copy.start()
        flying.append(copy)
        return copy

    def wide(value):
        return value.astype(F32)

    copies = {}

    def acc(m, stage, cols, yy, zz, xx):
        g = grads[m]
        total = wide(g[yy, c, zz, xx, :, cols]) + wide(rc[m, yy, zz, xx, :, cols])
        if cols is lo:
            if stage >= 2:
                total += wide(ra1[m, yy, zz])
            if stage >= 3:
                total += wide(ra2[m, zz])
        else:
            if stage >= 2:
                total += wide(rb1[m, zz, xx])
            if stage >= 3:
                total += wide(rb2[m, zz])
        return total

    def step0(m):
        copies[m, 0] = start(grads[m].at[:, 1 - c], rc.at[m], m, 0, core_peer)

    def step1(m):
        copies[m, 0].wait_recv()

        @pl.loop(0, 4)
        def _(zz):
            for i in range(2):
                sa1[m, i, zz] = acc(m, 1, lo, i, zz, 1 - x).astype(BF)
                sb1[m, zz, i] = acc(m, 1, hi, 1 - y, zz, i).astype(BF)

        copies[m, 1] = start(sa1.at[m], ra1.at[m], m, 1, x_peer)
        copies[m, 2] = start(sb1.at[m], rb1.at[m], m, 2, y_peer)

    def step2(m):
        copies[m, 1].wait_recv()
        copies[m, 2].wait_recv()

        @pl.loop(0, 4)
        def _(zz):
            sa2[m, zz] = acc(m, 2, lo, 1 - y, zz, x).astype(BF)
            sb2[m, zz] = acc(m, 2, hi, y, zz, 1 - x).astype(BF)

        copies[m, 3] = start(sa2.at[m], ra2.at[m], m, 3, y_peer)
        copies[m, 4] = start(sb2.at[m], rb2.at[m], m, 4, x_peer)

    def step3(m):
        copies[m, 3].wait_recv()
        copies[m, 4].wait_recv()
        for j in (1, 2, 3):
            zz = lax.rem(z + j, 4)
            sz[m, j - 1, :, lo] = acc(m, 3, lo, y, zz, x).astype(BF)
            sz[m, j - 1, :, hi] = acc(m, 3, hi, y, zz, x).astype(BF)
            copies[m, 4 + j] = start(sz.at[m, j - 1], rz.at[m, j - 1], m, 4 + j, z_peer(j))

    def step4(m):
        for j in (1, 2, 3):
            copies[m, 4 + j].wait_recv()
        for cols in (lo, hi):
            total = acc(m, 3, cols, y, z, x)
            for j in range(3):
                total += wide(rz[m, j, :, cols])
            if m < gathered:
                whole[m, y, c, z, x, :, cols] = total.astype(BF)
            else:
                pieces[m - gathered, :, cols] = total
        if m < gathered:
            for j in (1, 2, 3):
                mine = whole.at[m, y, c, z, x]
                copies[m, 7 + j] = start(mine, mine, m, 7 + j, z_peer(j))

    def step5(m):
        for j in (1, 2, 3):
            copies[m, 7 + j].wait_recv()
        ours = whole.at[m, y, c, :, x, :, lo]
        copies[m, 11] = start(ours, ours, m, 11, y_peer)
        ours = whole.at[m, y, c, :, x, :, hi]
        copies[m, 12] = start(ours, ours, m, 12, x_peer)

    def step6(m):
        copies[m, 11].wait_recv()
        copies[m, 12].wait_recv()
        ours = whole.at[m, :, c, :, x, :, lo]
        copies[m, 13] = start(ours, ours, m, 13, x_peer)
        ours = whole.at[m, y, c, :, :, :, hi]
        copies[m, 14] = start(ours, ours, m, 14, y_peer)

    def step7(m):
        copies[m, 13].wait_recv()
        copies[m, 14].wait_recv()
        ours = whole.at[m, :, c]
        copies[m, 15] = start(ours, ours, m, 15, core_peer)

    def step8(m):
        copies[m, 15].wait_recv()

    t = units

    def table0():
        copies[t, 0] = start(table_ref.at[:, 1 - c], rtc, t, 0, core_peer)

    def table1():
        copies[t, 0].wait_recv()

        @pl.loop(0, 8)
        def _(i):
            rows = pl.ds(pl.multiple_of(i * 32, 32), 32)
            st[rows] = (wide(table_ref[1 - y, c, rows]) + wide(rtc[1 - y, rows])).astype(BF)

        copies[t, 1] = start(st, rt, t, 1, y_peer)

    def table2():
        copies[t, 1].wait_recv()

        @pl.loop(0, 8)
        def _(i):
            rows = pl.ds(pl.multiple_of(i * 32, 32), 32)
            total = wide(table_ref[y, c, rows]) + wide(rtc[y, rows]) + wide(rt[rows])
            table_out[y, c, rows] = total.astype(BF)

        ours = table_out.at[y, c]
        copies[t, 2] = start(ours, ours, t, 2, y_peer)

    def table3():
        copies[t, 2].wait_recv()
        ours = table_out.at[:, c]
        copies[t, 3] = start(ours, ours, t, 3, core_peer)

    def table4():
        copies[t, 3].wait_recv()

    s = units + 1

    def small0():
        copies[s, 0] = start(small_ref.at[1 - c], rm.at[0], s, 0, core_peer)

    def small1():
        copies[s, 0].wait_recv()
        sm[0] = small_ref[c] + rm[0]
        copies[s, 1] = start(sm.at[0], rm.at[1], s, 1, x_peer)

    def small2():
        copies[s, 1].wait_recv()
        sm[1] = sm[0] + rm[1]
        copies[s, 2] = start(sm.at[1], rm.at[2], s, 2, y_peer)

    def small3():
        copies[s, 2].wait_recv()
        sm[2] = sm[1] + rm[2]
        for j in (1, 2, 3):
            copies[s, 2 + j] = start(sm.at[2], rmz.at[j - 1], s, 2 + j, z_peer(j))

    def small4():
        for j in (1, 2, 3):
            copies[s, 2 + j].wait_recv()
        even = lax.rem(z, 2)
        near = [sm[2], rmz[0], rmz[1], rmz[2]]
        first = near[0] + near[2]
        second = near[1] + near[3]
        small_out[c] = jnp.where(even == 0, first, second) + jnp.where(even == 0, second, first)
        ours = small_out.at[c]
        copies[s, 6] = start(ours, ours, s, 6, core_peer)

    def small5():
        copies[s, 6].wait_recv()

    small0()
    for m in range(units):
        step0(m)
    table0()
    steps = [step1, step2, step3, step4, step5, step6, step7, step8]
    extras = [small1, small2, table1, small3, table2, small4, table3, small5, table4]
    for now in range(units + len(steps)):
        for k, step in enumerate(steps):
            m = now - k
            if 0 <= m < units and (k < 4 or m < gathered):
                step(m)
        if now < len(extras):
            extras[now]()
    for copy in flying:
        copy.wait_send()


def reduce_all(grads, gathered, table_g, small):
    units = len(grads)
    piece = (32, 1024)
    vmem = pl.BlockSpec(memory_space=pltpu.VMEM)
    outs = pl.pallas_call(
        lambda *refs: reduce_kernel(units, gathered, *refs),
        out_shape=[
            jax.ShapeDtypeStruct((gathered,) + VIEW + piece, BF),
            jax.ShapeDtypeStruct((units - gathered,) + piece, F32),
            jax.ShapeDtypeStruct((2, 2, 256, 1024), BF),
            jax.ShapeDtypeStruct((2, 16, 1024), F32),
        ],
        in_specs=[vmem] * (units + 2),
        out_specs=[vmem] * 4,
        scratch_shapes=[
            pltpu.VMEM((units, 2, 4, 2) + piece, BF),
            pltpu.VMEM((units, 2, 4, 32, 512), BF),
            pltpu.VMEM((units, 2, 4, 32, 512), BF),
            pltpu.VMEM((units, 4, 2, 32, 512), BF),
            pltpu.VMEM((units, 4, 2, 32, 512), BF),
            pltpu.VMEM((units, 4, 32, 512), BF),
            pltpu.VMEM((units, 4, 32, 512), BF),
            pltpu.VMEM((units, 4, 32, 512), BF),
            pltpu.VMEM((units, 4, 32, 512), BF),
            pltpu.VMEM((units, 3) + piece, BF),
            pltpu.VMEM((units, 3) + piece, BF),
            pltpu.VMEM((2, 256, 1024), BF),
            pltpu.VMEM((256, 1024), BF),
            pltpu.VMEM((256, 1024), BF),
            pltpu.VMEM((3, 16, 1024), F32),
            pltpu.VMEM((3, 16, 1024), F32),
            pltpu.VMEM((3, 16, 1024), F32),
            pltpu.SemaphoreType.DMA((units + 2, 16)),
            pltpu.SemaphoreType.DMA((units + 2, 16)),
        ],
        compiler_params=pltpu.CompilerParams(
            collective_id=0, has_side_effects=True, vmem_limit_bytes=56 * 2**20
        ),
        name="reduce_all",
    )(
        *[g.reshape(VIEW + piece) for g in grads],
        table_g.reshape(2, 2, 256, 1024),
        small.reshape(2, 16, 1024),
    )
    whole, pieces, table_sum, small_sum = outs
    return (
        whole.reshape(gathered, 1024, 1024),
        pieces,
        table_sum.reshape(1024, 1024),
        small_sum.reshape(-1),
    )


def body(
    ids,
    dense,
    labels,
    table,
    cross_weight,
    cross_bias,
    tower_in,
    tower_in_bias,
    tower_out,
    tower_out_bias,
    head_weight,
    head_bias,
):
    groups = lax.axis_size("dp")
    sections = lax.axis_size("section")
    device_count = groups * sections
    examples, fields = ids.shape
    table_rows, edim = table.shape[1:]
    layers, width = cross_weight.shape[:2]
    hidden = tower_out.shape[0]
    capacity = examples // groups
    sparse = fields * edim
    me = lax.axis_index("section") * groups + lax.axis_index("dp")

    idt = ids.T
    owner = idt // table_rows
    local = idt % table_rows
    owner_hot = owner[:, None, :] == jnp.arange(groups, dtype=jnp.int32)[None, :, None]
    lane = jnp.arange(examples, dtype=jnp.int32)
    before = (lane[:, None] < lane[None, :]).astype(BF)
    counts = mm(owner_hot.reshape(fields * groups, examples).astype(BF), before, (1, 0))
    rank = jnp.sum(jnp.where(owner_hot, counts.reshape(fields, groups, examples), 0.0), axis=1)
    slot = owner * capacity + rank.astype(jnp.int32)
    slot_hot = (slot[:, None, :] == lane[None, :, None]).astype(BF)
    halves = jnp.stack([local // 32, local % 32], axis=1).astype(BF)
    sent = lax.dot_general(
        halves, slot_hot, (((2,), (2,)), ((0,), (0,))), preferred_element_type=F32
    )
    requests = (sent[:, 0] * 32 + sent[:, 1]).astype(jnp.int32)
    requests = requests.reshape(fields, groups, capacity).transpose(1, 0, 2)
    arrived = lax.all_to_all(requests, "dp", 0, 0, tiled=True)
    arrived = arrived.transpose(1, 0, 2).reshape(fields, examples)
    row_hot = (
        arrived[:, None, :] == jnp.arange(table_rows, dtype=jnp.int32)[None, :, None]
    ).astype(BF)
    table_t = table.transpose(0, 2, 1)
    found = lax.dot_general(
        table_t, row_hot, (((2,), (1,)), ((0,), (0,))), preferred_element_type=F32
    ).astype(BF)
    found = found.reshape(sparse, groups, capacity).transpose(1, 0, 2)
    replies = lax.all_to_all(found, "dp", 0, 0, tiled=True)
    replies = replies.transpose(1, 0, 2).reshape(fields, edim, examples)
    embedded = lax.dot_general(
        replies, slot_hot, (((2,), (1,)), ((0,), (0,))), preferred_element_type=F32
    ).astype(BF)
    x0 = jnp.concatenate([embedded.reshape(sparse, examples), dense.T], axis=0)

    x0w = x0.astype(F32)
    xs, us = [x0], []
    for layer in range(layers):
        u = mm(cross_weight[layer], xs[-1], (0, 0)) + cross_bias[layer][:, None]
        us.append(u)
        xs.append((x0w * u + xs[-1].astype(F32)).astype(BF))
    p1 = mm(tower_in, x0, (0, 0)) + tower_in_bias[:, None]
    a1, d1 = gelu_parts(p1)
    h1 = a1.astype(BF)
    p2 = mm(tower_out, h1, (0, 0)) + tower_out_bias[:, None]
    h2, d2 = gelu_parts(p2)
    head_cross, head_tower = head_weight[:width], head_weight[width:]
    last = xs[-1].astype(F32)
    z = (
        jnp.sum(last * head_cross[:, None], axis=0)
        + jnp.sum(h2 * head_tower[:, None], axis=0)
        + head_bias[0]
    )
    probs = jax.nn.sigmoid(z)
    target = labels.astype(F32)
    loss = jnp.sum(jnp.logaddexp(0.0, z) - target * z)
    s = probs - target
    head_grad = jnp.concatenate([jnp.sum(s * last, axis=1), jnp.sum(s * h2, axis=1)])

    q2 = (s[None, :] * head_tower[:, None] * d2).astype(BF)
    tower_out_g = mm(q2, h1, (1, 1))
    q1 = (mm(tower_out, q2, (1, 0)) * d1).astype(BF)
    tower_in_g = mm(q1, x0, (1, 1))
    tower_biases = [jnp.sum(q1.astype(F32), axis=1), jnp.sum(q2.astype(F32), axis=1)]
    dx0 = mm(tower_in, q1, (1, 0))
    g = (s[None, :] * head_cross[:, None]).astype(BF)
    cross_g, cross_b = [None] * layers, [None] * layers
    for layer in reversed(range(layers)):
        gw = g.astype(F32)
        v = (gw * x0w).astype(BF)
        cross_g[layer] = mm(xs[layer], v, (1, 1))
        cross_b[layer] = jnp.sum(v.astype(F32), axis=1)
        dx0 = dx0 + gw * us[layer]
        g = gw + mm(cross_weight[layer], v, (1, 0))
        if layer:
            g = g.astype(BF)
    dx0 = dx0 + g

    packed = lax.dot_general(
        dx0[:sparse].astype(BF).reshape(fields, edim, examples),
        slot_hot,
        (((2,), (2,)), ((0,), (0,))),
        preferred_element_type=F32,
    ).astype(BF)
    packed = packed.reshape(sparse, groups, capacity).transpose(1, 0, 2)
    delivered = lax.all_to_all(packed, "dp", 0, 0, tiled=True)
    delivered = delivered.transpose(1, 0, 2).reshape(fields, edim, examples)
    table_g = lax.dot_general(
        delivered, row_hot, (((2,), (2,)), ((0,), (0,))), preferred_element_type=F32
    )
    small = jnp.concatenate(
        cross_b + [head_grad, jnp.sum(s).reshape(1), loss.reshape(1)] + tower_biases
    )
    both = ("section", "dp")
    share = hidden // device_count
    main = hidden
    if (sections, groups) == (4, 8):
        edges = [jnp.concatenate([g[main:].reshape(-1), g[:main, main:].reshape(-1)]) for g in cross_g]
        edges.append(tower_in_g[:, main:].reshape(-1))
        flat = jnp.concatenate([small] + edges)
        filled = jnp.zeros((32 * 1024,), F32).at[: flat.shape[0]].set(flat)
        table_flat = jnp.pad(
            table_g.astype(BF).reshape(sparse, table_rows), ((0, 1024 - sparse), (0, 0))
        )
        whole, pieces32, table_sum, flat = reduce_all(
            [g[:main, :main].astype(BF) for g in cross_g]
            + [tower_in_g[:, :main].astype(BF), tower_out_g.astype(BF)],
            layers,
            table_flat,
            filled.reshape(32, 1024),
        )
        table_g = table_sum[:sparse].reshape(fields, edim, table_rows)
        at = small.shape[0]
        small = flat[:at]
        rest = width - main
        crosses = []
        for layer in range(layers):
            bottom = flat[at : at + rest * width].reshape(rest, width)
            at += rest * width
            side = flat[at : at + main * rest].reshape(main, rest)
            at += main * rest
            top = jnp.concatenate([whole[layer].astype(F32), side], axis=1)
            crosses.append(jnp.concatenate([top, bottom], axis=0))
        cross_out = jnp.stack(crosses)
        side = lax.dynamic_slice(
            flat[at : at + hidden * rest].reshape(hidden, rest), (me * share, 0), (share, rest)
        )
        tower_in_out = jnp.concatenate([pieces32[0], side], axis=1)
        tower_out_out = pieces32[1]
    else:
        table_g = lax.psum(table_g, "section")
        small = lax.psum(small, both)
        cross_out = lax.psum(jnp.stack(cross_g), both)
        tower_in_out = lax.psum_scatter(tower_in_g, both, scatter_dimension=0, tiled=True)
        tower_out_out = lax.psum_scatter(tower_out_g, both, scatter_dimension=0, tiled=True)
    table_g = table_g.astype(F32).transpose(0, 2, 1)
    sizes = [layers * width, width + hidden, 1, 1, hidden, hidden]
    ends = [sum(sizes[: i + 1]) for i in range(len(sizes))]
    pieces = [small[e - n : e] for e, n in zip(ends, sizes)]
    cross_b_out = pieces[0].reshape(layers, width)
    bias_in, bias_out = (lax.dynamic_slice(p, (me * share,), (share,)) for p in pieces[4:])
    return (
        probs,
        pieces[3] / (examples * device_count),
        dx0[sparse:].T,
        table_g,
        cross_out,
        cross_b_out,
        tower_in_out.T,
        bias_in,
        tower_out_out.T,
        bias_out,
        pieces[1],
        pieces[2],
    )


def solution(mesh):
    both = ("section", "dp")
    return jax.shard_map(
        body,
        mesh=mesh,
        in_specs=(P(both, None), P(both, None), P(both), P(None, "dp", None)) + (P(),) * 8,
        out_specs=(
            P(both),
            P(),
            P(both, None),
            P(None, "dp", None),
            P(),
            P(),
            P(None, both),
            P(both),
            P(None, both),
            P(both),
            P(),
            P(),
        ),
        check_vma=False,
    )
```

```python
import functools

import jax
import jax.numpy as jnp
from jax import lax
from jax.experimental import pallas as pl
from jax.experimental.pallas import tpu as pltpu
from jax.sharding import PartitionSpec as P

BF = jnp.bfloat16
F32 = jnp.float32


def mm(left, right, contract):
    return lax.dot_general(
        left, right, ((contract[:1], contract[1:]), ((), ())), preferred_element_type=F32
    )


def gelu_parts(pre):
    act, back = jax.vjp(jax.nn.gelu, pre)
    return act, back(jnp.ones_like(pre))[0]


VIEW = (2, 2, 4, 2)


def reduce_kernel(
    units, gathered, *refs
):
    grads = refs[:units]
    table_ref, small_ref = refs[units : units + 2]
    whole, pieces, table_out, small_out = refs[units + 2 : units + 6]
    (rc, sa1, ra1, sb1, rb1, sa2, ra2, sb2, rb2, sz, rz, rtc, st, rt, sm, rm, rmz, send, recv) = refs[units + 6 :]
    section, dp = lax.axis_index("section"), lax.axis_index("dp")
    y, c = section // 2, section % 2
    z, x = dp // 2, dp % 2
    core_peer = (y * 2 + 1 - c, dp)
    y_peer = ((1 - y) * 2 + c, dp)
    x_peer = (section, z * 2 + 1 - x)
    half = 512
    lo, hi = pl.ds(0, half), pl.ds(half, half)

    def z_peer(j):
        return (section, lax.rem(z + j, 4) * 2 + x)

    peers = [core_peer, y_peer, x_peer] + [z_peer(j) for j in (1, 2, 3)]
    barrier = pltpu.get_barrier_semaphore()
    for peer in peers:
        pl.semaphore_signal(barrier, inc=1, device_id=peer, device_id_type=pl.DeviceIdType.MESH)
    pl.semaphore_wait(barrier, len(peers))

    flying = []

    def start(src, dst, m, k, peer):
        copy = pltpu.make_async_remote_copy(
            src_ref=src,
            dst_ref=dst,
            send_sem=send.at[m, k],
            recv_sem=recv.at[m, k],
            device_id=peer,
            device_id_type=pl.DeviceIdType.MESH,
        )
        copy.start()
        flying.append(copy)
        return copy

    def wide(value):
        return value.astype(F32)

    copies = {}

    def acc(m, stage, cols, yy, zz, xx):
        g = grads[m]
        total = wide(g[yy, c, zz, xx, :, cols]) + wide(rc[m, yy, zz, xx, :, cols])
        if cols is lo:
            if stage >= 2:
                total += wide(ra1[m, yy, zz])
            if stage >= 3:
                total += wide(ra2[m, zz])
        else:
            if stage >= 2:
                total += wide(rb1[m, zz, xx])
            if stage >= 3:
                total += wide(rb2[m, zz])
        return total

    def step0(m):
        copies[m, 0] = start(grads[m].at[:, 1 - c], rc.at[m], m, 0, core_peer)

    def step1(m):
        copies[m, 0].wait_recv()

        @pl.loop(0, 4)
        def _(zz):
            for i in range(2):
                sa1[m, i, zz] = acc(m, 1, lo, i, zz, 1 - x).astype(BF)
                sb1[m, zz, i] = acc(m, 1, hi, 1 - y, zz, i).astype(BF)

        copies[m, 1] = start(sa1.at[m], ra1.at[m], m, 1, x_peer)
        copies[m, 2] = start(sb1.at[m], rb1.at[m], m, 2, y_peer)

    def step2(m):
        copies[m, 1].wait_recv()
        copies[m, 2].wait_recv()

        @pl.loop(0, 4)
        def _(zz):
            sa2[m, zz] = acc(m, 2, lo, 1 - y, zz, x).astype(BF)
            sb2[m, zz] = acc(m, 2, hi, y, zz, 1 - x).astype(BF)

        copies[m, 3] = start(sa2.at[m], ra2.at[m], m, 3, y_peer)
        copies[m, 4] = start(sb2.at[m], rb2.at[m], m, 4, x_peer)

    def step3(m):
        copies[m, 3].wait_recv()
        copies[m, 4].wait_recv()
        for j in (1, 2, 3):
            zz = lax.rem(z + j, 4)
            sz[m, j - 1, :, lo] = acc(m, 3, lo, y, zz, x).astype(BF)
            sz[m, j - 1, :, hi] = acc(m, 3, hi, y, zz, x).astype(BF)
            copies[m, 4 + j] = start(sz.at[m, j - 1], rz.at[m, j - 1], m, 4 + j, z_peer(j))

    def step4(m):
        for j in (1, 2, 3):
            copies[m, 4 + j].wait_recv()
        for cols in (lo, hi):
            total = acc(m, 3, cols, y, z, x)
            for j in range(3):
                total += wide(rz[m, j, :, cols])
            if m < gathered:
                whole[m, y, c, z, x, :, cols] = total.astype(BF)
            else:
                pieces[m - gathered, :, cols] = total
        if m < gathered:
            for j in (1, 2, 3):
                mine = whole.at[m, y, c, z, x]
                copies[m, 7 + j] = start(mine, mine, m, 7 + j, z_peer(j))

    def step5(m):
        for j in (1, 2, 3):
            copies[m, 7 + j].wait_recv()
        ours = whole.at[m, y, c, :, x, :, lo]
        copies[m, 11] = start(ours, ours, m, 11, y_peer)
        ours = whole.at[m, y, c, :, x, :, hi]
        copies[m, 12] = start(ours, ours, m, 12, x_peer)

    def step6(m):
        copies[m, 11].wait_recv()
        copies[m, 12].wait_recv()
        ours = whole.at[m, :, c, :, x, :, lo]
        copies[m, 13] = start(ours, ours, m, 13, x_peer)
        ours = whole.at[m, y, c, :, :, :, hi]
        copies[m, 14] = start(ours, ours, m, 14, y_peer)

    def step7(m):
        copies[m, 13].wait_recv()
        copies[m, 14].wait_recv()
        ours = whole.at[m, :, c]
        copies[m, 15] = start(ours, ours, m, 15, core_peer)

    def step8(m):
        copies[m, 15].wait_recv()

    t = units

    def table0():
        copies[t, 0] = start(table_ref.at[:, 1 - c], rtc, t, 0, core_peer)

    def table1():
        copies[t, 0].wait_recv()

        @pl.loop(0, 8)
        def _(i):
            rows = pl.ds(pl.multiple_of(i * 32, 32), 32)
            st[rows] = (wide(table_ref[1 - y, c, rows]) + wide(rtc[1 - y, rows])).astype(BF)

        copies[t, 1] = start(st, rt, t, 1, y_peer)

    def table2():
        copies[t, 1].wait_recv()

        @pl.loop(0, 8)
        def _(i):
            rows = pl.ds(pl.multiple_of(i * 32, 32), 32)
            total = wide(table_ref[y, c, rows]) + wide(rtc[y, rows]) + wide(rt[rows])
            table_out[y, c, rows] = total.astype(BF)

        ours = table_out.at[y, c]
        copies[t, 2] = start(ours, ours, t, 2, y_peer)

    def table3():
        copies[t, 2].wait_recv()
        ours = table_out.at[:, c]
        copies[t, 3] = start(ours, ours, t, 3, core_peer)

    def table4():
        copies[t, 3].wait_recv()

    s = units + 1

    def small0():
        copies[s, 0] = start(small_ref.at[1 - c], rm.at[0], s, 0, core_peer)

    def small1():
        copies[s, 0].wait_recv()
        sm[0] = small_ref[c] + rm[0]
        copies[s, 1] = start(sm.at[0], rm.at[1], s, 1, x_peer)

    def small2():
        copies[s, 1].wait_recv()
        sm[1] = sm[0] + rm[1]
        copies[s, 2] = start(sm.at[1], rm.at[2], s, 2, y_peer)

    def small3():
        copies[s, 2].wait_recv()
        sm[2] = sm[1] + rm[2]
        for j in (1, 2, 3):
            copies[s, 2 + j] = start(sm.at[2], rmz.at[j - 1], s, 2 + j, z_peer(j))

    def small4():
        for j in (1, 2, 3):
            copies[s, 2 + j].wait_recv()
        even = lax.rem(z, 2)
        near = [sm[2], rmz[0], rmz[1], rmz[2]]
        first = near[0] + near[2]
        second = near[1] + near[3]
        small_out[c] = jnp.where(even == 0, first, second) + jnp.where(even == 0, second, first)
        ours = small_out.at[c]
        copies[s, 6] = start(ours, ours, s, 6, core_peer)

    def small5():
        copies[s, 6].wait_recv()

    small0()
    for m in range(units):
        step0(m)
    table0()
    steps = [step1, step2, step3, step4, step5, step6, step7, step8]
    extras = [small1, small2, table1, small3, table2, small4, table3, small5, table4]
    for now in range(units + len(steps)):
        for k, step in enumerate(steps):
            m = now - k
            if 0 <= m < units and (k < 4 or m < gathered):
                step(m)
        if now < len(extras):
            extras[now]()
    for copy in flying:
        copy.wait_send()


def reduce_all(grads, gathered, table_g, small):
    units = len(grads)
    piece = (32, 1024)
    vmem = pl.BlockSpec(memory_space=pltpu.VMEM)
    outs = pl.pallas_call(
        lambda *refs: reduce_kernel(units, gathered, *refs),
        out_shape=[
            jax.ShapeDtypeStruct((gathered,) + VIEW + piece, BF),
            jax.ShapeDtypeStruct((units - gathered,) + piece, F32),
            jax.ShapeDtypeStruct((2, 2, 256, 1024), BF),
            jax.ShapeDtypeStruct((2, 16, 1024), F32),
        ],
        in_specs=[vmem] * (units + 2),
        out_specs=[vmem] * 4,
        scratch_shapes=[
            pltpu.VMEM((units, 2, 4, 2) + piece, BF),
            pltpu.VMEM((units, 2, 4, 32, 512), BF),
            pltpu.VMEM((units, 2, 4, 32, 512), BF),
            pltpu.VMEM((units, 4, 2, 32, 512), BF),
            pltpu.VMEM((units, 4, 2, 32, 512), BF),
            pltpu.VMEM((units, 4, 32, 512), BF),
            pltpu.VMEM((units, 4, 32, 512), BF),
            pltpu.VMEM((units, 4, 32, 512), BF),
            pltpu.VMEM((units, 4, 32, 512), BF),
            pltpu.VMEM((units, 3) + piece, BF),
            pltpu.VMEM((units, 3) + piece, BF),
            pltpu.VMEM((2, 256, 1024), BF),
            pltpu.VMEM((256, 1024), BF),
            pltpu.VMEM((256, 1024), BF),
            pltpu.VMEM((3, 16, 1024), F32),
            pltpu.VMEM((3, 16, 1024), F32),
            pltpu.VMEM((3, 16, 1024), F32),
            pltpu.SemaphoreType.DMA((units + 2, 16)),
            pltpu.SemaphoreType.DMA((units + 2, 16)),
        ],
        compiler_params=pltpu.CompilerParams(
            collective_id=0, has_side_effects=True, vmem_limit_bytes=56 * 2**20
        ),
        name="reduce_all",
    )(
        *[g.reshape(VIEW + piece) for g in grads],
        table_g.reshape(2, 2, 256, 1024),
        small.reshape(2, 16, 1024),
    )
    whole, pieces, table_sum, small_sum = outs
    return (
        whole.reshape(gathered, 1024, 1024),
        pieces,
        table_sum.reshape(1024, 1024),
        small_sum.reshape(-1),
    )


def one_hot(places, count):
    rows = lax.broadcasted_iota(jnp.int32, (count, places.shape[1]), 0)
    return (rows == places).astype(F32).astype(BF)


def lookup_kernel(
    fields, edim, ids_ref, table_ref, dense_ref, x0_ref, arr_ref, inv_ref,
    ids, slots, req, found, rep, pair, wide_rows, x0f, id_send, id_recv, send, recv,
):
    section, me = lax.axis_index("section"), lax.axis_index("dp")
    dot = functools.partial(jnp.dot, preferred_element_type=F32)
    count = ids.shape[1]

    def peer(j):
        return lax.rem(me + j, 8)

    def lanes(place):
        return pl.ds(pl.multiple_of(place * 128, 128), 128)

    barrier = pltpu.get_barrier_semaphore()
    for j in range(1, 8):
        pl.semaphore_signal(
            barrier, inc=1, device_id=(section, peer(j)), device_id_type=pl.DeviceIdType.MESH
        )

    ids[...] = jnp.zeros_like(ids)
    ids[:fields] = ids_ref[...]
    every = ids[...]
    owner = lax.shift_right_logical(every, 10)
    hot = jnp.concatenate([(owner == o).astype(F32) for o in range(8)], axis=0).astype(BF)
    before = (
        lax.broadcasted_iota(jnp.int32, (count, count), 0)
        < lax.broadcasted_iota(jnp.int32, (count, count), 1)
    )
    ranks = dot(hot, before.astype(F32).astype(BF))
    rank = jnp.zeros((32, count), F32)
    for o in range(8):
        rank = jnp.where(owner == o, ranks[32 * o : 32 * o + 32], rank)
    slots[...] = owner * 128 + rank.astype(jnp.int32)
    ids[...] = every & 1023
    @pl.loop(0, 4)
    def _(group):
        eight = pl.ds(pl.multiple_of(8 * group, 8), 8)
        slot8, local8 = slots[eight], ids[eight]
        place = lax.broadcasted_iota(jnp.int32, (1, count), 1)
        column = lax.broadcasted_iota(jnp.int32, (8, count), 0)
        wanted, source = [], []
        for k in range(8):
            slot, local = slot8[k : k + 1], local8[k : k + 1]
            owners = column == lax.shift_right_logical(slot, 7)
            parts = [local >> 5, local & 31, place >> 5, place & 31]
            left = jnp.concatenate(
                [jnp.where(owners, p.astype(F32), 0.0) for p in parts], axis=0
            ).astype(BF)
            right = one_hot(slot & 127, 128)
            sent = lax.dot_general(
                left, right, (((1,), (1,)), ((), ())), preferred_element_type=F32
            )
            rows = [
                (sent[n : n + 8] * 32 + sent[n + 8 : n + 16]).astype(jnp.int32) for n in (0, 16)
            ]
            for taken, r in zip((wanted, source), rows):
                taken.append(jnp.concatenate([r[o : o + 1] for o in range(8)], axis=1))
        req[eight] = jnp.concatenate(wanted, axis=0)
        inv_ref[eight] = jnp.concatenate(source, axis=0)

    def id_copy(j):
        return pltpu.make_async_remote_copy(
            src_ref=req.at[:, lanes(peer(j))],
            dst_ref=arr_ref.at[:, lanes(me)],
            send_sem=id_send.at[j],
            recv_sem=id_recv.at[j],
            device_id=(section, peer(j)),
            device_id_type=pl.DeviceIdType.MESH,
        )

    pl.semaphore_wait(barrier, 7)
    for j in range(1, 8):
        id_copy(j).start()
    arr_ref[:, lanes(me)] = req[:, lanes(me)]
    for j in range(1, 8):
        id_copy(j).wait_recv()

    def row_copy(i, j):
        return pltpu.make_async_remote_copy(
            src_ref=found.at[i, :, lanes(peer(j))],
            dst_ref=rep.at[i, :, lanes(me)],
            send_sem=send.at[i, j],
            recv_sem=recv.at[i, j],
            device_id=(section, peer(j)),
            device_id_type=pl.DeviceIdType.MESH,
        )

    pair[...] = jnp.zeros_like(pair)

    @pl.loop(0, fields // 2)
    def _(i):
        for h in range(2):
            hot = one_hot(arr_ref[pl.ds(2 * i + h, 1)], count)
            pair[40 * h : 40 * h + edim] = dot(table_ref[2 * i + h], hot)
        found[i] = pair[...].astype(BF)
        for j in range(1, 8):
            row_copy(i, j).start()
        rep[i, :, lanes(me)] = found[i, :, lanes(me)]

    @pl.loop(0, fields // 2)
    def _(i):
        for j in range(1, 8):
            row_copy(i, j).wait_recv()
        wide_rows[2 * i] = dot(rep[i, 0:48], one_hot(slots[pl.ds(2 * i, 1)], count))[0:40]
        wide_rows[2 * i + 1] = dot(rep[i, 32:80], one_hot(slots[pl.ds(2 * i + 1, 1)], count))[8:48]

    sparse, extra = fields * edim, dense_ref.shape[0]
    x0f[sparse // 8 * 8 :] = jnp.zeros_like(x0f[sparse // 8 * 8 :])
    for f in range(fields):
        x0f[f * edim : f * edim + edim] = wide_rows[f, :edim]
    x0f[sparse : sparse + extra] = dense_ref[...].astype(F32)
    x0_ref[...] = x0f[...].astype(BF)

    @pl.loop(0, fields // 2)
    def _(i):
        for j in range(1, 8):
            row_copy(i, j).wait_send()

    for j in range(1, 8):
        id_copy(j).wait_send()


def look_up(ids_t, table_t, dense_t):
    fields, count = ids_t.shape
    edim = table_t.shape[1]
    tall = -(-(fields * edim + dense_t.shape[0]) // 16) * 16
    vmem = pl.BlockSpec(memory_space=pltpu.VMEM)
    return pl.pallas_call(
        functools.partial(lookup_kernel, fields, edim),
        out_shape=[
            jax.ShapeDtypeStruct((tall, count), BF),
            jax.ShapeDtypeStruct((32, count), jnp.int32),
            jax.ShapeDtypeStruct((32, count), jnp.int32),
        ],
        in_specs=[vmem] * 3,
        out_specs=[vmem] * 3,
        scratch_shapes=[
            pltpu.VMEM((32, count), jnp.int32),
            pltpu.VMEM((32, count), jnp.int32),
            pltpu.VMEM((32, count), jnp.int32),
            pltpu.VMEM((fields // 2, 80, count), BF),
            pltpu.VMEM((fields // 2, 80, count), BF),
            pltpu.VMEM((80, count), F32),
            pltpu.VMEM((fields, 40, count), F32),
            pltpu.VMEM((tall, count), F32),
            pltpu.SemaphoreType.DMA((8,)),
            pltpu.SemaphoreType.DMA((8,)),
            pltpu.SemaphoreType.DMA((fields // 2, 8)),
            pltpu.SemaphoreType.DMA((fields // 2, 8)),
        ],
        compiler_params=pltpu.CompilerParams(
            collective_id=1, has_side_effects=True, vmem_limit_bytes=48 * 2**20
        ),
        name="look_up",
    )(ids_t, table_t, dense_t)


def body(
    ids,
    dense,
    labels,
    table,
    cross_weight,
    cross_bias,
    tower_in,
    tower_in_bias,
    tower_out,
    tower_out_bias,
    head_weight,
    head_bias,
):
    groups = lax.axis_size("dp")
    sections = lax.axis_size("section")
    device_count = groups * sections
    examples, fields = ids.shape
    table_rows, edim = table.shape[1:]
    layers, width = cross_weight.shape[:2]
    hidden = tower_out.shape[0]
    capacity = examples // groups
    sparse = fields * edim
    me = lax.axis_index("section") * groups + lax.axis_index("dp")

    idt = ids.T
    table_t = table.transpose(0, 2, 1)
    lane = jnp.arange(examples, dtype=jnp.int32)
    here = (sections, groups, capacity, table_rows) == (4, 8, 128, 1024)
    if here:
        x0, arrived, source = look_up(idt, table_t, dense.T)
        x0 = x0[:width]
        arrived, source = arrived[:fields], source[:fields]
    else:
        owner = idt // table_rows
        local = idt % table_rows
        owner_hot = owner[:, None, :] == jnp.arange(groups, dtype=jnp.int32)[None, :, None]
        before = (lane[:, None] < lane[None, :]).astype(BF)
        counts = mm(owner_hot.reshape(fields * groups, examples).astype(BF), before, (1, 0))
        rank = jnp.sum(jnp.where(owner_hot, counts.reshape(fields, groups, examples), 0.0), axis=1)
        slot = owner * capacity + rank.astype(jnp.int32)
        slot_hot = (slot[:, None, :] == lane[None, :, None]).astype(BF)
        values = [local // 32, local % 32] + [
            jnp.broadcast_to(part, idt.shape) for part in (lane // 32, lane % 32)
        ]
        sent = lax.dot_general(
            jnp.stack(values, axis=1).astype(BF),
            slot_hot,
            (((2,), (2,)), ((0,), (0,))),
            preferred_element_type=F32,
        )
        requests = (sent[:, 0] * 32 + sent[:, 1]).astype(jnp.int32)
        source = (sent[:, 2] * 32 + sent[:, 3]).astype(jnp.int32)
        requests = requests.reshape(fields, groups, capacity).transpose(1, 0, 2)
        arrived = lax.all_to_all(requests, "dp", 0, 0, tiled=True)
        arrived = arrived.transpose(1, 0, 2).reshape(fields, examples)
        row_hot = (
            arrived[:, None, :] == jnp.arange(table_rows, dtype=jnp.int32)[None, :, None]
        ).astype(BF)
        found = lax.dot_general(
            table_t, row_hot, (((2,), (1,)), ((0,), (0,))), preferred_element_type=F32
        ).astype(BF)
        found = found.reshape(sparse, groups, capacity).transpose(1, 0, 2)
        replies = lax.all_to_all(found, "dp", 0, 0, tiled=True)
        replies = replies.transpose(1, 0, 2).reshape(fields, edim, examples)
        embedded = lax.dot_general(
            replies, slot_hot, (((2,), (1,)), ((0,), (0,))), preferred_element_type=F32
        ).astype(BF)
        x0 = jnp.concatenate([embedded.reshape(sparse, examples), dense.T], axis=0)

    x0w = x0.astype(F32)
    xs, us = [x0], []
    for layer in range(layers):
        u = mm(cross_weight[layer], xs[-1], (0, 0)) + cross_bias[layer][:, None]
        us.append(u)
        xs.append((x0w * u + xs[-1].astype(F32)).astype(BF))
    p1 = mm(tower_in, x0, (0, 0)) + tower_in_bias[:, None]
    a1, d1 = gelu_parts(p1)
    h1 = a1.astype(BF)
    p2 = mm(tower_out, h1, (0, 0)) + tower_out_bias[:, None]
    h2, d2 = gelu_parts(p2)
    head_cross, head_tower = head_weight[:width], head_weight[width:]
    last = xs[-1].astype(F32)
    z = (
        jnp.sum(last * head_cross[:, None], axis=0)
        + jnp.sum(h2 * head_tower[:, None], axis=0)
        + head_bias[0]
    )
    probs = jax.nn.sigmoid(z)
    target = labels.astype(F32)
    loss = jnp.sum(jnp.logaddexp(0.0, z) - target * z)
    s = probs - target
    head_grad = jnp.concatenate([jnp.sum(s * last, axis=1), jnp.sum(s * h2, axis=1)])

    q2 = (s[None, :] * head_tower[:, None] * d2).astype(BF)
    tower_out_g = mm(q2, h1, (1, 1))
    q1 = (mm(tower_out, q2, (1, 0)) * d1).astype(BF)
    tower_in_g = mm(q1, x0, (1, 1))
    tower_biases = [jnp.sum(q1.astype(F32), axis=1), jnp.sum(q2.astype(F32), axis=1)]
    dx0 = mm(tower_in, q1, (1, 0))
    g = (s[None, :] * head_cross[:, None]).astype(BF)
    cross_g, cross_b = [None] * layers, [None] * layers
    for layer in reversed(range(layers)):
        gw = g.astype(F32)
        v = (gw * x0w).astype(BF)
        cross_g[layer] = mm(xs[layer], v, (1, 1))
        cross_b[layer] = jnp.sum(v.astype(F32), axis=1)
        dx0 = dx0 + gw * us[layer]
        g = gw + mm(cross_weight[layer], v, (1, 0))
        if layer:
            g = g.astype(BF)
    dx0 = dx0 + g

    packed = lax.dot_general(
        dx0[:sparse].astype(BF).reshape(fields, edim, examples),
        (source[:, None, :] == lane[None, :, None]).astype(BF),
        (((2,), (1,)), ((0,), (0,))),
        preferred_element_type=F32,
    ).astype(BF)
    packed = packed.reshape(sparse, groups, capacity).transpose(1, 0, 2)
    delivered = lax.all_to_all(packed, "dp", 0, 0, tiled=True)
    delivered = delivered.transpose(1, 0, 2).reshape(fields, edim, examples)
    row_hot = (
        arrived[:, :, None] == jnp.arange(table_rows, dtype=jnp.int32)[None, None, :]
    ).astype(BF)
    table_g = lax.dot_general(
        delivered, row_hot, (((2,), (1,)), ((0,), (0,))), preferred_element_type=F32
    )
    small = jnp.concatenate(
        cross_b + [head_grad, jnp.sum(s).reshape(1), loss.reshape(1)] + tower_biases
    )
    both = ("section", "dp")
    share = hidden // device_count
    main = hidden
    if here:
        edges = [jnp.concatenate([g[main:].reshape(-1), g[:main, main:].reshape(-1)]) for g in cross_g]
        edges.append(tower_in_g[:, main:].reshape(-1))
        flat = jnp.concatenate([small] + edges)
        filled = jnp.zeros((32 * 1024,), F32).at[: flat.shape[0]].set(flat)
        table_flat = jnp.pad(
            table_g.astype(BF).reshape(sparse, table_rows), ((0, 1024 - sparse), (0, 0))
        )
        whole, pieces32, table_sum, flat = reduce_all(
            [g[:main, :main].astype(BF) for g in cross_g]
            + [tower_in_g[:, :main].astype(BF), tower_out_g.astype(BF)],
            layers,
            table_flat,
            filled.reshape(32, 1024),
        )
        table_g = table_sum[:sparse].reshape(fields, edim, table_rows)
        at = small.shape[0]
        small = flat[:at]
        rest = width - main
        crosses = []
        for layer in range(layers):
            bottom = flat[at : at + rest * width].reshape(rest, width)
            at += rest * width
            side = flat[at : at + main * rest].reshape(main, rest)
            at += main * rest
            top = jnp.concatenate([whole[layer].astype(F32), side], axis=1)
            crosses.append(jnp.concatenate([top, bottom], axis=0))
        cross_out = jnp.stack(crosses)
        side = lax.dynamic_slice(
            flat[at : at + hidden * rest].reshape(hidden, rest), (me * share, 0), (share, rest)
        )
        tower_in_out = jnp.concatenate([pieces32[0], side], axis=1)
        tower_out_out = pieces32[1]
    else:
        table_g = lax.psum(table_g, "section")
        small = lax.psum(small, both)
        cross_out = lax.psum(jnp.stack(cross_g), both)
        tower_in_out = lax.psum_scatter(tower_in_g, both, scatter_dimension=0, tiled=True)
        tower_out_out = lax.psum_scatter(tower_out_g, both, scatter_dimension=0, tiled=True)
    table_g = table_g.astype(F32).transpose(0, 2, 1)
    sizes = [layers * width, width + hidden, 1, 1, hidden, hidden]
    ends = [sum(sizes[: i + 1]) for i in range(len(sizes))]
    pieces = [small[e - n : e] for e, n in zip(ends, sizes)]
    cross_b_out = pieces[0].reshape(layers, width)
    bias_in, bias_out = (lax.dynamic_slice(p, (me * share,), (share,)) for p in pieces[4:])
    return (
        probs,
        pieces[3] / (examples * device_count),
        dx0[sparse:].T,
        table_g,
        cross_out,
        cross_b_out,
        tower_in_out.T,
        bias_in,
        tower_out_out.T,
        bias_out,
        pieces[1],
        pieces[2],
    )


def solution(mesh):
    both = ("section", "dp")
    return jax.shard_map(
        body,
        mesh=mesh,
        in_specs=(P(both, None), P(both, None), P(both), P(None, "dp", None)) + (P(),) * 8,
        out_specs=(
            P(both),
            P(),
            P(both, None),
            P(None, "dp", None),
            P(),
            P(),
            P(None, both),
            P(both),
            P(None, both),
            P(both),
            P(),
            P(),
        ),
        check_vma=False,
    )
```

```python
import functools

import jax
import jax.numpy as jnp
from jax import lax
from jax.experimental import pallas as pl
from jax.experimental.pallas import tpu as pltpu
from jax.sharding import PartitionSpec as P

BF = jnp.bfloat16
F32 = jnp.float32


def mm(left, right, contract):
    return lax.dot_general(
        left, right, ((contract[:1], contract[1:]), ((), ())), preferred_element_type=F32
    )


def gelu_parts(pre):
    act, back = jax.vjp(jax.nn.gelu, pre)
    return act, back(jnp.ones_like(pre))[0]


VIEW = (2, 2, 4, 2)


def reduce_kernel(units, gathered, *refs):
    grads = refs[:units]
    rows_ref, inv_ref, arr_ref, small_ref = refs[units : units + 4]
    whole, pieces, table_out, small_out = refs[units + 4 : units + 8]
    (
        rc, sa1, ra1, sb1, rb1, sa2, ra2, sb2, rb2, sz, rz, packed, back, summed, stc, rtc, st, rt, sm, rm, rmz,
        send, recv, row_send, row_recv, table_send, table_recv,
    ) = refs[units + 8 :]
    pairs, count = rows_ref.shape[0], rows_ref.shape[2]
    section, dp = lax.axis_index("section"), lax.axis_index("dp")
    y, c = section // 2, section % 2
    z, x = dp // 2, dp % 2
    core_peer = (y * 2 + 1 - c, dp)
    y_peer = ((1 - y) * 2 + c, dp)
    x_peer = (section, z * 2 + 1 - x)
    half = 512
    lo, hi = pl.ds(0, half), pl.ds(half, half)

    def z_peer(j):
        return (section, lax.rem(z + j, 4) * 2 + x)

    def dp_peer(j):
        return (section, lax.rem(dp + j, 8))

    peers = [core_peer, y_peer] + [dp_peer(j) for j in range(1, 8)]
    barrier = pltpu.get_barrier_semaphore()
    for peer in peers:
        pl.semaphore_signal(barrier, inc=1, device_id=peer, device_id_type=pl.DeviceIdType.MESH)
    pl.semaphore_wait(barrier, len(peers))

    flying = []

    def start(src, dst, m, k, peer, sems=(send, recv)):
        copy = pltpu.make_async_remote_copy(
            src_ref=src,
            dst_ref=dst,
            send_sem=sems[0].at[m, k],
            recv_sem=sems[1].at[m, k],
            device_id=peer,
            device_id_type=pl.DeviceIdType.MESH,
        )
        copy.start()
        flying.append(copy)
        return copy

    def wide(value):
        return value.astype(F32)

    copies = {}

    def acc(m, stage, cols, yy, zz, xx):
        g = grads[m]
        total = wide(g[yy, c, zz, xx, :, cols]) + wide(rc[m, yy, zz, xx, :, cols])
        if cols is lo:
            if stage >= 2:
                total += wide(ra1[m, yy, zz])
            if stage >= 3:
                total += wide(ra2[m, zz])
        else:
            if stage >= 2:
                total += wide(rb1[m, zz, xx])
            if stage >= 3:
                total += wide(rb2[m, zz])
        return total

    def step0(m):
        copies[m, 0] = start(grads[m].at[:, 1 - c], rc.at[m], m, 0, core_peer)

    def step1(m):
        copies[m, 0].wait_recv()

        @pl.loop(0, 4)
        def _(zz):
            for i in range(2):
                sa1[m, i, zz] = acc(m, 1, lo, i, zz, 1 - x).astype(BF)
                sb1[m, zz, i] = acc(m, 1, hi, 1 - y, zz, i).astype(BF)

        copies[m, 1] = start(sa1.at[m], ra1.at[m], m, 1, x_peer)
        copies[m, 2] = start(sb1.at[m], rb1.at[m], m, 2, y_peer)

    def step2(m):
        copies[m, 1].wait_recv()
        copies[m, 2].wait_recv()

        @pl.loop(0, 4)
        def _(zz):
            sa2[m, zz] = acc(m, 2, lo, 1 - y, zz, x).astype(BF)
            sb2[m, zz] = acc(m, 2, hi, y, zz, 1 - x).astype(BF)

        copies[m, 3] = start(sa2.at[m], ra2.at[m], m, 3, y_peer)
        copies[m, 4] = start(sb2.at[m], rb2.at[m], m, 4, x_peer)

    def step3(m):
        copies[m, 3].wait_recv()
        copies[m, 4].wait_recv()
        for j in (1, 2, 3):
            zz = lax.rem(z + j, 4)
            sz[m, j - 1, :, lo] = acc(m, 3, lo, y, zz, x).astype(BF)
            sz[m, j - 1, :, hi] = acc(m, 3, hi, y, zz, x).astype(BF)
            copies[m, 4 + j] = start(sz.at[m, j - 1], rz.at[m, j - 1], m, 4 + j, z_peer(j))

    def step4(m):
        for j in (1, 2, 3):
            copies[m, 4 + j].wait_recv()
        for cols in (lo, hi):
            total = acc(m, 3, cols, y, z, x)
            for j in range(3):
                total += wide(rz[m, j, :, cols])
            if m < gathered:
                whole[m, y, c, z, x, :, cols] = total.astype(BF)
            else:
                pieces[m - gathered, :, cols] = total
        if m < gathered:
            for j in (1, 2, 3):
                mine = whole.at[m, y, c, z, x]
                copies[m, 7 + j] = start(mine, mine, m, 7 + j, z_peer(j))

    def step5(m):
        for j in (1, 2, 3):
            copies[m, 7 + j].wait_recv()
        ours = whole.at[m, y, c, :, x, :, lo]
        copies[m, 11] = start(ours, ours, m, 11, y_peer)
        ours = whole.at[m, y, c, :, x, :, hi]
        copies[m, 12] = start(ours, ours, m, 12, x_peer)

    def step6(m):
        copies[m, 11].wait_recv()
        copies[m, 12].wait_recv()
        ours = whole.at[m, :, c, :, x, :, lo]
        copies[m, 13] = start(ours, ours, m, 13, x_peer)
        ours = whole.at[m, y, c, :, :, :, hi]
        copies[m, 14] = start(ours, ours, m, 14, y_peer)

    def step7(m):
        copies[m, 13].wait_recv()
        copies[m, 14].wait_recv()
        ours = whole.at[m, :, c]
        copies[m, 15] = start(ours, ours, m, 15, core_peer)

    def step8(m):
        copies[m, 15].wait_recv()

    def lanes(place, size):
        return pl.ds(pl.multiple_of(place * size, size), size)

    def row_copy(i, j):
        return pltpu.make_async_remote_copy(
            src_ref=packed.at[i, :, lanes(lax.rem(dp + j, 8), 128)],
            dst_ref=back.at[i, :, lanes(dp, 128)],
            send_sem=row_send.at[i, j],
            recv_sem=row_recv.at[i, j],
            device_id=dp_peer(j),
            device_id_type=pl.DeviceIdType.MESH,
        )

    def pack():
        @pl.loop(0, pairs)
        def _(i):
            first = jnp.dot(
                rows_ref[i, 0:48],
                one_hot(inv_ref[pl.ds(2 * i, 1)], count),
                preferred_element_type=F32,
            )
            second = jnp.dot(
                rows_ref[i, 32:80],
                one_hot(inv_ref[pl.ds(2 * i + 1, 1)], count),
                preferred_element_type=F32,
            )
            packed[i] = jnp.concatenate([first[0:40], second[8:48]], axis=0).astype(BF)
            for j in range(1, 8):
                row_copy(i, j).start()
            back[i, :, lanes(dp, 128)] = packed[i, :, lanes(dp, 128)]

    cuts = [pairs * q // 4 for q in range(5)]

    def scatter(q):
        @pl.loop(cuts[q], cuts[q + 1])
        def _(i):
            for j in range(1, 8):
                row_copy(i, j).wait_recv()
            for h, (low, at) in enumerate(((0, 0), (32, 8))):
                total = lax.dot_general(
                    back[i, low : low + 48],
                    one_hot(arr_ref[pl.ds(2 * i + h, 1)], count),
                    (((1,), (1,)), ((), ())),
                    preferred_element_type=F32,
                )
                summed[i, 40 * h : 40 * h + 40] = total[at : at + 40]
            stc[i] = summed[i, :, lanes(1 - c, half)].astype(BF)

        part = pl.ds(cuts[q], cuts[q + 1] - cuts[q])
        copies["t", q, 0] = start(stc.at[part], rtc.at[part], q, 0, core_peer, (table_send, table_recv))

    quarter = half // 2

    def quarter_of(yy):
        return lanes(2 * c + yy, quarter)

    def table1(q):
        copies["t", q, 0].wait_recv()

        @pl.loop(cuts[q], cuts[q + 1])
        def _(i):
            st[i] = (summed[i, :, quarter_of(1 - y)] + wide(rtc[i, :, lanes(1 - y, quarter)])).astype(BF)

        part = pl.ds(cuts[q], cuts[q + 1] - cuts[q])
        copies["t", q, 1] = start(st.at[part], rt.at[part], q, 1, y_peer, (table_send, table_recv))

    def table2(q):
        copies["t", q, 1].wait_recv()

        @pl.loop(cuts[q], cuts[q + 1])
        def _(i):
            total = summed[i, :, quarter_of(y)] + wide(rtc[i, :, lanes(y, quarter)]) + wide(rt[i])
            table_out[i, :, quarter_of(y)] = total.astype(BF)

        part = pl.ds(cuts[q], cuts[q + 1] - cuts[q])
        ours = table_out.at[part, :, quarter_of(y)]
        copies["t", q, 2] = start(ours, ours, q, 2, y_peer, (table_send, table_recv))

    def table3(q):
        copies["t", q, 2].wait_recv()
        part = pl.ds(cuts[q], cuts[q + 1] - cuts[q])
        ours = table_out.at[part, :, lanes(c, half)]
        copies["t", q, 3] = start(ours, ours, q, 3, core_peer, (table_send, table_recv))

    def table4(q):
        copies["t", q, 3].wait_recv()

    s = units

    def small0():
        copies[s, 0] = start(small_ref.at[1 - c], rm.at[0], s, 0, core_peer)

    def small1():
        copies[s, 0].wait_recv()
        sm[0] = small_ref[c] + rm[0]
        copies[s, 1] = start(sm.at[0], rm.at[1], s, 1, x_peer)

    def small2():
        copies[s, 1].wait_recv()
        sm[1] = sm[0] + rm[1]
        copies[s, 2] = start(sm.at[1], rm.at[2], s, 2, y_peer)

    def small3():
        copies[s, 2].wait_recv()
        sm[2] = sm[1] + rm[2]
        for j in (1, 2, 3):
            copies[s, 2 + j] = start(sm.at[2], rmz.at[j - 1], s, 2 + j, z_peer(j))

    def small4():
        for j in (1, 2, 3):
            copies[s, 2 + j].wait_recv()
        even = lax.rem(z, 2)
        near = [sm[2], rmz[0], rmz[1], rmz[2]]
        first = near[0] + near[2]
        second = near[1] + near[3]
        small_out[c] = jnp.where(even == 0, first, second) + jnp.where(even == 0, second, first)
        ours = small_out.at[c]
        copies[s, 6] = start(ours, ours, s, 6, core_peer)

    def small5():
        copies[s, 6].wait_recv()

    small0()
    for m in range(units):
        step0(m)
    pack()
    steps = [step1, step2, step3, step4, step5, step6, step7, step8]
    smalls = [small1, small2, small3, small4, small5]
    tables = [scatter, table1, table2, table3, table4]
    for now in range(units + len(steps)):
        for k, step in enumerate(steps):
            m = now - k
            if 0 <= m < units and (k < 4 or m < gathered):
                step(m)
        if now < len(smalls):
            smalls[now]()
        for k in reversed(range(len(tables))):
            q = now - 1 - k
            if 0 <= q < 4:
                tables[k](q)
    for copy in flying:
        copy.wait_send()

    @pl.loop(0, pairs)
    def _(i):
        for j in range(1, 8):
            row_copy(i, j).wait_send()


def reduce_all(grads, gathered, rows, source, arrived, small):
    units = len(grads)
    pairs, _, count = rows.shape
    piece = (32, 1024)
    vmem = pl.BlockSpec(memory_space=pltpu.VMEM)
    whole, pieces, table_sum, small_sum = pl.pallas_call(
        lambda *refs: reduce_kernel(units, gathered, *refs),
        out_shape=[
            jax.ShapeDtypeStruct((gathered,) + VIEW + piece, BF),
            jax.ShapeDtypeStruct((units - gathered,) + piece, F32),
            jax.ShapeDtypeStruct((pairs, 80, count), BF),
            jax.ShapeDtypeStruct((2, 16, 1024), F32),
        ],
        in_specs=[vmem] * (units + 4),
        out_specs=[vmem] * 4,
        scratch_shapes=[
            pltpu.VMEM((units, 2, 4, 2) + piece, BF),
            pltpu.VMEM((units, 2, 4, 32, 512), BF),
            pltpu.VMEM((units, 2, 4, 32, 512), BF),
            pltpu.VMEM((units, 4, 2, 32, 512), BF),
            pltpu.VMEM((units, 4, 2, 32, 512), BF),
            pltpu.VMEM((units, 4, 32, 512), BF),
            pltpu.VMEM((units, 4, 32, 512), BF),
            pltpu.VMEM((units, 4, 32, 512), BF),
            pltpu.VMEM((units, 4, 32, 512), BF),
            pltpu.VMEM((units, 3) + piece, BF),
            pltpu.VMEM((units, 3) + piece, BF),
            pltpu.VMEM((pairs, 80, count), BF),
            pltpu.VMEM((pairs, 80, count), BF),
            pltpu.VMEM((pairs, 80, count), F32),
            pltpu.VMEM((pairs, 80, count // 2), BF),
            pltpu.VMEM((pairs, 80, count // 2), BF),
            pltpu.VMEM((pairs, 80, count // 4), BF),
            pltpu.VMEM((pairs, 80, count // 4), BF),
            pltpu.VMEM((3, 16, 1024), F32),
            pltpu.VMEM((3, 16, 1024), F32),
            pltpu.VMEM((3, 16, 1024), F32),
            pltpu.SemaphoreType.DMA((units + 1, 16)),
            pltpu.SemaphoreType.DMA((units + 1, 16)),
            pltpu.SemaphoreType.DMA((pairs, 8)),
            pltpu.SemaphoreType.DMA((pairs, 8)),
            pltpu.SemaphoreType.DMA((4, 4)),
            pltpu.SemaphoreType.DMA((4, 4)),
        ],
        compiler_params=pltpu.CompilerParams(
            collective_id=0, has_side_effects=True, vmem_limit_bytes=60 * 2**20
        ),
        name="reduce_all",
    )(
        *[g.reshape(VIEW + piece) for g in grads],
        rows,
        source,
        arrived,
        small.reshape(2, 16, 1024),
    )
    return whole.reshape(gathered, 1024, 1024), pieces, table_sum, small_sum.reshape(-1)


def one_hot(places, count):
    rows = lax.broadcasted_iota(jnp.int32, (count, places.shape[1]), 0)
    return (rows == places).astype(F32).astype(BF)


def lookup_kernel(
    fields, edim, ids_ref, table_ref, dense_ref, x0_ref, arr_ref, inv_ref,
    ids, slots, req, found, rep, pair, wide_rows, x0f, id_send, id_recv, send, recv,
):
    section, me = lax.axis_index("section"), lax.axis_index("dp")
    dot = functools.partial(jnp.dot, preferred_element_type=F32)
    count = ids.shape[1]

    def peer(j):
        return lax.rem(me + j, 8)

    def lanes(place):
        return pl.ds(pl.multiple_of(place * 128, 128), 128)

    barrier = pltpu.get_barrier_semaphore()
    for j in range(1, 8):
        pl.semaphore_signal(
            barrier, inc=1, device_id=(section, peer(j)), device_id_type=pl.DeviceIdType.MESH
        )

    ids[...] = jnp.zeros_like(ids)
    ids[:fields] = ids_ref[...]
    every = ids[...]
    owner = lax.shift_right_logical(every, 10)
    hot = jnp.concatenate([(owner == o).astype(F32) for o in range(8)], axis=0).astype(BF)
    before = (
        lax.broadcasted_iota(jnp.int32, (count, count), 0)
        < lax.broadcasted_iota(jnp.int32, (count, count), 1)
    )
    ranks = dot(hot, before.astype(F32).astype(BF))
    rank = jnp.zeros((32, count), F32)
    for o in range(8):
        rank = jnp.where(owner == o, ranks[32 * o : 32 * o + 32], rank)
    slots[...] = owner * 128 + rank.astype(jnp.int32)
    ids[...] = every & 1023
    @pl.loop(0, 4)
    def _(group):
        eight = pl.ds(pl.multiple_of(8 * group, 8), 8)
        slot8, local8 = slots[eight], ids[eight]
        place = lax.broadcasted_iota(jnp.int32, (1, count), 1)
        column = lax.broadcasted_iota(jnp.int32, (8, count), 0)
        wanted, source = [], []
        for k in range(8):
            slot, local = slot8[k : k + 1], local8[k : k + 1]
            owners = column == lax.shift_right_logical(slot, 7)
            parts = [local >> 5, local & 31, place >> 5, place & 31]
            left = jnp.concatenate(
                [jnp.where(owners, p.astype(F32), 0.0) for p in parts], axis=0
            ).astype(BF)
            right = one_hot(slot & 127, 128)
            sent = lax.dot_general(
                left, right, (((1,), (1,)), ((), ())), preferred_element_type=F32
            )
            rows = [
                (sent[n : n + 8] * 32 + sent[n + 8 : n + 16]).astype(jnp.int32) for n in (0, 16)
            ]
            for taken, r in zip((wanted, source), rows):
                taken.append(jnp.concatenate([r[o : o + 1] for o in range(8)], axis=1))
        req[eight] = jnp.concatenate(wanted, axis=0)
        inv_ref[eight] = jnp.concatenate(source, axis=0)

    def id_copy(j):
        return pltpu.make_async_remote_copy(
            src_ref=req.at[:, lanes(peer(j))],
            dst_ref=arr_ref.at[:, lanes(me)],
            send_sem=id_send.at[j],
            recv_sem=id_recv.at[j],
            device_id=(section, peer(j)),
            device_id_type=pl.DeviceIdType.MESH,
        )

    pl.semaphore_wait(barrier, 7)
    for j in range(1, 8):
        id_copy(j).start()
    arr_ref[:, lanes(me)] = req[:, lanes(me)]
    for j in range(1, 8):
        id_copy(j).wait_recv()

    def row_copy(i, j):
        return pltpu.make_async_remote_copy(
            src_ref=found.at[i, :, lanes(peer(j))],
            dst_ref=rep.at[i, :, lanes(me)],
            send_sem=send.at[i, j],
            recv_sem=recv.at[i, j],
            device_id=(section, peer(j)),
            device_id_type=pl.DeviceIdType.MESH,
        )

    pair[...] = jnp.zeros_like(pair)

    @pl.loop(0, fields // 2)
    def _(i):
        for h in range(2):
            hot = one_hot(arr_ref[pl.ds(2 * i + h, 1)], count)
            pair[40 * h : 40 * h + edim] = dot(table_ref[2 * i + h], hot)
        found[i] = pair[...].astype(BF)
        for j in range(1, 8):
            row_copy(i, j).start()
        rep[i, :, lanes(me)] = found[i, :, lanes(me)]

    @pl.loop(0, fields // 2)
    def _(i):
        for j in range(1, 8):
            row_copy(i, j).wait_recv()
        wide_rows[2 * i] = dot(rep[i, 0:48], one_hot(slots[pl.ds(2 * i, 1)], count))[0:40]
        wide_rows[2 * i + 1] = dot(rep[i, 32:80], one_hot(slots[pl.ds(2 * i + 1, 1)], count))[8:48]

    sparse, extra = fields * edim, dense_ref.shape[0]
    x0f[sparse // 8 * 8 :] = jnp.zeros_like(x0f[sparse // 8 * 8 :])
    for f in range(fields):
        x0f[f * edim : f * edim + edim] = wide_rows[f, :edim]
    x0f[sparse : sparse + extra] = dense_ref[...].astype(F32)
    x0_ref[...] = x0f[...].astype(BF)

    @pl.loop(0, fields // 2)
    def _(i):
        for j in range(1, 8):
            row_copy(i, j).wait_send()

    for j in range(1, 8):
        id_copy(j).wait_send()


def look_up(ids_t, table_t, dense_t):
    fields, count = ids_t.shape
    edim = table_t.shape[1]
    tall = -(-(fields * edim + dense_t.shape[0]) // 16) * 16
    vmem = pl.BlockSpec(memory_space=pltpu.VMEM)
    return pl.pallas_call(
        functools.partial(lookup_kernel, fields, edim),
        out_shape=[
            jax.ShapeDtypeStruct((tall, count), BF),
            jax.ShapeDtypeStruct((32, count), jnp.int32),
            jax.ShapeDtypeStruct((32, count), jnp.int32),
        ],
        in_specs=[vmem] * 3,
        out_specs=[vmem] * 3,
        scratch_shapes=[
            pltpu.VMEM((32, count), jnp.int32),
            pltpu.VMEM((32, count), jnp.int32),
            pltpu.VMEM((32, count), jnp.int32),
            pltpu.VMEM((fields // 2, 80, count), BF),
            pltpu.VMEM((fields // 2, 80, count), BF),
            pltpu.VMEM((80, count), F32),
            pltpu.VMEM((fields, 40, count), F32),
            pltpu.VMEM((tall, count), F32),
            pltpu.SemaphoreType.DMA((8,)),
            pltpu.SemaphoreType.DMA((8,)),
            pltpu.SemaphoreType.DMA((fields // 2, 8)),
            pltpu.SemaphoreType.DMA((fields // 2, 8)),
        ],
        compiler_params=pltpu.CompilerParams(
            collective_id=1, has_side_effects=True, vmem_limit_bytes=48 * 2**20
        ),
        name="look_up",
    )(ids_t, table_t, dense_t)


def body(
    ids,
    dense,
    labels,
    table,
    cross_weight,
    cross_bias,
    tower_in,
    tower_in_bias,
    tower_out,
    tower_out_bias,
    head_weight,
    head_bias,
):
    groups = lax.axis_size("dp")
    sections = lax.axis_size("section")
    device_count = groups * sections
    examples, fields = ids.shape
    table_rows, edim = table.shape[1:]
    layers, width = cross_weight.shape[:2]
    hidden = tower_out.shape[0]
    capacity = examples // groups
    sparse = fields * edim
    me = lax.axis_index("section") * groups + lax.axis_index("dp")

    idt = ids.T
    table_t = table.transpose(0, 2, 1)
    lane = jnp.arange(examples, dtype=jnp.int32)
    here = (sections, groups, capacity, table_rows) == (4, 8, 128, 1024)
    if here:
        x0, arrived, source = look_up(idt, table_t, dense.T)
        x0 = x0[:width]
    else:
        owner = idt // table_rows
        local = idt % table_rows
        owner_hot = owner[:, None, :] == jnp.arange(groups, dtype=jnp.int32)[None, :, None]
        before = (lane[:, None] < lane[None, :]).astype(BF)
        counts = mm(owner_hot.reshape(fields * groups, examples).astype(BF), before, (1, 0))
        rank = jnp.sum(jnp.where(owner_hot, counts.reshape(fields, groups, examples), 0.0), axis=1)
        slot = owner * capacity + rank.astype(jnp.int32)
        slot_hot = (slot[:, None, :] == lane[None, :, None]).astype(BF)
        values = [local // 32, local % 32] + [
            jnp.broadcast_to(part, idt.shape) for part in (lane // 32, lane % 32)
        ]
        sent = lax.dot_general(
            jnp.stack(values, axis=1).astype(BF),
            slot_hot,
            (((2,), (2,)), ((0,), (0,))),
            preferred_element_type=F32,
        )
        requests = (sent[:, 0] * 32 + sent[:, 1]).astype(jnp.int32)
        source = (sent[:, 2] * 32 + sent[:, 3]).astype(jnp.int32)
        requests = requests.reshape(fields, groups, capacity).transpose(1, 0, 2)
        arrived = lax.all_to_all(requests, "dp", 0, 0, tiled=True)
        arrived = arrived.transpose(1, 0, 2).reshape(fields, examples)
        row_hot = (
            arrived[:, None, :] == jnp.arange(table_rows, dtype=jnp.int32)[None, :, None]
        ).astype(BF)
        found = lax.dot_general(
            table_t, row_hot, (((2,), (1,)), ((0,), (0,))), preferred_element_type=F32
        ).astype(BF)
        found = found.reshape(sparse, groups, capacity).transpose(1, 0, 2)
        replies = lax.all_to_all(found, "dp", 0, 0, tiled=True)
        replies = replies.transpose(1, 0, 2).reshape(fields, edim, examples)
        embedded = lax.dot_general(
            replies, slot_hot, (((2,), (1,)), ((0,), (0,))), preferred_element_type=F32
        ).astype(BF)
        x0 = jnp.concatenate([embedded.reshape(sparse, examples), dense.T], axis=0)

    x0w = x0.astype(F32)
    xs, us = [x0], []
    for layer in range(layers):
        u = mm(cross_weight[layer], xs[-1], (0, 0)) + cross_bias[layer][:, None]
        us.append(u)
        xs.append((x0w * u + xs[-1].astype(F32)).astype(BF))
    p1 = mm(tower_in, x0, (0, 0)) + tower_in_bias[:, None]
    a1, d1 = gelu_parts(p1)
    h1 = a1.astype(BF)
    p2 = mm(tower_out, h1, (0, 0)) + tower_out_bias[:, None]
    h2, d2 = gelu_parts(p2)
    head_cross, head_tower = head_weight[:width], head_weight[width:]
    last = xs[-1].astype(F32)
    z = (
        jnp.sum(last * head_cross[:, None], axis=0)
        + jnp.sum(h2 * head_tower[:, None], axis=0)
        + head_bias[0]
    )
    probs = jax.nn.sigmoid(z)
    target = labels.astype(F32)
    loss = jnp.sum(jnp.logaddexp(0.0, z) - target * z)
    s = probs - target
    head_grad = jnp.concatenate([jnp.sum(s * last, axis=1), jnp.sum(s * h2, axis=1)])

    q2 = (s[None, :] * head_tower[:, None] * d2).astype(BF)
    tower_out_g = mm(q2, h1, (1, 1))
    q1 = (mm(tower_out, q2, (1, 0)) * d1).astype(BF)
    tower_in_g = mm(q1, x0, (1, 1))
    tower_biases = [jnp.sum(q1.astype(F32), axis=1), jnp.sum(q2.astype(F32), axis=1)]
    dx0 = mm(tower_in, q1, (1, 0))
    g = (s[None, :] * head_cross[:, None]).astype(BF)
    cross_g, cross_b = [None] * layers, [None] * layers
    for layer in reversed(range(layers)):
        gw = g.astype(F32)
        v = (gw * x0w).astype(BF)
        cross_g[layer] = mm(xs[layer], v, (1, 1))
        cross_b[layer] = jnp.sum(v.astype(F32), axis=1)
        dx0 = dx0 + gw * us[layer]
        g = gw + mm(cross_weight[layer], v, (1, 0))
        if layer:
            g = g.astype(BF)
    dx0 = dx0 + g

    small = jnp.concatenate(
        cross_b + [head_grad, jnp.sum(s).reshape(1), loss.reshape(1)] + tower_biases
    )
    both = ("section", "dp")
    share = hidden // device_count
    main = hidden
    if here:
        edges = [jnp.concatenate([g[main:].reshape(-1), g[:main, main:].reshape(-1)]) for g in cross_g]
        edges.append(tower_in_g[:, main:].reshape(-1))
        flat = jnp.concatenate([small] + edges)
        filled = jnp.zeros((32 * 1024,), F32).at[: flat.shape[0]].set(flat)
        rows = jnp.pad(
            dx0[:sparse].astype(BF).reshape(fields, edim, examples),
            ((0, 0), (0, 40 - edim), (0, 0)),
        ).reshape(fields // 2, 80, examples)
        whole, pieces32, table_sum, flat = reduce_all(
            [g[:main, :main].astype(BF) for g in cross_g]
            + [tower_in_g[:, :main].astype(BF), tower_out_g.astype(BF)],
            layers,
            rows,
            source,
            arrived,
            filled.reshape(32, 1024),
        )
        table_g = table_sum.reshape(fields, 40, table_rows)[:, :edim]
        at = small.shape[0]
        small = flat[:at]
        rest = width - main
        crosses = []
        for layer in range(layers):
            bottom = flat[at : at + rest * width].reshape(rest, width)
            at += rest * width
            side = flat[at : at + main * rest].reshape(main, rest)
            at += main * rest
            top = jnp.concatenate([whole[layer].astype(F32), side], axis=1)
            crosses.append(jnp.concatenate([top, bottom], axis=0))
        cross_out = jnp.stack(crosses)
        side = lax.dynamic_slice(
            flat[at : at + hidden * rest].reshape(hidden, rest), (me * share, 0), (share, rest)
        )
        tower_in_out = jnp.concatenate([pieces32[0], side], axis=1)
        tower_out_out = pieces32[1]
    else:
        packed = lax.dot_general(
            dx0[:sparse].astype(BF).reshape(fields, edim, examples),
            (source[:, None, :] == lane[None, :, None]).astype(BF),
            (((2,), (1,)), ((0,), (0,))),
            preferred_element_type=F32,
        ).astype(BF)
        packed = packed.reshape(sparse, groups, capacity).transpose(1, 0, 2)
        delivered = lax.all_to_all(packed, "dp", 0, 0, tiled=True)
        delivered = delivered.transpose(1, 0, 2).reshape(fields, edim, examples)
        row_hot = (
            arrived[:, :, None] == jnp.arange(table_rows, dtype=jnp.int32)[None, None, :]
        ).astype(BF)
        table_g = lax.dot_general(
            delivered, row_hot, (((2,), (1,)), ((0,), (0,))), preferred_element_type=F32
        )
        table_g = lax.psum(table_g, "section")
        small = lax.psum(small, both)
        cross_out = lax.psum(jnp.stack(cross_g), both)
        tower_in_out = lax.psum_scatter(tower_in_g, both, scatter_dimension=0, tiled=True)
        tower_out_out = lax.psum_scatter(tower_out_g, both, scatter_dimension=0, tiled=True)
    table_g = table_g.astype(F32).transpose(0, 2, 1)
    sizes = [layers * width, width + hidden, 1, 1, hidden, hidden]
    ends = [sum(sizes[: i + 1]) for i in range(len(sizes))]
    pieces = [small[e - n : e] for e, n in zip(ends, sizes)]
    cross_b_out = pieces[0].reshape(layers, width)
    bias_in, bias_out = (lax.dynamic_slice(p, (me * share,), (share,)) for p in pieces[4:])
    return (
        probs,
        pieces[3] / (examples * device_count),
        dx0[sparse:].T,
        table_g,
        cross_out,
        cross_b_out,
        tower_in_out.T,
        bias_in,
        tower_out_out.T,
        bias_out,
        pieces[1],
        pieces[2],
    )


def solution(mesh):
    both = ("section", "dp")
    return jax.shard_map(
        body,
        mesh=mesh,
        in_specs=(P(both, None), P(both, None), P(both), P(None, "dp", None)) + (P(),) * 8,
        out_specs=(
            P(both),
            P(),
            P(both, None),
            P(None, "dp", None),
            P(),
            P(),
            P(None, both),
            P(both),
            P(None, both),
            P(both),
            P(),
            P(),
        ),
        check_vma=False,
    )
```

```python
import functools
import math

import jax
import jax.numpy as jnp
from jax import lax
from jax.experimental import pallas as pl
from jax.experimental.pallas import tpu as pltpu
from jax.sharding import PartitionSpec as P

BF = jnp.bfloat16
F32 = jnp.float32


def mm(left, right, contract):
    return lax.dot_general(
        left, right, ((contract[:1], contract[1:]), ((), ())), preferred_element_type=F32
    )


def gelu_parts(pre):
    act, back = jax.vjp(jax.nn.gelu, pre)
    return act, back(jnp.ones_like(pre))[0]


VIEW = (2, 2, 4, 2)


def reduce_kernel(units, gathered, *refs):
    grads = refs[:units]
    rows_ref, inv_ref, arr_ref, small_ref = refs[units : units + 4]
    whole, pieces, table_out, small_out = refs[units + 4 : units + 8]
    (
        rc, sa1, ra1, sb1, rb1, sa2, ra2, sb2, rb2, sz, rz, packed, back, summed, stc, rtc, st, rt, sm, rm, rmz,
        send, recv, row_send, row_recv, table_send, table_recv,
    ) = refs[units + 8 :]
    pairs, count = rows_ref.shape[0], rows_ref.shape[2]
    section, dp = lax.axis_index("section"), lax.axis_index("dp")
    y, c = section // 2, section % 2
    z, x = dp // 2, dp % 2
    core_peer = (y * 2 + 1 - c, dp)
    y_peer = ((1 - y) * 2 + c, dp)
    x_peer = (section, z * 2 + 1 - x)
    half = 512
    lo, hi = pl.ds(0, half), pl.ds(half, half)

    def z_peer(j):
        return (section, lax.rem(z + j, 4) * 2 + x)

    def dp_peer(j):
        return (section, lax.rem(dp + j, 8))

    peers = [core_peer, y_peer] + [dp_peer(j) for j in range(1, 8)]
    barrier = pltpu.get_barrier_semaphore()
    for peer in peers:
        pl.semaphore_signal(barrier, inc=1, device_id=peer, device_id_type=pl.DeviceIdType.MESH)
    pl.semaphore_wait(barrier, len(peers))

    flying = []

    def start(src, dst, m, k, peer, sems=(send, recv)):
        copy = pltpu.make_async_remote_copy(
            src_ref=src,
            dst_ref=dst,
            send_sem=sems[0].at[m, k],
            recv_sem=sems[1].at[m, k],
            device_id=peer,
            device_id_type=pl.DeviceIdType.MESH,
        )
        copy.start()
        flying.append(copy)
        return copy

    def wide(value):
        return value.astype(F32)

    copies = {}

    def acc(m, stage, cols, yy, zz, xx):
        g = grads[m]
        total = wide(g[yy, c, zz, xx, :, cols]) + wide(rc[m, yy, zz, xx, :, cols])
        if cols is lo:
            if stage >= 2:
                total += wide(ra1[m, yy, zz])
            if stage >= 3:
                total += wide(ra2[m, zz])
        else:
            if stage >= 2:
                total += wide(rb1[m, zz, xx])
            if stage >= 3:
                total += wide(rb2[m, zz])
        return total

    def step0(m):
        copies[m, 0] = start(grads[m].at[:, 1 - c], rc.at[m], m, 0, core_peer)

    def step1(m):
        copies[m, 0].wait_recv()

        @pl.loop(0, 4)
        def _(zz):
            for i in range(2):
                sa1[m, i, zz] = acc(m, 1, lo, i, zz, 1 - x).astype(BF)
                sb1[m, zz, i] = acc(m, 1, hi, 1 - y, zz, i).astype(BF)

        copies[m, 1] = start(sa1.at[m], ra1.at[m], m, 1, x_peer)
        copies[m, 2] = start(sb1.at[m], rb1.at[m], m, 2, y_peer)

    def step2(m):
        copies[m, 1].wait_recv()
        copies[m, 2].wait_recv()

        @pl.loop(0, 4)
        def _(zz):
            sa2[m, zz] = acc(m, 2, lo, 1 - y, zz, x).astype(BF)
            sb2[m, zz] = acc(m, 2, hi, y, zz, 1 - x).astype(BF)

        copies[m, 3] = start(sa2.at[m], ra2.at[m], m, 3, y_peer)
        copies[m, 4] = start(sb2.at[m], rb2.at[m], m, 4, x_peer)

    def step3(m):
        copies[m, 3].wait_recv()
        copies[m, 4].wait_recv()
        for j in (1, 2, 3):
            zz = lax.rem(z + j, 4)
            sz[m, j - 1, :, lo] = acc(m, 3, lo, y, zz, x).astype(BF)
            sz[m, j - 1, :, hi] = acc(m, 3, hi, y, zz, x).astype(BF)
            copies[m, 4 + j] = start(sz.at[m, j - 1], rz.at[m, j - 1], m, 4 + j, z_peer(j))

    def step4(m):
        for j in (1, 2, 3):
            copies[m, 4 + j].wait_recv()
        for cols in (lo, hi):
            total = acc(m, 3, cols, y, z, x)
            for j in range(3):
                total += wide(rz[m, j, :, cols])
            if m < gathered:
                whole[m, y, c, z, x, :, cols] = total.astype(BF)
            else:
                pieces[m - gathered, :, cols] = total
        if m < gathered:
            for j in (1, 2, 3):
                mine = whole.at[m, y, c, z, x]
                copies[m, 7 + j] = start(mine, mine, m, 7 + j, z_peer(j))

    def step5(m):
        for j in (1, 2, 3):
            copies[m, 7 + j].wait_recv()
        ours = whole.at[m, y, c, :, x, :, lo]
        copies[m, 11] = start(ours, ours, m, 11, y_peer)
        ours = whole.at[m, y, c, :, x, :, hi]
        copies[m, 12] = start(ours, ours, m, 12, x_peer)

    def step6(m):
        copies[m, 11].wait_recv()
        copies[m, 12].wait_recv()
        ours = whole.at[m, :, c, :, x, :, lo]
        copies[m, 13] = start(ours, ours, m, 13, x_peer)
        ours = whole.at[m, y, c, :, :, :, hi]
        copies[m, 14] = start(ours, ours, m, 14, y_peer)

    def step7(m):
        copies[m, 13].wait_recv()
        copies[m, 14].wait_recv()
        ours = whole.at[m, :, c]
        copies[m, 15] = start(ours, ours, m, 15, core_peer)

    def step8(m):
        copies[m, 15].wait_recv()

    def lanes(place, size):
        return pl.ds(pl.multiple_of(place * size, size), size)

    def row_copy(i, j):
        return pltpu.make_async_remote_copy(
            src_ref=packed.at[i, :, lanes(lax.rem(dp + j, 8), 128)],
            dst_ref=back.at[i, :, lanes(dp, 128)],
            send_sem=row_send.at[i, j],
            recv_sem=row_recv.at[i, j],
            device_id=dp_peer(j),
            device_id_type=pl.DeviceIdType.MESH,
        )

    def pack():
        @pl.loop(0, pairs)
        def _(i):
            first = jnp.dot(
                rows_ref[i, 0:48],
                one_hot(inv_ref[pl.ds(2 * i, 1)], count),
                preferred_element_type=F32,
            )
            second = jnp.dot(
                rows_ref[i, 32:80],
                one_hot(inv_ref[pl.ds(2 * i + 1, 1)], count),
                preferred_element_type=F32,
            )
            packed[i] = jnp.concatenate([first[0:40], second[8:48]], axis=0).astype(BF)
            for j in range(1, 8):
                row_copy(i, j).start()
            back[i, :, lanes(dp, 128)] = packed[i, :, lanes(dp, 128)]

    cuts = [pairs * q // 4 for q in range(5)]

    def scatter(q):
        @pl.loop(cuts[q], cuts[q + 1])
        def _(i):
            for j in range(1, 8):
                row_copy(i, j).wait_recv()
            for h, (low, at) in enumerate(((0, 0), (32, 8))):
                total = lax.dot_general(
                    back[i, low : low + 48],
                    one_hot(arr_ref[pl.ds(2 * i + h, 1)], count),
                    (((1,), (1,)), ((), ())),
                    preferred_element_type=F32,
                )
                summed[i, 40 * h : 40 * h + 40] = total[at : at + 40]
            stc[i] = summed[i, :, lanes(1 - c, half)].astype(BF)

        part = pl.ds(cuts[q], cuts[q + 1] - cuts[q])
        copies["t", q, 0] = start(stc.at[part], rtc.at[part], q, 0, core_peer, (table_send, table_recv))

    quarter = half // 2

    def quarter_of(yy):
        return lanes(2 * c + yy, quarter)

    def table1(q):
        copies["t", q, 0].wait_recv()

        @pl.loop(cuts[q], cuts[q + 1])
        def _(i):
            st[i] = (summed[i, :, quarter_of(1 - y)] + wide(rtc[i, :, lanes(1 - y, quarter)])).astype(BF)

        part = pl.ds(cuts[q], cuts[q + 1] - cuts[q])
        copies["t", q, 1] = start(st.at[part], rt.at[part], q, 1, y_peer, (table_send, table_recv))

    def table2(q):
        copies["t", q, 1].wait_recv()

        @pl.loop(cuts[q], cuts[q + 1])
        def _(i):
            total = summed[i, :, quarter_of(y)] + wide(rtc[i, :, lanes(y, quarter)]) + wide(rt[i])
            table_out[i, :, quarter_of(y)] = total.astype(BF)

        part = pl.ds(cuts[q], cuts[q + 1] - cuts[q])
        ours = table_out.at[part, :, quarter_of(y)]
        copies["t", q, 2] = start(ours, ours, q, 2, y_peer, (table_send, table_recv))

    def table3(q):
        copies["t", q, 2].wait_recv()
        part = pl.ds(cuts[q], cuts[q + 1] - cuts[q])
        ours = table_out.at[part, :, lanes(c, half)]
        copies["t", q, 3] = start(ours, ours, q, 3, core_peer, (table_send, table_recv))

    def table4(q):
        copies["t", q, 3].wait_recv()

    s = units

    def small0():
        copies[s, 0] = start(small_ref.at[1 - c], rm.at[0], s, 0, core_peer)

    def small1():
        copies[s, 0].wait_recv()
        sm[0] = small_ref[c] + rm[0]
        copies[s, 1] = start(sm.at[0], rm.at[1], s, 1, x_peer)

    def small2():
        copies[s, 1].wait_recv()
        sm[1] = sm[0] + rm[1]
        copies[s, 2] = start(sm.at[1], rm.at[2], s, 2, y_peer)

    def small3():
        copies[s, 2].wait_recv()
        sm[2] = sm[1] + rm[2]
        for j in (1, 2, 3):
            copies[s, 2 + j] = start(sm.at[2], rmz.at[j - 1], s, 2 + j, z_peer(j))

    def small4():
        for j in (1, 2, 3):
            copies[s, 2 + j].wait_recv()
        even = lax.rem(z, 2)
        near = [sm[2], rmz[0], rmz[1], rmz[2]]
        first = near[0] + near[2]
        second = near[1] + near[3]
        small_out[c] = jnp.where(even == 0, first, second) + jnp.where(even == 0, second, first)
        ours = small_out.at[c]
        copies[s, 6] = start(ours, ours, s, 6, core_peer)

    def small5():
        copies[s, 6].wait_recv()

    small0()
    for m in range(units):
        step0(m)
    pack()
    steps = [step1, step2, step3, step4, step5, step6, step7, step8]
    smalls = [small1, small2, small3, small4, small5]
    tables = [scatter, table1, table2, table3, table4]
    for now in range(units + len(steps)):
        for k, step in enumerate(steps):
            m = now - k
            if 0 <= m < units and (k < 4 or m < gathered):
                step(m)
        if now < len(smalls):
            smalls[now]()
        for k in reversed(range(len(tables))):
            q = now - 1 - k
            if 0 <= q < 4:
                tables[k](q)
    for copy in flying:
        copy.wait_send()

    @pl.loop(0, pairs)
    def _(i):
        for j in range(1, 8):
            row_copy(i, j).wait_send()


def reduce_all(grads, gathered, rows, source, arrived, small):
    units = len(grads)
    pairs, _, count = rows.shape
    piece = (32, 1024)
    vmem = pl.BlockSpec(memory_space=pltpu.VMEM)
    whole, pieces, table_sum, small_sum = pl.pallas_call(
        lambda *refs: reduce_kernel(units, gathered, *refs),
        out_shape=[
            jax.ShapeDtypeStruct((gathered,) + VIEW + piece, BF),
            jax.ShapeDtypeStruct((units - gathered,) + piece, F32),
            jax.ShapeDtypeStruct((pairs, 80, count), BF),
            jax.ShapeDtypeStruct((2, 16, 1024), F32),
        ],
        in_specs=[vmem] * (units + 4),
        out_specs=[vmem] * 4,
        scratch_shapes=[
            pltpu.VMEM((units, 2, 4, 2) + piece, BF),
            pltpu.VMEM((units, 2, 4, 32, 512), BF),
            pltpu.VMEM((units, 2, 4, 32, 512), BF),
            pltpu.VMEM((units, 4, 2, 32, 512), BF),
            pltpu.VMEM((units, 4, 2, 32, 512), BF),
            pltpu.VMEM((units, 4, 32, 512), BF),
            pltpu.VMEM((units, 4, 32, 512), BF),
            pltpu.VMEM((units, 4, 32, 512), BF),
            pltpu.VMEM((units, 4, 32, 512), BF),
            pltpu.VMEM((units, 3) + piece, BF),
            pltpu.VMEM((units, 3) + piece, BF),
            pltpu.VMEM((pairs, 80, count), BF),
            pltpu.VMEM((pairs, 80, count), BF),
            pltpu.VMEM((pairs, 80, count), F32),
            pltpu.VMEM((pairs, 80, count // 2), BF),
            pltpu.VMEM((pairs, 80, count // 2), BF),
            pltpu.VMEM((pairs, 80, count // 4), BF),
            pltpu.VMEM((pairs, 80, count // 4), BF),
            pltpu.VMEM((3, 16, 1024), F32),
            pltpu.VMEM((3, 16, 1024), F32),
            pltpu.VMEM((3, 16, 1024), F32),
            pltpu.SemaphoreType.DMA((units + 1, 16)),
            pltpu.SemaphoreType.DMA((units + 1, 16)),
            pltpu.SemaphoreType.DMA((pairs, 8)),
            pltpu.SemaphoreType.DMA((pairs, 8)),
            pltpu.SemaphoreType.DMA((4, 4)),
            pltpu.SemaphoreType.DMA((4, 4)),
        ],
        compiler_params=pltpu.CompilerParams(
            collective_id=0, has_side_effects=True, vmem_limit_bytes=60 * 2**20
        ),
        name="reduce_all",
    )(
        *[g.reshape(VIEW + piece) for g in grads],
        rows,
        source,
        arrived,
        small.reshape(2, 16, 1024),
    )
    return whole.reshape(gathered, 1024, 1024), pieces, table_sum, small_sum.reshape(-1)


def one_hot(places, count):
    rows = lax.broadcasted_iota(jnp.int32, (count, places.shape[1]), 0)
    return (rows == places).astype(F32).astype(BF)


def lookup_kernel(
    fields, edim, ids_ref, table_ref, dense_ref, x0_ref, arr_ref, inv_ref,
    ids, slots, req, found, rep, pair, wide_rows, x0f, id_send, id_recv, send, recv,
):
    section, me = lax.axis_index("section"), lax.axis_index("dp")
    dot = functools.partial(jnp.dot, preferred_element_type=F32)
    count = ids.shape[1]

    def peer(j):
        return lax.rem(me + j, 8)

    def lanes(place):
        return pl.ds(pl.multiple_of(place * 128, 128), 128)

    barrier = pltpu.get_barrier_semaphore()
    for j in range(1, 8):
        pl.semaphore_signal(
            barrier, inc=1, device_id=(section, peer(j)), device_id_type=pl.DeviceIdType.MESH
        )

    ids[...] = jnp.zeros_like(ids)
    ids[:fields] = ids_ref[...]
    every = ids[...]
    owner = lax.shift_right_logical(every, 10)
    hot = jnp.concatenate([(owner == o).astype(F32) for o in range(8)], axis=0).astype(BF)
    before = (
        lax.broadcasted_iota(jnp.int32, (count, count), 0)
        < lax.broadcasted_iota(jnp.int32, (count, count), 1)
    )
    ranks = dot(hot, before.astype(F32).astype(BF))
    rank = jnp.zeros((32, count), F32)
    for o in range(8):
        rank = jnp.where(owner == o, ranks[32 * o : 32 * o + 32], rank)
    slots[...] = owner * 128 + rank.astype(jnp.int32)
    ids[...] = every & 1023
    @pl.loop(0, 4)
    def _(group):
        eight = pl.ds(pl.multiple_of(8 * group, 8), 8)
        slot8, local8 = slots[eight], ids[eight]
        place = lax.broadcasted_iota(jnp.int32, (1, count), 1)
        column = lax.broadcasted_iota(jnp.int32, (8, count), 0)
        wanted, source = [], []
        for k in range(8):
            slot, local = slot8[k : k + 1], local8[k : k + 1]
            owners = column == lax.shift_right_logical(slot, 7)
            parts = [local >> 5, local & 31, place >> 5, place & 31]
            left = jnp.concatenate(
                [jnp.where(owners, p.astype(F32), 0.0) for p in parts], axis=0
            ).astype(BF)
            right = one_hot(slot & 127, 128)
            sent = lax.dot_general(
                left, right, (((1,), (1,)), ((), ())), preferred_element_type=F32
            )
            rows = [
                (sent[n : n + 8] * 32 + sent[n + 8 : n + 16]).astype(jnp.int32) for n in (0, 16)
            ]
            for taken, r in zip((wanted, source), rows):
                taken.append(jnp.concatenate([r[o : o + 1] for o in range(8)], axis=1))
        req[eight] = jnp.concatenate(wanted, axis=0)
        inv_ref[eight] = jnp.concatenate(source, axis=0)

    def id_copy(j):
        return pltpu.make_async_remote_copy(
            src_ref=req.at[:, lanes(peer(j))],
            dst_ref=arr_ref.at[:, lanes(me)],
            send_sem=id_send.at[j],
            recv_sem=id_recv.at[j],
            device_id=(section, peer(j)),
            device_id_type=pl.DeviceIdType.MESH,
        )

    pl.semaphore_wait(barrier, 7)
    for j in range(1, 8):
        id_copy(j).start()
    arr_ref[:, lanes(me)] = req[:, lanes(me)]
    for j in range(1, 8):
        id_copy(j).wait_recv()

    def row_copy(i, j):
        return pltpu.make_async_remote_copy(
            src_ref=found.at[i, :, lanes(peer(j))],
            dst_ref=rep.at[i, :, lanes(me)],
            send_sem=send.at[i, j],
            recv_sem=recv.at[i, j],
            device_id=(section, peer(j)),
            device_id_type=pl.DeviceIdType.MESH,
        )

    pair[...] = jnp.zeros_like(pair)

    @pl.loop(0, fields // 2)
    def _(i):
        for h in range(2):
            hot = one_hot(arr_ref[pl.ds(2 * i + h, 1)], count)
            pair[40 * h : 40 * h + edim] = dot(table_ref[2 * i + h], hot)
        found[i] = pair[...].astype(BF)
        for j in range(1, 8):
            row_copy(i, j).start()
        rep[i, :, lanes(me)] = found[i, :, lanes(me)]

    @pl.loop(0, fields // 2)
    def _(i):
        for j in range(1, 8):
            row_copy(i, j).wait_recv()
        wide_rows[2 * i] = dot(rep[i, 0:48], one_hot(slots[pl.ds(2 * i, 1)], count))[0:40]
        wide_rows[2 * i + 1] = dot(rep[i, 32:80], one_hot(slots[pl.ds(2 * i + 1, 1)], count))[8:48]

    sparse, extra = fields * edim, dense_ref.shape[0]
    x0f[sparse // 8 * 8 :] = jnp.zeros_like(x0f[sparse // 8 * 8 :])
    for f in range(fields):
        x0f[f * edim : f * edim + edim] = wide_rows[f, :edim]
    x0f[sparse : sparse + extra] = dense_ref[...].astype(F32)
    x0f[sparse + extra : sparse + extra + 1] = jnp.ones_like(x0f[:1])
    x0_ref[...] = x0f[...].astype(BF)

    @pl.loop(0, fields // 2)
    def _(i):
        for j in range(1, 8):
            row_copy(i, j).wait_send()

    for j in range(1, 8):
        id_copy(j).wait_send()


def look_up(ids_t, table_t, dense_t):
    fields, count = ids_t.shape
    edim = table_t.shape[1]
    tall = (fields * edim + dense_t.shape[0]) // 16 * 16 + 16
    vmem = pl.BlockSpec(memory_space=pltpu.VMEM)
    return pl.pallas_call(
        functools.partial(lookup_kernel, fields, edim),
        out_shape=[
            jax.ShapeDtypeStruct((tall, count), BF),
            jax.ShapeDtypeStruct((32, count), jnp.int32),
            jax.ShapeDtypeStruct((32, count), jnp.int32),
        ],
        in_specs=[vmem] * 3,
        out_specs=[vmem] * 3,
        scratch_shapes=[
            pltpu.VMEM((32, count), jnp.int32),
            pltpu.VMEM((32, count), jnp.int32),
            pltpu.VMEM((32, count), jnp.int32),
            pltpu.VMEM((fields // 2, 80, count), BF),
            pltpu.VMEM((fields // 2, 80, count), BF),
            pltpu.VMEM((80, count), F32),
            pltpu.VMEM((fields, 40, count), F32),
            pltpu.VMEM((tall, count), F32),
            pltpu.SemaphoreType.DMA((8,)),
            pltpu.SemaphoreType.DMA((8,)),
            pltpu.SemaphoreType.DMA((fields // 2, 8)),
            pltpu.SemaphoreType.DMA((fields // 2, 8)),
        ],
        compiler_params=pltpu.CompilerParams(
            collective_id=1, has_side_effects=True, vmem_limit_bytes=48 * 2**20
        ),
        name="look_up",
    )(ids_t, table_t, dense_t)


def gelu_and_slope(pre):
    root = (2.0 / math.pi) ** 0.5
    square = pre * pre
    tanh = jnp.tanh(root * pre * (1.0 + 0.044715 * square))
    cdf = 0.5 + 0.5 * tanh
    bend = 0.5 * root * (1.0 - tanh * tanh) * (1.0 + 3 * 0.044715 * square)
    return pre * cdf, cdf + pre * bend


def network_kernel(
    width, edim, x0_ref, labels_ref, weight_ref, in_ref, out_ref, cols_ref, hb_ref,
    probs_ref, rows_ref, dense_ref, small_ref, *rest,
):
    layers = weight_ref.shape[0]
    grads = rest[: layers + 2]
    xs, vs, h1s, q1s, q2s, us, d1s, d2s, dxs, accx, acch, accs, stage, leave = rest[layers + 2 :]
    main = in_ref.shape[1]
    edge = slice(main, main + 16)
    count = x0_ref.shape[1]
    block = us.shape[2]
    pairs = rows_ref.shape[0]

    def dot(a, b, ca, cb):
        return lax.dot_general(a, b, (((ca,), (cb,)), ((), ())), preferred_element_type=F32)

    def fold(value):
        return functools.reduce(
            lambda a, b: a + b, [value[:, n : n + 128] for n in range(0, value.shape[1], 128)]
        )

    for layer in range(1, layers):
        xs[layer - 1, edge] = x0_ref[edge]
    for layer in range(layers):
        vs[layer, main:] = jnp.zeros_like(vs[layer, main:])
    accx[...] = jnp.zeros_like(accx)
    acch[...] = jnp.zeros_like(acch)
    accs[...] = jnp.zeros_like(accs)

    @pl.loop(0, count // block)
    def _(n):
        at = pl.ds(pl.multiple_of(n * block, block), block)

        def x_of(layer):
            return x0_ref[:width, at] if layer == 0 else xs[layer - 1, :width, at]

        def col(k, size):
            return cols_ref[:size, k : k + 1]

        for layer in range(layers):
            u = dot(weight_ref[layer], x_of(layer), 0, 0) + col(layer, width)
            us[layer, :width] = u
            x = (x_of(0).astype(F32) * u + x_of(layer).astype(F32)).astype(BF)
            if layer + 1 < layers:
                xs[layer, :width, at] = x
        last = x.astype(F32)
        h1, d1 = gelu_and_slope(dot(in_ref[...], x_of(0), 0, 0) + col(layers, main))
        d1s[...] = d1
        h1s[:, at] = h1.astype(BF)
        h2, d2 = gelu_and_slope(dot(out_ref[...], h1s[:, at], 0, 0) + col(layers + 1, main))
        d2s[...] = d2
        head_cross, head_tower = col(layers + 2, width), col(layers + 3, main)
        z = (
            jnp.sum(last * head_cross, axis=0, keepdims=True)
            + jnp.sum(h2 * head_tower, axis=0, keepdims=True)
            + hb_ref[0]
        )
        probs = jax.nn.sigmoid(z)
        target = labels_ref[:, at].astype(F32)
        probs_ref[:, at] = probs
        s = probs - target
        loss = jnp.maximum(z, 0.0) + jnp.log1p(jnp.exp(-jnp.abs(z))) - target * z
        accs[0:1] += fold(s)
        accs[1:2] += fold(loss)
        accx[:width] += fold(s * last)
        acch[...] += fold(s * h2)

        q2 = ((s * head_tower) * d2s[...]).astype(BF)
        q2s[:, at] = q2
        q1 = (dot(out_ref[...], q2, 1, 0) * d1s[...]).astype(BF)
        q1s[:, at] = q1
        dxs[:width] = dot(in_ref[...], q1, 1, 0)
        g = (s * head_cross).astype(BF)
        for layer in reversed(range(layers)):
            wide = g.astype(F32)
            v = (wide * x_of(0).astype(F32)).astype(BF)
            vs[layer, :width, at] = v
            dxs[:width] += wide * us[layer, :width]
            g = wide + dot(weight_ref[layer], v, 1, 0)
            if layer:
                g = g.astype(BF)
        dxs[:width] += g
        for i in range(pairs):
            low = 2 * i * edim
            both = [dxs[low : low + 40], dxs[low + edim : low + edim + 40]]
            rows_ref[i, :, at] = jnp.concatenate(both, axis=0).astype(BF)
        dense_ref[:, at] = dxs[2 * pairs * edim : width]

    def x_all(layer, part):
        return x0_ref[part] if layer == 0 else xs[layer - 1, part]

    body = slice(0, main)

    def copy_out(m):
        return pltpu.make_async_copy(stage.at[m % 2], grads[m], leave.at[m % 2])

    def store(m, value):
        if m >= 2:
            copy_out(m - 2).wait()
        stage[m % 2] = value.astype(BF)
        copy_out(m).start()

    for layer in range(layers):
        store(layer, dot(x_all(layer, body), vs[layer, body], 1, 1))
        bottom = dot(x_all(layer, edge), vs[layer], 1, 1)
        side = dot(vs[layer, edge], x_all(layer, body), 1, 1)
        corner = jnp.concatenate(
            [bottom[r : r + 1, main : main + 128] for r in range(4)]
            + [jnp.zeros((1, main - 512), F32)],
            axis=1,
        )
        small_ref[8 * layer : 8 * layer + 8] = jnp.concatenate(
            [bottom[0:4, :main], side[0:3], corner], axis=0
        )
    store(layers, dot(q1s[...], x0_ref[body], 1, 1))
    store(layers + 1, dot(q2s[...], h1s[...], 1, 1))
    in_edge = dot(x0_ref[edge], q1s[...], 1, 1)
    out_edge = dot(x0_ref[edge], q2s[...], 1, 1)
    head_x = jnp.sum(accx[...].T, axis=0, keepdims=True)
    head_h = jnp.sum(acch[...].T, axis=0, keepdims=True)
    sums = [
        jnp.broadcast_to(jnp.sum(accs[k : k + 1], axis=1, keepdims=True), (1, 128)) for k in (0, 1)
    ]
    misc = jnp.concatenate([head_x[:, main:]] + sums + [jnp.zeros((1, main - 384), F32)], axis=1)
    small_ref[8 * layers :] = jnp.concatenate(
        [in_edge[0:4], out_edge[3:4], head_x[:, :main], head_h, misc], axis=0
    )
    copy_out(layers).wait()
    copy_out(layers + 1).wait()


def network(x0, labels, cross_weight, tower_in, tower_out, cols, head_bias, edim, pairs):
    layers, width = cross_weight.shape[:2]
    main = tower_out.shape[0]
    count = x0.shape[1]
    block = 256
    tall = x0.shape[0]
    vmem = pl.BlockSpec(memory_space=pltpu.VMEM)
    return pl.pallas_call(
        functools.partial(network_kernel, width, edim),
        out_shape=[
            jax.ShapeDtypeStruct((1, count), F32),
            jax.ShapeDtypeStruct((pairs, 80, count), BF),
            jax.ShapeDtypeStruct((width - 2 * pairs * edim, count), F32),
            jax.ShapeDtypeStruct((8 * layers + 8, main), F32),
        ]
        + [jax.ShapeDtypeStruct((main, main), BF)] * (layers + 2),
        in_specs=[vmem] * 6 + [pl.BlockSpec(memory_space=pltpu.SMEM)],
        out_specs=[vmem] * 4 + [pl.BlockSpec(memory_space=pl.ANY)] * (layers + 2),
        scratch_shapes=[
            pltpu.VMEM((layers - 1, tall, count), BF),
            pltpu.VMEM((layers, main + 128, count), BF),
            pltpu.VMEM((main, count), BF),
            pltpu.VMEM((main, count), BF),
            pltpu.VMEM((main, count), BF),
            pltpu.VMEM((layers, tall, block), F32),
            pltpu.VMEM((main, block), F32),
            pltpu.VMEM((main, block), F32),
            pltpu.VMEM((tall, block), F32),
            pltpu.VMEM((main + 128, 128), F32),
            pltpu.VMEM((main, 128), F32),
            pltpu.VMEM((8, 128), F32),
            pltpu.VMEM((2, main, main), BF),
            pltpu.SemaphoreType.DMA((2,)),
        ],
        compiler_params=pltpu.CompilerParams(vmem_limit_bytes=60 * 2**20),
        name="network",
    )(x0, labels, cross_weight, tower_in, tower_out, cols, head_bias)


def finish_kernel(whole_ref, small_ref, out_ref):
    main = whole_ref.shape[2]
    rest = out_ref.shape[2] - main
    block = pl.program_id(1)
    layer = pl.program_id(0)
    rows = whole_ref.shape[1]

    @pl.when(block * rows < main)
    def _():
        out_ref[0, :, :main] = whole_ref[0].astype(F32)
        at = pl.ds(pl.multiple_of(block * rows, rows), rows)
        side = small_ref[0, :, at]
        out_ref[0, :, main:] = side.T[:, 4 : 4 + rest]

    @pl.when(block * rows == main)
    def _():
        out_ref[0, :rest, :main] = small_ref[0, :rest]
        corner = [small_ref[0, 7:8, 128 * r : 128 * r + rest] for r in range(rest)]
        out_ref[0, :rest, main:] = jnp.concatenate(corner, axis=0)


def finish(whole, small, width):
    layers, main = whole.shape[:2]
    rows = 256
    blocks = main // rows
    return pl.pallas_call(
        finish_kernel,
        out_shape=jax.ShapeDtypeStruct((layers, width, width), F32),
        grid=(layers, blocks + 1),
        in_specs=[
            pl.BlockSpec((1, rows, main), lambda i, j: (i, jnp.minimum(j, blocks - 1), 0)),
            pl.BlockSpec((1, 8, main), lambda i, j: (i, 0, 0)),
        ],
        out_specs=pl.BlockSpec((1, rows, width), lambda i, j: (i, j, 0)),
        compiler_params=pltpu.CompilerParams(vmem_limit_bytes=32 * 2**20),
        name="finish",
    )(whole, small)


def general_body(
    ids,
    dense,
    labels,
    table,
    cross_weight,
    cross_bias,
    tower_in,
    tower_in_bias,
    tower_out,
    tower_out_bias,
    head_weight,
    head_bias,
):
    groups = lax.axis_size("dp")
    sections = lax.axis_size("section")
    device_count = groups * sections
    examples, fields = ids.shape
    table_rows, edim = table.shape[1:]
    layers, width = cross_weight.shape[:2]
    hidden = tower_out.shape[0]
    capacity = examples // groups
    sparse = fields * edim
    me = lax.axis_index("section") * groups + lax.axis_index("dp")

    idt = ids.T
    owner = idt // table_rows
    local = idt % table_rows
    owner_hot = owner[:, None, :] == jnp.arange(groups, dtype=jnp.int32)[None, :, None]
    lane = jnp.arange(examples, dtype=jnp.int32)
    before = (lane[:, None] < lane[None, :]).astype(BF)
    counts = mm(owner_hot.reshape(fields * groups, examples).astype(BF), before, (1, 0))
    rank = jnp.sum(jnp.where(owner_hot, counts.reshape(fields, groups, examples), 0.0), axis=1)
    slot = owner * capacity + rank.astype(jnp.int32)
    slot_hot = (slot[:, None, :] == lane[None, :, None]).astype(BF)
    halves = jnp.stack([local // 32, local % 32], axis=1).astype(BF)
    sent = lax.dot_general(
        halves, slot_hot, (((2,), (2,)), ((0,), (0,))), preferred_element_type=F32
    )
    requests = (sent[:, 0] * 32 + sent[:, 1]).astype(jnp.int32)
    requests = requests.reshape(fields, groups, capacity).transpose(1, 0, 2)
    arrived = lax.all_to_all(requests, "dp", 0, 0, tiled=True)
    arrived = arrived.transpose(1, 0, 2).reshape(fields, examples)
    row_hot = (
        arrived[:, None, :] == jnp.arange(table_rows, dtype=jnp.int32)[None, :, None]
    ).astype(BF)
    table_t = table.transpose(0, 2, 1)
    found = lax.dot_general(
        table_t, row_hot, (((2,), (1,)), ((0,), (0,))), preferred_element_type=F32
    ).astype(BF)
    found = found.reshape(sparse, groups, capacity).transpose(1, 0, 2)
    replies = lax.all_to_all(found, "dp", 0, 0, tiled=True)
    replies = replies.transpose(1, 0, 2).reshape(fields, edim, examples)
    embedded = lax.dot_general(
        replies, slot_hot, (((2,), (1,)), ((0,), (0,))), preferred_element_type=F32
    ).astype(BF)
    x0 = jnp.concatenate([embedded.reshape(sparse, examples), dense.T], axis=0)

    x0w = x0.astype(F32)
    xs, us = [x0], []
    for layer in range(layers):
        u = mm(cross_weight[layer], xs[-1], (0, 0)) + cross_bias[layer][:, None]
        us.append(u)
        xs.append((x0w * u + xs[-1].astype(F32)).astype(BF))
    p1 = mm(tower_in, x0, (0, 0)) + tower_in_bias[:, None]
    a1, d1 = gelu_parts(p1)
    h1 = a1.astype(BF)
    p2 = mm(tower_out, h1, (0, 0)) + tower_out_bias[:, None]
    h2, d2 = gelu_parts(p2)
    head_cross, head_tower = head_weight[:width], head_weight[width:]
    last = xs[-1].astype(F32)
    z = (
        jnp.sum(last * head_cross[:, None], axis=0)
        + jnp.sum(h2 * head_tower[:, None], axis=0)
        + head_bias[0]
    )
    probs = jax.nn.sigmoid(z)
    target = labels.astype(F32)
    loss = jnp.sum(jnp.logaddexp(0.0, z) - target * z)
    s = probs - target
    head_grad = jnp.concatenate([jnp.sum(s * last, axis=1), jnp.sum(s * h2, axis=1)])

    q2 = (s[None, :] * head_tower[:, None] * d2).astype(BF)
    tower_out_g = mm(q2, h1, (1, 1))
    q1 = (mm(tower_out, q2, (1, 0)) * d1).astype(BF)
    tower_in_g = mm(q1, x0, (1, 1))
    tower_biases = [jnp.sum(q1.astype(F32), axis=1), jnp.sum(q2.astype(F32), axis=1)]
    dx0 = mm(tower_in, q1, (1, 0))
    g = (s[None, :] * head_cross[:, None]).astype(BF)
    cross_g, cross_b = [None] * layers, [None] * layers
    for layer in reversed(range(layers)):
        gw = g.astype(F32)
        v = (gw * x0w).astype(BF)
        cross_g[layer] = mm(xs[layer], v, (1, 1))
        cross_b[layer] = jnp.sum(v.astype(F32), axis=1)
        dx0 = dx0 + gw * us[layer]
        g = gw + mm(cross_weight[layer], v, (1, 0))
        if layer:
            g = g.astype(BF)
    dx0 = dx0 + g

    packed = lax.dot_general(
        dx0[:sparse].astype(BF).reshape(fields, edim, examples),
        slot_hot,
        (((2,), (2,)), ((0,), (0,))),
        preferred_element_type=F32,
    ).astype(BF)
    packed = packed.reshape(sparse, groups, capacity).transpose(1, 0, 2)
    delivered = lax.all_to_all(packed, "dp", 0, 0, tiled=True)
    delivered = delivered.transpose(1, 0, 2).reshape(fields, edim, examples)
    table_g = lax.dot_general(
        delivered, row_hot, (((2,), (2,)), ((0,), (0,))), preferred_element_type=F32
    )
    table_g = lax.psum(table_g, "section").transpose(0, 2, 1)

    small = jnp.concatenate(
        cross_b + [head_grad, jnp.sum(s).reshape(1), loss.reshape(1)] + tower_biases
    )
    small = lax.psum(small, ("section", "dp"))
    sizes = [layers * width, width + hidden, 1, 1, hidden, hidden]
    ends = [sum(sizes[: i + 1]) for i in range(len(sizes))]
    pieces = [small[e - n : e] for e, n in zip(ends, sizes)]
    cross_b_out = pieces[0].reshape(layers, width)
    share = hidden // device_count
    bias_in, bias_out = (lax.dynamic_slice(p, (me * share,), (share,)) for p in pieces[4:])
    cross_out = lax.psum(jnp.stack(cross_g), ("section", "dp"))
    tower_in_out = lax.psum_scatter(
        tower_in_g, ("section", "dp"), scatter_dimension=0, tiled=True
    )
    tower_out_out = lax.psum_scatter(
        tower_out_g, ("section", "dp"), scatter_dimension=0, tiled=True
    )
    return (
        probs,
        pieces[3] / (examples * device_count),
        dx0[sparse:].T,
        table_g,
        cross_out,
        cross_b_out,
        tower_in_out.T,
        bias_in,
        tower_out_out.T,
        bias_out,
        pieces[1],
        pieces[2],
    )


def body(
    ids,
    dense,
    labels,
    table,
    cross_weight,
    cross_bias,
    tower_in,
    tower_in_bias,
    tower_out,
    tower_out_bias,
    head_weight,
    head_bias,
):
    groups = lax.axis_size("dp")
    sections = lax.axis_size("section")
    device_count = groups * sections
    examples, fields = ids.shape
    table_rows, edim = table.shape[1:]
    layers, width = cross_weight.shape[:2]
    hidden = tower_out.shape[0]
    capacity = examples // groups
    me = lax.axis_index("section") * groups + lax.axis_index("dp")
    idt = ids.T
    table_t = table.transpose(0, 2, 1)
    here = (sections, groups, capacity, table_rows) == (4, 8, 128, 1024)
    if here:
        x0, arrived, source = look_up(idt, table_t, dense.T)
        tall = x0.shape[0]

        def column(vector):
            return jnp.pad(vector, (0, tall - vector.shape[0]))

        columns = list(cross_bias) + [tower_in_bias, tower_out_bias]
        columns += [head_weight[:width], head_weight[width:]]
        probs, rows, dense_g, small, *grads = network(
            x0,
            labels.reshape(1, examples),
            cross_weight,
            tower_in,
            tower_out,
            jnp.stack([column(c) for c in columns], axis=1),
            head_bias,
            edim,
            fields // 2,
        )
        whole, pieces, table_sum, small = reduce_all(grads, layers, rows, source, arrived, small)
        small = small.reshape(8 * layers + 8, hidden)
        main, rest = hidden, width - hidden
        edges = small.reshape(layers + 1, 8, hidden)
        cross_out = finish(whole, edges, width)
        table_g = table_sum.reshape(fields, 40, table_rows)[:, :edim].astype(F32)
        cross_b_out = jnp.concatenate(
            [edges[:layers, 3], edges[:layers, 7, 384 : 384 + rest]], axis=1
        )
        share = hidden // device_count
        mine = lax.dynamic_slice(edges[layers], (0, me * share), (5, share))
        tower_in_out = jnp.concatenate([pieces[0], mine[:rest].T], axis=1)
        misc = edges[layers, 7]
        head_out = jnp.concatenate([edges[layers, 5], misc[:rest], edges[layers, 6]])
        return (
            probs.reshape(examples),
            misc[256:257] / (examples * device_count),
            dense_g.T,
            table_g.transpose(0, 2, 1),
            cross_out,
            cross_b_out,
            tower_in_out.T,
            mine[3],
            pieces[1].T,
            mine[4],
            head_out,
            misc[128:129],
        )
    return general_body(
        ids, dense, labels, table, cross_weight, cross_bias, tower_in, tower_in_bias, tower_out,
        tower_out_bias, head_weight, head_bias,
    )


def solution(mesh):
    both = ("section", "dp")
    return jax.shard_map(
        body,
        mesh=mesh,
        in_specs=(P(both, None), P(both, None), P(both), P(None, "dp", None)) + (P(),) * 8,
        out_specs=(
            P(both),
            P(),
            P(both, None),
            P(None, "dp", None),
            P(),
            P(),
            P(None, both),
            P(both),
            P(None, both),
            P(both),
            P(),
            P(),
        ),
        check_vma=False,
    )
```

```python
import functools
import math

import jax
import jax.numpy as jnp
from jax import lax
from jax.experimental import pallas as pl
from jax.experimental.pallas import tpu as pltpu
from jax.sharding import PartitionSpec as P

BF = jnp.bfloat16
F32 = jnp.float32


def mm(left, right, contract):
    return lax.dot_general(
        left, right, ((contract[:1], contract[1:]), ((), ())), preferred_element_type=F32
    )


def gelu_parts(pre):
    act, back = jax.vjp(jax.nn.gelu, pre)
    return act, back(jnp.ones_like(pre))[0]


ORDER = [
    "C0 P2 C2 u10",
    "P1 C1 u12 P0",
    "u11 C4 u20 C3",
    "n0 u14 u22 P3",
    "u13 S0 S1 n1",
    "T10 u21 u30 S2",
    "T11 T20 n2 u32",
    "T12 u24 T21 u40",
    "S3 n3 T22 u23",
    "u31 T31 u42 u50",
    "n4 T13 u60 u41",
    "u52 u34 T23 n5",
    "u33 T32 T41 u70",
    "u51 u62 u61 u72",
    "u44 T42 u43 T33",
    "u80 T30 T40 u71",
    "u82 T43 u81",
]
VIEW = (2, 2, 4, 2)


def reduce_kernel(units, gathered, *refs):
    lefts, rights = refs[:units], refs[units : 2 * units]
    rows_ref, inv_ref, arr_ref, part_ref = refs[2 * units : 2 * units + 4]
    whole, pieces, table_out, small_out = refs[2 * units + 4 : 2 * units + 8]
    (
        grads, left, right, load, small, rc, sa1, ra1, sb1, rb1, sa2, ra2, sb2, rb2, sz, rz, packed, back, summed,
        stc, rtc, st, rt, sm, rm, rmz, send, recv, row_send, row_recv, table_send, table_recv,
    ) = refs[2 * units + 8 :]
    pairs, count = rows_ref.shape[0], rows_ref.shape[2]
    section, dp = lax.axis_index("section"), lax.axis_index("dp")
    y, c = section // 2, section % 2
    z, x = dp // 2, dp % 2
    core_peer = (y * 2 + 1 - c, dp)
    y_peer = ((1 - y) * 2 + c, dp)
    x_peer = (section, z * 2 + 1 - x)
    half = 512
    lo, hi = pl.ds(0, half), pl.ds(half, half)

    def z_peer(j):
        return (section, lax.rem(z + j, 4) * 2 + x)

    def dp_peer(j):
        return (section, lax.rem(dp + j, 8))

    peers = [core_peer, y_peer] + [dp_peer(j) for j in range(1, 8)]
    barrier = pltpu.get_barrier_semaphore()
    for peer in peers:
        pl.semaphore_signal(barrier, inc=1, device_id=peer, device_id_type=pl.DeviceIdType.MESH)

    flying = []

    def start(src, dst, m, k, peer, sems=(send, recv)):
        copy = pltpu.make_async_remote_copy(
            src_ref=src,
            dst_ref=dst,
            send_sem=sems[0].at[m, k],
            recv_sem=sems[1].at[m, k],
            device_id=peer,
            device_id_type=pl.DeviceIdType.MESH,
        )
        copy.start()
        flying.append(copy)
        return copy

    def wide(value):
        return value.astype(F32)

    copies = {}

    def acc(m, stage, cols, yy, zz, xx):
        total = wide(grads[m, yy, c, zz, xx, :, cols]) + wide(rc[m, yy, zz, xx, :, cols])
        if cols is lo:
            if stage >= 2:
                total += wide(ra1[m, yy, zz])
            if stage >= 3:
                total += wide(ra2[m, zz])
        else:
            if stage >= 2:
                total += wide(rb1[m, zz, xx])
            if stage >= 3:
                total += wide(rb2[m, zz])
        return total

    tokens = " ".join(ORDER).split()
    made = [int(t[1]) for t in tokens if t[0] == "C"]

    def height(m):
        return min(lefts[m].shape[0], left.shape[1])

    def loads(turn):
        m, slot = made[turn], turn % 2
        return [
            pltpu.make_async_copy(ref.at[:rows], buf.at[slot, :rows], load.at[slot, k])
            for k, (ref, buf, rows) in enumerate(
                ((lefts[m], left, height(m)), (rights[m], right, rights[m].shape[0]))
            )
        ]

    def make(m):
        turn = made.index(m)
        slot = turn % 2
        for copy in loads(turn):
            copy.wait()
        tall = height(m) - 1024
        across = rights[m].shape[0]
        for r in range(2):
            total = lax.dot_general(
                left[slot, 512 * r : 512 * r + 512 + r * tall],
                right[slot, :across],
                (((1,), (1,)), ((), ())),
                preferred_element_type=F32,
            )
            grads[m, r] = total[:512, :1024].astype(BF).reshape(2, 4, 2, 32, 1024)
            if across > 1024:
                side = total[:512, 1024:].T
                group, at = m // 2, m % 2 * 8
                if tall:
                    small[group, at + 4 : at + 7, 512 * r : 512 * r + 512] = side[0:3]
                else:
                    small[group, at : at + 4, 512 * r : 512 * r + 512] = side[0:4]
                if tall and r:
                    small[group, at : at + 4] = total[512:516, :1024]
                    small[group, at + 7 : at + 8, 512:] = jnp.zeros((1, 512), F32)
                    for k in range(4):
                        small[group, at + 7 : at + 8, 128 * k : 128 * k + 128] = total[
                            512 + k : 513 + k, 1024:
                        ]
        if turn + 2 < units:
            for copy in loads(turn + 2):
                copy.start()

    def step0(m):
        make(m)
        copies[m, 0] = start(grads.at[m, :, 1 - c], rc.at[m], m, 0, core_peer)

    def step1(m):
        copies[m, 0].wait_recv()

        @pl.loop(0, 4)
        def _(zz):
            for i in range(2):
                sa1[m, i, zz] = acc(m, 1, lo, i, zz, 1 - x).astype(BF)
                sb1[m, zz, i] = acc(m, 1, hi, 1 - y, zz, i).astype(BF)

        copies[m, 1] = start(sa1.at[m], ra1.at[m], m, 1, x_peer)
        copies[m, 2] = start(sb1.at[m], rb1.at[m], m, 2, y_peer)

    def step2(m):
        copies[m, 1].wait_recv()
        copies[m, 2].wait_recv()

        @pl.loop(0, 4)
        def _(zz):
            sa2[m, zz] = acc(m, 2, lo, 1 - y, zz, x).astype(BF)
            sb2[m, zz] = acc(m, 2, hi, y, zz, 1 - x).astype(BF)

        copies[m, 3] = start(sa2.at[m], ra2.at[m], m, 3, y_peer)
        copies[m, 4] = start(sb2.at[m], rb2.at[m], m, 4, x_peer)

    def step3(m):
        copies[m, 3].wait_recv()
        copies[m, 4].wait_recv()
        for j in (1, 2, 3):
            zz = lax.rem(z + j, 4)
            sz[m, j - 1, :, lo] = acc(m, 3, lo, y, zz, x).astype(BF)
            sz[m, j - 1, :, hi] = acc(m, 3, hi, y, zz, x).astype(BF)
            copies[m, 4 + j] = start(sz.at[m, j - 1], rz.at[m, j - 1], m, 4 + j, z_peer(j))

    def step4(m):
        for j in (1, 2, 3):
            copies[m, 4 + j].wait_recv()
        for cols in (lo, hi):
            total = acc(m, 3, cols, y, z, x)
            for j in range(3):
                total += wide(rz[m, j, :, cols])
            if m < gathered:
                whole[m, y, c, z, x, :, cols] = total.astype(BF)
            else:
                pieces[m - gathered, :, cols] = total
        if m < gathered:
            for j in (1, 2, 3):
                mine = whole.at[m, y, c, z, x]
                copies[m, 7 + j] = start(mine, mine, m, 7 + j, z_peer(j))

    def step5(m):
        for j in (1, 2, 3):
            copies[m, 7 + j].wait_recv()
        ours = whole.at[m, y, c, :, x, :, lo]
        copies[m, 11] = start(ours, ours, m, 11, y_peer)
        ours = whole.at[m, y, c, :, x, :, hi]
        copies[m, 12] = start(ours, ours, m, 12, x_peer)

    def step6(m):
        copies[m, 11].wait_recv()
        copies[m, 12].wait_recv()
        ours = whole.at[m, :, c, :, x, :, lo]
        copies[m, 13] = start(ours, ours, m, 13, x_peer)
        ours = whole.at[m, y, c, :, :, :, hi]
        copies[m, 14] = start(ours, ours, m, 14, y_peer)

    def step7(m):
        copies[m, 13].wait_recv()
        copies[m, 14].wait_recv()
        ours = whole.at[m, :, c]
        copies[m, 15] = start(ours, ours, m, 15, core_peer)

    def step8(m):
        copies[m, 15].wait_recv()

    def lanes(place, size):
        return pl.ds(pl.multiple_of(place * size, size), size)

    def row_copy(i, j):
        return pltpu.make_async_remote_copy(
            src_ref=packed.at[i, :, lanes(lax.rem(dp + j, 8), 128)],
            dst_ref=back.at[i, :, lanes(dp, 128)],
            send_sem=row_send.at[i, j],
            recv_sem=row_recv.at[i, j],
            device_id=dp_peer(j),
            device_id_type=pl.DeviceIdType.MESH,
        )

    cuts = [pairs * q // 4 for q in range(5)]

    def pack(q):
        @pl.loop(cuts[q], cuts[q + 1])
        def _(i):
            first = jnp.dot(
                rows_ref[i, 0:48],
                one_hot(inv_ref[pl.ds(2 * i, 1)], count),
                preferred_element_type=F32,
            )
            second = jnp.dot(
                rows_ref[i, 32:80],
                one_hot(inv_ref[pl.ds(2 * i + 1, 1)], count),
                preferred_element_type=F32,
            )
            packed[i] = jnp.concatenate([first[0:40], second[8:48]], axis=0).astype(BF)
            for j in range(1, 8):
                row_copy(i, j).start()
            back[i, :, lanes(dp, 128)] = packed[i, :, lanes(dp, 128)]

    def scatter(q):
        @pl.loop(cuts[q], cuts[q + 1])
        def _(i):
            for j in range(1, 8):
                row_copy(i, j).wait_recv()
            for h, (low, at) in enumerate(((0, 0), (32, 8))):
                total = lax.dot_general(
                    back[i, low : low + 48],
                    one_hot(arr_ref[pl.ds(2 * i + h, 1)], count),
                    (((1,), (1,)), ((), ())),
                    preferred_element_type=F32,
                )
                summed[i, 40 * h : 40 * h + 40] = total[at : at + 40]
            stc[i] = summed[i, :, lanes(1 - c, half)].astype(BF)

        part = pl.ds(cuts[q], cuts[q + 1] - cuts[q])
        copies["t", q, 0] = start(stc.at[part], rtc.at[part], q, 0, core_peer, (table_send, table_recv))

    quarter = half // 2

    def quarter_of(yy):
        return lanes(2 * c + yy, quarter)

    def table1(q):
        copies["t", q, 0].wait_recv()

        @pl.loop(cuts[q], cuts[q + 1])
        def _(i):
            st[i] = (summed[i, :, quarter_of(1 - y)] + wide(rtc[i, :, lanes(1 - y, quarter)])).astype(BF)

        part = pl.ds(cuts[q], cuts[q + 1] - cuts[q])
        copies["t", q, 1] = start(st.at[part], rt.at[part], q, 1, y_peer, (table_send, table_recv))

    def table2(q):
        copies["t", q, 1].wait_recv()

        @pl.loop(cuts[q], cuts[q + 1])
        def _(i):
            total = summed[i, :, quarter_of(y)] + wide(rtc[i, :, lanes(y, quarter)]) + wide(rt[i])
            table_out[i, :, quarter_of(y)] = total.astype(BF)

        part = pl.ds(cuts[q], cuts[q + 1] - cuts[q])
        ours = table_out.at[part, :, quarter_of(y)]
        copies["t", q, 2] = start(ours, ours, q, 2, y_peer, (table_send, table_recv))

    def table3(q):
        copies["t", q, 2].wait_recv()
        part = pl.ds(cuts[q], cuts[q + 1] - cuts[q])
        ours = table_out.at[part, :, lanes(c, half)]
        copies["t", q, 3] = start(ours, ours, q, 3, core_peer, (table_send, table_recv))

    def table4(q):
        copies["t", q, 3].wait_recv()

    s = units

    def small0():
        small[1, 12:16] = part_ref[0:4]
        copies[s, 0] = start(small.at[1 - c], rm.at[0], s, 0, core_peer)

    def small1():
        copies[s, 0].wait_recv()
        sm[0] = small[c] + rm[0]
        copies[s, 1] = start(sm.at[0], rm.at[1], s, 1, x_peer)

    def small2():
        copies[s, 1].wait_recv()
        sm[1] = sm[0] + rm[1]
        copies[s, 2] = start(sm.at[1], rm.at[2], s, 2, y_peer)

    def small3():
        copies[s, 2].wait_recv()
        sm[2] = sm[1] + rm[2]
        for j in (1, 2, 3):
            copies[s, 2 + j] = start(sm.at[2], rmz.at[j - 1], s, 2 + j, z_peer(j))

    def small4():
        for j in (1, 2, 3):
            copies[s, 2 + j].wait_recv()
        even = lax.rem(z, 2)
        near = [sm[2], rmz[0], rmz[1], rmz[2]]
        first = near[0] + near[2]
        second = near[1] + near[3]
        small_out[c] = jnp.where(even == 0, first, second) + jnp.where(even == 0, second, first)
        ours = small_out.at[c]
        copies[s, 6] = start(ours, ours, s, 6, core_peer)

    def small5():
        copies[s, 6].wait_recv()

    steps = [step1, step2, step3, step4, step5, step6, step7, step8]
    smalls = [small0, small1, small2, small3, small4, small5]
    tables = [table1, table2, table3, table4]
    for copy in loads(0) + loads(1):
        copy.start()
    pl.semaphore_wait(barrier, len(peers))
    for token in tokens:
        kind, numbers = token[0], [int(n) for n in token[1:]]
        if kind == "C":
            step0(*numbers)
        elif kind == "P":
            pack(*numbers)
        elif kind == "S":
            scatter(*numbers)
        elif kind == "n":
            smalls[numbers[0]]()
        else:
            {"u": steps, "T": tables}[kind][numbers[0] - 1](numbers[1])
    for copy in flying:
        copy.wait_send()

    @pl.loop(0, pairs)
    def _(i):
        for j in range(1, 8):
            row_copy(i, j).wait_send()


def reduce_all(lefts, rights, gathered, rows, source, arrived, small):
    units = len(lefts)
    pairs, _, count = rows.shape
    piece = (32, 1024)
    vmem = pl.BlockSpec(memory_space=pltpu.VMEM)
    whole, pieces, table_sum, small_sum = pl.pallas_call(
        lambda *refs: reduce_kernel(units, gathered, *refs),
        out_shape=[
            jax.ShapeDtypeStruct((gathered,) + VIEW + piece, BF),
            jax.ShapeDtypeStruct((units - gathered,) + piece, F32),
            jax.ShapeDtypeStruct((pairs, 80, count), BF),
            jax.ShapeDtypeStruct((2, 16, 1024), F32),
        ],
        in_specs=[pl.BlockSpec(memory_space=pl.ANY)] * (2 * units) + [vmem] * 4,
        out_specs=[vmem] * 4,
        scratch_shapes=[
            pltpu.VMEM((units,) + VIEW + piece, BF),
            pltpu.VMEM((2, 1040, count), BF),
            pltpu.VMEM((2, 1152, count), BF),
            pltpu.SemaphoreType.DMA((2, 2)),
            pltpu.VMEM((2, 16, 1024), F32),
            pltpu.VMEM((units, 2, 4, 2) + piece, BF),
            pltpu.VMEM((units, 2, 4, 32, 512), BF),
            pltpu.VMEM((units, 2, 4, 32, 512), BF),
            pltpu.VMEM((units, 4, 2, 32, 512), BF),
            pltpu.VMEM((units, 4, 2, 32, 512), BF),
            pltpu.VMEM((units, 4, 32, 512), BF),
            pltpu.VMEM((units, 4, 32, 512), BF),
            pltpu.VMEM((units, 4, 32, 512), BF),
            pltpu.VMEM((units, 4, 32, 512), BF),
            pltpu.VMEM((units, 3) + piece, BF),
            pltpu.VMEM((units, 3) + piece, BF),
            pltpu.VMEM((pairs, 80, count), BF),
            pltpu.VMEM((pairs, 80, count), BF),
            pltpu.VMEM((pairs, 80, count), F32),
            pltpu.VMEM((pairs, 80, count // 2), BF),
            pltpu.VMEM((pairs, 80, count // 2), BF),
            pltpu.VMEM((pairs, 80, count // 4), BF),
            pltpu.VMEM((pairs, 80, count // 4), BF),
            pltpu.VMEM((3, 16, 1024), F32),
            pltpu.VMEM((3, 16, 1024), F32),
            pltpu.VMEM((3, 16, 1024), F32),
            pltpu.SemaphoreType.DMA((units + 1, 16)),
            pltpu.SemaphoreType.DMA((units + 1, 16)),
            pltpu.SemaphoreType.DMA((pairs, 8)),
            pltpu.SemaphoreType.DMA((pairs, 8)),
            pltpu.SemaphoreType.DMA((4, 4)),
            pltpu.SemaphoreType.DMA((4, 4)),
        ],
        compiler_params=pltpu.CompilerParams(
            collective_id=0, has_side_effects=True, vmem_limit_bytes=62 * 2**20
        ),
        name="reduce_all",
    )(
        *lefts,
        *rights,
        rows,
        source,
        arrived,
        small,
    )
    return whole.reshape(gathered, 1024, 1024), pieces, table_sum, small_sum.reshape(-1)


def one_hot(places, count):
    rows = lax.broadcasted_iota(jnp.int32, (count, places.shape[1]), 0)
    return (rows == places).astype(F32).astype(BF)


def lookup_kernel(
    fields, edim, ids_ref, table_ref, dense_ref, x0_ref, arr_ref, inv_ref,
    ids, slots, req, found, rep, pair, wide_rows, x0f, id_send, id_recv, send, recv,
):
    section, me = lax.axis_index("section"), lax.axis_index("dp")
    dot = functools.partial(jnp.dot, preferred_element_type=F32)
    count = ids.shape[1]

    def peer(j):
        return lax.rem(me + j, 8)

    def lanes(place):
        return pl.ds(pl.multiple_of(place * 128, 128), 128)

    barrier = pltpu.get_barrier_semaphore()
    for j in range(1, 8):
        pl.semaphore_signal(
            barrier, inc=1, device_id=(section, peer(j)), device_id_type=pl.DeviceIdType.MESH
        )

    ids[...] = jnp.zeros_like(ids)
    ids[:fields] = ids_ref[...]
    every = ids[...]
    owner = lax.shift_right_logical(every, 10)
    hot = jnp.concatenate([(owner == o).astype(F32) for o in range(8)], axis=0).astype(BF)
    before = (
        lax.broadcasted_iota(jnp.int32, (count, count), 0)
        < lax.broadcasted_iota(jnp.int32, (count, count), 1)
    )
    ranks = dot(hot, before.astype(F32).astype(BF))
    rank = jnp.zeros((32, count), F32)
    for o in range(8):
        rank = jnp.where(owner == o, ranks[32 * o : 32 * o + 32], rank)
    slots[...] = owner * 128 + rank.astype(jnp.int32)
    ids[...] = every & 1023
    @pl.loop(0, 4)
    def _(group):
        eight = pl.ds(pl.multiple_of(8 * group, 8), 8)
        slot8, local8 = slots[eight], ids[eight]
        place = lax.broadcasted_iota(jnp.int32, (1, count), 1)
        column = lax.broadcasted_iota(jnp.int32, (8, count), 0)
        wanted, source = [], []
        for k in range(8):
            slot, local = slot8[k : k + 1], local8[k : k + 1]
            owners = column == lax.shift_right_logical(slot, 7)
            parts = [local >> 5, local & 31, place >> 5, place & 31]
            left = jnp.concatenate(
                [jnp.where(owners, p.astype(F32), 0.0) for p in parts], axis=0
            ).astype(BF)
            right = one_hot(slot & 127, 128)
            sent = lax.dot_general(
                left, right, (((1,), (1,)), ((), ())), preferred_element_type=F32
            )
            rows = [
                (sent[n : n + 8] * 32 + sent[n + 8 : n + 16]).astype(jnp.int32) for n in (0, 16)
            ]
            for taken, r in zip((wanted, source), rows):
                taken.append(jnp.concatenate([r[o : o + 1] for o in range(8)], axis=1))
        req[eight] = jnp.concatenate(wanted, axis=0)
        inv_ref[eight] = jnp.concatenate(source, axis=0)

    def id_copy(j):
        return pltpu.make_async_remote_copy(
            src_ref=req.at[:, lanes(peer(j))],
            dst_ref=arr_ref.at[:, lanes(me)],
            send_sem=id_send.at[j],
            recv_sem=id_recv.at[j],
            device_id=(section, peer(j)),
            device_id_type=pl.DeviceIdType.MESH,
        )

    pl.semaphore_wait(barrier, 7)
    for j in range(1, 8):
        id_copy(j).start()
    arr_ref[:, lanes(me)] = req[:, lanes(me)]
    for j in range(1, 8):
        id_copy(j).wait_recv()

    def row_copy(i, j):
        return pltpu.make_async_remote_copy(
            src_ref=found.at[i, :, lanes(peer(j))],
            dst_ref=rep.at[i, :, lanes(me)],
            send_sem=send.at[i, j],
            recv_sem=recv.at[i, j],
            device_id=(section, peer(j)),
            device_id_type=pl.DeviceIdType.MESH,
        )

    pair[...] = jnp.zeros_like(pair)

    @pl.loop(0, fields // 2)
    def _(i):
        for h in range(2):
            hot = one_hot(arr_ref[pl.ds(2 * i + h, 1)], count)
            pair[40 * h : 40 * h + edim] = dot(table_ref[2 * i + h], hot)
        found[i] = pair[...].astype(BF)
        for j in range(1, 8):
            row_copy(i, j).start()
        rep[i, :, lanes(me)] = found[i, :, lanes(me)]

    @pl.loop(0, fields // 2)
    def _(i):
        for j in range(1, 8):
            row_copy(i, j).wait_recv()
        wide_rows[2 * i] = dot(rep[i, 0:48], one_hot(slots[pl.ds(2 * i, 1)], count))[0:40]
        wide_rows[2 * i + 1] = dot(rep[i, 32:80], one_hot(slots[pl.ds(2 * i + 1, 1)], count))[8:48]

    sparse, extra = fields * edim, dense_ref.shape[0]
    x0f[sparse // 8 * 8 :] = jnp.zeros_like(x0f[sparse // 8 * 8 :])
    for f in range(fields):
        x0f[f * edim : f * edim + edim] = wide_rows[f, :edim]
    x0f[sparse : sparse + extra] = dense_ref[...].astype(F32)
    x0f[sparse + extra : sparse + extra + 1] = jnp.ones_like(x0f[:1])
    x0_ref[...] = x0f[...].astype(BF)

    @pl.loop(0, fields // 2)
    def _(i):
        for j in range(1, 8):
            row_copy(i, j).wait_send()

    for j in range(1, 8):
        id_copy(j).wait_send()


def look_up(ids_t, table_t, dense_t):
    fields, count = ids_t.shape
    edim = table_t.shape[1]
    tall = (fields * edim + dense_t.shape[0]) // 128 * 128 + 128
    vmem = pl.BlockSpec(memory_space=pltpu.VMEM)
    return pl.pallas_call(
        functools.partial(lookup_kernel, fields, edim),
        out_shape=[
            jax.ShapeDtypeStruct((tall, count), BF),
            jax.ShapeDtypeStruct((32, count), jnp.int32),
            jax.ShapeDtypeStruct((32, count), jnp.int32),
        ],
        in_specs=[vmem] * 3,
        out_specs=[vmem] * 3,
        scratch_shapes=[
            pltpu.VMEM((32, count), jnp.int32),
            pltpu.VMEM((32, count), jnp.int32),
            pltpu.VMEM((32, count), jnp.int32),
            pltpu.VMEM((fields // 2, 80, count), BF),
            pltpu.VMEM((fields // 2, 80, count), BF),
            pltpu.VMEM((80, count), F32),
            pltpu.VMEM((fields, 40, count), F32),
            pltpu.VMEM((tall, count), F32),
            pltpu.SemaphoreType.DMA((8,)),
            pltpu.SemaphoreType.DMA((8,)),
            pltpu.SemaphoreType.DMA((fields // 2, 8)),
            pltpu.SemaphoreType.DMA((fields // 2, 8)),
        ],
        compiler_params=pltpu.CompilerParams(
            collective_id=1, has_side_effects=True, vmem_limit_bytes=48 * 2**20
        ),
        name="look_up",
    )(ids_t, table_t, dense_t)


def gelu_and_slope(pre):
    root = (2.0 / math.pi) ** 0.5
    square = pre * pre
    tanh = jnp.tanh(root * pre * (1.0 + 0.044715 * square))
    cdf = 0.5 + 0.5 * tanh
    bend = 0.5 * root * (1.0 - tanh * tanh) * (1.0 + 3 * 0.044715 * square)
    return pre * cdf, cdf + pre * bend


def network_kernel(
    width, edim, x0_ref, labels_ref, weight_ref, in_ref, out_ref, bias_ref, in_bias_ref, out_bias_ref, head_ref, hb_ref,
    probs_ref, rows_ref, dense_ref, small_ref, *rest,
):
    layers = weight_ref.shape[0]
    kept = 2 * layers + 2
    outs = rest[:kept]
    xs, vs, h1s, q1s, q2s, us, d1s, d2s, dxs, accx, acch, accq, accs, lines, cols, leave = rest[kept:]
    main = in_ref.shape[1]
    edge = slice(main, main + 16)
    count = x0_ref.shape[1]
    block = us.shape[2]
    pairs = rows_ref.shape[0]

    def leaving(k, n):
        at = pl.ds(pl.multiple_of(n * block, block), block)
        here = [xs.at[i] for i in range(layers - 1)] + [vs.at[i] for i in range(layers)]
        here += [h1s, q1s, q2s]
        return pltpu.make_async_copy(here[k].at[:, at], outs[k].at[:, at], leave.at[n, k])

    def dot(a, b, ca, cb):
        return lax.dot_general(a, b, (((ca,), (cb,)), ((), ())), preferred_element_type=F32)

    def fold(value):
        return functools.reduce(
            lambda a, b: a + b, [value[:, n : n + 128] for n in range(0, value.shape[1], 128)]
        )

    for layer in range(1, layers):
        xs[layer - 1, edge] = x0_ref[edge]
    for layer in range(layers):
        vs[layer, main:] = jnp.zeros_like(vs[layer, main:])
    accx[...] = jnp.zeros_like(accx)
    acch[...] = jnp.zeros_like(acch)
    accq[...] = jnp.zeros_like(accq)
    accs[...] = jnp.zeros_like(accs)
    lines[...] = jnp.zeros_like(lines)
    lines[0:layers, :width] = bias_ref[...]
    lines[layers : layers + 1, :main] = in_bias_ref[...]
    lines[layers + 1 : layers + 2, :main] = out_bias_ref[...]
    lines[layers + 2 : layers + 3, :width] = head_ref[:, :width]
    lines[layers + 3 : layers + 4, :main] = head_ref[:, width:]
    cols[...] = lines[...].T

    @pl.loop(0, count // block)
    def _(n):
        at = pl.ds(pl.multiple_of(n * block, block), block)

        def x_of(layer):
            return x0_ref[:width, at] if layer == 0 else xs[layer - 1, :width, at]

        def col(k, size):
            return cols[:size, k : k + 1]

        for layer in range(layers):
            u = dot(weight_ref[layer], x_of(layer), 0, 0) + col(layer, width)
            us[layer, :width] = u
            x = (x_of(0).astype(F32) * u + x_of(layer).astype(F32)).astype(BF)
            if layer + 1 < layers:
                xs[layer, :width, at] = x
        last = x.astype(F32)
        h1, d1 = gelu_and_slope(dot(in_ref[...], x_of(0), 0, 0) + col(layers, main))
        d1s[...] = d1
        h1s[:, at] = h1.astype(BF)
        h2, d2 = gelu_and_slope(dot(out_ref[...], h1s[:, at], 0, 0) + col(layers + 1, main))
        d2s[...] = d2
        head_cross, head_tower = col(layers + 2, width), col(layers + 3, main)
        z = (
            jnp.sum(last * head_cross, axis=0, keepdims=True)
            + jnp.sum(h2 * head_tower, axis=0, keepdims=True)
            + hb_ref[0]
        )
        probs = jax.nn.sigmoid(z)
        target = labels_ref[:, at].astype(F32)
        probs_ref[:, at] = probs
        s = probs - target
        loss = jnp.maximum(z, 0.0) + jnp.log1p(jnp.exp(-jnp.abs(z))) - target * z
        accs[0:1] += fold(s)
        accs[1:2] += fold(loss)
        accx[:width] += fold(s * last)
        acch[...] += fold(s * h2)

        q2 = ((s * head_tower) * d2s[...]).astype(BF)
        q2s[:, at] = q2
        acc = fold(q2.astype(F32))
        accq[...] += acc
        q1 = (dot(out_ref[...], q2, 1, 0) * d1s[...]).astype(BF)
        q1s[:, at] = q1
        dxs[:width] = dot(in_ref[...], q1, 1, 0)
        g = (s * head_cross).astype(BF)
        for layer in reversed(range(layers)):
            wide = g.astype(F32)
            v = (wide * x_of(0).astype(F32)).astype(BF)
            vs[layer, :width, at] = v
            dxs[:width] += wide * us[layer, :width]
            g = wide + dot(weight_ref[layer], v, 1, 0)
            if layer:
                g = g.astype(BF)
        dxs[:width] += g
        for i in range(pairs):
            low = 2 * i * edim
            both = [dxs[low : low + 40], dxs[low + edim : low + edim + 40]]
            rows_ref[i, :, at] = jnp.concatenate(both, axis=0).astype(BF)
        dense_ref[:, at] = dxs[2 * pairs * edim : width]

        for k in range(kept):
            leaving(k, n).start()

    @pl.loop(0, count // block)
    def _(n):
        for k in range(kept):
            leaving(k, n).wait()

    head_x = jnp.sum(accx[...].T, axis=0, keepdims=True)
    head_h = jnp.sum(acch[...].T, axis=0, keepdims=True)
    sums = [
        jnp.broadcast_to(jnp.sum(accs[k : k + 1], axis=1, keepdims=True), (1, 128)) for k in (0, 1)
    ]
    misc = jnp.concatenate([head_x[:, main:]] + sums + [jnp.zeros((1, main - 384), F32)], axis=1)
    bias = jnp.sum(accq[...].T, axis=0, keepdims=True)
    small_ref[0:4] = jnp.concatenate([bias, head_x[:, :main], head_h, misc], axis=0)
    small_ref[4:] = jnp.zeros_like(small_ref[4:])


def network(
    x0, labels, cross_weight, tower_in, tower_out, cross_bias, in_bias, out_bias, head, head_bias, edim, pairs
):
    layers, width = cross_weight.shape[:2]
    main = tower_out.shape[0]
    count = x0.shape[1]
    block = 256
    tall = main + 16
    vmem = pl.BlockSpec(memory_space=pltpu.VMEM)
    return pl.pallas_call(
        functools.partial(network_kernel, width, edim),
        out_shape=[
            jax.ShapeDtypeStruct((1, count), F32),
            jax.ShapeDtypeStruct((pairs, 80, count), BF),
            jax.ShapeDtypeStruct((width - 2 * pairs * edim, count), F32),
            jax.ShapeDtypeStruct((8, main), F32),
        ]
        + [jax.ShapeDtypeStruct((tall, count), BF)] * (layers - 1)
        + [jax.ShapeDtypeStruct((main + 128, count), BF)] * layers
        + [jax.ShapeDtypeStruct((main, count), BF)] * 3,
        in_specs=[vmem] * 9 + [pl.BlockSpec(memory_space=pltpu.SMEM)],
        out_specs=[vmem] * 4 + [pl.BlockSpec(memory_space=pl.ANY)] * (2 * layers + 2),
        scratch_shapes=[
            pltpu.VMEM((layers - 1, tall, count), BF),
            pltpu.VMEM((layers, main + 128, count), BF),
            pltpu.VMEM((main, count), BF),
            pltpu.VMEM((main, count), BF),
            pltpu.VMEM((main, count), BF),
            pltpu.VMEM((layers, tall, block), F32),
            pltpu.VMEM((main, block), F32),
            pltpu.VMEM((main, block), F32),
            pltpu.VMEM((tall, block), F32),
            pltpu.VMEM((main + 128, 128), F32),
            pltpu.VMEM((main, 128), F32),
            pltpu.VMEM((main, 128), F32),
            pltpu.VMEM((8, 128), F32),
            pltpu.VMEM((128, main + 128), F32),
            pltpu.VMEM((main + 128, 128), F32),
            pltpu.SemaphoreType.DMA((count // block, 2 * layers + 2)),
        ],
        compiler_params=pltpu.CompilerParams(vmem_limit_bytes=60 * 2**20),
        name="network",
    )(x0, labels, cross_weight, tower_in, tower_out, cross_bias, in_bias, out_bias, head, head_bias)


def finish_kernel(
    whole_ref, small_ref, rows_ref, pieces_ref, out_ref, table_ref, bias_ref, in_ref, share_ref, out_piece_ref,
    head_ref, sums_ref, turned,
):
    layers, main = small_ref.shape[0] - 1, small_ref.shape[2]
    rest = out_ref.shape[2] - main
    width = main + rest
    layer = pl.program_id(0)
    edim = table_ref.shape[1]

    edge = small_ref[layer]
    out_ref[0, :main, :main] = whole_ref[0].astype(F32)
    out_ref[0, :main, main:] = edge.T[:, 4 : 4 + rest]
    out_ref[0, main:, :main] = edge[:rest]
    for r in range(rest):
        out_ref[0, main + r : main + r + 1, main:] = edge[7:8, 128 * r : 128 * r + rest]
    for f in range(table_ref.shape[0]):
        table_ref[f] = rows_ref[f // 2, 40 * (f % 2) : 40 * (f % 2) + 40].astype(F32)[:edim]

    @pl.when(layer == 0)
    def _():
        for k in range(layers):
            bias_ref[k : k + 1, :main] = small_ref[k, 3:4]
            bias_ref[k : k + 1, main:] = small_ref[k, 7:8, 384 : 384 + rest]
        last = small_ref[layers]
        turned[...] = last.T
        share = in_ref.shape[0]
        me = lax.axis_index("section") * lax.axis_size("dp") + lax.axis_index("dp")
        mine = turned[pl.ds(pl.multiple_of(me * share, share), share)]
        share_ref[...] = mine
        in_ref[:, :main] = pieces_ref[0]
        in_ref[:, main:] = mine[:, :rest]
        out_piece_ref[...] = pieces_ref[1]
        head_ref[:, :main] = last[5:6]
        head_ref[:, main:width] = last[7:8, :rest]
        head_ref[:, width:] = last[6:7]
        sums_ref[...] = last[7:8, 128:384]


def finish(whole, small, rows, pieces, width, fields, edim):
    layers, main = whole.shape[:2]
    share = pieces.shape[1]
    pairs, _, count = rows.shape
    parts = 3
    step = -(-pairs // parts)

    def all_of(*shape):
        return pl.BlockSpec(shape, lambda i: (0,) * len(shape))

    return pl.pallas_call(
        finish_kernel,
        out_shape=[
            jax.ShapeDtypeStruct((layers, width, width), F32),
            jax.ShapeDtypeStruct((fields, edim, count), F32),
            jax.ShapeDtypeStruct((layers, width), F32),
            jax.ShapeDtypeStruct((share, width), F32),
            jax.ShapeDtypeStruct((share, 8), F32),
            jax.ShapeDtypeStruct((share, main), F32),
            jax.ShapeDtypeStruct((1, width + main), F32),
            jax.ShapeDtypeStruct((1, 256), F32),
        ],
        grid=(layers,),
        in_specs=[
            pl.BlockSpec((1, main, main), lambda i: (i, 0, 0)),
            all_of(layers + 1, 8, main),
            pl.BlockSpec((step, 80, count), lambda i: (i, 0, 0)),
            all_of(2, share, main),
        ],
        out_specs=[
            pl.BlockSpec((1, width, width), lambda i: (i, 0, 0)),
            pl.BlockSpec((2 * step, edim, count), lambda i: (i, 0, 0)),
            all_of(layers, width),
            all_of(share, width),
            all_of(share, 8),
            all_of(share, main),
            all_of(1, width + main),
            all_of(1, 256),
        ],
        scratch_shapes=[pltpu.VMEM((main, 8), F32)],
        compiler_params=pltpu.CompilerParams(vmem_limit_bytes=48 * 2**20),
        name="finish",
    )(whole, small, rows, pieces)


def general_body(
    ids,
    dense,
    labels,
    table,
    cross_weight,
    cross_bias,
    tower_in,
    tower_in_bias,
    tower_out,
    tower_out_bias,
    head_weight,
    head_bias,
):
    groups = lax.axis_size("dp")
    sections = lax.axis_size("section")
    device_count = groups * sections
    examples, fields = ids.shape
    table_rows, edim = table.shape[1:]
    layers, width = cross_weight.shape[:2]
    hidden = tower_out.shape[0]
    capacity = examples // groups
    sparse = fields * edim
    me = lax.axis_index("section") * groups + lax.axis_index("dp")

    idt = ids.T
    owner = idt // table_rows
    local = idt % table_rows
    owner_hot = owner[:, None, :] == jnp.arange(groups, dtype=jnp.int32)[None, :, None]
    lane = jnp.arange(examples, dtype=jnp.int32)
    before = (lane[:, None] < lane[None, :]).astype(BF)
    counts = mm(owner_hot.reshape(fields * groups, examples).astype(BF), before, (1, 0))
    rank = jnp.sum(jnp.where(owner_hot, counts.reshape(fields, groups, examples), 0.0), axis=1)
    slot = owner * capacity + rank.astype(jnp.int32)
    slot_hot = (slot[:, None, :] == lane[None, :, None]).astype(BF)
    halves = jnp.stack([local // 32, local % 32], axis=1).astype(BF)
    sent = lax.dot_general(
        halves, slot_hot, (((2,), (2,)), ((0,), (0,))), preferred_element_type=F32
    )
    requests = (sent[:, 0] * 32 + sent[:, 1]).astype(jnp.int32)
    requests = requests.reshape(fields, groups, capacity).transpose(1, 0, 2)
    arrived = lax.all_to_all(requests, "dp", 0, 0, tiled=True)
    arrived = arrived.transpose(1, 0, 2).reshape(fields, examples)
    row_hot = (
        arrived[:, None, :] == jnp.arange(table_rows, dtype=jnp.int32)[None, :, None]
    ).astype(BF)
    table_t = table.transpose(0, 2, 1)
    found = lax.dot_general(
        table_t, row_hot, (((2,), (1,)), ((0,), (0,))), preferred_element_type=F32
    ).astype(BF)
    found = found.reshape(sparse, groups, capacity).transpose(1, 0, 2)
    replies = lax.all_to_all(found, "dp", 0, 0, tiled=True)
    replies = replies.transpose(1, 0, 2).reshape(fields, edim, examples)
    embedded = lax.dot_general(
        replies, slot_hot, (((2,), (1,)), ((0,), (0,))), preferred_element_type=F32
    ).astype(BF)
    x0 = jnp.concatenate([embedded.reshape(sparse, examples), dense.T], axis=0)

    x0w = x0.astype(F32)
    xs, us = [x0], []
    for layer in range(layers):
        u = mm(cross_weight[layer], xs[-1], (0, 0)) + cross_bias[layer][:, None]
        us.append(u)
        xs.append((x0w * u + xs[-1].astype(F32)).astype(BF))
    p1 = mm(tower_in, x0, (0, 0)) + tower_in_bias[:, None]
    a1, d1 = gelu_parts(p1)
    h1 = a1.astype(BF)
    p2 = mm(tower_out, h1, (0, 0)) + tower_out_bias[:, None]
    h2, d2 = gelu_parts(p2)
    head_cross, head_tower = head_weight[:width], head_weight[width:]
    last = xs[-1].astype(F32)
    z = (
        jnp.sum(last * head_cross[:, None], axis=0)
        + jnp.sum(h2 * head_tower[:, None], axis=0)
        + head_bias[0]
    )
    probs = jax.nn.sigmoid(z)
    target = labels.astype(F32)
    loss = jnp.sum(jnp.logaddexp(0.0, z) - target * z)
    s = probs - target
    head_grad = jnp.concatenate([jnp.sum(s * last, axis=1), jnp.sum(s * h2, axis=1)])

    q2 = (s[None, :] * head_tower[:, None] * d2).astype(BF)
    tower_out_g = mm(q2, h1, (1, 1))
    q1 = (mm(tower_out, q2, (1, 0)) * d1).astype(BF)
    tower_in_g = mm(q1, x0, (1, 1))
    tower_biases = [jnp.sum(q1.astype(F32), axis=1), jnp.sum(q2.astype(F32), axis=1)]
    dx0 = mm(tower_in, q1, (1, 0))
    g = (s[None, :] * head_cross[:, None]).astype(BF)
    cross_g, cross_b = [None] * layers, [None] * layers
    for layer in reversed(range(layers)):
        gw = g.astype(F32)
        v = (gw * x0w).astype(BF)
        cross_g[layer] = mm(xs[layer], v, (1, 1))
        cross_b[layer] = jnp.sum(v.astype(F32), axis=1)
        dx0 = dx0 + gw * us[layer]
        g = gw + mm(cross_weight[layer], v, (1, 0))
        if layer:
            g = g.astype(BF)
    dx0 = dx0 + g

    packed = lax.dot_general(
        dx0[:sparse].astype(BF).reshape(fields, edim, examples),
        slot_hot,
        (((2,), (2,)), ((0,), (0,))),
        preferred_element_type=F32,
    ).astype(BF)
    packed = packed.reshape(sparse, groups, capacity).transpose(1, 0, 2)
    delivered = lax.all_to_all(packed, "dp", 0, 0, tiled=True)
    delivered = delivered.transpose(1, 0, 2).reshape(fields, edim, examples)
    table_g = lax.dot_general(
        delivered, row_hot, (((2,), (2,)), ((0,), (0,))), preferred_element_type=F32
    )
    table_g = lax.psum(table_g, "section").transpose(0, 2, 1)

    small = jnp.concatenate(
        cross_b + [head_grad, jnp.sum(s).reshape(1), loss.reshape(1)] + tower_biases
    )
    small = lax.psum(small, ("section", "dp"))
    sizes = [layers * width, width + hidden, 1, 1, hidden, hidden]
    ends = [sum(sizes[: i + 1]) for i in range(len(sizes))]
    pieces = [small[e - n : e] for e, n in zip(ends, sizes)]
    cross_b_out = pieces[0].reshape(layers, width)
    share = hidden // device_count
    bias_in, bias_out = (lax.dynamic_slice(p, (me * share,), (share,)) for p in pieces[4:])
    cross_out = lax.psum(jnp.stack(cross_g), ("section", "dp"))
    tower_in_out = lax.psum_scatter(
        tower_in_g, ("section", "dp"), scatter_dimension=0, tiled=True
    )
    tower_out_out = lax.psum_scatter(
        tower_out_g, ("section", "dp"), scatter_dimension=0, tiled=True
    )
    return (
        probs,
        pieces[3] / (examples * device_count),
        dx0[sparse:].T,
        table_g,
        cross_out,
        cross_b_out,
        tower_in_out.T,
        bias_in,
        tower_out_out.T,
        bias_out,
        pieces[1],
        pieces[2],
    )


def body(
    ids,
    dense,
    labels,
    table,
    cross_weight,
    cross_bias,
    tower_in,
    tower_in_bias,
    tower_out,
    tower_out_bias,
    head_weight,
    head_bias,
):
    groups = lax.axis_size("dp")
    sections = lax.axis_size("section")
    device_count = groups * sections
    examples, fields = ids.shape
    table_rows, edim = table.shape[1:]
    layers, width = cross_weight.shape[:2]
    hidden = tower_out.shape[0]
    capacity = examples // groups
    me = lax.axis_index("section") * groups + lax.axis_index("dp")
    idt = ids.T
    table_t = table.transpose(0, 2, 1)
    here = (sections, groups, capacity, table_rows) == (4, 8, 128, 1024)
    if here:
        x0, arrived, source = look_up(idt, table_t, dense.T)
        probs, rows, dense_g, small, *kept = network(
            x0,
            labels.reshape(1, examples),
            cross_weight,
            tower_in,
            tower_out,
            cross_bias,
            tower_in_bias.reshape(1, hidden),
            tower_out_bias.reshape(1, hidden),
            head_weight.reshape(1, width + hidden),
            head_bias,
            edim,
            fields // 2,
        )
        xs, vs = [x0] + kept[: layers - 1], kept[layers - 1 : 2 * layers - 1]
        h1, q1, q2 = kept[2 * layers - 1 :]
        whole, pieces, table_sum, small = reduce_all(
            xs + [q1, q2], vs + [x0, h1], layers, rows, source, arrived, small
        )
        small = small.reshape(layers + 1, 8, hidden)
        cross_out, table_g, cross_b_out, in_out, mine, out_out, head_out, sums = finish(
            whole, small, table_sum, pieces, width, fields, edim
        )
        return (
            probs.reshape(examples),
            sums[0, 128:129] / (examples * device_count),
            dense_g.T,
            table_g.transpose(0, 2, 1),
            cross_out,
            cross_b_out,
            in_out.T,
            mine[:, 3],
            out_out.T,
            mine[:, 4],
            head_out.reshape(width + hidden),
            sums[0, 0:1],
        )
    return general_body(
        ids, dense, labels, table, cross_weight, cross_bias, tower_in, tower_in_bias, tower_out,
        tower_out_bias, head_weight, head_bias,
    )


def solution(mesh):
    both = ("section", "dp")
    return jax.shard_map(
        body,
        mesh=mesh,
        in_specs=(P(both, None), P(both, None), P(both), P(None, "dp", None)) + (P(),) * 8,
        out_specs=(
            P(both),
            P(),
            P(both, None),
            P(None, "dp", None),
            P(),
            P(),
            P(None, both),
            P(both),
            P(None, both),
            P(both),
            P(),
            P(),
        ),
        check_vma=False,
    )
```

```python
import functools
import math

import jax
import jax.numpy as jnp
from jax import lax
from jax.experimental import pallas as pl
from jax.experimental.pallas import tpu as pltpu
from jax.sharding import PartitionSpec as P

BF = jnp.bfloat16
F32 = jnp.float32


def mm(left, right, contract):
    return lax.dot_general(
        left, right, ((contract[:1], contract[1:]), ((), ())), preferred_element_type=F32
    )


def gelu_parts(pre):
    act, back = jax.vjp(jax.nn.gelu, pre)
    return act, back(jnp.ones_like(pre))[0]


ORDER = [
    "C1 P0 u11 C0",
    "P1 u10 S0 C2",
    "u21 T10 P2 u12",
    "S1 u20 C3 u31",
    "T20 T11 u13 P3",
    "T21 C4 n0 T30",
    "u22 S2 u23 u41",
    "n1 u14 S3 u30",
    "u32 T13 n2 u51",
    "T40 T23 u61 u40",
    "n3 u42 u24 u50",
    "T12 u71 n4 u52",
    "u34 u60 u33 u62",
    "n5 u70 T33 T22",
    "u43 T43 u72 u44",
    "T31 T32 T42 T41",
    "u81 u80 u82",
]
VIEW = (2, 2, 4, 2)


def one_hot(places, count):
    rows = lax.broadcasted_iota(jnp.int32, (count, places.shape[1]), 0)
    return (rows == places).astype(F32).astype(BF)


def pick(slab, places):
    low, block = places & 255, lax.shift_right_logical(places, 8)
    blocks = [slab[:, 256 * b : 256 * b + 256] for b in range(4)]
    rows = slab.shape[0]
    every = jnp.dot(
        jnp.concatenate(blocks, axis=0), one_hot(low, 256), preferred_element_type=F32
    )
    chosen = every[:rows]
    for b in range(1, 4):
        chosen = jnp.where(block == b, every[rows * b : rows * b + rows], chosen)
    return chosen


def add_up(slab, places):
    low, block = places & 255, lax.shift_right_logical(places, 8)
    rows = slab.shape[0]
    masked = [slab * (block == b).astype(F32).astype(BF) for b in range(4)]
    every = lax.dot_general(
        jnp.concatenate(masked, axis=0),
        one_hot(low, 256),
        (((1,), (1,)), ((), ())),
        preferred_element_type=F32,
    )
    return jnp.concatenate([every[rows * b : rows * b + rows] for b in range(4)], axis=1)


def reduce_kernel(units, gathered, *refs):
    lefts, rights = refs[:units], refs[units : 2 * units]
    rows_ref, inv_ref, arr_ref, part_ref = refs[2 * units : 2 * units + 4]
    whole_out, pieces, table_hbm, small_out = refs[2 * units + 4 : 2 * units + 8]
    (
        whole, table_out, leave, grads, left, right, load, small, rc, sa1, ra1, sb1, rb1, sa2, ra2, sb2, rb2, sz, rz, packed, back, summed,
        stc, rtc, st, rt, sm, rm, rmz, send, recv, row_send, row_recv, table_send, table_recv,
    ) = refs[2 * units + 8 :]
    pairs, count = rows_ref.shape[0], rows_ref.shape[2]
    section, dp = lax.axis_index("section"), lax.axis_index("dp")
    y, c = section // 2, section % 2
    z, x = dp // 2, dp % 2
    core_peer = (y * 2 + 1 - c, dp)
    y_peer = ((1 - y) * 2 + c, dp)
    x_peer = (section, z * 2 + 1 - x)
    half = 512
    lo, hi = pl.ds(0, half), pl.ds(half, half)

    def z_peer(j):
        return (section, lax.rem(z + j, 4) * 2 + x)

    def dp_peer(j):
        return (section, lax.rem(dp + j, 8))

    peers = [core_peer, y_peer] + [dp_peer(j) for j in range(1, 8)]
    barrier = pltpu.get_barrier_semaphore()
    for peer in peers:
        pl.semaphore_signal(barrier, inc=1, device_id=peer, device_id_type=pl.DeviceIdType.MESH)

    flying = []

    def start(src, dst, m, k, peer, sems=(send, recv)):
        copy = pltpu.make_async_remote_copy(
            src_ref=src,
            dst_ref=dst,
            send_sem=sems[0].at[m, k],
            recv_sem=sems[1].at[m, k],
            device_id=peer,
            device_id_type=pl.DeviceIdType.MESH,
        )
        copy.start()
        flying.append(copy)
        return copy

    def wide(value):
        return value.astype(F32)

    copies = {}
    gone = []

    def leave_with(src, dst, k):
        copy = pltpu.make_async_copy(src, dst, leave.at[k])
        copy.start()
        gone.append(copy)

    def acc(m, stage, cols, yy, zz, xx):
        total = wide(grads[m, yy, c, zz, xx, :, cols]) + wide(rc[m, yy, zz, xx, :, cols])
        if cols is lo:
            if stage >= 2:
                total += wide(ra1[m, yy, zz])
            if stage >= 3:
                total += wide(ra2[m, zz])
        else:
            if stage >= 2:
                total += wide(rb1[m, zz, xx])
            if stage >= 3:
                total += wide(rb2[m, zz])
        return total

    tokens = " ".join(ORDER).split()
    made = [int(t[1]) for t in tokens if t[0] == "C"]

    def height(m):
        return min(lefts[m].shape[0], left.shape[1])

    def loads(turn):
        m, slot = made[turn], turn % 2
        return [
            pltpu.make_async_copy(ref.at[:rows], buf.at[slot, :rows], load.at[slot, k])
            for k, (ref, buf, rows) in enumerate(
                ((lefts[m], left, height(m)), (rights[m], right, rights[m].shape[0]))
            )
        ]

    def make(m):
        turn = made.index(m)
        slot = turn % 2
        for copy in loads(turn):
            copy.wait()
        tall = height(m) - 1024
        across = rights[m].shape[0]
        for r in range(2):
            total = lax.dot_general(
                left[slot, 512 * r : 512 * r + 512 + r * tall],
                right[slot, :across],
                (((1,), (1,)), ((), ())),
                preferred_element_type=F32,
            )
            grads[m, r] = total[:512, :1024].astype(BF).reshape(2, 4, 2, 32, 1024)
            if across > 1024:
                side = total[:512, 1024:].T
                group, at = m // 2, m % 2 * 8
                if tall:
                    small[group, at + 4 : at + 7, 512 * r : 512 * r + 512] = side[0:3]
                else:
                    small[group, at : at + 4, 512 * r : 512 * r + 512] = side[0:4]
                if tall and r:
                    small[group, at : at + 4] = total[512:516, :1024]
                    small[group, at + 7 : at + 8, 512:] = jnp.zeros((1, 512), F32)
                    for k in range(4):
                        small[group, at + 7 : at + 8, 128 * k : 128 * k + 128] = total[
                            512 + k : 513 + k, 1024:
                        ]
        if turn + 2 < units:
            for copy in loads(turn + 2):
                copy.start()

    def step0(m):
        make(m)
        copies[m, 0] = start(grads.at[m, :, 1 - c], rc.at[m], m, 0, core_peer)

    def step1(m):
        copies[m, 0].wait_recv()

        @pl.loop(0, 4)
        def _(zz):
            for i in range(2):
                sa1[m, i, zz] = acc(m, 1, lo, i, zz, 1 - x).astype(BF)
                sb1[m, zz, i] = acc(m, 1, hi, 1 - y, zz, i).astype(BF)

        copies[m, 1] = start(sa1.at[m], ra1.at[m], m, 1, x_peer)
        copies[m, 2] = start(sb1.at[m], rb1.at[m], m, 2, y_peer)

    def step2(m):
        copies[m, 1].wait_recv()
        copies[m, 2].wait_recv()

        @pl.loop(0, 4)
        def _(zz):
            sa2[m, zz] = acc(m, 2, lo, 1 - y, zz, x).astype(BF)
            sb2[m, zz] = acc(m, 2, hi, y, zz, 1 - x).astype(BF)

        copies[m, 3] = start(sa2.at[m], ra2.at[m], m, 3, y_peer)
        copies[m, 4] = start(sb2.at[m], rb2.at[m], m, 4, x_peer)

    def step3(m):
        copies[m, 3].wait_recv()
        copies[m, 4].wait_recv()
        for j in (1, 2, 3):
            zz = lax.rem(z + j, 4)
            sz[m, j - 1, :, lo] = acc(m, 3, lo, y, zz, x).astype(BF)
            sz[m, j - 1, :, hi] = acc(m, 3, hi, y, zz, x).astype(BF)
            copies[m, 4 + j] = start(sz.at[m, j - 1], rz.at[m, j - 1], m, 4 + j, z_peer(j))

    def step4(m):
        for j in (1, 2, 3):
            copies[m, 4 + j].wait_recv()
        for cols in (lo, hi):
            total = acc(m, 3, cols, y, z, x)
            for j in range(3):
                total += wide(rz[m, j, :, cols])
            if m < gathered:
                whole[m, y, c, z, x, :, cols] = total.astype(BF)
            else:
                pieces[m - gathered, :, cols] = total
        if m < gathered:
            for j in (1, 2, 3):
                mine = whole.at[m, y, c, z, x]
                copies[m, 7 + j] = start(mine, mine, m, 7 + j, z_peer(j))

    def step5(m):
        for j in (1, 2, 3):
            copies[m, 7 + j].wait_recv()
        ours = whole.at[m, y, c, :, x, :, lo]
        copies[m, 11] = start(ours, ours, m, 11, y_peer)
        ours = whole.at[m, y, c, :, x, :, hi]
        copies[m, 12] = start(ours, ours, m, 12, x_peer)

    def step6(m):
        copies[m, 11].wait_recv()
        copies[m, 12].wait_recv()
        ours = whole.at[m, :, c, :, x, :, lo]
        copies[m, 13] = start(ours, ours, m, 13, x_peer)
        ours = whole.at[m, y, c, :, :, :, hi]
        copies[m, 14] = start(ours, ours, m, 14, y_peer)

    def step7(m):
        copies[m, 13].wait_recv()
        copies[m, 14].wait_recv()
        ours = whole.at[m, :, c]
        copies[m, 15] = start(ours, ours, m, 15, core_peer)

    def step8(m):
        copies[m, 15].wait_recv()
        leave_with(whole.at[m], whole_out.at[m], m)

    def lanes(place, size):
        return pl.ds(pl.multiple_of(place * size, size), size)

    def row_copy(i, j):
        return pltpu.make_async_remote_copy(
            src_ref=packed.at[i, :, lanes(lax.rem(dp + j, 8), 128)],
            dst_ref=back.at[i, :, lanes(dp, 128)],
            send_sem=row_send.at[i, j],
            recv_sem=row_recv.at[i, j],
            device_id=dp_peer(j),
            device_id_type=pl.DeviceIdType.MESH,
        )

    cuts = [pairs * q // 4 for q in range(5)]

    def pack(q):
        @pl.loop(cuts[q], cuts[q + 1])
        def _(i):
            first = pick(rows_ref[i, 0:48], inv_ref[pl.ds(2 * i, 1)])
            second = pick(rows_ref[i, 32:80], inv_ref[pl.ds(2 * i + 1, 1)])
            packed[i] = jnp.concatenate([first[0:40], second[8:48]], axis=0).astype(BF)
            for j in range(1, 8):
                row_copy(i, j).start()
            back[i, :, lanes(dp, 128)] = packed[i, :, lanes(dp, 128)]

    def scatter(q):
        @pl.loop(cuts[q], cuts[q + 1])
        def _(i):
            for j in range(1, 8):
                row_copy(i, j).wait_recv()
            for h, (low, at) in enumerate(((0, 0), (32, 8))):
                total = add_up(back[i, low : low + 48], arr_ref[pl.ds(2 * i + h, 1)])
                summed[i, 40 * h : 40 * h + 40] = total[at : at + 40]
            stc[i] = summed[i, :, lanes(1 - c, half)].astype(BF)

        part = pl.ds(cuts[q], cuts[q + 1] - cuts[q])
        copies["t", q, 0] = start(stc.at[part], rtc.at[part], q, 0, core_peer, (table_send, table_recv))

    quarter = half // 2

    def quarter_of(yy):
        return lanes(2 * c + yy, quarter)

    def table1(q):
        copies["t", q, 0].wait_recv()

        @pl.loop(cuts[q], cuts[q + 1])
        def _(i):
            st[i] = (summed[i, :, quarter_of(1 - y)] + wide(rtc[i, :, lanes(1 - y, quarter)])).astype(BF)

        part = pl.ds(cuts[q], cuts[q + 1] - cuts[q])
        copies["t", q, 1] = start(st.at[part], rt.at[part], q, 1, y_peer, (table_send, table_recv))

    def table2(q):
        copies["t", q, 1].wait_recv()

        @pl.loop(cuts[q], cuts[q + 1])
        def _(i):
            total = summed[i, :, quarter_of(y)] + wide(rtc[i, :, lanes(y, quarter)]) + wide(rt[i])
            table_out[i, :, quarter_of(y)] = total.astype(BF)

        part = pl.ds(cuts[q], cuts[q + 1] - cuts[q])
        ours = table_out.at[part, :, quarter_of(y)]
        copies["t", q, 2] = start(ours, ours, q, 2, y_peer, (table_send, table_recv))

    def table3(q):
        copies["t", q, 2].wait_recv()
        part = pl.ds(cuts[q], cuts[q + 1] - cuts[q])
        ours = table_out.at[part, :, lanes(c, half)]
        copies["t", q, 3] = start(ours, ours, q, 3, core_peer, (table_send, table_recv))

    def table4(q):
        copies["t", q, 3].wait_recv()
        part = pl.ds(cuts[q], cuts[q + 1] - cuts[q])
        leave_with(table_out.at[part], table_hbm.at[part], gathered + q)

    s = units

    def small0():
        small[1, 12:16] = part_ref[0:4]
        copies[s, 0] = start(small.at[1 - c], rm.at[0], s, 0, core_peer)

    def small1():
        copies[s, 0].wait_recv()
        sm[0] = small[c] + rm[0]
        copies[s, 1] = start(sm.at[0], rm.at[1], s, 1, x_peer)

    def small2():
        copies[s, 1].wait_recv()
        sm[1] = sm[0] + rm[1]
        copies[s, 2] = start(sm.at[1], rm.at[2], s, 2, y_peer)

    def small3():
        copies[s, 2].wait_recv()
        sm[2] = sm[1] + rm[2]
        for j in (1, 2, 3):
            copies[s, 2 + j] = start(sm.at[2], rmz.at[j - 1], s, 2 + j, z_peer(j))

    def small4():
        for j in (1, 2, 3):
            copies[s, 2 + j].wait_recv()
        even = lax.rem(z, 2)
        near = [sm[2], rmz[0], rmz[1], rmz[2]]
        first = near[0] + near[2]
        second = near[1] + near[3]
        small_out[c] = jnp.where(even == 0, first, second) + jnp.where(even == 0, second, first)
        ours = small_out.at[c]
        copies[s, 6] = start(ours, ours, s, 6, core_peer)

    def small5():
        copies[s, 6].wait_recv()

    steps = [step1, step2, step3, step4, step5, step6, step7, step8]
    smalls = [small0, small1, small2, small3, small4, small5]
    tables = [table1, table2, table3, table4]
    for copy in loads(0) + loads(1):
        copy.start()
    pl.semaphore_wait(barrier, len(peers))
    for token in tokens:
        kind, numbers = token[0], [int(n) for n in token[1:]]
        if kind == "C":
            step0(*numbers)
        elif kind == "P":
            pack(*numbers)
        elif kind == "S":
            scatter(*numbers)
        elif kind == "n":
            smalls[numbers[0]]()
        else:
            {"u": steps, "T": tables}[kind][numbers[0] - 1](numbers[1])
    for copy in flying:
        copy.wait_send()
    for copy in gone:
        copy.wait()

    @pl.loop(0, pairs)
    def _(i):
        for j in range(1, 8):
            row_copy(i, j).wait_send()


def reduce_all(lefts, rights, gathered, rows, source, arrived, small):
    units = len(lefts)
    pairs, _, count = rows.shape
    piece = (32, 1024)
    vmem = pl.BlockSpec(memory_space=pltpu.VMEM)
    hbm = pl.BlockSpec(memory_space=pl.ANY)
    whole, pieces, table_sum, small_sum = pl.pallas_call(
        lambda *refs: reduce_kernel(units, gathered, *refs),
        out_shape=[
            jax.ShapeDtypeStruct((gathered,) + VIEW + piece, BF),
            jax.ShapeDtypeStruct((units - gathered,) + piece, F32),
            jax.ShapeDtypeStruct((pairs, 80, count), BF),
            jax.ShapeDtypeStruct((2, 16, 1024), F32),
        ],
        in_specs=[hbm] * (2 * units) + [vmem] * 4,
        out_specs=[hbm, vmem, hbm, vmem],
        scratch_shapes=[
            pltpu.VMEM((gathered,) + VIEW + piece, BF),
            pltpu.VMEM((pairs, 80, count), BF),
            pltpu.SemaphoreType.DMA((gathered + 4,)),
            pltpu.VMEM((units,) + VIEW + piece, BF),
            pltpu.VMEM((2, 1040, count), BF),
            pltpu.VMEM((2, 1152, count), BF),
            pltpu.SemaphoreType.DMA((2, 2)),
            pltpu.VMEM((2, 16, 1024), F32),
            pltpu.VMEM((units, 2, 4, 2) + piece, BF),
            pltpu.VMEM((units, 2, 4, 32, 512), BF),
            pltpu.VMEM((units, 2, 4, 32, 512), BF),
            pltpu.VMEM((units, 4, 2, 32, 512), BF),
            pltpu.VMEM((units, 4, 2, 32, 512), BF),
            pltpu.VMEM((units, 4, 32, 512), BF),
            pltpu.VMEM((units, 4, 32, 512), BF),
            pltpu.VMEM((units, 4, 32, 512), BF),
            pltpu.VMEM((units, 4, 32, 512), BF),
            pltpu.VMEM((units, 3) + piece, BF),
            pltpu.VMEM((units, 3) + piece, BF),
            pltpu.VMEM((pairs, 80, count), BF),
            pltpu.VMEM((pairs, 80, count), BF),
            pltpu.VMEM((pairs, 80, count), F32),
            pltpu.VMEM((pairs, 80, count // 2), BF),
            pltpu.VMEM((pairs, 80, count // 2), BF),
            pltpu.VMEM((pairs, 80, count // 4), BF),
            pltpu.VMEM((pairs, 80, count // 4), BF),
            pltpu.VMEM((3, 16, 1024), F32),
            pltpu.VMEM((3, 16, 1024), F32),
            pltpu.VMEM((3, 16, 1024), F32),
            pltpu.SemaphoreType.DMA((units + 1, 16)),
            pltpu.SemaphoreType.DMA((units + 1, 16)),
            pltpu.SemaphoreType.DMA((pairs, 8)),
            pltpu.SemaphoreType.DMA((pairs, 8)),
            pltpu.SemaphoreType.DMA((4, 4)),
            pltpu.SemaphoreType.DMA((4, 4)),
        ],
        compiler_params=pltpu.CompilerParams(
            collective_id=0, has_side_effects=True, vmem_limit_bytes=63 * 2**20
        ),
        name="reduce_all",
    )(
        *lefts,
        *rights,
        rows,
        source,
        arrived,
        small,
    )
    return whole.reshape(gathered, 1024, 1024), pieces, table_sum, small_sum.reshape(-1)


def lookup_kernel(
    fields, edim, ids_ref, table_ref, dense_ref, x0_ref, arr_ref, inv_ref,
    ids, slots, req, found, rep, held, pair, wide_rows, x0f, id_send, id_recv, send, recv,
):
    section, me = lax.axis_index("section"), lax.axis_index("dp")
    dot = functools.partial(jnp.dot, preferred_element_type=F32)
    count = ids.shape[1]

    def peer(j):
        return lax.rem(me + j, 8)

    def lanes(place):
        return pl.ds(pl.multiple_of(place * 128, 128), 128)

    barrier = pltpu.get_barrier_semaphore()
    for j in range(1, 8):
        pl.semaphore_signal(
            barrier, inc=1, device_id=(section, peer(j)), device_id_type=pl.DeviceIdType.MESH
        )

    ids[...] = jnp.zeros_like(ids)
    ids[:fields] = ids_ref[...]
    every = ids[...]
    owner = lax.shift_right_logical(every, 10)
    hot = jnp.concatenate([(owner == o).astype(F32) for o in range(8)], axis=0).astype(BF)
    before = (
        lax.broadcasted_iota(jnp.int32, (count, count), 0)
        < lax.broadcasted_iota(jnp.int32, (count, count), 1)
    )
    ranks = dot(hot, before.astype(F32).astype(BF))
    rank = jnp.zeros((32, count), F32)
    for o in range(8):
        rank = jnp.where(owner == o, ranks[32 * o : 32 * o + 32], rank)
    slots[...] = owner * 128 + rank.astype(jnp.int32)
    ids[...] = every & 1023
    @pl.loop(0, 4)
    def _(group):
        eight = pl.ds(pl.multiple_of(8 * group, 8), 8)
        slot8, local8 = slots[eight], ids[eight]
        place = lax.broadcasted_iota(jnp.int32, (1, count), 1)
        column = lax.broadcasted_iota(jnp.int32, (8, count), 0)
        wanted, source = [], []
        for k in range(8):
            slot, local = slot8[k : k + 1], local8[k : k + 1]
            owners = column == lax.shift_right_logical(slot, 7)
            parts = [local >> 5, local & 31, place >> 5, place & 31]
            left = jnp.concatenate(
                [jnp.where(owners, p.astype(F32), 0.0) for p in parts], axis=0
            ).astype(BF)
            right = one_hot(slot & 127, 128)
            sent = lax.dot_general(
                left, right, (((1,), (1,)), ((), ())), preferred_element_type=F32
            )
            rows = [
                (sent[n : n + 8] * 32 + sent[n + 8 : n + 16]).astype(jnp.int32) for n in (0, 16)
            ]
            for taken, r in zip((wanted, source), rows):
                taken.append(jnp.concatenate([r[o : o + 1] for o in range(8)], axis=1))
        req[eight] = jnp.concatenate(wanted, axis=0)
        inv_ref[eight] = jnp.concatenate(source, axis=0)

    def id_copy(j):
        return pltpu.make_async_remote_copy(
            src_ref=req.at[:, lanes(peer(j))],
            dst_ref=arr_ref.at[:, lanes(me)],
            send_sem=id_send.at[j],
            recv_sem=id_recv.at[j],
            device_id=(section, peer(j)),
            device_id_type=pl.DeviceIdType.MESH,
        )

    pl.semaphore_wait(barrier, 7)
    for j in range(1, 8):
        id_copy(j).start()
    arr_ref[:, lanes(me)] = req[:, lanes(me)]
    for j in range(1, 8):
        id_copy(j).wait_recv()

    def row_copy(i, j):
        return pltpu.make_async_remote_copy(
            src_ref=found.at[i, :, lanes(peer(j))],
            dst_ref=rep.at[i, :, lanes(me)],
            send_sem=send.at[i, j],
            recv_sem=recv.at[i, j],
            device_id=(section, peer(j)),
            device_id_type=pl.DeviceIdType.MESH,
        )

    pair[...] = jnp.zeros_like(pair)
    held[...] = jnp.zeros_like(held)

    @pl.loop(0, fields // 2)
    def _(i):
        for h in range(2):
            held[h, :edim] = table_ref[2 * i + h]
            chosen = pick(held[h], arr_ref[pl.ds(2 * i + h, 1)])
            pair[40 * h : 40 * h + edim] = chosen[:edim]
        found[i] = pair[...].astype(BF)
        for j in range(1, 8):
            row_copy(i, j).start()
        rep[i, :, lanes(me)] = found[i, :, lanes(me)]

    @pl.loop(0, fields // 2)
    def _(i):
        for j in range(1, 8):
            row_copy(i, j).wait_recv()
        wide_rows[2 * i] = pick(rep[i, 0:48], slots[pl.ds(2 * i, 1)])[0:40]
        wide_rows[2 * i + 1] = pick(rep[i, 32:80], slots[pl.ds(2 * i + 1, 1)])[8:48]

    sparse, extra = fields * edim, dense_ref.shape[0]
    x0f[sparse // 8 * 8 :] = jnp.zeros_like(x0f[sparse // 8 * 8 :])
    for f in range(fields):
        x0f[f * edim : f * edim + edim] = wide_rows[f, :edim]
    x0f[sparse : sparse + extra] = dense_ref[...].astype(F32)
    x0f[sparse + extra : sparse + extra + 1] = jnp.ones_like(x0f[:1])
    x0_ref[...] = x0f[...].astype(BF)

    @pl.loop(0, fields // 2)
    def _(i):
        for j in range(1, 8):
            row_copy(i, j).wait_send()

    for j in range(1, 8):
        id_copy(j).wait_send()


def look_up(ids_t, table_t, dense_t):
    fields, count = ids_t.shape
    edim = table_t.shape[1]
    tall = (fields * edim + dense_t.shape[0]) // 128 * 128 + 128
    vmem = pl.BlockSpec(memory_space=pltpu.VMEM)
    return pl.pallas_call(
        functools.partial(lookup_kernel, fields, edim),
        out_shape=[
            jax.ShapeDtypeStruct((tall, count), BF),
            jax.ShapeDtypeStruct((32, count), jnp.int32),
            jax.ShapeDtypeStruct((32, count), jnp.int32),
        ],
        in_specs=[vmem] * 3,
        out_specs=[vmem] * 3,
        scratch_shapes=[
            pltpu.VMEM((32, count), jnp.int32),
            pltpu.VMEM((32, count), jnp.int32),
            pltpu.VMEM((32, count), jnp.int32),
            pltpu.VMEM((fields // 2, 80, count), BF),
            pltpu.VMEM((fields // 2, 80, count), BF),
            pltpu.VMEM((2, 48, count), BF),
            pltpu.VMEM((80, count), F32),
            pltpu.VMEM((fields, 40, count), F32),
            pltpu.VMEM((tall, count), F32),
            pltpu.SemaphoreType.DMA((8,)),
            pltpu.SemaphoreType.DMA((8,)),
            pltpu.SemaphoreType.DMA((fields // 2, 8)),
            pltpu.SemaphoreType.DMA((fields // 2, 8)),
        ],
        compiler_params=pltpu.CompilerParams(
            collective_id=1, has_side_effects=True, vmem_limit_bytes=63 * 2**20
        ),
        name="look_up",
    )(ids_t, table_t, dense_t)


def gelu_and_slope(pre):
    root = (2.0 / math.pi) ** 0.5
    square = pre * pre
    tanh = jnp.tanh(root * pre * (1.0 + 0.044715 * square))
    cdf = 0.5 + 0.5 * tanh
    bend = 0.5 * root * (1.0 - tanh * tanh) * (1.0 + 3 * 0.044715 * square)
    return pre * cdf, cdf + pre * bend


def network_kernel(
    width, edim, x0_hbm, labels_ref, weight_hbm, in_hbm, out_hbm, bias_ref, in_bias_ref, out_bias_ref, head_ref, hb_ref,
    probs_ref, rows_ref, dense_ref, small_ref, *rest,
):
    layers = weight_hbm.shape[0]
    kept = 2 * layers + 2
    outs = rest[:kept]
    (
        x0_ref, weight_ref, in_ref, out_ref, xs, vs, h1s, q1s, q2s, gs, us, d1s, d2s, dxs, accx, acch, accq, accs,
        lines, cols, enter, leave,
    ) = rest[kept:]
    main = in_hbm.shape[1]
    edge = slice(main, main + 16)
    count = x0_hbm.shape[1]
    block = us.shape[2]
    pairs = rows_ref.shape[0]

    entering = [
        pltpu.make_async_copy(src, dst, enter.at[k])
        for k, (src, dst) in enumerate(
            [(x0_hbm, x0_ref)]
            + [(weight_hbm.at[i], weight_ref.at[i]) for i in range(layers)]
            + [(in_hbm, in_ref), (out_hbm, out_ref)]
        )
    ]
    for copy in entering:
        copy.start()

    def leaving(k, n):
        at = pl.ds(pl.multiple_of(n * block, block), block)
        here = [xs.at[i, :, at] for i in range(layers - 1)] + [vs.at[i] for i in range(layers)]
        here += [h1s.at[:, at], q1s, q2s]
        return pltpu.make_async_copy(here[k], outs[k].at[:, at], leave.at[n, k])

    def dot(a, b, ca, cb):
        return lax.dot_general(a, b, (((ca,), (cb,)), ((), ())), preferred_element_type=F32)

    def fold(value):
        return functools.reduce(
            lambda a, b: a + b, [value[:, n : n + 128] for n in range(0, value.shape[1], 128)]
        )

    for layer in range(layers):
        vs[layer, main:] = jnp.zeros_like(vs[layer, main:])
    accx[...] = jnp.zeros_like(accx)
    acch[...] = jnp.zeros_like(acch)
    accq[...] = jnp.zeros_like(accq)
    accs[...] = jnp.zeros_like(accs)
    lines[...] = jnp.zeros_like(lines)
    lines[0:layers, :width] = bias_ref[...]
    lines[layers : layers + 1, :main] = in_bias_ref[...]
    lines[layers + 1 : layers + 2, :main] = out_bias_ref[...]
    lines[layers + 2 : layers + 3, :width] = head_ref[:, :width]
    lines[layers + 3 : layers + 4, :main] = head_ref[:, width:]
    cols[...] = lines[...].T
    entering[0].wait()
    for layer in range(1, layers):
        xs[layer - 1, edge] = x0_ref[edge]
    for copy in entering[1:]:
        copy.wait()

    blocks = count // block

    def one_block(n):
        at = slice(n * block, n * block + block)

        def before(*which):
            if n:
                for k in which:
                    leaving(k, n - 1).wait()

        def x_of(layer):
            return x0_ref[:width, at] if layer == 0 else xs[layer - 1, :width, at]

        def col(k, size):
            return cols[:size, k : k + 1]

        for layer in range(layers):
            u = dot(weight_ref[layer], x_of(layer), 0, 0) + col(layer, width)
            us[layer, :width] = u
            x = (x_of(0).astype(F32) * u + x_of(layer).astype(F32)).astype(BF)
            if layer + 1 < layers:
                xs[layer, :width, at] = x
        last = x.astype(F32)
        h1, d1 = gelu_and_slope(dot(in_ref[...], x_of(0), 0, 0) + col(layers, main))
        d1s[...] = d1
        h1s[:, at] = h1.astype(BF)
        h2, d2 = gelu_and_slope(dot(out_ref[...], h1s[:, at], 0, 0) + col(layers + 1, main))
        d2s[...] = d2
        head_cross, head_tower = col(layers + 2, width), col(layers + 3, main)
        z = (
            jnp.sum(last * head_cross, axis=0, keepdims=True)
            + jnp.sum(h2 * head_tower, axis=0, keepdims=True)
            + hb_ref[0]
        )
        probs = jax.nn.sigmoid(z)
        target = labels_ref[:, at].astype(F32)
        probs_ref[:, at] = probs
        s = probs - target
        loss = jnp.maximum(z, 0.0) + jnp.log1p(jnp.exp(-jnp.abs(z))) - target * z
        accs[0:1] += fold(s)
        accs[1:2] += fold(loss)
        accx[:width] += fold(s * last)
        acch[...] += fold(s * h2)

        q2 = ((s * head_tower) * d2s[...]).astype(BF)
        before(2 * layers + 1)
        q2s[...] = q2
        acc = fold(q2.astype(F32))
        accq[...] += acc
        q1 = (dot(out_ref[...], q2, 1, 0) * d1s[...]).astype(BF)
        before(2 * layers)
        q1s[...] = q1
        g = (s * head_cross).astype(BF)
        before(*range(layers - 1, 2 * layers - 1))
        for layer in reversed(range(layers)):
            gs[layer, :width] = g
            v = (g.astype(F32) * x_of(0).astype(F32)).astype(BF)
            vs[layer, :width] = v
            g = g.astype(F32) + dot(weight_ref[layer], v, 1, 0)
            if layer:
                g = g.astype(BF)
        g += dot(in_ref[...], q1, 1, 0)
        for layer in range(layers):
            g += gs[layer, :width].astype(F32) * us[layer, :width]
        dxs[:width] = g
        for i in range(pairs):
            low = 2 * i * edim
            both = [dxs[low : low + 40], dxs[low + edim : low + edim + 40]]
            rows_ref[i, :, at] = jnp.concatenate(both, axis=0).astype(BF)
        dense_ref[:, at] = dxs[2 * pairs * edim : width]

        for k in range(kept):
            leaving(k, n).start()

    for n in range(blocks):
        one_block(n)
    for n in range(blocks):
        for k in range(kept):
            if n == blocks - 1 or k < layers - 1 or k == 2 * layers - 1:
                leaving(k, n).wait()

    head_x = jnp.sum(accx[...].T, axis=0, keepdims=True)
    head_h = jnp.sum(acch[...].T, axis=0, keepdims=True)
    sums = [
        jnp.broadcast_to(jnp.sum(accs[k : k + 1], axis=1, keepdims=True), (1, 128)) for k in (0, 1)
    ]
    misc = jnp.concatenate([head_x[:, main:]] + sums + [jnp.zeros((1, main - 384), F32)], axis=1)
    bias = jnp.sum(accq[...].T, axis=0, keepdims=True)
    small_ref[0:4] = jnp.concatenate([bias, head_x[:, :main], head_h, misc], axis=0)
    small_ref[4:] = jnp.zeros_like(small_ref[4:])


def network(
    x0, labels, cross_weight, tower_in, tower_out, cross_bias, in_bias, out_bias, head, head_bias, edim, pairs
):
    layers, width = cross_weight.shape[:2]
    main = tower_out.shape[0]
    count = x0.shape[1]
    block = 512
    tall = main + 16
    vmem = pl.BlockSpec(memory_space=pltpu.VMEM)
    hbm = pl.BlockSpec(memory_space=pl.ANY)
    return pl.pallas_call(
        functools.partial(network_kernel, width, edim),
        out_shape=[
            jax.ShapeDtypeStruct((1, count), F32),
            jax.ShapeDtypeStruct((pairs, 80, count), BF),
            jax.ShapeDtypeStruct((width - 2 * pairs * edim, count), F32),
            jax.ShapeDtypeStruct((8, main), F32),
        ]
        + [jax.ShapeDtypeStruct((tall, count), BF)] * (layers - 1)
        + [jax.ShapeDtypeStruct((main + 128, count), BF)] * layers
        + [jax.ShapeDtypeStruct((main, count), BF)] * 3,
        in_specs=[hbm, vmem, hbm, hbm, hbm] + [vmem] * 4 + [pl.BlockSpec(memory_space=pltpu.SMEM)],
        out_specs=[vmem] * 4 + [pl.BlockSpec(memory_space=pl.ANY)] * (2 * layers + 2),
        scratch_shapes=[
            pltpu.VMEM(x0.shape, BF),
            pltpu.VMEM(cross_weight.shape, BF),
            pltpu.VMEM(tower_in.shape, BF),
            pltpu.VMEM(tower_out.shape, BF),
            pltpu.VMEM((layers - 1, tall, count), BF),
            pltpu.VMEM((layers, main + 128, block), BF),
            pltpu.VMEM((main, count), BF),
            pltpu.VMEM((main, block), BF),
            pltpu.VMEM((main, block), BF),
            pltpu.VMEM((layers, tall, block), BF),
            pltpu.VMEM((layers, tall, block), F32),
            pltpu.VMEM((main, block), F32),
            pltpu.VMEM((main, block), F32),
            pltpu.VMEM((tall, block), F32),
            pltpu.VMEM((main + 128, 128), F32),
            pltpu.VMEM((main, 128), F32),
            pltpu.VMEM((main, 128), F32),
            pltpu.VMEM((8, 128), F32),
            pltpu.VMEM((128, main + 128), F32),
            pltpu.VMEM((main + 128, 128), F32),
            pltpu.SemaphoreType.DMA((layers + 3,)),
            pltpu.SemaphoreType.DMA((count // block, 2 * layers + 2)),
        ],
        compiler_params=pltpu.CompilerParams(vmem_limit_bytes=63 * 2**20),
        name="network",
    )(x0, labels, cross_weight, tower_in, tower_out, cross_bias, in_bias, out_bias, head, head_bias)


def finish_kernel(
    whole_ref, small_ref, rows_ref, pieces_ref, out_ref, table_ref, bias_ref, in_ref, share_ref, out_piece_ref,
    head_ref, sums_ref, turned,
):
    layers, main = small_ref.shape[0] - 1, small_ref.shape[2]
    rest = out_ref.shape[2] - main
    width = main + rest
    layer = pl.program_id(0)
    edim = table_ref.shape[1]

    edge = small_ref[layer]
    out_ref[0, :main, :main] = whole_ref[0].astype(F32)
    out_ref[0, :main, main:] = edge.T[:, 4 : 4 + rest]
    out_ref[0, main:, :main] = edge[:rest]
    for r in range(rest):
        out_ref[0, main + r : main + r + 1, main:] = edge[7:8, 128 * r : 128 * r + rest]
    for f in range(table_ref.shape[0]):
        table_ref[f] = rows_ref[f // 2, 40 * (f % 2) : 40 * (f % 2) + 40].astype(F32)[:edim]

    @pl.when(layer == 0)
    def _():
        for k in range(layers):
            bias_ref[k : k + 1, :main] = small_ref[k, 3:4]
            bias_ref[k : k + 1, main:] = small_ref[k, 7:8, 384 : 384 + rest]
        last = small_ref[layers]
        turned[...] = last.T
        share = in_ref.shape[0]
        me = lax.axis_index("section") * lax.axis_size("dp") + lax.axis_index("dp")
        mine = turned[pl.ds(pl.multiple_of(me * share, share), share)]
        share_ref[...] = mine
        in_ref[:, :main] = pieces_ref[0]
        in_ref[:, main:] = mine[:, :rest]
        out_piece_ref[...] = pieces_ref[1]
        head_ref[:, :main] = last[5:6]
        head_ref[:, main:width] = last[7:8, :rest]
        head_ref[:, width:] = last[6:7]
        sums_ref[...] = last[7:8, 128:384]


def finish(whole, small, rows, pieces, width, fields, edim):
    layers, main = whole.shape[:2]
    share = pieces.shape[1]
    pairs, _, count = rows.shape
    parts = 3
    step = -(-pairs // parts)

    def all_of(*shape):
        return pl.BlockSpec(shape, lambda i: (0,) * len(shape))

    return pl.pallas_call(
        finish_kernel,
        out_shape=[
            jax.ShapeDtypeStruct((layers, width, width), F32),
            jax.ShapeDtypeStruct((fields, edim, count), F32),
            jax.ShapeDtypeStruct((layers, width), F32),
            jax.ShapeDtypeStruct((share, width), F32),
            jax.ShapeDtypeStruct((share, 8), F32),
            jax.ShapeDtypeStruct((share, main), F32),
            jax.ShapeDtypeStruct((1, width + main), F32),
            jax.ShapeDtypeStruct((1, 256), F32),
        ],
        grid=(layers,),
        in_specs=[
            pl.BlockSpec((1, main, main), lambda i: (i, 0, 0)),
            all_of(layers + 1, 8, main),
            pl.BlockSpec((step, 80, count), lambda i: (i, 0, 0)),
            all_of(2, share, main),
        ],
        out_specs=[
            pl.BlockSpec((1, width, width), lambda i: (i, 0, 0)),
            pl.BlockSpec((2 * step, edim, count), lambda i: (i, 0, 0)),
            all_of(layers, width),
            all_of(share, width),
            all_of(share, 8),
            all_of(share, main),
            all_of(1, width + main),
            all_of(1, 256),
        ],
        scratch_shapes=[pltpu.VMEM((main, 8), F32)],
        compiler_params=pltpu.CompilerParams(vmem_limit_bytes=63 * 2**20),
        name="finish",
    )(whole, small, rows, pieces)


def general_body(
    ids,
    dense,
    labels,
    table,
    cross_weight,
    cross_bias,
    tower_in,
    tower_in_bias,
    tower_out,
    tower_out_bias,
    head_weight,
    head_bias,
):
    groups = lax.axis_size("dp")
    sections = lax.axis_size("section")
    device_count = groups * sections
    examples, fields = ids.shape
    table_rows, edim = table.shape[1:]
    layers, width = cross_weight.shape[:2]
    hidden = tower_out.shape[0]
    capacity = examples // groups
    sparse = fields * edim
    me = lax.axis_index("section") * groups + lax.axis_index("dp")

    idt = ids.T
    owner = idt // table_rows
    local = idt % table_rows
    owner_hot = owner[:, None, :] == jnp.arange(groups, dtype=jnp.int32)[None, :, None]
    lane = jnp.arange(examples, dtype=jnp.int32)
    before = (lane[:, None] < lane[None, :]).astype(BF)
    counts = mm(owner_hot.reshape(fields * groups, examples).astype(BF), before, (1, 0))
    rank = jnp.sum(jnp.where(owner_hot, counts.reshape(fields, groups, examples), 0.0), axis=1)
    slot = owner * capacity + rank.astype(jnp.int32)
    slot_hot = (slot[:, None, :] == lane[None, :, None]).astype(BF)
    halves = jnp.stack([local // 32, local % 32], axis=1).astype(BF)
    sent = lax.dot_general(
        halves, slot_hot, (((2,), (2,)), ((0,), (0,))), preferred_element_type=F32
    )
    requests = (sent[:, 0] * 32 + sent[:, 1]).astype(jnp.int32)
    requests = requests.reshape(fields, groups, capacity).transpose(1, 0, 2)
    arrived = lax.all_to_all(requests, "dp", 0, 0, tiled=True)
    arrived = arrived.transpose(1, 0, 2).reshape(fields, examples)
    row_hot = (
        arrived[:, None, :] == jnp.arange(table_rows, dtype=jnp.int32)[None, :, None]
    ).astype(BF)
    table_t = table.transpose(0, 2, 1)
    found = lax.dot_general(
        table_t, row_hot, (((2,), (1,)), ((0,), (0,))), preferred_element_type=F32
    ).astype(BF)
    found = found.reshape(sparse, groups, capacity).transpose(1, 0, 2)
    replies = lax.all_to_all(found, "dp", 0, 0, tiled=True)
    replies = replies.transpose(1, 0, 2).reshape(fields, edim, examples)
    embedded = lax.dot_general(
        replies, slot_hot, (((2,), (1,)), ((0,), (0,))), preferred_element_type=F32
    ).astype(BF)
    x0 = jnp.concatenate([embedded.reshape(sparse, examples), dense.T], axis=0)

    x0w = x0.astype(F32)
    xs, us = [x0], []
    for layer in range(layers):
        u = mm(cross_weight[layer], xs[-1], (0, 0)) + cross_bias[layer][:, None]
        us.append(u)
        xs.append((x0w * u + xs[-1].astype(F32)).astype(BF))
    p1 = mm(tower_in, x0, (0, 0)) + tower_in_bias[:, None]
    a1, d1 = gelu_parts(p1)
    h1 = a1.astype(BF)
    p2 = mm(tower_out, h1, (0, 0)) + tower_out_bias[:, None]
    h2, d2 = gelu_parts(p2)
    head_cross, head_tower = head_weight[:width], head_weight[width:]
    last = xs[-1].astype(F32)
    z = (
        jnp.sum(last * head_cross[:, None], axis=0)
        + jnp.sum(h2 * head_tower[:, None], axis=0)
        + head_bias[0]
    )
    probs = jax.nn.sigmoid(z)
    target = labels.astype(F32)
    loss = jnp.sum(jnp.logaddexp(0.0, z) - target * z)
    s = probs - target
    head_grad = jnp.concatenate([jnp.sum(s * last, axis=1), jnp.sum(s * h2, axis=1)])

    q2 = (s[None, :] * head_tower[:, None] * d2).astype(BF)
    tower_out_g = mm(q2, h1, (1, 1))
    q1 = (mm(tower_out, q2, (1, 0)) * d1).astype(BF)
    tower_in_g = mm(q1, x0, (1, 1))
    tower_biases = [jnp.sum(q1.astype(F32), axis=1), jnp.sum(q2.astype(F32), axis=1)]
    dx0 = mm(tower_in, q1, (1, 0))
    g = (s[None, :] * head_cross[:, None]).astype(BF)
    cross_g, cross_b = [None] * layers, [None] * layers
    for layer in reversed(range(layers)):
        gw = g.astype(F32)
        v = (gw * x0w).astype(BF)
        cross_g[layer] = mm(xs[layer], v, (1, 1))
        cross_b[layer] = jnp.sum(v.astype(F32), axis=1)
        dx0 = dx0 + gw * us[layer]
        g = gw + mm(cross_weight[layer], v, (1, 0))
        if layer:
            g = g.astype(BF)
    dx0 = dx0 + g

    packed = lax.dot_general(
        dx0[:sparse].astype(BF).reshape(fields, edim, examples),
        slot_hot,
        (((2,), (2,)), ((0,), (0,))),
        preferred_element_type=F32,
    ).astype(BF)
    packed = packed.reshape(sparse, groups, capacity).transpose(1, 0, 2)
    delivered = lax.all_to_all(packed, "dp", 0, 0, tiled=True)
    delivered = delivered.transpose(1, 0, 2).reshape(fields, edim, examples)
    table_g = lax.dot_general(
        delivered, row_hot, (((2,), (2,)), ((0,), (0,))), preferred_element_type=F32
    )
    table_g = lax.psum(table_g, "section").transpose(0, 2, 1)

    small = jnp.concatenate(
        cross_b + [head_grad, jnp.sum(s).reshape(1), loss.reshape(1)] + tower_biases
    )
    small = lax.psum(small, ("section", "dp"))
    sizes = [layers * width, width + hidden, 1, 1, hidden, hidden]
    ends = [sum(sizes[: i + 1]) for i in range(len(sizes))]
    pieces = [small[e - n : e] for e, n in zip(ends, sizes)]
    cross_b_out = pieces[0].reshape(layers, width)
    share = hidden // device_count
    bias_in, bias_out = (lax.dynamic_slice(p, (me * share,), (share,)) for p in pieces[4:])
    cross_out = lax.psum(jnp.stack(cross_g), ("section", "dp"))
    tower_in_out = lax.psum_scatter(
        tower_in_g, ("section", "dp"), scatter_dimension=0, tiled=True
    )
    tower_out_out = lax.psum_scatter(
        tower_out_g, ("section", "dp"), scatter_dimension=0, tiled=True
    )
    return (
        probs,
        pieces[3] / (examples * device_count),
        dx0[sparse:].T,
        table_g,
        cross_out,
        cross_b_out,
        tower_in_out.T,
        bias_in,
        tower_out_out.T,
        bias_out,
        pieces[1],
        pieces[2],
    )


def body(
    ids,
    dense,
    labels,
    table,
    cross_weight,
    cross_bias,
    tower_in,
    tower_in_bias,
    tower_out,
    tower_out_bias,
    head_weight,
    head_bias,
):
    groups = lax.axis_size("dp")
    sections = lax.axis_size("section")
    device_count = groups * sections
    examples, fields = ids.shape
    table_rows, edim = table.shape[1:]
    layers, width = cross_weight.shape[:2]
    hidden = tower_out.shape[0]
    capacity = examples // groups
    me = lax.axis_index("section") * groups + lax.axis_index("dp")
    idt = ids.T
    table_t = table.transpose(0, 2, 1)
    here = (sections, groups, capacity, table_rows) == (4, 8, 128, 1024)
    if here:
        x0, arrived, source = look_up(idt, table_t, dense.T)
        probs, rows, dense_g, small, *kept = network(
            x0,
            labels.reshape(1, examples),
            cross_weight,
            tower_in,
            tower_out,
            cross_bias,
            tower_in_bias.reshape(1, hidden),
            tower_out_bias.reshape(1, hidden),
            head_weight.reshape(1, width + hidden),
            head_bias,
            edim,
            fields // 2,
        )
        xs, vs = [x0] + kept[: layers - 1], kept[layers - 1 : 2 * layers - 1]
        h1, q1, q2 = kept[2 * layers - 1 :]
        whole, pieces, table_sum, small = reduce_all(
            xs + [q1, q2], vs + [x0, h1], layers, rows, source, arrived, small
        )
        small = small.reshape(layers + 1, 8, hidden)
        cross_out, table_g, cross_b_out, in_out, mine, out_out, head_out, sums = finish(
            whole, small, table_sum, pieces, width, fields, edim
        )
        return (
            probs.reshape(examples),
            sums[0, 128:129] / (examples * device_count),
            dense_g.T,
            table_g.transpose(0, 2, 1),
            cross_out,
            cross_b_out,
            in_out.T,
            mine[:, 3],
            out_out.T,
            mine[:, 4],
            head_out.reshape(width + hidden),
            sums[0, 0:1],
        )
    return general_body(
        ids, dense, labels, table, cross_weight, cross_bias, tower_in, tower_in_bias, tower_out,
        tower_out_bias, head_weight, head_bias,
    )


def solution(mesh):
    both = ("section", "dp")
    return jax.shard_map(
        body,
        mesh=mesh,
        in_specs=(P(both, None), P(both, None), P(both), P(None, "dp", None)) + (P(),) * 8,
        out_specs=(
            P(both),
            P(),
            P(both, None),
            P(None, "dp", None),
            P(),
            P(),
            P(None, both),
            P(both),
            P(None, both),
            P(both),
            P(),
            P(),
        ),
        check_vma=False,
    )
```

```python
import functools
import math

import jax
import jax.numpy as jnp
from jax import lax
from jax.experimental import pallas as pl
from jax.experimental.pallas import tpu as pltpu
from jax.sharding import PartitionSpec as P

BF = jnp.bfloat16
F32 = jnp.float32


def mm(left, right, contract):
    return lax.dot_general(
        left, right, ((contract[:1], contract[1:]), ((), ())), preferred_element_type=F32
    )


def gelu_parts(pre):
    act, back = jax.vjp(jax.nn.gelu, pre)
    return act, back(jnp.ones_like(pre))[0]


ORDER = [
    "P3 P4 C1 P1",
    "u11 C2 C0 u12",
    "u21 P0 u10 C4",
    "S1 u31 T11 u14",
    "S4 T21 P5 u22",
    "T14 C3 u20 u41",
    "T24 u13 S5 u32",
    "u24 n0 T15 u30",
    "n1 S0 u51 T10",
    "u42 u23 T25 T20",
    "u61 u40 S3 n2",
    "T13 T30 u52 P2",
    "T31 T34 u50 T40",
    "n3 u62 u60 u33",
    "T35 u71 u34 S2",
    "T12 u72 n4 T23",
    "T22 u70 T33 n5",
    "T32 u80 u43 T43",
    "u44 u82 T44 T42",
    "T41 T45 u81",
]
PARTS = 6
VIEW = (2, 2, 4, 2)


def one_hot(places, count):
    rows = lax.broadcasted_iota(jnp.int32, (count, places.shape[1]), 0)
    return (rows == places).astype(F32).astype(BF)


def pick(slab, places):
    low, block = places & 255, lax.shift_right_logical(places, 8)
    blocks = [slab[:, 256 * b : 256 * b + 256] for b in range(4)]
    rows = slab.shape[0]
    every = jnp.dot(
        jnp.concatenate(blocks, axis=0), one_hot(low, 256), preferred_element_type=F32
    )
    chosen = every[:rows]
    for b in range(1, 4):
        chosen = jnp.where(block == b, every[rows * b : rows * b + rows], chosen)
    return chosen


def add_up(slab, places):
    low, block = places & 255, lax.shift_right_logical(places, 8)
    rows = slab.shape[0]
    masked = [slab * (block == b).astype(F32).astype(BF) for b in range(4)]
    every = lax.dot_general(
        jnp.concatenate(masked, axis=0),
        one_hot(low, 256),
        (((1,), (1,)), ((), ())),
        preferred_element_type=F32,
    )
    return jnp.concatenate([every[rows * b : rows * b + rows] for b in range(4)], axis=1)


def reduce_kernel(units, gathered, *refs):
    lefts, rights = refs[:units], refs[units : 2 * units]
    rows_ref, inv_ref, arr_ref, part_ref = refs[2 * units : 2 * units + 4]
    whole_out, pieces, table_hbm, small_out = refs[2 * units + 4 : 2 * units + 8]
    (
        whole, table_out, leave, grads, left, right, load, small, rc, sa1, ra1, sb1, rb1, sa2, ra2, sb2, rb2, sz, rz, packed, back, summed,
        stc, rtc, st, rt, sm, rm, rmz, send, recv, row_send, row_recv, table_send, table_recv,
    ) = refs[2 * units + 8 :]
    pairs, count = rows_ref.shape[0], rows_ref.shape[2]
    section, dp = lax.axis_index("section"), lax.axis_index("dp")
    y, c = section // 2, section % 2
    z, x = dp // 2, dp % 2
    core_peer = (y * 2 + 1 - c, dp)
    y_peer = ((1 - y) * 2 + c, dp)
    x_peer = (section, z * 2 + 1 - x)
    half = 512
    lo, hi = pl.ds(0, half), pl.ds(half, half)

    def z_peer(j):
        return (section, lax.rem(z + j, 4) * 2 + x)

    def dp_peer(j):
        return (section, lax.rem(dp + j, 8))

    peers = [core_peer, y_peer] + [dp_peer(j) for j in range(1, 8)]
    barrier = pltpu.get_barrier_semaphore()
    for peer in peers:
        pl.semaphore_signal(barrier, inc=1, device_id=peer, device_id_type=pl.DeviceIdType.MESH)

    flying = []

    def start(src, dst, m, k, peer, sems=(send, recv)):
        copy = pltpu.make_async_remote_copy(
            src_ref=src,
            dst_ref=dst,
            send_sem=sems[0].at[m, k],
            recv_sem=sems[1].at[m, k],
            device_id=peer,
            device_id_type=pl.DeviceIdType.MESH,
        )
        copy.start()
        flying.append(copy)
        return copy

    def wide(value):
        return value.astype(F32)

    copies = {}
    gone = []

    def leave_with(src, dst, k):
        copy = pltpu.make_async_copy(src, dst, leave.at[k])
        copy.start()
        gone.append(copy)

    def acc(m, stage, cols, yy, zz, xx):
        total = wide(grads[m, yy, c, zz, xx, :, cols]) + wide(rc[m, yy, zz, xx, :, cols])
        if cols is lo:
            if stage >= 2:
                total += wide(ra1[m, yy, zz])
            if stage >= 3:
                total += wide(ra2[m, zz])
        else:
            if stage >= 2:
                total += wide(rb1[m, zz, xx])
            if stage >= 3:
                total += wide(rb2[m, zz])
        return total

    tokens = " ".join(ORDER).split()
    made = [int(t[1]) for t in tokens if t[0] == "C"]

    def height(m):
        return min(lefts[m].shape[0], left.shape[1])

    def loads(turn):
        m, slot = made[turn], turn % 2
        return [
            pltpu.make_async_copy(ref.at[:rows], buf.at[slot, :rows], load.at[slot, k])
            for k, (ref, buf, rows) in enumerate(
                ((lefts[m], left, height(m)), (rights[m], right, rights[m].shape[0]))
            )
        ]

    def make(m):
        turn = made.index(m)
        slot = turn % 2
        for copy in loads(turn):
            copy.wait()
        tall = height(m) - 1024
        across = rights[m].shape[0]
        for r in range(2):
            total = lax.dot_general(
                left[slot, 512 * r : 512 * r + 512 + r * tall],
                right[slot, :across],
                (((1,), (1,)), ((), ())),
                preferred_element_type=F32,
            )
            grads[m, r] = total[:512, :1024].astype(BF).reshape(2, 4, 2, 32, 1024)
            if across > 1024:
                side = total[:512, 1024:].T
                group, at = m // 2, m % 2 * 8
                if tall:
                    small[group, at + 4 : at + 7, 512 * r : 512 * r + 512] = side[0:3]
                else:
                    small[group, at : at + 4, 512 * r : 512 * r + 512] = side[0:4]
                if tall and r:
                    small[group, at : at + 4] = total[512:516, :1024]
                    small[group, at + 7 : at + 8, 512:] = jnp.zeros((1, 512), F32)
                    for k in range(4):
                        small[group, at + 7 : at + 8, 128 * k : 128 * k + 128] = total[
                            512 + k : 513 + k, 1024:
                        ]
        if turn + 2 < units:
            for copy in loads(turn + 2):
                copy.start()

    def step0(m):
        make(m)
        copies[m, 0] = start(grads.at[m, :, 1 - c], rc.at[m], m, 0, core_peer)

    def step1(m):
        copies[m, 0].wait_recv()

        @pl.loop(0, 4)
        def _(zz):
            for i in range(2):
                sa1[m, i, zz] = acc(m, 1, lo, i, zz, 1 - x).astype(BF)
                sb1[m, zz, i] = acc(m, 1, hi, 1 - y, zz, i).astype(BF)

        copies[m, 1] = start(sa1.at[m], ra1.at[m], m, 1, x_peer)
        copies[m, 2] = start(sb1.at[m], rb1.at[m], m, 2, y_peer)

    def step2(m):
        copies[m, 1].wait_recv()
        copies[m, 2].wait_recv()

        @pl.loop(0, 4)
        def _(zz):
            sa2[m, zz] = acc(m, 2, lo, 1 - y, zz, x).astype(BF)
            sb2[m, zz] = acc(m, 2, hi, y, zz, 1 - x).astype(BF)

        copies[m, 3] = start(sa2.at[m], ra2.at[m], m, 3, y_peer)
        copies[m, 4] = start(sb2.at[m], rb2.at[m], m, 4, x_peer)

    def step3(m):
        copies[m, 3].wait_recv()
        copies[m, 4].wait_recv()
        for j in (1, 2, 3):
            zz = lax.rem(z + j, 4)
            sz[m, j - 1, :, lo] = acc(m, 3, lo, y, zz, x).astype(BF)
            sz[m, j - 1, :, hi] = acc(m, 3, hi, y, zz, x).astype(BF)
            copies[m, 4 + j] = start(sz.at[m, j - 1], rz.at[m, j - 1], m, 4 + j, z_peer(j))

    def step4(m):
        for j in (1, 2, 3):
            copies[m, 4 + j].wait_recv()
        for cols in (lo, hi):
            total = acc(m, 3, cols, y, z, x)
            for j in range(3):
                total += wide(rz[m, j, :, cols])
            if m < gathered:
                whole[m, y, c, z, x, :, cols] = total.astype(BF)
            else:
                pieces[m - gathered, :, cols] = total
        if m < gathered:
            for j in (1, 2, 3):
                mine = whole.at[m, y, c, z, x]
                copies[m, 7 + j] = start(mine, mine, m, 7 + j, z_peer(j))

    def step5(m):
        for j in (1, 2, 3):
            copies[m, 7 + j].wait_recv()
        ours = whole.at[m, y, c, :, x, :, lo]
        copies[m, 11] = start(ours, ours, m, 11, y_peer)
        ours = whole.at[m, y, c, :, x, :, hi]
        copies[m, 12] = start(ours, ours, m, 12, x_peer)

    def step6(m):
        copies[m, 11].wait_recv()
        copies[m, 12].wait_recv()
        ours = whole.at[m, :, c, :, x, :, lo]
        copies[m, 13] = start(ours, ours, m, 13, x_peer)
        ours = whole.at[m, y, c, :, :, :, hi]
        copies[m, 14] = start(ours, ours, m, 14, y_peer)

    def step7(m):
        copies[m, 13].wait_recv()
        copies[m, 14].wait_recv()
        ours = whole.at[m, :, c]
        copies[m, 15] = start(ours, ours, m, 15, core_peer)

    def step8(m):
        copies[m, 15].wait_recv()
        leave_with(whole.at[m], whole_out.at[m], m)

    def lanes(place, size):
        return pl.ds(pl.multiple_of(place * size, size), size)

    def row_copy(i, j):
        return pltpu.make_async_remote_copy(
            src_ref=packed.at[i, :, lanes(lax.rem(dp + j, 8), 128)],
            dst_ref=back.at[i, :, lanes(dp, 128)],
            send_sem=row_send.at[i, j],
            recv_sem=row_recv.at[i, j],
            device_id=dp_peer(j),
            device_id_type=pl.DeviceIdType.MESH,
        )

    cuts = [pairs * q // PARTS for q in range(PARTS + 1)]

    def pack(q):
        @pl.loop(cuts[q], cuts[q + 1])
        def _(i):
            first = pick(rows_ref[i, 0:48], inv_ref[pl.ds(2 * i, 1)])
            second = pick(rows_ref[i, 32:80], inv_ref[pl.ds(2 * i + 1, 1)])
            packed[i] = jnp.concatenate([first[0:40], second[8:48]], axis=0).astype(BF)
            for j in range(1, 8):
                row_copy(i, j).start()
            back[i, :, lanes(dp, 128)] = packed[i, :, lanes(dp, 128)]

    def scatter(q):
        @pl.loop(cuts[q], cuts[q + 1])
        def _(i):
            for j in range(1, 8):
                row_copy(i, j).wait_recv()
            for h, (low, at) in enumerate(((0, 0), (32, 8))):
                total = add_up(back[i, low : low + 48], arr_ref[pl.ds(2 * i + h, 1)])
                summed[i, 40 * h : 40 * h + 40] = total[at : at + 40]
            stc[i] = summed[i, :, lanes(1 - c, half)].astype(BF)

        part = pl.ds(cuts[q], cuts[q + 1] - cuts[q])
        copies["t", q, 0] = start(stc.at[part], rtc.at[part], q, 0, core_peer, (table_send, table_recv))

    quarter = half // 2

    def quarter_of(yy):
        return lanes(2 * c + yy, quarter)

    def table1(q):
        copies["t", q, 0].wait_recv()

        @pl.loop(cuts[q], cuts[q + 1])
        def _(i):
            st[i] = (summed[i, :, quarter_of(1 - y)] + wide(rtc[i, :, lanes(1 - y, quarter)])).astype(BF)

        part = pl.ds(cuts[q], cuts[q + 1] - cuts[q])
        copies["t", q, 1] = start(st.at[part], rt.at[part], q, 1, y_peer, (table_send, table_recv))

    def table2(q):
        copies["t", q, 1].wait_recv()

        @pl.loop(cuts[q], cuts[q + 1])
        def _(i):
            total = summed[i, :, quarter_of(y)] + wide(rtc[i, :, lanes(y, quarter)]) + wide(rt[i])
            table_out[i, :, quarter_of(y)] = total.astype(BF)

        part = pl.ds(cuts[q], cuts[q + 1] - cuts[q])
        ours = table_out.at[part, :, quarter_of(y)]
        copies["t", q, 2] = start(ours, ours, q, 2, y_peer, (table_send, table_recv))

    def table3(q):
        copies["t", q, 2].wait_recv()
        part = pl.ds(cuts[q], cuts[q + 1] - cuts[q])
        ours = table_out.at[part, :, lanes(c, half)]
        copies["t", q, 3] = start(ours, ours, q, 3, core_peer, (table_send, table_recv))

    def table4(q):
        copies["t", q, 3].wait_recv()
        part = pl.ds(cuts[q], cuts[q + 1] - cuts[q])
        leave_with(table_out.at[part], table_hbm.at[part], gathered + q)

    s = units

    def small0():
        small[1, 12:16] = part_ref[0:4]
        copies[s, 0] = start(small.at[1 - c], rm.at[0], s, 0, core_peer)

    def small1():
        copies[s, 0].wait_recv()
        sm[0] = small[c] + rm[0]
        copies[s, 1] = start(sm.at[0], rm.at[1], s, 1, x_peer)

    def small2():
        copies[s, 1].wait_recv()
        sm[1] = sm[0] + rm[1]
        copies[s, 2] = start(sm.at[1], rm.at[2], s, 2, y_peer)

    def small3():
        copies[s, 2].wait_recv()
        sm[2] = sm[1] + rm[2]
        for j in (1, 2, 3):
            copies[s, 2 + j] = start(sm.at[2], rmz.at[j - 1], s, 2 + j, z_peer(j))

    def small4():
        for j in (1, 2, 3):
            copies[s, 2 + j].wait_recv()
        even = lax.rem(z, 2)
        near = [sm[2], rmz[0], rmz[1], rmz[2]]
        first = near[0] + near[2]
        second = near[1] + near[3]
        small_out[c] = jnp.where(even == 0, first, second) + jnp.where(even == 0, second, first)
        ours = small_out.at[c]
        copies[s, 6] = start(ours, ours, s, 6, core_peer)

    def small5():
        copies[s, 6].wait_recv()

    steps = [step1, step2, step3, step4, step5, step6, step7, step8]
    smalls = [small0, small1, small2, small3, small4, small5]
    tables = [table1, table2, table3, table4]
    for copy in loads(0) + loads(1):
        copy.start()
    pl.semaphore_wait(barrier, len(peers))
    for token in tokens:
        kind, numbers = token[0], [int(n) for n in token[1:]]
        if kind == "C":
            step0(*numbers)
        elif kind == "P":
            pack(*numbers)
        elif kind == "S":
            scatter(*numbers)
        elif kind == "n":
            smalls[numbers[0]]()
        else:
            {"u": steps, "T": tables}[kind][numbers[0] - 1](numbers[1])
    for copy in flying:
        copy.wait_send()
    for copy in gone:
        copy.wait()

    @pl.loop(0, pairs)
    def _(i):
        for j in range(1, 8):
            row_copy(i, j).wait_send()


def reduce_all(lefts, rights, gathered, rows, source, arrived, small):
    units = len(lefts)
    pairs, _, count = rows.shape
    piece = (32, 1024)
    vmem = pl.BlockSpec(memory_space=pltpu.VMEM)
    hbm = pl.BlockSpec(memory_space=pl.ANY)
    whole, pieces, table_sum, small_sum = pl.pallas_call(
        lambda *refs: reduce_kernel(units, gathered, *refs),
        out_shape=[
            jax.ShapeDtypeStruct((gathered,) + VIEW + piece, BF),
            jax.ShapeDtypeStruct((units - gathered,) + piece, F32),
            jax.ShapeDtypeStruct((pairs, 80, count), BF),
            jax.ShapeDtypeStruct((2, 16, 1024), F32),
        ],
        in_specs=[hbm] * (2 * units) + [vmem] * 4,
        out_specs=[hbm, vmem, hbm, vmem],
        scratch_shapes=[
            pltpu.VMEM((gathered,) + VIEW + piece, BF),
            pltpu.VMEM((pairs, 80, count), BF),
            pltpu.SemaphoreType.DMA((gathered + PARTS,)),
            pltpu.VMEM((units,) + VIEW + piece, BF),
            pltpu.VMEM((2, 1040, count), BF),
            pltpu.VMEM((2, 1152, count), BF),
            pltpu.SemaphoreType.DMA((2, 2)),
            pltpu.VMEM((2, 16, 1024), F32),
            pltpu.VMEM((units, 2, 4, 2) + piece, BF),
            pltpu.VMEM((units, 2, 4, 32, 512), BF),
            pltpu.VMEM((units, 2, 4, 32, 512), BF),
            pltpu.VMEM((units, 4, 2, 32, 512), BF),
            pltpu.VMEM((units, 4, 2, 32, 512), BF),
            pltpu.VMEM((units, 4, 32, 512), BF),
            pltpu.VMEM((units, 4, 32, 512), BF),
            pltpu.VMEM((units, 4, 32, 512), BF),
            pltpu.VMEM((units, 4, 32, 512), BF),
            pltpu.VMEM((units, 3) + piece, BF),
            pltpu.VMEM((units, 3) + piece, BF),
            pltpu.VMEM((pairs, 80, count), BF),
            pltpu.VMEM((pairs, 80, count), BF),
            pltpu.VMEM((pairs, 80, count), F32),
            pltpu.VMEM((pairs, 80, count // 2), BF),
            pltpu.VMEM((pairs, 80, count // 2), BF),
            pltpu.VMEM((pairs, 80, count // 4), BF),
            pltpu.VMEM((pairs, 80, count // 4), BF),
            pltpu.VMEM((3, 16, 1024), F32),
            pltpu.VMEM((3, 16, 1024), F32),
            pltpu.VMEM((3, 16, 1024), F32),
            pltpu.SemaphoreType.DMA((units + 1, 16)),
            pltpu.SemaphoreType.DMA((units + 1, 16)),
            pltpu.SemaphoreType.DMA((pairs, 8)),
            pltpu.SemaphoreType.DMA((pairs, 8)),
            pltpu.SemaphoreType.DMA((PARTS, 4)),
            pltpu.SemaphoreType.DMA((PARTS, 4)),
        ],
        compiler_params=pltpu.CompilerParams(
            collective_id=0, has_side_effects=True, vmem_limit_bytes=63 * 2**20
        ),
        name="reduce_all",
    )(
        *lefts,
        *rights,
        rows,
        source,
        arrived,
        small,
    )
    return whole.reshape(gathered, 1024, 1024), pieces, table_sum, small_sum.reshape(-1)


def lookup_kernel(
    fields, edim, ids_ref, table_ref, dense_ref, x0_ref, arr_ref, inv_ref,
    ids, slots, req, found, rep, held, pair, wide_rows, x0f, far, arr_far,
    id_send, id_recv, send, recv, far_send, far_recv, far_id_send, far_id_recv, half_send, half_recv,
):
    section, me = lax.axis_index("section"), lax.axis_index("dp")
    direct = fields // 2 - far.shape[0] // 2
    half, spot = me // 4, lax.rem(me, 4)
    twin = lax.rem(me + 4, 8)
    y, core = section // 2, lax.rem(section, 2)
    core_peer = (y * 2 + 1 - core, me)
    y_peer = ((1 - y) * 2 + core, me)
    dot = functools.partial(jnp.dot, preferred_element_type=F32)
    count = ids.shape[1]

    def peer(j):
        return lax.rem(me + j, 8)

    def near(j):
        return lax.rem(spot + j, 4)

    def lanes(place, size=128):
        return pl.ds(pl.multiple_of(place * size, size), size)

    barrier = pltpu.get_barrier_semaphore()
    for j in range(1, 8):
        pl.semaphore_signal(
            barrier, inc=1, device_id=(section, peer(j)), device_id_type=pl.DeviceIdType.MESH
        )
    for other in (core_peer, y_peer):
        pl.semaphore_signal(barrier, inc=1, device_id=other, device_id_type=pl.DeviceIdType.MESH)

    def far_copy(k):
        quarter = section if k < 3 else (1 - y) * 2 + core
        window = far.at[:, :, lanes(quarter, count // 4)]
        return pltpu.make_async_remote_copy(
            src_ref=window if k else table_ref.at[2 * direct :, :, lanes(quarter, count // 4)],
            dst_ref=window,
            send_sem=far_send.at[k],
            recv_sem=far_recv.at[k],
            device_id=((section, twin), core_peer, y_peer, core_peer)[k],
            device_id_type=pl.DeviceIdType.MESH,
        )

    ids[...] = jnp.zeros_like(ids)
    ids[:fields] = ids_ref[...]
    every = ids[...]
    owner = lax.shift_right_logical(every, 10)
    hot = jnp.concatenate([(owner == o).astype(F32) for o in range(8)], axis=0).astype(BF)
    before = (
        lax.broadcasted_iota(jnp.int32, (count, count), 0)
        < lax.broadcasted_iota(jnp.int32, (count, count), 1)
    )
    ranks = dot(hot, before.astype(F32).astype(BF))
    rank = jnp.zeros((32, count), F32)
    for o in range(8):
        rank = jnp.where(owner == o, ranks[32 * o : 32 * o + 32], rank)
    slots[...] = owner * 128 + rank.astype(jnp.int32)
    pl.semaphore_wait(barrier, 9)
    far_copy(0).start()
    ids[...] = every & 1023
    def id_copy(group, j):
        eight = pl.ds(pl.multiple_of(8 * group, 8), 8)
        return pltpu.make_async_remote_copy(
            src_ref=req.at[eight, lanes(peer(j))],
            dst_ref=arr_ref.at[eight, lanes(me)],
            send_sem=id_send.at[group, j],
            recv_sem=id_recv.at[group, j],
            device_id=(section, peer(j)),
            device_id_type=pl.DeviceIdType.MESH,
        )

    def far_id_copy(group, j):
        eight = pl.ds(pl.multiple_of(8 * group, 8), 8)
        return pltpu.make_async_remote_copy(
            src_ref=req.at[eight, lanes(4 * (1 - half) + near(j))],
            dst_ref=arr_far.at[eight, lanes(spot)],
            send_sem=far_id_send.at[group, j],
            recv_sem=far_id_recv.at[group, j],
            device_id=(section, 4 * half + near(j)),
            device_id_type=pl.DeviceIdType.MESH,
        )

    @pl.loop(0, 4)
    def _(group):
        eight = pl.ds(pl.multiple_of(8 * group, 8), 8)
        slot8, local8 = slots[eight], ids[eight]
        place = lax.broadcasted_iota(jnp.int32, (1, count), 1)
        column = lax.broadcasted_iota(jnp.int32, (8, count), 0)
        wanted, source = [], []
        for k in range(8):
            slot, local = slot8[k : k + 1], local8[k : k + 1]
            owners = column == lax.shift_right_logical(slot, 7)
            parts = [local >> 5, local & 31, place >> 5, place & 31]
            left = jnp.concatenate(
                [jnp.where(owners, p.astype(F32), 0.0) for p in parts], axis=0
            ).astype(BF)
            right = one_hot(slot & 127, 128)
            sent = lax.dot_general(
                left, right, (((1,), (1,)), ((), ())), preferred_element_type=F32
            )
            rows = [
                (sent[n : n + 8] * 32 + sent[n + 8 : n + 16]).astype(jnp.int32) for n in (0, 16)
            ]
            for taken, r in zip((wanted, source), rows):
                taken.append(jnp.concatenate([r[o : o + 1] for o in range(8)], axis=1))
        req[eight] = jnp.concatenate(wanted, axis=0)
        inv_ref[eight] = jnp.concatenate(source, axis=0)
        for j in range(1, 8):
            id_copy(group, j).start()
        for j in range(1, 4):
            far_id_copy(group, j).start()
        arr_ref[eight, lanes(me)] = req[eight, lanes(me)]
        arr_far[eight, lanes(spot)] = req[eight, lanes(4 * (1 - half) + spot)]

    def ids_of(group):
        for j in range(1, 8):
            id_copy(group, j).wait_recv()


    def row_copy(i, j):
        return pltpu.make_async_remote_copy(
            src_ref=found.at[i, :, lanes(peer(j))],
            dst_ref=rep.at[i, :, lanes(me)],
            send_sem=send.at[i, j],
            recv_sem=recv.at[i, j],
            device_id=(section, peer(j)),
            device_id_type=pl.DeviceIdType.MESH,
        )

    pair[...] = jnp.zeros_like(pair)
    held[...] = jnp.zeros_like(held)

    def half_copy(i, j, far_side):
        owner_place = 4 * (1 - half) + spot if far_side else me
        return pltpu.make_async_remote_copy(
            src_ref=found.at[i, :, lanes(4 * far_side + near(j))],
            dst_ref=rep.at[i, :, lanes(owner_place)],
            send_sem=half_send.at[far_side, i - direct, j],
            recv_sem=half_recv.at[far_side, i - direct, j],
            device_id=(section, 4 * half + near(j)),
            device_id_type=pl.DeviceIdType.MESH,
        )

    assert direct % 4 == 0

    @pl.loop(0, direct)
    def _(i):
        @pl.when(lax.rem(i, 4) == 0)
        def _():
            ids_of(i // 4)

        for h in range(2):
            held[h, :edim] = table_ref[2 * i + h]
            chosen = pick(held[h], arr_ref[pl.ds(2 * i + h, 1)])
            pair[40 * h : 40 * h + edim] = chosen[:edim]
        found[i] = pair[...].astype(BF)
        for j in range(1, 8):
            row_copy(i, j).start()
        rep[i, :, lanes(me)] = found[i, :, lanes(me)]

    for group in range(direct // 4, 4):
        ids_of(group)

    @pl.loop(direct, fields // 2)
    def _(i):
        for h in range(2):
            held[h, :edim] = table_ref[2 * i + h]
            places = arr_ref[pl.ds(2 * i + h, 1), lanes(half, count // 2)]
            pair[40 * h : 40 * h + edim, : count // 2] = pick(held[h], places)[:edim]
        found[i, :, : count // 2] = pair[:, : count // 2].astype(BF)
        for j in range(1, 4):
            half_copy(i, j, 0).start()
        rep[i, :, lanes(me)] = found[i, :, lanes(spot)]

    far_copy(0).wait_recv()
    far_copy(2).start()
    far_copy(1).start()
    for group in range(4):
        for j in range(1, 4):
            far_id_copy(group, j).wait_recv()
    far_copy(2).wait_recv()
    far_copy(3).start()
    far_copy(1).wait_recv()
    far_copy(3).wait_recv()

    @pl.loop(direct, fields // 2)
    def _(i):
        for h in range(2):
            held[h, :edim] = far[2 * (i - direct) + h]
            places = arr_far[pl.ds(2 * i + h, 1)]
            pair[40 * h : 40 * h + edim, count // 2 :] = pick(held[h], places)[:edim]
        found[i, :, count // 2 :] = pair[:, count // 2 :].astype(BF)
        for j in range(1, 4):
            half_copy(i, j, 1).start()
        rep[i, :, lanes(4 * (1 - half) + spot)] = found[i, :, lanes(4 + spot)]

    def unpack(i):
        wide_rows[2 * i] = pick(rep[i, 0:48], slots[pl.ds(2 * i, 1)])[0:40]
        wide_rows[2 * i + 1] = pick(rep[i, 32:80], slots[pl.ds(2 * i + 1, 1)])[8:48]

    @pl.loop(0, direct)
    def _(i):
        for j in range(1, 8):
            row_copy(i, j).wait_recv()
        unpack(i)

    @pl.loop(direct, fields // 2)
    def _(i):
        for j in range(1, 4):
            half_copy(i, j, 0).wait_recv()
            half_copy(i, j, 1).wait_recv()
        unpack(i)

    sparse, extra = fields * edim, dense_ref.shape[0]
    x0f[sparse // 8 * 8 :] = jnp.zeros_like(x0f[sparse // 8 * 8 :])
    for f in range(fields):
        x0f[f * edim : f * edim + edim] = wide_rows[f, :edim]
    x0f[sparse : sparse + extra] = dense_ref[...].astype(F32)
    x0f[sparse + extra : sparse + extra + 1] = jnp.ones_like(x0f[:1])
    x0_ref[...] = x0f[...].astype(BF)

    @pl.loop(0, direct)
    def _(i):
        for j in range(1, 8):
            row_copy(i, j).wait_send()

    @pl.loop(direct, fields // 2)
    def _(i):
        for j in range(1, 4):
            half_copy(i, j, 0).wait_send()
            half_copy(i, j, 1).wait_send()

    for group in range(4):
        for j in range(1, 8):
            id_copy(group, j).wait_send()
        for j in range(1, 4):
            far_id_copy(group, j).wait_send()
    for n in range(4):
        far_copy(n).wait_send()


def look_up(ids_t, table_t, dense_t):
    fields, count = ids_t.shape
    edim = table_t.shape[1]
    tall = (fields * edim + dense_t.shape[0]) // 128 * 128 + 128
    mirrored = fields // 4 - 1
    vmem = pl.BlockSpec(memory_space=pltpu.VMEM)
    return pl.pallas_call(
        functools.partial(lookup_kernel, fields, edim),
        out_shape=[
            jax.ShapeDtypeStruct((tall, count), BF),
            jax.ShapeDtypeStruct((32, count), jnp.int32),
            jax.ShapeDtypeStruct((32, count), jnp.int32),
        ],
        in_specs=[vmem] * 3,
        out_specs=[vmem] * 3,
        scratch_shapes=[
            pltpu.VMEM((32, count), jnp.int32),
            pltpu.VMEM((32, count), jnp.int32),
            pltpu.VMEM((32, count), jnp.int32),
            pltpu.VMEM((fields // 2, 80, count), BF),
            pltpu.VMEM((fields // 2, 80, count), BF),
            pltpu.VMEM((2, 48, count), BF),
            pltpu.VMEM((80, count), F32),
            pltpu.VMEM((fields, 40, count), F32),
            pltpu.VMEM((tall, count), F32),
            pltpu.VMEM((2 * mirrored, edim, count), BF),
            pltpu.VMEM((32, count // 2), jnp.int32),
            pltpu.SemaphoreType.DMA((4, 8)),
            pltpu.SemaphoreType.DMA((4, 8)),
            pltpu.SemaphoreType.DMA((fields // 2, 8)),
            pltpu.SemaphoreType.DMA((fields // 2, 8)),
            pltpu.SemaphoreType.DMA((4,)),
            pltpu.SemaphoreType.DMA((4,)),
            pltpu.SemaphoreType.DMA((4, 4)),
            pltpu.SemaphoreType.DMA((4, 4)),
            pltpu.SemaphoreType.DMA((2, mirrored, 4)),
            pltpu.SemaphoreType.DMA((2, mirrored, 4)),
        ],
        compiler_params=pltpu.CompilerParams(
            collective_id=1, has_side_effects=True, vmem_limit_bytes=63 * 2**20
        ),
        name="look_up",
    )(ids_t, table_t, dense_t)


def gelu_and_slope(pre):
    root = (2.0 / math.pi) ** 0.5
    square = pre * pre
    tanh = jnp.tanh(root * pre * (1.0 + 0.044715 * square))
    cdf = 0.5 + 0.5 * tanh
    bend = 0.5 * root * (1.0 - tanh * tanh) * (1.0 + 3 * 0.044715 * square)
    return pre * cdf, cdf + pre * bend


def network_kernel(
    width, edim, x0_hbm, labels_ref, weight_hbm, in_hbm, out_hbm, bias_ref, in_bias_ref, out_bias_ref, head_ref, hb_ref,
    probs_ref, rows_ref, dense_ref, small_ref, *rest,
):
    layers = weight_hbm.shape[0]
    kept = 2 * layers + 2
    outs = rest[:kept]
    (
        x0_ref, weight_ref, in_ref, out_ref, xs, vs, h1s, q1s, q2s, gs, us, d1s, d2s, dxs, accx, acch, accq, accs,
        lines, cols, enter, leave,
    ) = rest[kept:]
    main = in_hbm.shape[1]
    edge = slice(main, main + 16)
    count = x0_hbm.shape[1]
    block = us.shape[2]
    pairs = rows_ref.shape[0]

    entering = [
        pltpu.make_async_copy(src, dst, enter.at[k])
        for k, (src, dst) in enumerate(
            [(x0_hbm, x0_ref)]
            + [(weight_hbm.at[i], weight_ref.at[i]) for i in range(layers)]
            + [(in_hbm, in_ref), (out_hbm, out_ref)]
        )
    ]
    for copy in entering:
        copy.start()

    def leaving(k, n):
        at = pl.ds(pl.multiple_of(n * block, block), block)
        here = [xs.at[i, :, at] for i in range(layers - 1)] + [vs.at[i] for i in range(layers)]
        here += [h1s.at[:, at], q1s, q2s]
        return pltpu.make_async_copy(here[k], outs[k].at[:, at], leave.at[n, k])

    def dot(a, b, ca, cb):
        return lax.dot_general(a, b, (((ca,), (cb,)), ((), ())), preferred_element_type=F32)

    def fold(value):
        return functools.reduce(
            lambda a, b: a + b, [value[:, n : n + 128] for n in range(0, value.shape[1], 128)]
        )

    for layer in range(layers):
        vs[layer, main:] = jnp.zeros_like(vs[layer, main:])
    accx[...] = jnp.zeros_like(accx)
    acch[...] = jnp.zeros_like(acch)
    accq[...] = jnp.zeros_like(accq)
    accs[...] = jnp.zeros_like(accs)
    lines[...] = jnp.zeros_like(lines)
    lines[0:layers, :width] = bias_ref[...]
    lines[layers : layers + 1, :main] = in_bias_ref[...]
    lines[layers + 1 : layers + 2, :main] = out_bias_ref[...]
    lines[layers + 2 : layers + 3, :width] = head_ref[:, :width]
    lines[layers + 3 : layers + 4, :main] = head_ref[:, width:]
    cols[...] = lines[...].T
    entering[0].wait()
    for layer in range(1, layers):
        xs[layer - 1, edge] = x0_ref[edge]
    for copy in entering[1:]:
        copy.wait()

    blocks = count // block

    def one_block(n):
        at = slice(n * block, n * block + block)

        def before(*which):
            if n:
                for k in which:
                    leaving(k, n - 1).wait()

        def x_of(layer):
            return x0_ref[:width, at] if layer == 0 else xs[layer - 1, :width, at]

        def col(k, size):
            return cols[:size, k : k + 1]

        for layer in range(layers):
            u = dot(weight_ref[layer], x_of(layer), 0, 0) + col(layer, width)
            us[layer, :width] = u
            x = (x_of(0).astype(F32) * u + x_of(layer).astype(F32)).astype(BF)
            if layer + 1 < layers:
                xs[layer, :width, at] = x
        last = x.astype(F32)
        h1, d1 = gelu_and_slope(dot(in_ref[...], x_of(0), 0, 0) + col(layers, main))
        d1s[...] = d1
        h1s[:, at] = h1.astype(BF)
        h2, d2 = gelu_and_slope(dot(out_ref[...], h1s[:, at], 0, 0) + col(layers + 1, main))
        d2s[...] = d2
        head_cross, head_tower = col(layers + 2, width), col(layers + 3, main)
        z = (
            jnp.sum(last * head_cross, axis=0, keepdims=True)
            + jnp.sum(h2 * head_tower, axis=0, keepdims=True)
            + hb_ref[0]
        )
        probs = jax.nn.sigmoid(z)
        target = labels_ref[:, at].astype(F32)
        probs_ref[:, at] = probs
        s = probs - target
        loss = jnp.maximum(z, 0.0) + jnp.log1p(jnp.exp(-jnp.abs(z))) - target * z
        accs[0:1] += fold(s)
        accs[1:2] += fold(loss)
        accx[:width] += fold(s * last)
        acch[...] += fold(s * h2)

        q2 = ((s * head_tower) * d2s[...]).astype(BF)
        before(2 * layers + 1)
        q2s[...] = q2
        acc = fold(q2.astype(F32))
        accq[...] += acc
        q1 = (dot(out_ref[...], q2, 1, 0) * d1s[...]).astype(BF)
        before(2 * layers)
        q1s[...] = q1
        g = (s * head_cross).astype(BF)
        before(*range(layers - 1, 2 * layers - 1))
        for layer in reversed(range(layers)):
            gs[layer, :width] = g
            v = (g.astype(F32) * x_of(0).astype(F32)).astype(BF)
            vs[layer, :width] = v
            g = g.astype(F32) + dot(weight_ref[layer], v, 1, 0)
            if layer:
                g = g.astype(BF)
        g += dot(in_ref[...], q1, 1, 0)
        for layer in range(layers):
            g += gs[layer, :width].astype(F32) * us[layer, :width]
        dxs[:width] = g
        for i in range(pairs):
            low = 2 * i * edim
            both = [dxs[low : low + 40], dxs[low + edim : low + edim + 40]]
            rows_ref[i, :, at] = jnp.concatenate(both, axis=0).astype(BF)
        dense_ref[:, at] = dxs[2 * pairs * edim : width]

        for k in range(kept):
            leaving(k, n).start()

    for n in range(blocks):
        one_block(n)
    for n in range(blocks):
        for k in range(kept):
            if n == blocks - 1 or k < layers - 1 or k == 2 * layers - 1:
                leaving(k, n).wait()

    head_x = jnp.sum(accx[...].T, axis=0, keepdims=True)
    head_h = jnp.sum(acch[...].T, axis=0, keepdims=True)
    sums = [
        jnp.broadcast_to(jnp.sum(accs[k : k + 1], axis=1, keepdims=True), (1, 128)) for k in (0, 1)
    ]
    misc = jnp.concatenate([head_x[:, main:]] + sums + [jnp.zeros((1, main - 384), F32)], axis=1)
    bias = jnp.sum(accq[...].T, axis=0, keepdims=True)
    small_ref[0:4] = jnp.concatenate([bias, head_x[:, :main], head_h, misc], axis=0)
    small_ref[4:] = jnp.zeros_like(small_ref[4:])


def network(
    x0, labels, cross_weight, tower_in, tower_out, cross_bias, in_bias, out_bias, head, head_bias, edim, pairs
):
    layers, width = cross_weight.shape[:2]
    main = tower_out.shape[0]
    count = x0.shape[1]
    block = 512
    tall = main + 16
    vmem = pl.BlockSpec(memory_space=pltpu.VMEM)
    hbm = pl.BlockSpec(memory_space=pl.ANY)
    return pl.pallas_call(
        functools.partial(network_kernel, width, edim),
        out_shape=[
            jax.ShapeDtypeStruct((1, count), F32),
            jax.ShapeDtypeStruct((pairs, 80, count), BF),
            jax.ShapeDtypeStruct((width - 2 * pairs * edim, count), F32),
            jax.ShapeDtypeStruct((8, main), F32),
        ]
        + [jax.ShapeDtypeStruct((tall, count), BF)] * (layers - 1)
        + [jax.ShapeDtypeStruct((main + 128, count), BF)] * layers
        + [jax.ShapeDtypeStruct((main, count), BF)] * 3,
        in_specs=[hbm, vmem, hbm, hbm, hbm] + [vmem] * 4 + [pl.BlockSpec(memory_space=pltpu.SMEM)],
        out_specs=[vmem] * 4 + [pl.BlockSpec(memory_space=pl.ANY)] * (2 * layers + 2),
        scratch_shapes=[
            pltpu.VMEM(x0.shape, BF),
            pltpu.VMEM(cross_weight.shape, BF),
            pltpu.VMEM(tower_in.shape, BF),
            pltpu.VMEM(tower_out.shape, BF),
            pltpu.VMEM((layers - 1, tall, count), BF),
            pltpu.VMEM((layers, main + 128, block), BF),
            pltpu.VMEM((main, count), BF),
            pltpu.VMEM((main, block), BF),
            pltpu.VMEM((main, block), BF),
            pltpu.VMEM((layers, tall, block), BF),
            pltpu.VMEM((layers, tall, block), F32),
            pltpu.VMEM((main, block), F32),
            pltpu.VMEM((main, block), F32),
            pltpu.VMEM((tall, block), F32),
            pltpu.VMEM((main + 128, 128), F32),
            pltpu.VMEM((main, 128), F32),
            pltpu.VMEM((main, 128), F32),
            pltpu.VMEM((8, 128), F32),
            pltpu.VMEM((128, main + 128), F32),
            pltpu.VMEM((main + 128, 128), F32),
            pltpu.SemaphoreType.DMA((layers + 3,)),
            pltpu.SemaphoreType.DMA((count // block, 2 * layers + 2)),
        ],
        compiler_params=pltpu.CompilerParams(vmem_limit_bytes=63 * 2**20),
        name="network",
    )(x0, labels, cross_weight, tower_in, tower_out, cross_bias, in_bias, out_bias, head, head_bias)


def finish_kernel(
    whole_ref, small_ref, rows_ref, pieces_ref, out_ref, table_ref, bias_ref, in_ref, share_ref, out_piece_ref,
    head_ref, sums_ref, turned,
):
    layers, main = small_ref.shape[0] - 1, small_ref.shape[2]
    rest = out_ref.shape[2] - main
    width = main + rest
    layer = pl.program_id(0)
    edim = table_ref.shape[1]

    edge = small_ref[layer]
    out_ref[0, :main, :main] = whole_ref[0].astype(F32)
    out_ref[0, :main, main:] = edge.T[:, 4 : 4 + rest]
    out_ref[0, main:, :main] = edge[:rest]
    for r in range(rest):
        out_ref[0, main + r : main + r + 1, main:] = edge[7:8, 128 * r : 128 * r + rest]
    for f in range(table_ref.shape[0]):
        table_ref[f] = rows_ref[f // 2, 40 * (f % 2) : 40 * (f % 2) + 40].astype(F32)[:edim]

    @pl.when(layer == 0)
    def _():
        for k in range(layers):
            bias_ref[k : k + 1, :main] = small_ref[k, 3:4]
            bias_ref[k : k + 1, main:] = small_ref[k, 7:8, 384 : 384 + rest]
        last = small_ref[layers]
        turned[...] = last.T
        share = in_ref.shape[0]
        me = lax.axis_index("section") * lax.axis_size("dp") + lax.axis_index("dp")
        mine = turned[pl.ds(pl.multiple_of(me * share, share), share)]
        share_ref[...] = mine
        in_ref[:, :main] = pieces_ref[0]
        in_ref[:, main:] = mine[:, :rest]
        out_piece_ref[...] = pieces_ref[1]
        head_ref[:, :main] = last[5:6]
        head_ref[:, main:width] = last[7:8, :rest]
        head_ref[:, width:] = last[6:7]
        sums_ref[...] = last[7:8, 128:384]


def finish(whole, small, rows, pieces, width, fields, edim):
    layers, main = whole.shape[:2]
    share = pieces.shape[1]
    pairs, _, count = rows.shape
    parts = 3
    step = -(-pairs // parts)

    def all_of(*shape):
        return pl.BlockSpec(shape, lambda i: (0,) * len(shape))

    return pl.pallas_call(
        finish_kernel,
        out_shape=[
            jax.ShapeDtypeStruct((layers, width, width), F32),
            jax.ShapeDtypeStruct((fields, edim, count), F32),
            jax.ShapeDtypeStruct((layers, width), F32),
            jax.ShapeDtypeStruct((share, width), F32),
            jax.ShapeDtypeStruct((share, 8), F32),
            jax.ShapeDtypeStruct((share, main), F32),
            jax.ShapeDtypeStruct((1, width + main), F32),
            jax.ShapeDtypeStruct((1, 256), F32),
        ],
        grid=(layers,),
        in_specs=[
            pl.BlockSpec((1, main, main), lambda i: (i, 0, 0)),
            all_of(layers + 1, 8, main),
            pl.BlockSpec((step, 80, count), lambda i: (i, 0, 0)),
            all_of(2, share, main),
        ],
        out_specs=[
            pl.BlockSpec((1, width, width), lambda i: (i, 0, 0)),
            pl.BlockSpec((2 * step, edim, count), lambda i: (i, 0, 0)),
            all_of(layers, width),
            all_of(share, width),
            all_of(share, 8),
            all_of(share, main),
            all_of(1, width + main),
            all_of(1, 256),
        ],
        scratch_shapes=[pltpu.VMEM((main, 8), F32)],
        compiler_params=pltpu.CompilerParams(vmem_limit_bytes=63 * 2**20),
        name="finish",
    )(whole, small, rows, pieces)


def general_body(
    ids,
    dense,
    labels,
    table,
    cross_weight,
    cross_bias,
    tower_in,
    tower_in_bias,
    tower_out,
    tower_out_bias,
    head_weight,
    head_bias,
):
    groups = lax.axis_size("dp")
    sections = lax.axis_size("section")
    device_count = groups * sections
    examples, fields = ids.shape
    table_rows, edim = table.shape[1:]
    layers, width = cross_weight.shape[:2]
    hidden = tower_out.shape[0]
    capacity = examples // groups
    sparse = fields * edim
    me = lax.axis_index("section") * groups + lax.axis_index("dp")

    idt = ids.T
    owner = idt // table_rows
    local = idt % table_rows
    owner_hot = owner[:, None, :] == jnp.arange(groups, dtype=jnp.int32)[None, :, None]
    lane = jnp.arange(examples, dtype=jnp.int32)
    before = (lane[:, None] < lane[None, :]).astype(BF)
    counts = mm(owner_hot.reshape(fields * groups, examples).astype(BF), before, (1, 0))
    rank = jnp.sum(jnp.where(owner_hot, counts.reshape(fields, groups, examples), 0.0), axis=1)
    slot = owner * capacity + rank.astype(jnp.int32)
    slot_hot = (slot[:, None, :] == lane[None, :, None]).astype(BF)
    halves = jnp.stack([local // 32, local % 32], axis=1).astype(BF)
    sent = lax.dot_general(
        halves, slot_hot, (((2,), (2,)), ((0,), (0,))), preferred_element_type=F32
    )
    requests = (sent[:, 0] * 32 + sent[:, 1]).astype(jnp.int32)
    requests = requests.reshape(fields, groups, capacity).transpose(1, 0, 2)
    arrived = lax.all_to_all(requests, "dp", 0, 0, tiled=True)
    arrived = arrived.transpose(1, 0, 2).reshape(fields, examples)
    row_hot = (
        arrived[:, None, :] == jnp.arange(table_rows, dtype=jnp.int32)[None, :, None]
    ).astype(BF)
    table_t = table.transpose(0, 2, 1)
    found = lax.dot_general(
        table_t, row_hot, (((2,), (1,)), ((0,), (0,))), preferred_element_type=F32
    ).astype(BF)
    found = found.reshape(sparse, groups, capacity).transpose(1, 0, 2)
    replies = lax.all_to_all(found, "dp", 0, 0, tiled=True)
    replies = replies.transpose(1, 0, 2).reshape(fields, edim, examples)
    embedded = lax.dot_general(
        replies, slot_hot, (((2,), (1,)), ((0,), (0,))), preferred_element_type=F32
    ).astype(BF)
    x0 = jnp.concatenate([embedded.reshape(sparse, examples), dense.T], axis=0)

    x0w = x0.astype(F32)
    xs, us = [x0], []
    for layer in range(layers):
        u = mm(cross_weight[layer], xs[-1], (0, 0)) + cross_bias[layer][:, None]
        us.append(u)
        xs.append((x0w * u + xs[-1].astype(F32)).astype(BF))
    p1 = mm(tower_in, x0, (0, 0)) + tower_in_bias[:, None]
    a1, d1 = gelu_parts(p1)
    h1 = a1.astype(BF)
    p2 = mm(tower_out, h1, (0, 0)) + tower_out_bias[:, None]
    h2, d2 = gelu_parts(p2)
    head_cross, head_tower = head_weight[:width], head_weight[width:]
    last = xs[-1].astype(F32)
    z = (
        jnp.sum(last * head_cross[:, None], axis=0)
        + jnp.sum(h2 * head_tower[:, None], axis=0)
        + head_bias[0]
    )
    probs = jax.nn.sigmoid(z)
    target = labels.astype(F32)
    loss = jnp.sum(jnp.logaddexp(0.0, z) - target * z)
    s = probs - target
    head_grad = jnp.concatenate([jnp.sum(s * last, axis=1), jnp.sum(s * h2, axis=1)])

    q2 = (s[None, :] * head_tower[:, None] * d2).astype(BF)
    tower_out_g = mm(q2, h1, (1, 1))
    q1 = (mm(tower_out, q2, (1, 0)) * d1).astype(BF)
    tower_in_g = mm(q1, x0, (1, 1))
    tower_biases = [jnp.sum(q1.astype(F32), axis=1), jnp.sum(q2.astype(F32), axis=1)]
    dx0 = mm(tower_in, q1, (1, 0))
    g = (s[None, :] * head_cross[:, None]).astype(BF)
    cross_g, cross_b = [None] * layers, [None] * layers
    for layer in reversed(range(layers)):
        gw = g.astype(F32)
        v = (gw * x0w).astype(BF)
        cross_g[layer] = mm(xs[layer], v, (1, 1))
        cross_b[layer] = jnp.sum(v.astype(F32), axis=1)
        dx0 = dx0 + gw * us[layer]
        g = gw + mm(cross_weight[layer], v, (1, 0))
        if layer:
            g = g.astype(BF)
    dx0 = dx0 + g

    packed = lax.dot_general(
        dx0[:sparse].astype(BF).reshape(fields, edim, examples),
        slot_hot,
        (((2,), (2,)), ((0,), (0,))),
        preferred_element_type=F32,
    ).astype(BF)
    packed = packed.reshape(sparse, groups, capacity).transpose(1, 0, 2)
    delivered = lax.all_to_all(packed, "dp", 0, 0, tiled=True)
    delivered = delivered.transpose(1, 0, 2).reshape(fields, edim, examples)
    table_g = lax.dot_general(
        delivered, row_hot, (((2,), (2,)), ((0,), (0,))), preferred_element_type=F32
    )
    table_g = lax.psum(table_g, "section").transpose(0, 2, 1)

    small = jnp.concatenate(
        cross_b + [head_grad, jnp.sum(s).reshape(1), loss.reshape(1)] + tower_biases
    )
    small = lax.psum(small, ("section", "dp"))
    sizes = [layers * width, width + hidden, 1, 1, hidden, hidden]
    ends = [sum(sizes[: i + 1]) for i in range(len(sizes))]
    pieces = [small[e - n : e] for e, n in zip(ends, sizes)]
    cross_b_out = pieces[0].reshape(layers, width)
    share = hidden // device_count
    bias_in, bias_out = (lax.dynamic_slice(p, (me * share,), (share,)) for p in pieces[4:])
    cross_out = lax.psum(jnp.stack(cross_g), ("section", "dp"))
    tower_in_out = lax.psum_scatter(
        tower_in_g, ("section", "dp"), scatter_dimension=0, tiled=True
    )
    tower_out_out = lax.psum_scatter(
        tower_out_g, ("section", "dp"), scatter_dimension=0, tiled=True
    )
    return (
        probs,
        pieces[3] / (examples * device_count),
        dx0[sparse:].T,
        table_g,
        cross_out,
        cross_b_out,
        tower_in_out.T,
        bias_in,
        tower_out_out.T,
        bias_out,
        pieces[1],
        pieces[2],
    )


def body(
    ids,
    dense,
    labels,
    table,
    cross_weight,
    cross_bias,
    tower_in,
    tower_in_bias,
    tower_out,
    tower_out_bias,
    head_weight,
    head_bias,
):
    groups = lax.axis_size("dp")
    sections = lax.axis_size("section")
    device_count = groups * sections
    examples, fields = ids.shape
    table_rows, edim = table.shape[1:]
    layers, width = cross_weight.shape[:2]
    hidden = tower_out.shape[0]
    capacity = examples // groups
    me = lax.axis_index("section") * groups + lax.axis_index("dp")
    idt = ids.T
    table_t = table.transpose(0, 2, 1)
    here = (sections, groups, capacity, table_rows) == (4, 8, 128, 1024)
    if here:
        x0, arrived, source = look_up(idt, table_t, dense.T)
        probs, rows, dense_g, small, *kept = network(
            x0,
            labels.reshape(1, examples),
            cross_weight,
            tower_in,
            tower_out,
            cross_bias,
            tower_in_bias.reshape(1, hidden),
            tower_out_bias.reshape(1, hidden),
            head_weight.reshape(1, width + hidden),
            head_bias,
            edim,
            fields // 2,
        )
        xs, vs = [x0] + kept[: layers - 1], kept[layers - 1 : 2 * layers - 1]
        h1, q1, q2 = kept[2 * layers - 1 :]
        whole, pieces, table_sum, small = reduce_all(
            xs + [q1, q2], vs + [x0, h1], layers, rows, source, arrived, small
        )
        small = small.reshape(layers + 1, 8, hidden)
        cross_out, table_g, cross_b_out, in_out, mine, out_out, head_out, sums = finish(
            whole, small, table_sum, pieces, width, fields, edim
        )
        return (
            probs.reshape(examples),
            sums[0, 128:129] / (examples * device_count),
            dense_g.T,
            table_g.transpose(0, 2, 1),
            cross_out,
            cross_b_out,
            in_out.T,
            mine[:, 3],
            out_out.T,
            mine[:, 4],
            head_out.reshape(width + hidden),
            sums[0, 0:1],
        )
    return general_body(
        ids, dense, labels, table, cross_weight, cross_bias, tower_in, tower_in_bias, tower_out,
        tower_out_bias, head_weight, head_bias,
    )


def solution(mesh):
    both = ("section", "dp")
    return jax.shard_map(
        body,
        mesh=mesh,
        in_specs=(P(both, None), P(both, None), P(both), P(None, "dp", None)) + (P(),) * 8,
        out_specs=(
            P(both),
            P(),
            P(both, None),
            P(None, "dp", None),
            P(),
            P(),
            P(None, both),
            P(both),
            P(None, both),
            P(both),
            P(),
            P(),
        ),
        check_vma=False,
    )
```

```python
import functools
import math

import jax
import jax.numpy as jnp
from jax import lax
from jax.experimental import pallas as pl
from jax.experimental.pallas import tpu as pltpu
from jax.sharding import PartitionSpec as P

BF = jnp.bfloat16
F32 = jnp.float32


def mm(left, right, contract):
    return lax.dot_general(
        left, right, ((contract[:1], contract[1:]), ((), ())), preferred_element_type=F32
    )


def gelu_parts(pre):
    act, back = jax.vjp(jax.nn.gelu, pre)
    return act, back(jnp.ones_like(pre))[0]


ORDER = [
    "P3 P4 C1 P1",
    "u11 C2 C0 u12",
    "u21 P0 u10 C4",
    "S1 u31 T11 u14",
    "S4 T21 P5 u22",
    "T14 C3 u20 u41",
    "T24 u13 S5 u32",
    "u24 n0 T15 u30",
    "n1 S0 u51 T10",
    "u42 u23 T25 T20",
    "u61 u40 S3 n2",
    "T13 T30 u52 P2",
    "T31 T34 u50 T40",
    "n3 u62 u60 u33",
    "T35 u71 u34 S2",
    "T12 u72 n4 T23",
    "T22 u70 T33 n5",
    "T32 u80 u43 T43",
    "u44 u82 T44 T42",
    "T41 T45 u81",
]
PARTS = 6
VIEW = (2, 2, 4, 2)


def one_hot(places, count):
    rows = lax.broadcasted_iota(jnp.int32, (count, places.shape[1]), 0)
    return (rows == places).astype(F32).astype(BF)


def pick(slab, places):
    low, block = places & 255, lax.shift_right_logical(places, 8)
    blocks = [slab[:, 256 * b : 256 * b + 256] for b in range(4)]
    rows = slab.shape[0]
    every = jnp.dot(
        jnp.concatenate(blocks, axis=0), one_hot(low, 256), preferred_element_type=F32
    )
    chosen = every[:rows]
    for b in range(1, 4):
        chosen = jnp.where(block == b, every[rows * b : rows * b + rows], chosen)
    return chosen


def add_up(slab, places):
    low, block = places & 255, lax.shift_right_logical(places, 8)
    rows = slab.shape[0]
    masked = [slab * (block == b).astype(F32).astype(BF) for b in range(4)]
    every = lax.dot_general(
        jnp.concatenate(masked, axis=0),
        one_hot(low, 256),
        (((1,), (1,)), ((), ())),
        preferred_element_type=F32,
    )
    return jnp.concatenate([every[rows * b : rows * b + rows] for b in range(4)], axis=1)


def reduce_kernel(units, gathered, *refs):
    lefts, rights = refs[:units], refs[units : 2 * units]
    rows_hbm, inv_ref, arr_ref, part_ref = refs[2 * units : 2 * units + 4]
    whole_out, pieces, table_hbm, small_out = refs[2 * units + 4 : 2 * units + 8]
    (
        rows_ref, rows_in, whole, table_out, leave, grads, left, right, load, small, rc, sa1, ra1, sb1, rb1, sa2, ra2, sb2, rb2, sz, rz, packed, back, summed,
        stc, rtc, st, rt, sm, rm, rmz, send, recv, row_send, row_recv, table_send, table_recv,
    ) = refs[2 * units + 8 :]
    pairs, count = rows_hbm.shape[0], rows_hbm.shape[2]
    section, dp = lax.axis_index("section"), lax.axis_index("dp")
    y, c = section // 2, section % 2
    z, x = dp // 2, dp % 2
    core_peer = (y * 2 + 1 - c, dp)
    y_peer = ((1 - y) * 2 + c, dp)
    x_peer = (section, z * 2 + 1 - x)
    half = 512
    lo, hi = pl.ds(0, half), pl.ds(half, half)

    def z_peer(j):
        return (section, lax.rem(z + j, 4) * 2 + x)

    def dp_peer(j):
        return (section, lax.rem(dp + j, 8))

    peers = [core_peer, y_peer] + [dp_peer(j) for j in range(1, 8)]
    barrier = pltpu.get_barrier_semaphore()
    for peer in peers:
        pl.semaphore_signal(barrier, inc=1, device_id=peer, device_id_type=pl.DeviceIdType.MESH)

    flying = []

    def start(src, dst, m, k, peer, sems=(send, recv)):
        copy = pltpu.make_async_remote_copy(
            src_ref=src,
            dst_ref=dst,
            send_sem=sems[0].at[m, k],
            recv_sem=sems[1].at[m, k],
            device_id=peer,
            device_id_type=pl.DeviceIdType.MESH,
        )
        copy.start()
        flying.append(copy)
        return copy

    def wide(value):
        return value.astype(F32)

    copies = {}
    gone = []

    def leave_with(src, dst, k):
        copy = pltpu.make_async_copy(src, dst, leave.at[k])
        copy.start()
        gone.append(copy)

    def acc(m, stage, cols, yy, zz, xx):
        total = wide(grads[m, yy, c, zz, xx, :, cols]) + wide(rc[m, yy, zz, xx, :, cols])
        if cols is lo:
            if stage >= 2:
                total += wide(ra1[m, yy, zz])
            if stage >= 3:
                total += wide(ra2[m, zz])
        else:
            if stage >= 2:
                total += wide(rb1[m, zz, xx])
            if stage >= 3:
                total += wide(rb2[m, zz])
        return total

    tokens = " ".join(ORDER).split()
    made = [int(t[1]) for t in tokens if t[0] == "C"]

    def height(m):
        return min(lefts[m].shape[0], left.shape[1])

    def loads(turn):
        m, slot = made[turn], turn % 2
        return [
            pltpu.make_async_copy(ref.at[:rows], buf.at[slot, :rows], load.at[slot, k])
            for k, (ref, buf, rows) in enumerate(
                ((lefts[m], left, height(m)), (rights[m], right, rights[m].shape[0]))
            )
        ]

    def make(m):
        turn = made.index(m)
        slot = turn % 2
        for copy in loads(turn):
            copy.wait()
        tall = height(m) - 1024
        across = rights[m].shape[0]
        for r in range(2):
            total = lax.dot_general(
                left[slot, 512 * r : 512 * r + 512 + r * tall],
                right[slot, :across],
                (((1,), (1,)), ((), ())),
                preferred_element_type=F32,
            )
            grads[m, r] = total[:512, :1024].astype(BF).reshape(2, 4, 2, 32, 1024)
            if across > 1024:
                side = total[:512, 1024:].T
                group, at = m // 2, m % 2 * 8
                if tall:
                    small[group, at + 4 : at + 7, 512 * r : 512 * r + 512] = side[0:3]
                else:
                    small[group, at : at + 4, 512 * r : 512 * r + 512] = side[0:4]
                if tall and r:
                    small[group, at : at + 4] = total[512:516, :1024]
                    small[group, at + 7 : at + 8, 512:] = jnp.zeros((1, 512), F32)
                    for k in range(4):
                        small[group, at + 7 : at + 8, 128 * k : 128 * k + 128] = total[
                            512 + k : 513 + k, 1024:
                        ]
        if turn + 2 < units:
            for copy in loads(turn + 2):
                copy.start()

    def step0(m):
        make(m)
        copies[m, 0] = start(grads.at[m, :, 1 - c], rc.at[m], m, 0, core_peer)

    def step1(m):
        copies[m, 0].wait_recv()

        @pl.loop(0, 4)
        def _(zz):
            for i in range(2):
                sa1[m, i, zz] = acc(m, 1, lo, i, zz, 1 - x).astype(BF)
                sb1[m, zz, i] = acc(m, 1, hi, 1 - y, zz, i).astype(BF)

        copies[m, 1] = start(sa1.at[m], ra1.at[m], m, 1, x_peer)
        copies[m, 2] = start(sb1.at[m], rb1.at[m], m, 2, y_peer)

    def step2(m):
        copies[m, 1].wait_recv()
        copies[m, 2].wait_recv()

        @pl.loop(0, 4)
        def _(zz):
            sa2[m, zz] = acc(m, 2, lo, 1 - y, zz, x).astype(BF)
            sb2[m, zz] = acc(m, 2, hi, y, zz, 1 - x).astype(BF)

        copies[m, 3] = start(sa2.at[m], ra2.at[m], m, 3, y_peer)
        copies[m, 4] = start(sb2.at[m], rb2.at[m], m, 4, x_peer)

    def step3(m):
        copies[m, 3].wait_recv()
        copies[m, 4].wait_recv()
        for j in (1, 2, 3):
            zz = lax.rem(z + j, 4)
            sz[m, j - 1, :, lo] = acc(m, 3, lo, y, zz, x).astype(BF)
            sz[m, j - 1, :, hi] = acc(m, 3, hi, y, zz, x).astype(BF)
            copies[m, 4 + j] = start(sz.at[m, j - 1], rz.at[m, j - 1], m, 4 + j, z_peer(j))

    def step4(m):
        for j in (1, 2, 3):
            copies[m, 4 + j].wait_recv()
        for cols in (lo, hi):
            total = acc(m, 3, cols, y, z, x)
            for j in range(3):
                total += wide(rz[m, j, :, cols])
            if m < gathered:
                whole[m, y, c, z, x, :, cols] = total.astype(BF)
            else:
                pieces[m - gathered, :, cols] = total
        if m < gathered:
            for j in (1, 2, 3):
                mine = whole.at[m, y, c, z, x]
                copies[m, 7 + j] = start(mine, mine, m, 7 + j, z_peer(j))

    def step5(m):
        for j in (1, 2, 3):
            copies[m, 7 + j].wait_recv()
        ours = whole.at[m, y, c, :, x, :, lo]
        copies[m, 11] = start(ours, ours, m, 11, y_peer)
        ours = whole.at[m, y, c, :, x, :, hi]
        copies[m, 12] = start(ours, ours, m, 12, x_peer)

    def step6(m):
        copies[m, 11].wait_recv()
        copies[m, 12].wait_recv()
        ours = whole.at[m, :, c, :, x, :, lo]
        copies[m, 13] = start(ours, ours, m, 13, x_peer)
        ours = whole.at[m, y, c, :, :, :, hi]
        copies[m, 14] = start(ours, ours, m, 14, y_peer)

    def step7(m):
        copies[m, 13].wait_recv()
        copies[m, 14].wait_recv()
        ours = whole.at[m, :, c]
        copies[m, 15] = start(ours, ours, m, 15, core_peer)

    def step8(m):
        copies[m, 15].wait_recv()
        leave_with(whole.at[m], whole_out.at[m], m)

    def lanes(place, size):
        return pl.ds(pl.multiple_of(place * size, size), size)

    cuts = [pairs * q // PARTS for q in range(PARTS + 1)]

    def row_copy(q, j):
        part = pl.ds(cuts[q], cuts[q + 1] - cuts[q])
        return pltpu.make_async_remote_copy(
            src_ref=packed.at[part, :, lanes(lax.rem(dp + j, 8), 128)],
            dst_ref=back.at[part, :, lanes(dp, 128)],
            send_sem=row_send.at[q, j],
            recv_sem=row_recv.at[q, j],
            device_id=dp_peer(j),
            device_id_type=pl.DeviceIdType.MESH,
        )

    def pack(q):
        @pl.loop(cuts[q], cuts[q + 1])
        def _(i):
            first = pick(rows_ref[i, 0:48], inv_ref[pl.ds(2 * i, 1)])
            second = pick(rows_ref[i, 32:80], inv_ref[pl.ds(2 * i + 1, 1)])
            packed[i] = jnp.concatenate([first[0:40], second[8:48]], axis=0).astype(BF)
            back[i, :, lanes(dp, 128)] = packed[i, :, lanes(dp, 128)]

        for j in range(1, 8):
            row_copy(q, j).start()

    def scatter(q):
        for j in range(1, 8):
            row_copy(q, j).wait_recv()

        @pl.loop(cuts[q], cuts[q + 1])
        def _(i):
            for h, (low, at) in enumerate(((0, 0), (32, 8))):
                total = add_up(back[i, low : low + 48], arr_ref[pl.ds(2 * i + h, 1)])
                summed[i, 40 * h : 40 * h + 40] = total[at : at + 40]
            stc[i] = summed[i, :, lanes(1 - c, half)].astype(BF)

        part = pl.ds(cuts[q], cuts[q + 1] - cuts[q])
        copies["t", q, 0] = start(stc.at[part], rtc.at[part], q, 0, core_peer, (table_send, table_recv))

    quarter = half // 2

    def quarter_of(yy):
        return lanes(2 * c + yy, quarter)

    def table1(q):
        copies["t", q, 0].wait_recv()

        @pl.loop(cuts[q], cuts[q + 1])
        def _(i):
            st[i] = (summed[i, :, quarter_of(1 - y)] + wide(rtc[i, :, lanes(1 - y, quarter)])).astype(BF)

        part = pl.ds(cuts[q], cuts[q + 1] - cuts[q])
        copies["t", q, 1] = start(st.at[part], rt.at[part], q, 1, y_peer, (table_send, table_recv))

    def table2(q):
        copies["t", q, 1].wait_recv()

        @pl.loop(cuts[q], cuts[q + 1])
        def _(i):
            total = summed[i, :, quarter_of(y)] + wide(rtc[i, :, lanes(y, quarter)]) + wide(rt[i])
            table_out[i, :, quarter_of(y)] = total.astype(BF)

        part = pl.ds(cuts[q], cuts[q + 1] - cuts[q])
        ours = table_out.at[part, :, quarter_of(y)]
        copies["t", q, 2] = start(ours, ours, q, 2, y_peer, (table_send, table_recv))

    def table3(q):
        copies["t", q, 2].wait_recv()
        part = pl.ds(cuts[q], cuts[q + 1] - cuts[q])
        ours = table_out.at[part, :, lanes(c, half)]
        copies["t", q, 3] = start(ours, ours, q, 3, core_peer, (table_send, table_recv))

    def table4(q):
        copies["t", q, 3].wait_recv()
        part = pl.ds(cuts[q], cuts[q + 1] - cuts[q])
        leave_with(table_out.at[part], table_hbm.at[part], gathered + q)

    s = units

    def small0():
        small[1, 12:16] = part_ref[0:4]
        copies[s, 0] = start(small.at[1 - c], rm.at[0], s, 0, core_peer)

    def small1():
        copies[s, 0].wait_recv()
        sm[0] = small[c] + rm[0]
        copies[s, 1] = start(sm.at[0], rm.at[1], s, 1, x_peer)

    def small2():
        copies[s, 1].wait_recv()
        sm[1] = sm[0] + rm[1]
        copies[s, 2] = start(sm.at[1], rm.at[2], s, 2, y_peer)

    def small3():
        copies[s, 2].wait_recv()
        sm[2] = sm[1] + rm[2]
        for j in (1, 2, 3):
            copies[s, 2 + j] = start(sm.at[2], rmz.at[j - 1], s, 2 + j, z_peer(j))

    def small4():
        for j in (1, 2, 3):
            copies[s, 2 + j].wait_recv()
        even = lax.rem(z, 2)
        near = [sm[2], rmz[0], rmz[1], rmz[2]]
        first = near[0] + near[2]
        second = near[1] + near[3]
        small_out[c] = jnp.where(even == 0, first, second) + jnp.where(even == 0, second, first)
        ours = small_out.at[c]
        copies[s, 6] = start(ours, ours, s, 6, core_peer)

    def small5():
        copies[s, 6].wait_recv()

    steps = [step1, step2, step3, step4, step5, step6, step7, step8]
    smalls = [small0, small1, small2, small3, small4, small5]
    tables = [table1, table2, table3, table4]
    rows_copy = pltpu.make_async_copy(rows_hbm, rows_ref, rows_in)
    rows_copy.start()
    for copy in loads(0) + loads(1):
        copy.start()
    pl.semaphore_wait(barrier, len(peers))
    rows_copy.wait()
    for token in tokens:
        kind, numbers = token[0], [int(n) for n in token[1:]]
        if kind == "C":
            step0(*numbers)
        elif kind == "P":
            pack(*numbers)
        elif kind == "S":
            scatter(*numbers)
        elif kind == "n":
            smalls[numbers[0]]()
        else:
            {"u": steps, "T": tables}[kind][numbers[0] - 1](numbers[1])
    for copy in flying:
        copy.wait_send()
    for copy in gone:
        copy.wait()

    for q in range(PARTS):
        for j in range(1, 8):
            row_copy(q, j).wait_send()


def reduce_all(lefts, rights, gathered, rows, source, arrived, small):
    units = len(lefts)
    pairs, _, count = rows.shape
    piece = (32, 1024)
    vmem = pl.BlockSpec(memory_space=pltpu.VMEM)
    hbm = pl.BlockSpec(memory_space=pl.ANY)
    whole, pieces, table_sum, small_sum = pl.pallas_call(
        lambda *refs: reduce_kernel(units, gathered, *refs),
        out_shape=[
            jax.ShapeDtypeStruct((gathered,) + VIEW + piece, BF),
            jax.ShapeDtypeStruct((units - gathered,) + piece, F32),
            jax.ShapeDtypeStruct((pairs, 80, count), BF),
            jax.ShapeDtypeStruct((2, 16, 1024), F32),
        ],
        in_specs=[hbm] * (2 * units + 1) + [vmem] * 3,
        out_specs=[hbm, vmem, hbm, vmem],
        scratch_shapes=[
            pltpu.VMEM((pairs, 80, count), BF),
            pltpu.SemaphoreType.DMA,
            pltpu.VMEM((gathered,) + VIEW + piece, BF),
            pltpu.VMEM((pairs, 80, count), BF),
            pltpu.SemaphoreType.DMA((gathered + PARTS,)),
            pltpu.VMEM((units,) + VIEW + piece, BF),
            pltpu.VMEM((2, 1040, count), BF),
            pltpu.VMEM((2, 1152, count), BF),
            pltpu.SemaphoreType.DMA((2, 2)),
            pltpu.VMEM((2, 16, 1024), F32),
            pltpu.VMEM((units, 2, 4, 2) + piece, BF),
            pltpu.VMEM((units, 2, 4, 32, 512), BF),
            pltpu.VMEM((units, 2, 4, 32, 512), BF),
            pltpu.VMEM((units, 4, 2, 32, 512), BF),
            pltpu.VMEM((units, 4, 2, 32, 512), BF),
            pltpu.VMEM((units, 4, 32, 512), BF),
            pltpu.VMEM((units, 4, 32, 512), BF),
            pltpu.VMEM((units, 4, 32, 512), BF),
            pltpu.VMEM((units, 4, 32, 512), BF),
            pltpu.VMEM((units, 3) + piece, BF),
            pltpu.VMEM((units, 3) + piece, BF),
            pltpu.VMEM((pairs, 80, count), BF),
            pltpu.VMEM((pairs, 80, count), BF),
            pltpu.VMEM((pairs, 80, count), F32),
            pltpu.VMEM((pairs, 80, count // 2), BF),
            pltpu.VMEM((pairs, 80, count // 2), BF),
            pltpu.VMEM((pairs, 80, count // 4), BF),
            pltpu.VMEM((pairs, 80, count // 4), BF),
            pltpu.VMEM((3, 16, 1024), F32),
            pltpu.VMEM((3, 16, 1024), F32),
            pltpu.VMEM((3, 16, 1024), F32),
            pltpu.SemaphoreType.DMA((units + 1, 16)),
            pltpu.SemaphoreType.DMA((units + 1, 16)),
            pltpu.SemaphoreType.DMA((PARTS, 8)),
            pltpu.SemaphoreType.DMA((PARTS, 8)),
            pltpu.SemaphoreType.DMA((PARTS, 4)),
            pltpu.SemaphoreType.DMA((PARTS, 4)),
        ],
        compiler_params=pltpu.CompilerParams(
            collective_id=0, has_side_effects=True, vmem_limit_bytes=63 * 2**20
        ),
        name="reduce_all",
    )(
        *lefts,
        *rights,
        rows,
        source,
        arrived,
        small,
    )
    return whole.reshape(gathered, 1024, 1024), pieces, table_sum, small_sum.reshape(-1)


def lookup_kernel(
    fields, edim, ids_ref, table_hbm, dense_ref, x0_ref, arr_ref, inv_ref,
    table_ref, table_in, ids, slots, req, found, rep, held, pair, wide_rows, x0f, far, arr_far,
    id_send, id_recv, send, recv, far_send, far_recv, far_id_send, far_id_recv, half_send, half_recv,
):
    section, me = lax.axis_index("section"), lax.axis_index("dp")
    direct = fields // 2 - far.shape[0] // 2
    half, spot = me // 4, lax.rem(me, 4)
    twin = lax.rem(me + 4, 8)
    y, core = section // 2, lax.rem(section, 2)
    core_peer = (y * 2 + 1 - core, me)
    y_peer = ((1 - y) * 2 + core, me)
    dot = functools.partial(jnp.dot, preferred_element_type=F32)
    count = ids.shape[1]

    table_copy = pltpu.make_async_copy(table_hbm, table_ref, table_in)
    table_copy.start()

    def peer(j):
        return lax.rem(me + j, 8)

    def near(j):
        return lax.rem(spot + j, 4)

    def lanes(place, size=128):
        return pl.ds(pl.multiple_of(place * size, size), size)

    barrier = pltpu.get_barrier_semaphore()
    for j in range(1, 8):
        pl.semaphore_signal(
            barrier, inc=1, device_id=(section, peer(j)), device_id_type=pl.DeviceIdType.MESH
        )
    for other in (core_peer, y_peer):
        pl.semaphore_signal(barrier, inc=1, device_id=other, device_id_type=pl.DeviceIdType.MESH)

    def far_copy(k):
        quarter = section if k < 3 else (1 - y) * 2 + core
        window = far.at[:, :, lanes(quarter, count // 4)]
        return pltpu.make_async_remote_copy(
            src_ref=window if k else table_ref.at[2 * direct :, :, lanes(quarter, count // 4)],
            dst_ref=window,
            send_sem=far_send.at[k],
            recv_sem=far_recv.at[k],
            device_id=((section, twin), core_peer, y_peer, core_peer)[k],
            device_id_type=pl.DeviceIdType.MESH,
        )

    ids[...] = jnp.zeros_like(ids)
    ids[:fields] = ids_ref[...]
    every = ids[...]
    owner = lax.shift_right_logical(every, 10)
    hot = jnp.concatenate([(owner == o).astype(F32) for o in range(8)], axis=0).astype(BF)
    before = (
        lax.broadcasted_iota(jnp.int32, (count, count), 0)
        < lax.broadcasted_iota(jnp.int32, (count, count), 1)
    )
    ranks = dot(hot, before.astype(F32).astype(BF))
    rank = jnp.zeros((32, count), F32)
    for o in range(8):
        rank = jnp.where(owner == o, ranks[32 * o : 32 * o + 32], rank)
    slots[...] = owner * 128 + rank.astype(jnp.int32)
    pl.semaphore_wait(barrier, 9)
    table_copy.wait()
    far_copy(0).start()
    ids[...] = every & 1023
    def id_copy(group, j):
        eight = pl.ds(pl.multiple_of(8 * group, 8), 8)
        return pltpu.make_async_remote_copy(
            src_ref=req.at[eight, lanes(peer(j))],
            dst_ref=arr_ref.at[eight, lanes(me)],
            send_sem=id_send.at[group, j],
            recv_sem=id_recv.at[group, j],
            device_id=(section, peer(j)),
            device_id_type=pl.DeviceIdType.MESH,
        )

    def far_id_copy(group, j):
        eight = pl.ds(pl.multiple_of(8 * group, 8), 8)
        return pltpu.make_async_remote_copy(
            src_ref=req.at[eight, lanes(4 * (1 - half) + near(j))],
            dst_ref=arr_far.at[eight, lanes(spot)],
            send_sem=far_id_send.at[group, j],
            recv_sem=far_id_recv.at[group, j],
            device_id=(section, 4 * half + near(j)),
            device_id_type=pl.DeviceIdType.MESH,
        )

    @pl.loop(0, 4)
    def _(group):
        eight = pl.ds(pl.multiple_of(8 * group, 8), 8)
        slot8, local8 = slots[eight], ids[eight]
        place = lax.broadcasted_iota(jnp.int32, (1, count), 1)
        column = lax.broadcasted_iota(jnp.int32, (8, count), 0)
        wanted, source = [], []
        for k in range(8):
            slot, local = slot8[k : k + 1], local8[k : k + 1]
            owners = column == lax.shift_right_logical(slot, 7)
            parts = [local >> 5, local & 31, place >> 5, place & 31]
            left = jnp.concatenate(
                [jnp.where(owners, p.astype(F32), 0.0) for p in parts], axis=0
            ).astype(BF)
            right = one_hot(slot & 127, 128)
            sent = lax.dot_general(
                left, right, (((1,), (1,)), ((), ())), preferred_element_type=F32
            )
            rows = [
                (sent[n : n + 8] * 32 + sent[n + 8 : n + 16]).astype(jnp.int32) for n in (0, 16)
            ]
            for taken, r in zip((wanted, source), rows):
                taken.append(jnp.concatenate([r[o : o + 1] for o in range(8)], axis=1))
        req[eight] = jnp.concatenate(wanted, axis=0)
        inv_ref[eight] = jnp.concatenate(source, axis=0)
        for j in range(1, 8):
            id_copy(group, j).start()
        for j in range(1, 4):
            far_id_copy(group, j).start()
        arr_ref[eight, lanes(me)] = req[eight, lanes(me)]
        arr_far[eight, lanes(spot)] = req[eight, lanes(4 * (1 - half) + spot)]

    def ids_of(group):
        for j in range(1, 8):
            id_copy(group, j).wait_recv()


    def row_copy(i, j):
        return pltpu.make_async_remote_copy(
            src_ref=found.at[i, :, lanes(peer(j))],
            dst_ref=rep.at[i, :, lanes(me)],
            send_sem=send.at[i, j],
            recv_sem=recv.at[i, j],
            device_id=(section, peer(j)),
            device_id_type=pl.DeviceIdType.MESH,
        )

    pair[...] = jnp.zeros_like(pair)
    held[...] = jnp.zeros_like(held)

    def half_copy(i, j, far_side):
        owner_place = 4 * (1 - half) + spot if far_side else me
        return pltpu.make_async_remote_copy(
            src_ref=found.at[i, :, lanes(4 * far_side + near(j))],
            dst_ref=rep.at[i, :, lanes(owner_place)],
            send_sem=half_send.at[far_side, i - direct, j],
            recv_sem=half_recv.at[far_side, i - direct, j],
            device_id=(section, 4 * half + near(j)),
            device_id_type=pl.DeviceIdType.MESH,
        )

    assert direct % 4 == 0

    @pl.loop(0, direct)
    def _(i):
        @pl.when(lax.rem(i, 4) == 0)
        def _():
            ids_of(i // 4)

        for h in range(2):
            held[h, :edim] = table_ref[2 * i + h]
            chosen = pick(held[h], arr_ref[pl.ds(2 * i + h, 1)])
            pair[40 * h : 40 * h + edim] = chosen[:edim]
        found[i] = pair[...].astype(BF)
        for j in range(1, 8):
            row_copy(i, j).start()
        rep[i, :, lanes(me)] = found[i, :, lanes(me)]

    for group in range(direct // 4, 4):
        ids_of(group)

    @pl.loop(direct, fields // 2)
    def _(i):
        for h in range(2):
            held[h, :edim] = table_ref[2 * i + h]
            places = arr_ref[pl.ds(2 * i + h, 1), lanes(half, count // 2)]
            pair[40 * h : 40 * h + edim, : count // 2] = pick(held[h], places)[:edim]
        found[i, :, : count // 2] = pair[:, : count // 2].astype(BF)
        for j in range(1, 4):
            half_copy(i, j, 0).start()
        rep[i, :, lanes(me)] = found[i, :, lanes(spot)]

    far_copy(0).wait_recv()
    far_copy(2).start()
    far_copy(1).start()
    for group in range(4):
        for j in range(1, 4):
            far_id_copy(group, j).wait_recv()
    far_copy(2).wait_recv()
    far_copy(3).start()
    far_copy(1).wait_recv()
    far_copy(3).wait_recv()

    @pl.loop(direct, fields // 2)
    def _(i):
        for h in range(2):
            held[h, :edim] = far[2 * (i - direct) + h]
            places = arr_far[pl.ds(2 * i + h, 1)]
            pair[40 * h : 40 * h + edim, count // 2 :] = pick(held[h], places)[:edim]
        found[i, :, count // 2 :] = pair[:, count // 2 :].astype(BF)
        for j in range(1, 4):
            half_copy(i, j, 1).start()
        rep[i, :, lanes(4 * (1 - half) + spot)] = found[i, :, lanes(4 + spot)]

    def unpack(i):
        wide_rows[2 * i] = pick(rep[i, 0:48], slots[pl.ds(2 * i, 1)])[0:40]
        wide_rows[2 * i + 1] = pick(rep[i, 32:80], slots[pl.ds(2 * i + 1, 1)])[8:48]

    @pl.loop(0, direct)
    def _(i):
        for j in range(1, 8):
            row_copy(i, j).wait_recv()
        unpack(i)

    @pl.loop(direct, fields // 2)
    def _(i):
        for j in range(1, 4):
            half_copy(i, j, 0).wait_recv()
            half_copy(i, j, 1).wait_recv()
        unpack(i)

    sparse, extra = fields * edim, dense_ref.shape[0]
    x0f[sparse // 8 * 8 :] = jnp.zeros_like(x0f[sparse // 8 * 8 :])
    for f in range(fields):
        x0f[f * edim : f * edim + edim] = wide_rows[f, :edim]
    x0f[sparse : sparse + extra] = dense_ref[...].astype(F32)
    x0f[sparse + extra : sparse + extra + 1] = jnp.ones_like(x0f[:1])
    x0_ref[...] = x0f[...].astype(BF)

    @pl.loop(0, direct)
    def _(i):
        for j in range(1, 8):
            row_copy(i, j).wait_send()

    @pl.loop(direct, fields // 2)
    def _(i):
        for j in range(1, 4):
            half_copy(i, j, 0).wait_send()
            half_copy(i, j, 1).wait_send()

    for group in range(4):
        for j in range(1, 8):
            id_copy(group, j).wait_send()
        for j in range(1, 4):
            far_id_copy(group, j).wait_send()
    for n in range(4):
        far_copy(n).wait_send()


def look_up(ids_t, table_t, dense_t):
    fields, count = ids_t.shape
    edim = table_t.shape[1]
    tall = (fields * edim + dense_t.shape[0]) // 128 * 128 + 128
    mirrored = fields // 4 - 1
    vmem = pl.BlockSpec(memory_space=pltpu.VMEM)
    return pl.pallas_call(
        functools.partial(lookup_kernel, fields, edim),
        out_shape=[
            jax.ShapeDtypeStruct((tall, count), BF),
            jax.ShapeDtypeStruct((32, count), jnp.int32),
            jax.ShapeDtypeStruct((32, count), jnp.int32),
        ],
        in_specs=[vmem, pl.BlockSpec(memory_space=pl.ANY), vmem],
        out_specs=[vmem] * 3,
        scratch_shapes=[
            pltpu.VMEM(table_t.shape, BF),
            pltpu.SemaphoreType.DMA,
            pltpu.VMEM((32, count), jnp.int32),
            pltpu.VMEM((32, count), jnp.int32),
            pltpu.VMEM((32, count), jnp.int32),
            pltpu.VMEM((fields // 2, 80, count), BF),
            pltpu.VMEM((fields // 2, 80, count), BF),
            pltpu.VMEM((2, 48, count), BF),
            pltpu.VMEM((80, count), F32),
            pltpu.VMEM((fields, 40, count), F32),
            pltpu.VMEM((tall, count), F32),
            pltpu.VMEM((2 * mirrored, edim, count), BF),
            pltpu.VMEM((32, count // 2), jnp.int32),
            pltpu.SemaphoreType.DMA((4, 8)),
            pltpu.SemaphoreType.DMA((4, 8)),
            pltpu.SemaphoreType.DMA((fields // 2, 8)),
            pltpu.SemaphoreType.DMA((fields // 2, 8)),
            pltpu.SemaphoreType.DMA((4,)),
            pltpu.SemaphoreType.DMA((4,)),
            pltpu.SemaphoreType.DMA((4, 4)),
            pltpu.SemaphoreType.DMA((4, 4)),
            pltpu.SemaphoreType.DMA((2, mirrored, 4)),
            pltpu.SemaphoreType.DMA((2, mirrored, 4)),
        ],
        compiler_params=pltpu.CompilerParams(
            collective_id=1, has_side_effects=True, vmem_limit_bytes=63 * 2**20
        ),
        name="look_up",
    )(ids_t, table_t, dense_t)


def gelu_and_slope(pre):
    root = (2.0 / math.pi) ** 0.5
    square = pre * pre
    tanh = jnp.tanh(root * pre * (1.0 + 0.044715 * square))
    cdf = 0.5 + 0.5 * tanh
    bend = 0.5 * root * (1.0 - tanh * tanh) * (1.0 + 3 * 0.044715 * square)
    return pre * cdf, cdf + pre * bend


def network_kernel(
    width, edim, x0_hbm, labels_ref, weight_hbm, in_hbm, out_hbm, bias_ref, in_bias_ref, out_bias_ref, head_ref, hb_ref,
    probs_ref, rows_ref, dense_ref, small_ref, *rest,
):
    layers = weight_hbm.shape[0]
    kept = 2 * layers + 2
    outs = rest[:kept]
    (
        x0_ref, weight_ref, in_ref, out_ref, xs, vs, h1s, q1s, q2s, gs, us, d1s, d2s, dxs, accx, acch, accq, accs,
        lines, cols, enter, leave,
    ) = rest[kept:]
    main = in_hbm.shape[1]
    edge = slice(main, main + 16)
    count = x0_hbm.shape[1]
    block = us.shape[2]
    pairs = rows_ref.shape[0]

    entering = [
        pltpu.make_async_copy(src, dst, enter.at[k])
        for k, (src, dst) in enumerate(
            [(x0_hbm, x0_ref)]
            + [(weight_hbm.at[i], weight_ref.at[i]) for i in range(layers)]
            + [(in_hbm, in_ref), (out_hbm, out_ref)]
        )
    ]
    for copy in entering:
        copy.start()

    def leaving(k, n):
        at = pl.ds(pl.multiple_of(n * block, block), block)
        here = [xs.at[i, :, at] for i in range(layers - 1)] + [vs.at[i] for i in range(layers)]
        here += [h1s.at[:, at], q1s, q2s]
        return pltpu.make_async_copy(here[k], outs[k].at[:, at], leave.at[n, k])

    def dot(a, b, ca, cb):
        return lax.dot_general(a, b, (((ca,), (cb,)), ((), ())), preferred_element_type=F32)

    def fold(value):
        return functools.reduce(
            lambda a, b: a + b, [value[:, n : n + 128] for n in range(0, value.shape[1], 128)]
        )

    for layer in range(layers):
        vs[layer, main:] = jnp.zeros_like(vs[layer, main:])
    accx[...] = jnp.zeros_like(accx)
    acch[...] = jnp.zeros_like(acch)
    accq[...] = jnp.zeros_like(accq)
    accs[...] = jnp.zeros_like(accs)
    lines[...] = jnp.zeros_like(lines)
    lines[0:layers, :width] = bias_ref[...]
    lines[layers : layers + 1, :main] = in_bias_ref[...]
    lines[layers + 1 : layers + 2, :main] = out_bias_ref[...]
    head = head_ref[...].reshape(1, width + main)
    lines[layers + 2 : layers + 3, :width] = head[:, :width]
    lines[layers + 3 : layers + 4, :main] = head[:, width:]
    cols[...] = lines[...].T
    entering[0].wait()
    for layer in range(1, layers):
        xs[layer - 1, edge] = x0_ref[edge]

    blocks = count // block

    def one_block(n):
        at = slice(n * block, n * block + block)

        def before(*which):
            if n:
                for k in which:
                    leaving(k, n - 1).wait()

        def arrived(k):
            if n == 0:
                entering[k].wait()

        def complete(k):
            leaving(k, n).start()

        def x_of(layer):
            return x0_ref[:width, at] if layer == 0 else xs[layer - 1, :width, at]

        def col(k, size):
            return cols[:size, k : k + 1]

        for layer in range(layers):
            arrived(1 + layer)
            u = dot(weight_ref[layer], x_of(layer), 0, 0) + col(layer, width)
            us[layer, :width] = u
            x = (x_of(0).astype(F32) * u + x_of(layer).astype(F32)).astype(BF)
            if layer + 1 < layers:
                xs[layer, :width, at] = x
                complete(layer)
        last = x.astype(F32)
        arrived(layers + 1)
        h1, d1 = gelu_and_slope(dot(in_ref[...], x_of(0), 0, 0) + col(layers, main))
        d1s[...] = d1
        h1s[:, at] = h1.astype(BF)
        complete(2 * layers - 1)
        arrived(layers + 2)
        h2, d2 = gelu_and_slope(dot(out_ref[...], h1s[:, at], 0, 0) + col(layers + 1, main))
        d2s[...] = d2
        head_cross, head_tower = col(layers + 2, width), col(layers + 3, main)
        z = (
            jnp.sum(last * head_cross, axis=0, keepdims=True)
            + jnp.sum(h2 * head_tower, axis=0, keepdims=True)
            + hb_ref[0]
        )
        probs = jax.nn.sigmoid(z)
        target = labels_ref[:, at].astype(F32)
        probs_ref[:, at] = probs
        s = probs - target
        loss = jnp.maximum(z, 0.0) + jnp.log1p(jnp.exp(-jnp.abs(z))) - target * z
        accs[0:1] += fold(s)
        accs[1:2] += fold(loss)
        accx[:width] += fold(s * last)
        acch[...] += fold(s * h2)

        q2 = ((s * head_tower) * d2s[...]).astype(BF)
        before(2 * layers + 1)
        q2s[...] = q2
        complete(2 * layers + 1)
        acc = fold(q2.astype(F32))
        accq[...] += acc
        q1 = (dot(out_ref[...], q2, 1, 0) * d1s[...]).astype(BF)
        before(2 * layers)
        q1s[...] = q1
        complete(2 * layers)
        g = (s * head_cross).astype(BF)
        before(*range(layers - 1, 2 * layers - 1))
        for layer in reversed(range(layers)):
            gs[layer, :width] = g
            v = (g.astype(F32) * x_of(0).astype(F32)).astype(BF)
            vs[layer, :width] = v
            complete(layers - 1 + layer)
            g = g.astype(F32) + dot(weight_ref[layer], v, 1, 0)
            if layer:
                g = g.astype(BF)
        g += dot(in_ref[...], q1, 1, 0)
        for layer in range(layers):
            g += gs[layer, :width].astype(F32) * us[layer, :width]
        dxs[:width] = g
        for i in range(pairs):
            low = 2 * i * edim
            both = [dxs[low : low + 40], dxs[low + edim : low + edim + 40]]
            rows_ref[i, :, at] = jnp.concatenate(both, axis=0).astype(BF)
        dense_ref[:, at] = dxs[2 * pairs * edim : width]

    for n in range(blocks):
        one_block(n)
    for n in range(blocks):
        for k in range(kept):
            if n == blocks - 1 or k < layers - 1 or k == 2 * layers - 1:
                leaving(k, n).wait()

    head_x = jnp.sum(accx[...].T, axis=0, keepdims=True)
    head_h = jnp.sum(acch[...].T, axis=0, keepdims=True)
    sums = [
        jnp.broadcast_to(jnp.sum(accs[k : k + 1], axis=1, keepdims=True), (1, 128)) for k in (0, 1)
    ]
    misc = jnp.concatenate([head_x[:, main:]] + sums + [jnp.zeros((1, main - 384), F32)], axis=1)
    bias = jnp.sum(accq[...].T, axis=0, keepdims=True)
    small_ref[0:4] = jnp.concatenate([bias, head_x[:, :main], head_h, misc], axis=0)
    small_ref[4:] = jnp.zeros_like(small_ref[4:])


def network(
    x0, labels, cross_weight, tower_in, tower_out, cross_bias, in_bias, out_bias, head, head_bias, edim, pairs
):
    layers, width = cross_weight.shape[:2]
    main = tower_out.shape[0]
    count = x0.shape[1]
    block = 512
    tall = main + 16
    vmem = pl.BlockSpec(memory_space=pltpu.VMEM)
    hbm = pl.BlockSpec(memory_space=pl.ANY)
    return pl.pallas_call(
        functools.partial(network_kernel, width, edim),
        out_shape=[
            jax.ShapeDtypeStruct((1, count), F32),
            jax.ShapeDtypeStruct((pairs, 80, count), BF),
            jax.ShapeDtypeStruct((width - 2 * pairs * edim, count), F32),
            jax.ShapeDtypeStruct((8, main), F32),
        ]
        + [jax.ShapeDtypeStruct((tall, count), BF)] * (layers - 1)
        + [jax.ShapeDtypeStruct((main + 128, count), BF)] * layers
        + [jax.ShapeDtypeStruct((main, count), BF)] * 3,
        in_specs=[hbm, vmem, hbm, hbm, hbm] + [vmem] * 4 + [pl.BlockSpec(memory_space=pltpu.SMEM)],
        out_specs=[vmem] * 4 + [pl.BlockSpec(memory_space=pl.ANY)] * (2 * layers + 2),
        scratch_shapes=[
            pltpu.VMEM(x0.shape, BF),
            pltpu.VMEM(cross_weight.shape, BF),
            pltpu.VMEM(tower_in.shape, BF),
            pltpu.VMEM(tower_out.shape, BF),
            pltpu.VMEM((layers - 1, tall, count), BF),
            pltpu.VMEM((layers, main + 128, block), BF),
            pltpu.VMEM((main, count), BF),
            pltpu.VMEM((main, block), BF),
            pltpu.VMEM((main, block), BF),
            pltpu.VMEM((layers, tall, block), BF),
            pltpu.VMEM((layers, tall, block), F32),
            pltpu.VMEM((main, block), F32),
            pltpu.VMEM((main, block), F32),
            pltpu.VMEM((tall, block), F32),
            pltpu.VMEM((main + 128, 128), F32),
            pltpu.VMEM((main, 128), F32),
            pltpu.VMEM((main, 128), F32),
            pltpu.VMEM((8, 128), F32),
            pltpu.VMEM((128, main + 128), F32),
            pltpu.VMEM((main + 128, 128), F32),
            pltpu.SemaphoreType.DMA((layers + 3,)),
            pltpu.SemaphoreType.DMA((count // block, 2 * layers + 2)),
        ],
        compiler_params=pltpu.CompilerParams(vmem_limit_bytes=63 * 2**20),
        name="network",
    )(x0, labels, cross_weight, tower_in, tower_out, cross_bias, in_bias, out_bias, head, head_bias)


def finish_kernel(
    examples, whole_ref, small_ref, rows_ref, pieces_ref, out_ref, table_ref, bias_ref, in_ref, in_bias_ref,
    out_bias_ref, out_piece_ref, head_ref, slope_ref, loss_ref, turned,
):
    layers, main = small_ref.shape[0] - 1, small_ref.shape[2]
    rest = out_ref.shape[2] - main
    width = main + rest
    layer = pl.program_id(0)
    edim = table_ref.shape[1]

    edge = small_ref[layer]
    out_ref[0, :main, :main] = whole_ref[0].astype(F32)
    out_ref[0, :main, main:] = edge.T[:, 4 : 4 + rest]
    out_ref[0, main:, :main] = edge[:rest]
    for r in range(rest):
        out_ref[0, main + r : main + r + 1, main:] = edge[7:8, 128 * r : 128 * r + rest]
    for f in range(table_ref.shape[0]):
        table_ref[f] = rows_ref[f // 2, 40 * (f % 2) : 40 * (f % 2) + 40].astype(F32)[:edim]

    @pl.when(layer == 0)
    def _():
        for k in range(layers):
            bias_ref[k : k + 1, :main] = small_ref[k, 3:4]
            bias_ref[k : k + 1, main:] = small_ref[k, 7:8, 384 : 384 + rest]
        last = small_ref[layers]
        turned[...] = last.T
        share = in_ref.shape[0]
        me = lax.axis_index("section") * lax.axis_size("dp") + lax.axis_index("dp")
        mine = turned[pl.ds(pl.multiple_of(me * share, share), share)]
        rolled = pltpu.roll(last, lax.rem(main - me * share, main), 1)
        in_bias_ref[...] = rolled[3:4, :share]
        out_bias_ref[...] = rolled[4:5, :share]
        in_ref[:, :main] = pieces_ref[0]
        in_ref[:, main:] = mine[:, :rest]
        out_piece_ref[...] = pieces_ref[1]
        head = jnp.concatenate([last[5:6], last[7:8, :rest], last[6:7]], axis=1)
        head_ref[...] = head.reshape(width + main)
        slope_ref[...] = last[7:8, 128:129]
        loss_ref[...] = last[7:8, 256:257] / examples


def finish(whole, small, rows, pieces, width, fields, edim, examples):
    layers, main = whole.shape[:2]
    share = pieces.shape[1]
    pairs, _, count = rows.shape
    parts = 3
    step = -(-pairs // parts)

    def all_of(*shape):
        return pl.BlockSpec(shape, lambda i: (0,) * len(shape))

    return pl.pallas_call(
        functools.partial(finish_kernel, examples),
        out_shape=[
            jax.ShapeDtypeStruct((layers, width, width), F32),
            jax.ShapeDtypeStruct((fields, edim, count), F32),
            jax.ShapeDtypeStruct((layers, width), F32),
            jax.ShapeDtypeStruct((share, width), F32),
            jax.ShapeDtypeStruct((1, share), F32),
            jax.ShapeDtypeStruct((1, share), F32),
            jax.ShapeDtypeStruct((share, main), F32),
            jax.ShapeDtypeStruct((width + main,), F32),
            jax.ShapeDtypeStruct((1, 1), F32),
            jax.ShapeDtypeStruct((1, 1), F32),
        ],
        grid=(layers,),
        in_specs=[
            pl.BlockSpec((1, main, main), lambda i: (i, 0, 0)),
            all_of(layers + 1, 8, main),
            pl.BlockSpec((step, 80, count), lambda i: (i, 0, 0)),
            all_of(2, share, main),
        ],
        out_specs=[
            pl.BlockSpec((1, width, width), lambda i: (i, 0, 0)),
            pl.BlockSpec((2 * step, edim, count), lambda i: (i, 0, 0)),
            all_of(layers, width),
            all_of(share, width),
            all_of(1, share),
            all_of(1, share),
            all_of(share, main),
            all_of(width + main),
            all_of(1, 1),
            all_of(1, 1),
        ],
        scratch_shapes=[pltpu.VMEM((main, 8), F32)],
        compiler_params=pltpu.CompilerParams(vmem_limit_bytes=63 * 2**20),
        name="finish",
    )(whole, small, rows, pieces)


def general_body(
    ids,
    dense,
    labels,
    table,
    cross_weight,
    cross_bias,
    tower_in,
    tower_in_bias,
    tower_out,
    tower_out_bias,
    head_weight,
    head_bias,
):
    groups = lax.axis_size("dp")
    sections = lax.axis_size("section")
    device_count = groups * sections
    examples, fields = ids.shape
    table_rows, edim = table.shape[1:]
    layers, width = cross_weight.shape[:2]
    hidden = tower_out.shape[0]
    capacity = examples // groups
    sparse = fields * edim
    me = lax.axis_index("section") * groups + lax.axis_index("dp")

    idt = ids.T
    owner = idt // table_rows
    local = idt % table_rows
    owner_hot = owner[:, None, :] == jnp.arange(groups, dtype=jnp.int32)[None, :, None]
    lane = jnp.arange(examples, dtype=jnp.int32)
    before = (lane[:, None] < lane[None, :]).astype(BF)
    counts = mm(owner_hot.reshape(fields * groups, examples).astype(BF), before, (1, 0))
    rank = jnp.sum(jnp.where(owner_hot, counts.reshape(fields, groups, examples), 0.0), axis=1)
    slot = owner * capacity + rank.astype(jnp.int32)
    slot_hot = (slot[:, None, :] == lane[None, :, None]).astype(BF)
    halves = jnp.stack([local // 32, local % 32], axis=1).astype(BF)
    sent = lax.dot_general(
        halves, slot_hot, (((2,), (2,)), ((0,), (0,))), preferred_element_type=F32
    )
    requests = (sent[:, 0] * 32 + sent[:, 1]).astype(jnp.int32)
    requests = requests.reshape(fields, groups, capacity).transpose(1, 0, 2)
    arrived = lax.all_to_all(requests, "dp", 0, 0, tiled=True)
    arrived = arrived.transpose(1, 0, 2).reshape(fields, examples)
    row_hot = (
        arrived[:, None, :] == jnp.arange(table_rows, dtype=jnp.int32)[None, :, None]
    ).astype(BF)
    table_t = table.transpose(0, 2, 1)
    found = lax.dot_general(
        table_t, row_hot, (((2,), (1,)), ((0,), (0,))), preferred_element_type=F32
    ).astype(BF)
    found = found.reshape(sparse, groups, capacity).transpose(1, 0, 2)
    replies = lax.all_to_all(found, "dp", 0, 0, tiled=True)
    replies = replies.transpose(1, 0, 2).reshape(fields, edim, examples)
    embedded = lax.dot_general(
        replies, slot_hot, (((2,), (1,)), ((0,), (0,))), preferred_element_type=F32
    ).astype(BF)
    x0 = jnp.concatenate([embedded.reshape(sparse, examples), dense.T], axis=0)

    x0w = x0.astype(F32)
    xs, us = [x0], []
    for layer in range(layers):
        u = mm(cross_weight[layer], xs[-1], (0, 0)) + cross_bias[layer][:, None]
        us.append(u)
        xs.append((x0w * u + xs[-1].astype(F32)).astype(BF))
    p1 = mm(tower_in, x0, (0, 0)) + tower_in_bias[:, None]
    a1, d1 = gelu_parts(p1)
    h1 = a1.astype(BF)
    p2 = mm(tower_out, h1, (0, 0)) + tower_out_bias[:, None]
    h2, d2 = gelu_parts(p2)
    head_cross, head_tower = head_weight[:width], head_weight[width:]
    last = xs[-1].astype(F32)
    z = (
        jnp.sum(last * head_cross[:, None], axis=0)
        + jnp.sum(h2 * head_tower[:, None], axis=0)
        + head_bias[0]
    )
    probs = jax.nn.sigmoid(z)
    target = labels.astype(F32)
    loss = jnp.sum(jnp.logaddexp(0.0, z) - target * z)
    s = probs - target
    head_grad = jnp.concatenate([jnp.sum(s * last, axis=1), jnp.sum(s * h2, axis=1)])

    q2 = (s[None, :] * head_tower[:, None] * d2).astype(BF)
    tower_out_g = mm(q2, h1, (1, 1))
    q1 = (mm(tower_out, q2, (1, 0)) * d1).astype(BF)
    tower_in_g = mm(q1, x0, (1, 1))
    tower_biases = [jnp.sum(q1.astype(F32), axis=1), jnp.sum(q2.astype(F32), axis=1)]
    dx0 = mm(tower_in, q1, (1, 0))
    g = (s[None, :] * head_cross[:, None]).astype(BF)
    cross_g, cross_b = [None] * layers, [None] * layers
    for layer in reversed(range(layers)):
        gw = g.astype(F32)
        v = (gw * x0w).astype(BF)
        cross_g[layer] = mm(xs[layer], v, (1, 1))
        cross_b[layer] = jnp.sum(v.astype(F32), axis=1)
        dx0 = dx0 + gw * us[layer]
        g = gw + mm(cross_weight[layer], v, (1, 0))
        if layer:
            g = g.astype(BF)
    dx0 = dx0 + g

    packed = lax.dot_general(
        dx0[:sparse].astype(BF).reshape(fields, edim, examples),
        slot_hot,
        (((2,), (2,)), ((0,), (0,))),
        preferred_element_type=F32,
    ).astype(BF)
    packed = packed.reshape(sparse, groups, capacity).transpose(1, 0, 2)
    delivered = lax.all_to_all(packed, "dp", 0, 0, tiled=True)
    delivered = delivered.transpose(1, 0, 2).reshape(fields, edim, examples)
    table_g = lax.dot_general(
        delivered, row_hot, (((2,), (2,)), ((0,), (0,))), preferred_element_type=F32
    )
    table_g = lax.psum(table_g, "section").transpose(0, 2, 1)

    small = jnp.concatenate(
        cross_b + [head_grad, jnp.sum(s).reshape(1), loss.reshape(1)] + tower_biases
    )
    small = lax.psum(small, ("section", "dp"))
    sizes = [layers * width, width + hidden, 1, 1, hidden, hidden]
    ends = [sum(sizes[: i + 1]) for i in range(len(sizes))]
    pieces = [small[e - n : e] for e, n in zip(ends, sizes)]
    cross_b_out = pieces[0].reshape(layers, width)
    share = hidden // device_count
    bias_in, bias_out = (lax.dynamic_slice(p, (me * share,), (share,)) for p in pieces[4:])
    cross_out = lax.psum(jnp.stack(cross_g), ("section", "dp"))
    tower_in_out = lax.psum_scatter(
        tower_in_g, ("section", "dp"), scatter_dimension=0, tiled=True
    )
    tower_out_out = lax.psum_scatter(
        tower_out_g, ("section", "dp"), scatter_dimension=0, tiled=True
    )
    return (
        probs,
        pieces[3] / (examples * device_count),
        dx0[sparse:].T,
        table_g,
        cross_out,
        cross_b_out,
        tower_in_out.T,
        bias_in,
        tower_out_out.T,
        bias_out,
        pieces[1],
        pieces[2],
    )


def body(
    ids,
    dense,
    labels,
    table,
    cross_weight,
    cross_bias,
    tower_in,
    tower_in_bias,
    tower_out,
    tower_out_bias,
    head_weight,
    head_bias,
):
    groups = lax.axis_size("dp")
    sections = lax.axis_size("section")
    device_count = groups * sections
    examples, fields = ids.shape
    table_rows, edim = table.shape[1:]
    layers, width = cross_weight.shape[:2]
    hidden = tower_out.shape[0]
    capacity = examples // groups
    me = lax.axis_index("section") * groups + lax.axis_index("dp")
    idt = ids.T
    table_t = table.transpose(0, 2, 1)
    here = (sections, groups, capacity, table_rows) == (4, 8, 128, 1024)
    if here:
        x0, arrived, source = look_up(idt, table_t, dense.T)
        probs, rows, dense_g, small, *kept = network(
            x0,
            labels.reshape(1, examples),
            cross_weight,
            tower_in,
            tower_out,
            cross_bias,
            tower_in_bias.reshape(1, hidden),
            tower_out_bias.reshape(1, hidden),
            head_weight,
            head_bias,
            edim,
            fields // 2,
        )
        xs, vs = [x0] + kept[: layers - 1], kept[layers - 1 : 2 * layers - 1]
        h1, q1, q2 = kept[2 * layers - 1 :]
        whole, pieces, table_sum, small = reduce_all(
            xs + [q1, q2], vs + [x0, h1], layers, rows, source, arrived, small
        )
        small = small.reshape(layers + 1, 8, hidden)
        cross_out, table_g, cross_b_out, in_out, in_b, out_b, out_out, head_out, slopes, loss = finish(
            whole, small, table_sum, pieces, width, fields, edim, examples * device_count
        )
        return (
            probs.reshape(examples),
            loss.reshape(1),
            dense_g.T,
            table_g.transpose(0, 2, 1),
            cross_out,
            cross_b_out,
            in_out.T,
            in_b.reshape(in_b.shape[1]),
            out_out.T,
            out_b.reshape(out_b.shape[1]),
            head_out,
            slopes.reshape(1),
        )
    return general_body(
        ids, dense, labels, table, cross_weight, cross_bias, tower_in, tower_in_bias, tower_out,
        tower_out_bias, head_weight, head_bias,
    )


def solution(mesh):
    both = ("section", "dp")
    return jax.shard_map(
        body,
        mesh=mesh,
        in_specs=(P(both, None), P(both, None), P(both), P(None, "dp", None)) + (P(),) * 8,
        out_specs=(
            P(both),
            P(),
            P(both, None),
            P(None, "dp", None),
            P(),
            P(),
            P(None, both),
            P(both),
            P(None, both),
            P(both),
            P(),
            P(),
        ),
        check_vma=False,
    )
```

```python
import functools
import math

import jax
import jax.numpy as jnp
from jax import lax
from jax.experimental import pallas as pl
from jax.experimental.pallas import tpu as pltpu
from jax.sharding import PartitionSpec as P

BF = jnp.bfloat16
F32 = jnp.float32


def mm(left, right, contract):
    return lax.dot_general(
        left, right, ((contract[:1], contract[1:]), ((), ())), preferred_element_type=F32
    )


def gelu_parts(pre):
    act, back = jax.vjp(jax.nn.gelu, pre)
    return act, back(jnp.ones_like(pre))[0]


ORDER = [
    "P4 C1 C2 u11",
    "C0 u12 S4 u21",
    "P5 T14 u10 C4",
    "u31 C3 u22 P3",
    "T24 u14 u41 S5",
    "u20 n0 u51 u32",
    "u13 T15 P2 u61",
    "S3 T25 u42 T13",
    "u30 n1 u24 P1",
    "u71 u52 T23 S2",
    "n2 T12 u62 u23",
    "u34 u40 u81 S1",
    "u72 u50 T11 T35",
    "u33 P0 T22 T33",
    "T21 u60 u82 S0",
    "T45 u70 T32 u43",
    "T34 T31 u92 n3",
    "T10 u44 u80 u53",
    "n4 u91 n5 T20",
    "T43 T41 u90 ua1",
    "T42 T30 u54 T44",
    "ua0 T40 ua2 n6",
]
PARTS = 6
VIEW = (2, 2, 2, 2, 2)


def one_hot(places, count):
    rows = lax.broadcasted_iota(jnp.int32, (count, places.shape[1]), 0)
    return (rows == places).astype(F32).astype(BF)


def pick(slab, places):
    low, block = places & 255, lax.shift_right_logical(places, 8)
    blocks = [slab[:, 256 * b : 256 * b + 256] for b in range(4)]
    rows = slab.shape[0]
    every = jnp.dot(
        jnp.concatenate(blocks, axis=0), one_hot(low, 256), preferred_element_type=F32
    )
    chosen = every[:rows]
    for b in range(1, 4):
        chosen = jnp.where(block == b, every[rows * b : rows * b + rows], chosen)
    return chosen


def add_up(slab, places):
    low, block = places & 255, lax.shift_right_logical(places, 8)
    rows = slab.shape[0]
    masked = [slab * (block == b).astype(F32).astype(BF) for b in range(4)]
    every = lax.dot_general(
        jnp.concatenate(masked, axis=0),
        one_hot(low, 256),
        (((1,), (1,)), ((), ())),
        preferred_element_type=F32,
    )
    return jnp.concatenate([every[rows * b : rows * b + rows] for b in range(4)], axis=1)


def reduce_kernel(units, gathered, *refs):
    lefts, rights = refs[:units], refs[units : 2 * units]
    rows_hbm, inv_ref, arr_ref, part_ref = refs[2 * units : 2 * units + 4]
    whole_out, pieces, table_hbm, small_out = refs[2 * units + 4 : 2 * units + 8]
    (
        rows_ref, rows_in, whole, table_out, leave, grads, left, right, load, small, rc, sa1, ra1, sb1, rb1, sa2, ra2, sb2, rb2, sz, rz, sf, rf, packed, back, summed,
        stc, rtc, st, rt, sm, rm, send, recv, row_send, row_recv, table_send, table_recv,
    ) = refs[2 * units + 8 :]
    pairs, count = rows_hbm.shape[0], rows_hbm.shape[2]
    section, dp = lax.axis_index("section"), lax.axis_index("dp")
    y, c = section // 2, section % 2
    z, x = dp // 2, dp % 2
    zh, zl = z // 2, z % 2
    core_peer = (y * 2 + 1 - c, dp)
    y_peer = ((1 - y) * 2 + c, dp)
    x_peer = (section, z * 2 + 1 - x)
    half = 512
    lo, hi = pl.ds(0, half), pl.ds(half, half)

    near_peer = (section, zh * 4 + (1 - zl) * 2 + x)
    far_peer = (section, (1 - zh) * 4 + zl * 2 + x)

    def dp_peer(j):
        return (section, lax.rem(dp + j, 8))

    peers = [core_peer, y_peer] + [dp_peer(j) for j in range(1, 8)]
    barrier = pltpu.get_barrier_semaphore()
    for peer in peers:
        pl.semaphore_signal(barrier, inc=1, device_id=peer, device_id_type=pl.DeviceIdType.MESH)

    flying = []

    def start(src, dst, m, k, peer, sems=(send, recv)):
        copy = pltpu.make_async_remote_copy(
            src_ref=src,
            dst_ref=dst,
            send_sem=sems[0].at[m, k],
            recv_sem=sems[1].at[m, k],
            device_id=peer,
            device_id_type=pl.DeviceIdType.MESH,
        )
        copy.start()
        flying.append(copy)
        return copy

    def wide(value):
        return value.astype(F32)

    copies = {}
    gone = []

    def leave_with(src, dst, k):
        copy = pltpu.make_async_copy(src, dst, leave.at[k])
        copy.start()
        gone.append(copy)

    def acc(m, stage, cols, yy, hh, ll, xx):
        zz = 2 * hh + ll
        total = wide(grads[m, yy, c, hh, ll, xx, :, cols]) + wide(rc[m, yy, hh, ll, xx, :, cols])
        if cols is lo:
            if stage >= 2:
                total += wide(ra1[m, yy, zz])
            if stage >= 3:
                total += wide(ra2[m, zz])
        else:
            if stage >= 2:
                total += wide(rb1[m, zz, xx])
            if stage >= 3:
                total += wide(rb2[m, zz])
        return total

    tokens = " ".join(ORDER).split()
    made = [int(t[1]) for t in tokens if t[0] == "C"]

    def height(m):
        return min(lefts[m].shape[0], left.shape[1])

    def loads(turn):
        m, slot = made[turn], turn % 2
        return [
            pltpu.make_async_copy(ref.at[:rows], buf.at[slot, :rows], load.at[slot, k])
            for k, (ref, buf, rows) in enumerate(
                ((lefts[m], left, height(m)), (rights[m], right, rights[m].shape[0]))
            )
        ]

    def make(m):
        turn = made.index(m)
        slot = turn % 2
        for copy in loads(turn):
            copy.wait()
        tall = height(m) - 1024
        across = rights[m].shape[0]
        for r in range(2):
            total = lax.dot_general(
                left[slot, 512 * r : 512 * r + 512 + r * tall],
                right[slot, :across],
                (((1,), (1,)), ((), ())),
                preferred_element_type=F32,
            )
            grads[m, r] = total[:512, :1024].astype(BF).reshape(2, 2, 2, 2, 32, 1024)
            if across > 1024:
                side = total[:512, 1024:].T
                group, at = m // 2, m % 2 * 8
                if tall:
                    small[group, at + 4 : at + 7, 512 * r : 512 * r + 512] = side[0:3]
                else:
                    small[group, at : at + 4, 512 * r : 512 * r + 512] = side[0:4]
                if tall and r:
                    small[group, at : at + 4] = total[512:516, :1024]
                    small[group, at + 7 : at + 8, 512:] = jnp.zeros((1, 512), F32)
                    for k in range(4):
                        small[group, at + 7 : at + 8, 128 * k : 128 * k + 128] = total[
                            512 + k : 513 + k, 1024:
                        ]
        if turn + 2 < units:
            for copy in loads(turn + 2):
                copy.start()

    def step0(m):
        make(m)
        copies[m, 0] = start(grads.at[m, :, 1 - c], rc.at[m], m, 0, core_peer)

    def step1(m):
        copies[m, 0].wait_recv()

        @pl.loop(0, 2)
        def _(hh):
            for ll in range(2):
                for i in range(2):
                    sa1[m, i, 2 * hh + ll] = acc(m, 1, lo, i, hh, ll, 1 - x).astype(BF)
                    sb1[m, 2 * hh + ll, i] = acc(m, 1, hi, 1 - y, hh, ll, i).astype(BF)

        copies[m, 1] = start(sa1.at[m], ra1.at[m], m, 1, x_peer)
        copies[m, 2] = start(sb1.at[m], rb1.at[m], m, 2, y_peer)

    def step2(m):
        copies[m, 1].wait_recv()
        copies[m, 2].wait_recv()

        @pl.loop(0, 2)
        def _(hh):
            for ll in range(2):
                sa2[m, 2 * hh + ll] = acc(m, 2, lo, 1 - y, hh, ll, x).astype(BF)
                sb2[m, 2 * hh + ll] = acc(m, 2, hi, y, hh, ll, 1 - x).astype(BF)

        copies[m, 3] = start(sa2.at[m], ra2.at[m], m, 3, y_peer)
        copies[m, 4] = start(sb2.at[m], rb2.at[m], m, 4, x_peer)

    def step3(m):
        copies[m, 3].wait_recv()
        copies[m, 4].wait_recv()
        for hh in range(2):
            for cols in (lo, hi):
                sz[m, hh, :, cols] = acc(m, 3, cols, y, hh, 1 - zl, x).astype(BF)
        copies[m, 5] = start(sz.at[m], rz.at[m], m, 5, near_peer)

    def step4(m):
        copies[m, 5].wait_recv()
        for cols in (lo, hi):
            total = acc(m, 3, cols, y, 1 - zh, zl, x) + wide(rz[m, 1 - zh, :, cols])
            sf[m, :, cols] = total.astype(BF)
        copies[m, 6] = start(sf.at[m], rf.at[m], m, 6, far_peer)

    def step5(m):
        copies[m, 6].wait_recv()
        for cols in (lo, hi):
            total = acc(m, 3, cols, y, zh, zl, x) + wide(rz[m, zh, :, cols]) + wide(rf[m, :, cols])
            if m < gathered:
                whole[m, y, c, zh, zl, x, :, cols] = total.astype(BF)
            else:
                pieces[m - gathered, :, cols] = total
        if m < gathered:
            ours = whole.at[m, y, c, zh, zl, x]
            copies[m, 7] = start(ours, ours, m, 7, far_peer)

    def step6(m):
        copies[m, 7].wait_recv()
        ours = whole.at[m, y, c, :, zl, x]
        copies[m, 8] = start(ours, ours, m, 8, near_peer)

    def step7(m):
        copies[m, 8].wait_recv()
        ours = whole.at[m, y, c, :, :, x, :, lo]
        copies[m, 11] = start(ours, ours, m, 11, y_peer)
        ours = whole.at[m, y, c, :, :, x, :, hi]
        copies[m, 12] = start(ours, ours, m, 12, x_peer)

    def step8(m):
        copies[m, 11].wait_recv()
        copies[m, 12].wait_recv()
        ours = whole.at[m, :, c, :, :, x, :, lo]
        copies[m, 13] = start(ours, ours, m, 13, x_peer)
        ours = whole.at[m, y, c, :, :, :, :, hi]
        copies[m, 14] = start(ours, ours, m, 14, y_peer)

    def step9(m):
        copies[m, 13].wait_recv()
        copies[m, 14].wait_recv()
        ours = whole.at[m, :, c]
        copies[m, 15] = start(ours, ours, m, 15, core_peer)

    def step10(m):
        copies[m, 15].wait_recv()
        leave_with(whole.at[m], whole_out.at[m], m)

    def lanes(place, size):
        return pl.ds(pl.multiple_of(place * size, size), size)

    cuts = [pairs * q // PARTS for q in range(PARTS + 1)]

    def row_copy(q, j):
        part = pl.ds(cuts[q], cuts[q + 1] - cuts[q])
        return pltpu.make_async_remote_copy(
            src_ref=packed.at[part, :, lanes(lax.rem(dp + j, 8), 128)],
            dst_ref=back.at[part, :, lanes(dp, 128)],
            send_sem=row_send.at[q, j],
            recv_sem=row_recv.at[q, j],
            device_id=dp_peer(j),
            device_id_type=pl.DeviceIdType.MESH,
        )

    def pack(q):
        @pl.loop(cuts[q], cuts[q + 1])
        def _(i):
            first = pick(rows_ref[i, 0:48], inv_ref[pl.ds(2 * i, 1)])
            second = pick(rows_ref[i, 32:80], inv_ref[pl.ds(2 * i + 1, 1)])
            packed[i] = jnp.concatenate([first[0:40], second[8:48]], axis=0).astype(BF)
            back[i, :, lanes(dp, 128)] = packed[i, :, lanes(dp, 128)]

        for j in range(1, 8):
            row_copy(q, j).start()

    def scatter(q):
        for j in range(1, 8):
            row_copy(q, j).wait_recv()

        @pl.loop(cuts[q], cuts[q + 1])
        def _(i):
            for h, (low, at) in enumerate(((0, 0), (32, 8))):
                total = add_up(back[i, low : low + 48], arr_ref[pl.ds(2 * i + h, 1)])
                summed[i, 40 * h : 40 * h + 40] = total[at : at + 40]
            stc[i] = summed[i, :, lanes(1 - c, half)].astype(BF)

        part = pl.ds(cuts[q], cuts[q + 1] - cuts[q])
        copies["t", q, 0] = start(stc.at[part], rtc.at[part], q, 0, core_peer, (table_send, table_recv))

    quarter = half // 2

    def quarter_of(yy):
        return lanes(2 * c + yy, quarter)

    def table1(q):
        copies["t", q, 0].wait_recv()

        @pl.loop(cuts[q], cuts[q + 1])
        def _(i):
            st[i] = (summed[i, :, quarter_of(1 - y)] + wide(rtc[i, :, lanes(1 - y, quarter)])).astype(BF)

        part = pl.ds(cuts[q], cuts[q + 1] - cuts[q])
        copies["t", q, 1] = start(st.at[part], rt.at[part], q, 1, y_peer, (table_send, table_recv))

    def table2(q):
        copies["t", q, 1].wait_recv()

        @pl.loop(cuts[q], cuts[q + 1])
        def _(i):
            total = summed[i, :, quarter_of(y)] + wide(rtc[i, :, lanes(y, quarter)]) + wide(rt[i])
            table_out[i, :, quarter_of(y)] = total.astype(BF)

        part = pl.ds(cuts[q], cuts[q + 1] - cuts[q])
        ours = table_out.at[part, :, quarter_of(y)]
        copies["t", q, 2] = start(ours, ours, q, 2, y_peer, (table_send, table_recv))

    def table3(q):
        copies["t", q, 2].wait_recv()
        part = pl.ds(cuts[q], cuts[q + 1] - cuts[q])
        ours = table_out.at[part, :, lanes(c, half)]
        copies["t", q, 3] = start(ours, ours, q, 3, core_peer, (table_send, table_recv))

    def table4(q):
        copies["t", q, 3].wait_recv()
        part = pl.ds(cuts[q], cuts[q + 1] - cuts[q])
        leave_with(table_out.at[part], table_hbm.at[part], gathered + q)

    s = units

    def small0():
        small[1, 12:16] = part_ref[0:4]
        copies[s, 0] = start(small.at[1 - c], rm.at[0], s, 0, core_peer)

    def small1():
        copies[s, 0].wait_recv()
        sm[0] = small[c] + rm[0]
        copies[s, 1] = start(sm.at[0], rm.at[1], s, 1, x_peer)

    def small2():
        copies[s, 1].wait_recv()
        sm[1] = sm[0] + rm[1]
        copies[s, 2] = start(sm.at[1], rm.at[2], s, 2, y_peer)

    def small3():
        copies[s, 2].wait_recv()
        sm[2] = sm[1] + rm[2]
        copies[s, 3] = start(sm.at[2], rm.at[3], s, 3, near_peer)

    def small4():
        copies[s, 3].wait_recv()
        sm[3] = sm[2] + rm[3]
        copies[s, 4] = start(sm.at[3], rm.at[4], s, 4, far_peer)

    def small5():
        copies[s, 4].wait_recv()
        small_out[c] = sm[3] + rm[4]
        ours = small_out.at[c]
        copies[s, 6] = start(ours, ours, s, 6, core_peer)

    def small6():
        copies[s, 6].wait_recv()

    steps = [step1, step2, step3, step4, step5, step6, step7, step8, step9, step10]
    smalls = [small0, small1, small2, small3, small4, small5, small6]
    tables = [table1, table2, table3, table4]
    rows_copy = pltpu.make_async_copy(rows_hbm, rows_ref, rows_in)
    rows_copy.start()
    for copy in loads(0) + loads(1):
        copy.start()
    pl.semaphore_wait(barrier, len(peers))
    rows_copy.wait()
    for token in tokens:
        kind, numbers = token[0], [int(n, 16) for n in token[1:]]
        if kind == "C":
            step0(*numbers)
        elif kind == "P":
            pack(*numbers)
        elif kind == "S":
            scatter(*numbers)
        elif kind == "n":
            smalls[numbers[0]]()
        else:
            {"u": steps, "T": tables}[kind][numbers[0] - 1](numbers[1])
    for copy in flying:
        copy.wait_send()
    for copy in gone:
        copy.wait()

    for q in range(PARTS):
        for j in range(1, 8):
            row_copy(q, j).wait_send()


def reduce_all(lefts, rights, gathered, rows, source, arrived, small):
    units = len(lefts)
    pairs, _, count = rows.shape
    piece = (32, 1024)
    vmem = pl.BlockSpec(memory_space=pltpu.VMEM)
    hbm = pl.BlockSpec(memory_space=pl.ANY)
    whole, pieces, table_sum, small_sum = pl.pallas_call(
        lambda *refs: reduce_kernel(units, gathered, *refs),
        out_shape=[
            jax.ShapeDtypeStruct((gathered,) + VIEW + piece, BF),
            jax.ShapeDtypeStruct((units - gathered,) + piece, F32),
            jax.ShapeDtypeStruct((pairs, 80, count), BF),
            jax.ShapeDtypeStruct((2, 16, 1024), F32),
        ],
        in_specs=[hbm] * (2 * units + 1) + [vmem] * 3,
        out_specs=[hbm, vmem, hbm, vmem],
        scratch_shapes=[
            pltpu.VMEM((pairs, 80, count), BF),
            pltpu.SemaphoreType.DMA,
            pltpu.VMEM((gathered,) + VIEW + piece, BF),
            pltpu.VMEM((pairs, 80, count), BF),
            pltpu.SemaphoreType.DMA((gathered + PARTS,)),
            pltpu.VMEM((units,) + VIEW + piece, BF),
            pltpu.VMEM((2, 1040, count), BF),
            pltpu.VMEM((2, 1152, count), BF),
            pltpu.SemaphoreType.DMA((2, 2)),
            pltpu.VMEM((2, 16, 1024), F32),
            pltpu.VMEM((units, 2, 2, 2, 2) + piece, BF),
            pltpu.VMEM((units, 2, 4, 32, 512), BF),
            pltpu.VMEM((units, 2, 4, 32, 512), BF),
            pltpu.VMEM((units, 4, 2, 32, 512), BF),
            pltpu.VMEM((units, 4, 2, 32, 512), BF),
            pltpu.VMEM((units, 4, 32, 512), BF),
            pltpu.VMEM((units, 4, 32, 512), BF),
            pltpu.VMEM((units, 4, 32, 512), BF),
            pltpu.VMEM((units, 4, 32, 512), BF),
            pltpu.VMEM((units, 2) + piece, BF),
            pltpu.VMEM((units, 2) + piece, BF),
            pltpu.VMEM((units,) + piece, BF),
            pltpu.VMEM((units,) + piece, BF),
            pltpu.VMEM((pairs, 80, count), BF),
            pltpu.VMEM((pairs, 80, count), BF),
            pltpu.VMEM((pairs, 80, count), F32),
            pltpu.VMEM((pairs, 80, count // 2), BF),
            pltpu.VMEM((pairs, 80, count // 2), BF),
            pltpu.VMEM((pairs, 80, count // 4), BF),
            pltpu.VMEM((pairs, 80, count // 4), BF),
            pltpu.VMEM((4, 16, 1024), F32),
            pltpu.VMEM((5, 16, 1024), F32),
            pltpu.SemaphoreType.DMA((units + 1, 16)),
            pltpu.SemaphoreType.DMA((units + 1, 16)),
            pltpu.SemaphoreType.DMA((PARTS, 8)),
            pltpu.SemaphoreType.DMA((PARTS, 8)),
            pltpu.SemaphoreType.DMA((PARTS, 4)),
            pltpu.SemaphoreType.DMA((PARTS, 4)),
        ],
        compiler_params=pltpu.CompilerParams(
            collective_id=0, has_side_effects=True, vmem_limit_bytes=63 * 2**20
        ),
        name="reduce_all",
    )(
        *lefts,
        *rights,
        rows,
        source,
        arrived,
        small,
    )
    return whole.reshape(gathered, 1024, 1024), pieces, table_sum, small_sum.reshape(-1)


def lookup_kernel(
    fields, edim, ids_ref, table_hbm, dense_ref, x0_ref, arr_ref, inv_ref,
    table_ref, table_in, ids, slots, req, found, rep, held, pair, wide_rows, x0f, far, arr_far,
    id_send, id_recv, send, recv, far_send, far_recv, far_id_send, far_id_recv, half_send, half_recv,
):
    section, me = lax.axis_index("section"), lax.axis_index("dp")
    direct = fields // 2 - far.shape[0] // 2
    half, spot = me // 4, lax.rem(me, 4)
    twin = lax.rem(me + 4, 8)
    y, core = section // 2, lax.rem(section, 2)
    core_peer = (y * 2 + 1 - core, me)
    y_peer = ((1 - y) * 2 + core, me)
    dot = functools.partial(jnp.dot, preferred_element_type=F32)
    count = ids.shape[1]

    table_copy = pltpu.make_async_copy(table_hbm, table_ref, table_in)
    table_copy.start()

    def peer(j):
        return lax.rem(me + j, 8)

    def near(j):
        return lax.rem(spot + j, 4)

    def lanes(place, size=128):
        return pl.ds(pl.multiple_of(place * size, size), size)

    barrier = pltpu.get_barrier_semaphore()
    for j in range(1, 8):
        pl.semaphore_signal(
            barrier, inc=1, device_id=(section, peer(j)), device_id_type=pl.DeviceIdType.MESH
        )
    for other in (core_peer, y_peer):
        pl.semaphore_signal(barrier, inc=1, device_id=other, device_id_type=pl.DeviceIdType.MESH)

    def far_copy(k):
        quarter = section if k < 3 else (1 - y) * 2 + core
        window = far.at[:, :, lanes(quarter, count // 4)]
        return pltpu.make_async_remote_copy(
            src_ref=window if k else table_ref.at[2 * direct :, :, lanes(quarter, count // 4)],
            dst_ref=window,
            send_sem=far_send.at[k],
            recv_sem=far_recv.at[k],
            device_id=((section, twin), core_peer, y_peer, core_peer)[k],
            device_id_type=pl.DeviceIdType.MESH,
        )

    ids[...] = jnp.zeros_like(ids)
    ids[:fields] = ids_ref[...]
    every = ids[...]
    owner = lax.shift_right_logical(every, 10)
    hot = jnp.concatenate([(owner == o).astype(F32) for o in range(8)], axis=0).astype(BF)
    before = (
        lax.broadcasted_iota(jnp.int32, (count, count), 0)
        < lax.broadcasted_iota(jnp.int32, (count, count), 1)
    )
    ranks = dot(hot, before.astype(F32).astype(BF))
    rank = jnp.zeros((32, count), F32)
    for o in range(8):
        rank = jnp.where(owner == o, ranks[32 * o : 32 * o + 32], rank)
    slots[...] = owner * 128 + rank.astype(jnp.int32)
    pl.semaphore_wait(barrier, 9)
    table_copy.wait()
    far_copy(0).start()
    ids[...] = every & 1023
    def id_copy(group, j):
        eight = pl.ds(pl.multiple_of(8 * group, 8), 8)
        return pltpu.make_async_remote_copy(
            src_ref=req.at[eight, lanes(peer(j))],
            dst_ref=arr_ref.at[eight, lanes(me)],
            send_sem=id_send.at[group, j],
            recv_sem=id_recv.at[group, j],
            device_id=(section, peer(j)),
            device_id_type=pl.DeviceIdType.MESH,
        )

    def far_id_copy(group, j):
        eight = pl.ds(pl.multiple_of(8 * group, 8), 8)
        return pltpu.make_async_remote_copy(
            src_ref=req.at[eight, lanes(4 * (1 - half) + near(j))],
            dst_ref=arr_far.at[eight, lanes(spot)],
            send_sem=far_id_send.at[group, j],
            recv_sem=far_id_recv.at[group, j],
            device_id=(section, 4 * half + near(j)),
            device_id_type=pl.DeviceIdType.MESH,
        )

    @pl.loop(0, 4)
    def _(group):
        eight = pl.ds(pl.multiple_of(8 * group, 8), 8)
        slot8, local8 = slots[eight], ids[eight]
        place = lax.broadcasted_iota(jnp.int32, (1, count), 1)
        column = lax.broadcasted_iota(jnp.int32, (8, count), 0)
        wanted, source = [], []
        for k in range(8):
            slot, local = slot8[k : k + 1], local8[k : k + 1]
            owners = column == lax.shift_right_logical(slot, 7)
            parts = [local >> 5, local & 31, place >> 5, place & 31]
            left = jnp.concatenate(
                [jnp.where(owners, p.astype(F32), 0.0) for p in parts], axis=0
            ).astype(BF)
            right = one_hot(slot & 127, 128)
            sent = lax.dot_general(
                left, right, (((1,), (1,)), ((), ())), preferred_element_type=F32
            )
            rows = [
                (sent[n : n + 8] * 32 + sent[n + 8 : n + 16]).astype(jnp.int32) for n in (0, 16)
            ]
            for taken, r in zip((wanted, source), rows):
                taken.append(jnp.concatenate([r[o : o + 1] for o in range(8)], axis=1))
        req[eight] = jnp.concatenate(wanted, axis=0)
        inv_ref[eight] = jnp.concatenate(source, axis=0)
        for j in range(1, 8):
            id_copy(group, j).start()
        for j in range(1, 4):
            far_id_copy(group, j).start()
        arr_ref[eight, lanes(me)] = req[eight, lanes(me)]
        arr_far[eight, lanes(spot)] = req[eight, lanes(4 * (1 - half) + spot)]

    def ids_of(group):
        for j in range(1, 8):
            id_copy(group, j).wait_recv()


    def row_copy(i, j):
        return pltpu.make_async_remote_copy(
            src_ref=found.at[i, :, lanes(peer(j))],
            dst_ref=rep.at[i, :, lanes(me)],
            send_sem=send.at[i, j],
            recv_sem=recv.at[i, j],
            device_id=(section, peer(j)),
            device_id_type=pl.DeviceIdType.MESH,
        )

    pair[...] = jnp.zeros_like(pair)
    held[...] = jnp.zeros_like(held)

    def half_copy(i, j, far_side):
        owner_place = 4 * (1 - half) + spot if far_side else me
        return pltpu.make_async_remote_copy(
            src_ref=found.at[i, :, lanes(4 * far_side + near(j))],
            dst_ref=rep.at[i, :, lanes(owner_place)],
            send_sem=half_send.at[far_side, i - direct, j],
            recv_sem=half_recv.at[far_side, i - direct, j],
            device_id=(section, 4 * half + near(j)),
            device_id_type=pl.DeviceIdType.MESH,
        )

    assert direct % 4 == 0

    @pl.loop(0, direct)
    def _(i):
        @pl.when(lax.rem(i, 4) == 0)
        def _():
            ids_of(i // 4)

        for h in range(2):
            held[h, :edim] = table_ref[2 * i + h]
            chosen = pick(held[h], arr_ref[pl.ds(2 * i + h, 1)])
            pair[40 * h : 40 * h + edim] = chosen[:edim]
        found[i] = pair[...].astype(BF)
        for j in range(1, 8):
            row_copy(i, j).start()
        rep[i, :, lanes(me)] = found[i, :, lanes(me)]

    for group in range(direct // 4, 4):
        ids_of(group)

    @pl.loop(direct, fields // 2)
    def _(i):
        for h in range(2):
            held[h, :edim] = table_ref[2 * i + h]
            places = arr_ref[pl.ds(2 * i + h, 1), lanes(half, count // 2)]
            pair[40 * h : 40 * h + edim, : count // 2] = pick(held[h], places)[:edim]
        found[i, :, : count // 2] = pair[:, : count // 2].astype(BF)
        for j in range(1, 4):
            half_copy(i, j, 0).start()
        rep[i, :, lanes(me)] = found[i, :, lanes(spot)]

    far_copy(0).wait_recv()
    far_copy(2).start()
    far_copy(1).start()
    for group in range(4):
        for j in range(1, 4):
            far_id_copy(group, j).wait_recv()
    far_copy(2).wait_recv()
    far_copy(3).start()
    far_copy(1).wait_recv()
    far_copy(3).wait_recv()

    @pl.loop(direct, fields // 2)
    def _(i):
        for h in range(2):
            held[h, :edim] = far[2 * (i - direct) + h]
            places = arr_far[pl.ds(2 * i + h, 1)]
            pair[40 * h : 40 * h + edim, count // 2 :] = pick(held[h], places)[:edim]
        found[i, :, count // 2 :] = pair[:, count // 2 :].astype(BF)
        for j in range(1, 4):
            half_copy(i, j, 1).start()
        rep[i, :, lanes(4 * (1 - half) + spot)] = found[i, :, lanes(4 + spot)]

    def unpack(i):
        wide_rows[2 * i] = pick(rep[i, 0:48], slots[pl.ds(2 * i, 1)])[0:40]
        wide_rows[2 * i + 1] = pick(rep[i, 32:80], slots[pl.ds(2 * i + 1, 1)])[8:48]

    @pl.loop(0, direct)
    def _(i):
        for j in range(1, 8):
            row_copy(i, j).wait_recv()
        unpack(i)

    @pl.loop(direct, fields // 2)
    def _(i):
        for j in range(1, 4):
            half_copy(i, j, 0).wait_recv()
            half_copy(i, j, 1).wait_recv()
        unpack(i)

    sparse, extra = fields * edim, dense_ref.shape[0]
    x0f[sparse // 8 * 8 :] = jnp.zeros_like(x0f[sparse // 8 * 8 :])
    for f in range(fields):
        x0f[f * edim : f * edim + edim] = wide_rows[f, :edim]
    x0f[sparse : sparse + extra] = dense_ref[...].astype(F32)
    x0f[sparse + extra : sparse + extra + 1] = jnp.ones_like(x0f[:1])
    x0_ref[...] = x0f[...].astype(BF)

    @pl.loop(0, direct)
    def _(i):
        for j in range(1, 8):
            row_copy(i, j).wait_send()

    @pl.loop(direct, fields // 2)
    def _(i):
        for j in range(1, 4):
            half_copy(i, j, 0).wait_send()
            half_copy(i, j, 1).wait_send()

    for group in range(4):
        for j in range(1, 8):
            id_copy(group, j).wait_send()
        for j in range(1, 4):
            far_id_copy(group, j).wait_send()
    for n in range(4):
        far_copy(n).wait_send()


def look_up(ids_t, table_t, dense_t):
    fields, count = ids_t.shape
    edim = table_t.shape[1]
    tall = (fields * edim + dense_t.shape[0]) // 128 * 128 + 128
    mirrored = fields // 4 - 1
    vmem = pl.BlockSpec(memory_space=pltpu.VMEM)
    return pl.pallas_call(
        functools.partial(lookup_kernel, fields, edim),
        out_shape=[
            jax.ShapeDtypeStruct((tall, count), BF),
            jax.ShapeDtypeStruct((32, count), jnp.int32),
            jax.ShapeDtypeStruct((32, count), jnp.int32),
        ],
        in_specs=[vmem, pl.BlockSpec(memory_space=pl.ANY), vmem],
        out_specs=[vmem] * 3,
        scratch_shapes=[
            pltpu.VMEM(table_t.shape, BF),
            pltpu.SemaphoreType.DMA,
            pltpu.VMEM((32, count), jnp.int32),
            pltpu.VMEM((32, count), jnp.int32),
            pltpu.VMEM((32, count), jnp.int32),
            pltpu.VMEM((fields // 2, 80, count), BF),
            pltpu.VMEM((fields // 2, 80, count), BF),
            pltpu.VMEM((2, 48, count), BF),
            pltpu.VMEM((80, count), F32),
            pltpu.VMEM((fields, 40, count), F32),
            pltpu.VMEM((tall, count), F32),
            pltpu.VMEM((2 * mirrored, edim, count), BF),
            pltpu.VMEM((32, count // 2), jnp.int32),
            pltpu.SemaphoreType.DMA((4, 8)),
            pltpu.SemaphoreType.DMA((4, 8)),
            pltpu.SemaphoreType.DMA((fields // 2, 8)),
            pltpu.SemaphoreType.DMA((fields // 2, 8)),
            pltpu.SemaphoreType.DMA((4,)),
            pltpu.SemaphoreType.DMA((4,)),
            pltpu.SemaphoreType.DMA((4, 4)),
            pltpu.SemaphoreType.DMA((4, 4)),
            pltpu.SemaphoreType.DMA((2, mirrored, 4)),
            pltpu.SemaphoreType.DMA((2, mirrored, 4)),
        ],
        compiler_params=pltpu.CompilerParams(
            collective_id=1, has_side_effects=True, vmem_limit_bytes=63 * 2**20
        ),
        name="look_up",
    )(ids_t, table_t, dense_t)


def gelu_and_slope(pre):
    root = (2.0 / math.pi) ** 0.5
    square = pre * pre
    tanh = jnp.tanh(root * pre * (1.0 + 0.044715 * square))
    cdf = 0.5 + 0.5 * tanh
    bend = 0.5 * root * (1.0 - tanh * tanh) * (1.0 + 3 * 0.044715 * square)
    return pre * cdf, cdf + pre * bend


def network_kernel(
    width, edim, x0_hbm, labels_ref, weight_hbm, in_hbm, out_hbm, bias_ref, in_bias_ref, out_bias_ref, head_ref, hb_ref,
    probs_ref, rows_ref, dense_ref, small_ref, *rest,
):
    layers = weight_hbm.shape[0]
    kept = 2 * layers + 2
    outs = rest[:kept]
    (
        x0_ref, weight_ref, in_ref, out_ref, xs, vs, h1s, q1s, q2s, gs, us, d1s, d2s, dxs, accx, acch, accq, accs,
        lines, cols, enter, leave,
    ) = rest[kept:]
    main = in_hbm.shape[1]
    edge = slice(main, main + 16)
    count = x0_hbm.shape[1]
    block = us.shape[2]
    pairs = rows_ref.shape[0]

    entering = [
        pltpu.make_async_copy(src, dst, enter.at[k])
        for k, (src, dst) in enumerate(
            [(x0_hbm, x0_ref)]
            + [(weight_hbm.at[i], weight_ref.at[i]) for i in range(layers)]
            + [(in_hbm, in_ref), (out_hbm, out_ref)]
        )
    ]
    for copy in entering:
        copy.start()

    def leaving(k, n):
        at = pl.ds(pl.multiple_of(n * block, block), block)
        here = [xs.at[i, :, at] for i in range(layers - 1)] + [vs.at[i] for i in range(layers)]
        here += [h1s.at[:, at], q1s, q2s]
        return pltpu.make_async_copy(here[k], outs[k].at[:, at], leave.at[n, k])

    def dot(a, b, ca, cb):
        return lax.dot_general(a, b, (((ca,), (cb,)), ((), ())), preferred_element_type=F32)

    def fold(value):
        return functools.reduce(
            lambda a, b: a + b, [value[:, n : n + 128] for n in range(0, value.shape[1], 128)]
        )

    for layer in range(layers):
        vs[layer, main:] = jnp.zeros_like(vs[layer, main:])
    accx[...] = jnp.zeros_like(accx)
    acch[...] = jnp.zeros_like(acch)
    accq[...] = jnp.zeros_like(accq)
    accs[...] = jnp.zeros_like(accs)
    lines[...] = jnp.zeros_like(lines)
    lines[0:layers, :width] = bias_ref[...]
    lines[layers : layers + 1, :main] = in_bias_ref[...]
    lines[layers + 1 : layers + 2, :main] = out_bias_ref[...]
    head = head_ref[...].reshape(1, width + main)
    lines[layers + 2 : layers + 3, :width] = head[:, :width]
    lines[layers + 3 : layers + 4, :main] = head[:, width:]
    cols[...] = lines[...].T
    entering[0].wait()
    for layer in range(1, layers):
        xs[layer - 1, edge] = x0_ref[edge]

    blocks = count // block

    def one_block(n):
        at = slice(n * block, n * block + block)

        def before(*which):
            if n:
                for k in which:
                    leaving(k, n - 1).wait()

        def arrived(k):
            if n == 0:
                entering[k].wait()

        def complete(k):
            leaving(k, n).start()

        def x_of(layer):
            return x0_ref[:width, at] if layer == 0 else xs[layer - 1, :width, at]

        def col(k, size):
            return cols[:size, k : k + 1]

        for layer in range(layers):
            arrived(1 + layer)
            u = dot(weight_ref[layer], x_of(layer), 0, 0) + col(layer, width)
            us[layer, :width] = u
            x = (x_of(0).astype(F32) * u + x_of(layer).astype(F32)).astype(BF)
            if layer + 1 < layers:
                xs[layer, :width, at] = x
                complete(layer)
        last = x.astype(F32)
        arrived(layers + 1)
        h1, d1 = gelu_and_slope(dot(in_ref[...], x_of(0), 0, 0) + col(layers, main))
        d1s[...] = d1
        h1s[:, at] = h1.astype(BF)
        complete(2 * layers - 1)
        arrived(layers + 2)
        h2, d2 = gelu_and_slope(dot(out_ref[...], h1s[:, at], 0, 0) + col(layers + 1, main))
        d2s[...] = d2
        head_cross, head_tower = col(layers + 2, width), col(layers + 3, main)
        z = (
            jnp.sum(last * head_cross, axis=0, keepdims=True)
            + jnp.sum(h2 * head_tower, axis=0, keepdims=True)
            + hb_ref[0]
        )
        probs = jax.nn.sigmoid(z)
        target = labels_ref[:, at].astype(F32)
        probs_ref[:, at] = probs
        s = probs - target
        loss = jnp.maximum(z, 0.0) + jnp.log1p(jnp.exp(-jnp.abs(z))) - target * z
        accs[0:1] += fold(s)
        accs[1:2] += fold(loss)
        accx[:width] += fold(s * last)
        acch[...] += fold(s * h2)

        q2 = ((s * head_tower) * d2s[...]).astype(BF)
        before(2 * layers + 1)
        q2s[...] = q2
        complete(2 * layers + 1)
        acc = fold(q2.astype(F32))
        accq[...] += acc
        q1 = (dot(out_ref[...], q2, 1, 0) * d1s[...]).astype(BF)
        before(2 * layers)
        q1s[...] = q1
        complete(2 * layers)
        g = (s * head_cross).astype(BF)
        before(*range(layers - 1, 2 * layers - 1))
        for layer in reversed(range(layers)):
            gs[layer, :width] = g
            v = (g.astype(F32) * x_of(0).astype(F32)).astype(BF)
            vs[layer, :width] = v
            complete(layers - 1 + layer)
            g = g.astype(F32) + dot(weight_ref[layer], v, 1, 0)
            if layer:
                g = g.astype(BF)
        g += dot(in_ref[...], q1, 1, 0)
        for layer in range(layers):
            g += gs[layer, :width].astype(F32) * us[layer, :width]
        dxs[:width] = g
        for i in range(pairs):
            low = 2 * i * edim
            both = [dxs[low : low + 40], dxs[low + edim : low + edim + 40]]
            rows_ref[i, :, at] = jnp.concatenate(both, axis=0).astype(BF)
        dense_ref[:, at] = dxs[2 * pairs * edim : width]

    for n in range(blocks):
        one_block(n)
    for n in range(blocks):
        for k in range(kept):
            if n == blocks - 1 or k < layers - 1 or k == 2 * layers - 1:
                leaving(k, n).wait()

    head_x = jnp.sum(accx[...].T, axis=0, keepdims=True)
    head_h = jnp.sum(acch[...].T, axis=0, keepdims=True)
    sums = [
        jnp.broadcast_to(jnp.sum(accs[k : k + 1], axis=1, keepdims=True), (1, 128)) for k in (0, 1)
    ]
    misc = jnp.concatenate([head_x[:, main:]] + sums + [jnp.zeros((1, main - 384), F32)], axis=1)
    bias = jnp.sum(accq[...].T, axis=0, keepdims=True)
    small_ref[0:4] = jnp.concatenate([bias, head_x[:, :main], head_h, misc], axis=0)
    small_ref[4:] = jnp.zeros_like(small_ref[4:])


def network(
    x0, labels, cross_weight, tower_in, tower_out, cross_bias, in_bias, out_bias, head, head_bias, edim, pairs
):
    layers, width = cross_weight.shape[:2]
    main = tower_out.shape[0]
    count = x0.shape[1]
    block = 512
    tall = main + 16
    vmem = pl.BlockSpec(memory_space=pltpu.VMEM)
    hbm = pl.BlockSpec(memory_space=pl.ANY)
    return pl.pallas_call(
        functools.partial(network_kernel, width, edim),
        out_shape=[
            jax.ShapeDtypeStruct((1, count), F32),
            jax.ShapeDtypeStruct((pairs, 80, count), BF),
            jax.ShapeDtypeStruct((width - 2 * pairs * edim, count), F32),
            jax.ShapeDtypeStruct((8, main), F32),
        ]
        + [jax.ShapeDtypeStruct((tall, count), BF)] * (layers - 1)
        + [jax.ShapeDtypeStruct((main + 128, count), BF)] * layers
        + [jax.ShapeDtypeStruct((main, count), BF)] * 3,
        in_specs=[hbm, vmem, hbm, hbm, hbm] + [vmem] * 4 + [pl.BlockSpec(memory_space=pltpu.SMEM)],
        out_specs=[vmem] * 4 + [pl.BlockSpec(memory_space=pl.ANY)] * (2 * layers + 2),
        scratch_shapes=[
            pltpu.VMEM(x0.shape, BF),
            pltpu.VMEM(cross_weight.shape, BF),
            pltpu.VMEM(tower_in.shape, BF),
            pltpu.VMEM(tower_out.shape, BF),
            pltpu.VMEM((layers - 1, tall, count), BF),
            pltpu.VMEM((layers, main + 128, block), BF),
            pltpu.VMEM((main, count), BF),
            pltpu.VMEM((main, block), BF),
            pltpu.VMEM((main, block), BF),
            pltpu.VMEM((layers, tall, block), BF),
            pltpu.VMEM((layers, tall, block), F32),
            pltpu.VMEM((main, block), F32),
            pltpu.VMEM((main, block), F32),
            pltpu.VMEM((tall, block), F32),
            pltpu.VMEM((main + 128, 128), F32),
            pltpu.VMEM((main, 128), F32),
            pltpu.VMEM((main, 128), F32),
            pltpu.VMEM((8, 128), F32),
            pltpu.VMEM((128, main + 128), F32),
            pltpu.VMEM((main + 128, 128), F32),
            pltpu.SemaphoreType.DMA((layers + 3,)),
            pltpu.SemaphoreType.DMA((count // block, 2 * layers + 2)),
        ],
        compiler_params=pltpu.CompilerParams(vmem_limit_bytes=63 * 2**20),
        name="network",
    )(x0, labels, cross_weight, tower_in, tower_out, cross_bias, in_bias, out_bias, head, head_bias)


def finish_kernel(
    examples, whole_ref, small_ref, rows_ref, pieces_ref, out_ref, table_ref, bias_ref, in_ref, in_bias_ref,
    out_bias_ref, out_piece_ref, head_ref, slope_ref, loss_ref, turned,
):
    layers, main = small_ref.shape[0] - 1, small_ref.shape[2]
    rest = out_ref.shape[2] - main
    width = main + rest
    layer = pl.program_id(0)
    edim = table_ref.shape[1]

    edge = small_ref[layer]
    out_ref[0, :main, :main] = whole_ref[0].astype(F32)
    out_ref[0, :main, main:] = edge.T[:, 4 : 4 + rest]
    out_ref[0, main:, :main] = edge[:rest]
    for r in range(rest):
        out_ref[0, main + r : main + r + 1, main:] = edge[7:8, 128 * r : 128 * r + rest]
    for f in range(table_ref.shape[0]):
        table_ref[f] = rows_ref[f // 2, 40 * (f % 2) : 40 * (f % 2) + 40].astype(F32)[:edim]

    @pl.when(layer == 0)
    def _():
        for k in range(layers):
            bias_ref[k : k + 1, :main] = small_ref[k, 3:4]
            bias_ref[k : k + 1, main:] = small_ref[k, 7:8, 384 : 384 + rest]
        last = small_ref[layers]
        turned[...] = last.T
        share = in_ref.shape[0]
        me = lax.axis_index("section") * lax.axis_size("dp") + lax.axis_index("dp")
        mine = turned[pl.ds(pl.multiple_of(me * share, share), share)]
        rolled = pltpu.roll(last, lax.rem(main - me * share, main), 1)
        in_bias_ref[...] = rolled[3:4, :share]
        out_bias_ref[...] = rolled[4:5, :share]
        in_ref[:, :main] = pieces_ref[0]
        in_ref[:, main:] = mine[:, :rest]
        out_piece_ref[...] = pieces_ref[1]
        head = jnp.concatenate([last[5:6], last[7:8, :rest], last[6:7]], axis=1)
        head_ref[...] = head.reshape(width + main)
        slope_ref[...] = last[7:8, 128:129]
        loss_ref[...] = last[7:8, 256:257] / examples


def finish(whole, small, rows, pieces, width, fields, edim, examples):
    layers, main = whole.shape[:2]
    share = pieces.shape[1]
    pairs, _, count = rows.shape
    parts = 3
    step = -(-pairs // parts)

    def all_of(*shape):
        return pl.BlockSpec(shape, lambda i: (0,) * len(shape))

    return pl.pallas_call(
        functools.partial(finish_kernel, examples),
        out_shape=[
            jax.ShapeDtypeStruct((layers, width, width), F32),
            jax.ShapeDtypeStruct((fields, edim, count), F32),
            jax.ShapeDtypeStruct((layers, width), F32),
            jax.ShapeDtypeStruct((share, width), F32),
            jax.ShapeDtypeStruct((1, share), F32),
            jax.ShapeDtypeStruct((1, share), F32),
            jax.ShapeDtypeStruct((share, main), F32),
            jax.ShapeDtypeStruct((width + main,), F32),
            jax.ShapeDtypeStruct((1, 1), F32),
            jax.ShapeDtypeStruct((1, 1), F32),
        ],
        grid=(layers,),
        in_specs=[
            pl.BlockSpec((1, main, main), lambda i: (i, 0, 0)),
            all_of(layers + 1, 8, main),
            pl.BlockSpec((step, 80, count), lambda i: (i, 0, 0)),
            all_of(2, share, main),
        ],
        out_specs=[
            pl.BlockSpec((1, width, width), lambda i: (i, 0, 0)),
            pl.BlockSpec((2 * step, edim, count), lambda i: (i, 0, 0)),
            all_of(layers, width),
            all_of(share, width),
            all_of(1, share),
            all_of(1, share),
            all_of(share, main),
            all_of(width + main),
            all_of(1, 1),
            all_of(1, 1),
        ],
        scratch_shapes=[pltpu.VMEM((main, 8), F32)],
        compiler_params=pltpu.CompilerParams(vmem_limit_bytes=63 * 2**20),
        name="finish",
    )(whole, small, rows, pieces)


def general_body(
    ids,
    dense,
    labels,
    table,
    cross_weight,
    cross_bias,
    tower_in,
    tower_in_bias,
    tower_out,
    tower_out_bias,
    head_weight,
    head_bias,
):
    groups = lax.axis_size("dp")
    sections = lax.axis_size("section")
    device_count = groups * sections
    examples, fields = ids.shape
    table_rows, edim = table.shape[1:]
    layers, width = cross_weight.shape[:2]
    hidden = tower_out.shape[0]
    capacity = examples // groups
    sparse = fields * edim
    me = lax.axis_index("section") * groups + lax.axis_index("dp")

    idt = ids.T
    owner = idt // table_rows
    local = idt % table_rows
    owner_hot = owner[:, None, :] == jnp.arange(groups, dtype=jnp.int32)[None, :, None]
    lane = jnp.arange(examples, dtype=jnp.int32)
    before = (lane[:, None] < lane[None, :]).astype(BF)
    counts = mm(owner_hot.reshape(fields * groups, examples).astype(BF), before, (1, 0))
    rank = jnp.sum(jnp.where(owner_hot, counts.reshape(fields, groups, examples), 0.0), axis=1)
    slot = owner * capacity + rank.astype(jnp.int32)
    slot_hot = (slot[:, None, :] == lane[None, :, None]).astype(BF)
    halves = jnp.stack([local // 32, local % 32], axis=1).astype(BF)
    sent = lax.dot_general(
        halves, slot_hot, (((2,), (2,)), ((0,), (0,))), preferred_element_type=F32
    )
    requests = (sent[:, 0] * 32 + sent[:, 1]).astype(jnp.int32)
    requests = requests.reshape(fields, groups, capacity).transpose(1, 0, 2)
    arrived = lax.all_to_all(requests, "dp", 0, 0, tiled=True)
    arrived = arrived.transpose(1, 0, 2).reshape(fields, examples)
    row_hot = (
        arrived[:, None, :] == jnp.arange(table_rows, dtype=jnp.int32)[None, :, None]
    ).astype(BF)
    table_t = table.transpose(0, 2, 1)
    found = lax.dot_general(
        table_t, row_hot, (((2,), (1,)), ((0,), (0,))), preferred_element_type=F32
    ).astype(BF)
    found = found.reshape(sparse, groups, capacity).transpose(1, 0, 2)
    replies = lax.all_to_all(found, "dp", 0, 0, tiled=True)
    replies = replies.transpose(1, 0, 2).reshape(fields, edim, examples)
    embedded = lax.dot_general(
        replies, slot_hot, (((2,), (1,)), ((0,), (0,))), preferred_element_type=F32
    ).astype(BF)
    x0 = jnp.concatenate([embedded.reshape(sparse, examples), dense.T], axis=0)

    x0w = x0.astype(F32)
    xs, us = [x0], []
    for layer in range(layers):
        u = mm(cross_weight[layer], xs[-1], (0, 0)) + cross_bias[layer][:, None]
        us.append(u)
        xs.append((x0w * u + xs[-1].astype(F32)).astype(BF))
    p1 = mm(tower_in, x0, (0, 0)) + tower_in_bias[:, None]
    a1, d1 = gelu_parts(p1)
    h1 = a1.astype(BF)
    p2 = mm(tower_out, h1, (0, 0)) + tower_out_bias[:, None]
    h2, d2 = gelu_parts(p2)
    head_cross, head_tower = head_weight[:width], head_weight[width:]
    last = xs[-1].astype(F32)
    z = (
        jnp.sum(last * head_cross[:, None], axis=0)
        + jnp.sum(h2 * head_tower[:, None], axis=0)
        + head_bias[0]
    )
    probs = jax.nn.sigmoid(z)
    target = labels.astype(F32)
    loss = jnp.sum(jnp.logaddexp(0.0, z) - target * z)
    s = probs - target
    head_grad = jnp.concatenate([jnp.sum(s * last, axis=1), jnp.sum(s * h2, axis=1)])

    q2 = (s[None, :] * head_tower[:, None] * d2).astype(BF)
    tower_out_g = mm(q2, h1, (1, 1))
    q1 = (mm(tower_out, q2, (1, 0)) * d1).astype(BF)
    tower_in_g = mm(q1, x0, (1, 1))
    tower_biases = [jnp.sum(q1.astype(F32), axis=1), jnp.sum(q2.astype(F32), axis=1)]
    dx0 = mm(tower_in, q1, (1, 0))
    g = (s[None, :] * head_cross[:, None]).astype(BF)
    cross_g, cross_b = [None] * layers, [None] * layers
    for layer in reversed(range(layers)):
        gw = g.astype(F32)
        v = (gw * x0w).astype(BF)
        cross_g[layer] = mm(xs[layer], v, (1, 1))
        cross_b[layer] = jnp.sum(v.astype(F32), axis=1)
        dx0 = dx0 + gw * us[layer]
        g = gw + mm(cross_weight[layer], v, (1, 0))
        if layer:
            g = g.astype(BF)
    dx0 = dx0 + g

    packed = lax.dot_general(
        dx0[:sparse].astype(BF).reshape(fields, edim, examples),
        slot_hot,
        (((2,), (2,)), ((0,), (0,))),
        preferred_element_type=F32,
    ).astype(BF)
    packed = packed.reshape(sparse, groups, capacity).transpose(1, 0, 2)
    delivered = lax.all_to_all(packed, "dp", 0, 0, tiled=True)
    delivered = delivered.transpose(1, 0, 2).reshape(fields, edim, examples)
    table_g = lax.dot_general(
        delivered, row_hot, (((2,), (2,)), ((0,), (0,))), preferred_element_type=F32
    )
    table_g = lax.psum(table_g, "section").transpose(0, 2, 1)

    small = jnp.concatenate(
        cross_b + [head_grad, jnp.sum(s).reshape(1), loss.reshape(1)] + tower_biases
    )
    small = lax.psum(small, ("section", "dp"))
    sizes = [layers * width, width + hidden, 1, 1, hidden, hidden]
    ends = [sum(sizes[: i + 1]) for i in range(len(sizes))]
    pieces = [small[e - n : e] for e, n in zip(ends, sizes)]
    cross_b_out = pieces[0].reshape(layers, width)
    share = hidden // device_count
    bias_in, bias_out = (lax.dynamic_slice(p, (me * share,), (share,)) for p in pieces[4:])
    cross_out = lax.psum(jnp.stack(cross_g), ("section", "dp"))
    tower_in_out = lax.psum_scatter(
        tower_in_g, ("section", "dp"), scatter_dimension=0, tiled=True
    )
    tower_out_out = lax.psum_scatter(
        tower_out_g, ("section", "dp"), scatter_dimension=0, tiled=True
    )
    return (
        probs,
        pieces[3] / (examples * device_count),
        dx0[sparse:].T,
        table_g,
        cross_out,
        cross_b_out,
        tower_in_out.T,
        bias_in,
        tower_out_out.T,
        bias_out,
        pieces[1],
        pieces[2],
    )


def body(
    ids,
    dense,
    labels,
    table,
    cross_weight,
    cross_bias,
    tower_in,
    tower_in_bias,
    tower_out,
    tower_out_bias,
    head_weight,
    head_bias,
):
    groups = lax.axis_size("dp")
    sections = lax.axis_size("section")
    device_count = groups * sections
    examples, fields = ids.shape
    table_rows, edim = table.shape[1:]
    layers, width = cross_weight.shape[:2]
    hidden = tower_out.shape[0]
    capacity = examples // groups
    me = lax.axis_index("section") * groups + lax.axis_index("dp")
    idt = ids.T
    table_t = table.transpose(0, 2, 1)
    here = (sections, groups, capacity, table_rows) == (4, 8, 128, 1024)
    if here:
        x0, arrived, source = look_up(idt, table_t, dense.T)
        probs, rows, dense_g, small, *kept = network(
            x0,
            labels.reshape(1, examples),
            cross_weight,
            tower_in,
            tower_out,
            cross_bias,
            tower_in_bias.reshape(1, hidden),
            tower_out_bias.reshape(1, hidden),
            head_weight,
            head_bias,
            edim,
            fields // 2,
        )
        xs, vs = [x0] + kept[: layers - 1], kept[layers - 1 : 2 * layers - 1]
        h1, q1, q2 = kept[2 * layers - 1 :]
        whole, pieces, table_sum, small = reduce_all(
            xs + [q1, q2], vs + [x0, h1], layers, rows, source, arrived, small
        )
        small = small.reshape(layers + 1, 8, hidden)
        cross_out, table_g, cross_b_out, in_out, in_b, out_b, out_out, head_out, slopes, loss = finish(
            whole, small, table_sum, pieces, width, fields, edim, examples * device_count
        )
        return (
            probs.reshape(examples),
            loss.reshape(1),
            dense_g.T,
            table_g.transpose(0, 2, 1),
            cross_out,
            cross_b_out,
            in_out.T,
            in_b.reshape(in_b.shape[1]),
            out_out.T,
            out_b.reshape(out_b.shape[1]),
            head_out,
            slopes.reshape(1),
        )
    return general_body(
        ids, dense, labels, table, cross_weight, cross_bias, tower_in, tower_in_bias, tower_out,
        tower_out_bias, head_weight, head_bias,
    )


def solution(mesh):
    both = ("section", "dp")
    return jax.shard_map(
        body,
        mesh=mesh,
        in_specs=(P(both, None), P(both, None), P(both), P(None, "dp", None)) + (P(),) * 8,
        out_specs=(
            P(both),
            P(),
            P(both, None),
            P(None, "dp", None),
            P(),
            P(),
            P(None, both),
            P(both),
            P(None, both),
            P(both),
            P(),
            P(),
        ),
        check_vma=False,
    )
```

```python
import functools
import math

import jax
import jax.numpy as jnp
from jax import lax
from jax.experimental import pallas as pl
from jax.experimental.pallas import tpu as pltpu
from jax.sharding import PartitionSpec as P

BF = jnp.bfloat16
F32 = jnp.float32


def mm(left, right, contract):
    return lax.dot_general(
        left, right, ((contract[:1], contract[1:]), ((), ())), preferred_element_type=F32
    )


def gelu_parts(pre):
    act, back = jax.vjp(jax.nn.gelu, pre)
    return act, back(jnp.ones_like(pre))[0]


ORDER = [
    "P4 C1 C2 u11",
    "C0 u12 S4 u21",
    "P5 T14 u10 C4",
    "u31 C3 u22 P3",
    "T24 u14 u41 S5",
    "u20 n0 u51 u32",
    "u13 T15 P2 u61",
    "S3 T25 u42 T13",
    "u30 n1 u24 P1",
    "u71 u52 T23 S2",
    "n2 T12 u62 u23",
    "u34 u40 u81 S1",
    "u72 u50 T11 T35",
    "u33 P0 T22 T33",
    "T21 u60 u82 S0",
    "T45 u70 T32 u43",
    "T34 T31 u92 n3",
    "T10 u44 u80 u53",
    "n4 u91 n5 T20",
    "T43 T41 u90 ua1",
    "T42 T30 u54 T44",
    "ua0 T40 ua2 n6",
]
PARTS = 6
VIEW = (2, 2, 2, 2, 2)


def one_hot(places, count):
    rows = lax.broadcasted_iota(jnp.int32, (count, places.shape[1]), 0)
    return (rows == places).astype(F32).astype(BF)


def pick(slab, places):
    low, block = places & 255, lax.shift_right_logical(places, 8)
    blocks = [slab[:, 256 * b : 256 * b + 256] for b in range(4)]
    rows = slab.shape[0]
    every = jnp.dot(
        jnp.concatenate(blocks, axis=0), one_hot(low, 256), preferred_element_type=F32
    )
    chosen = every[:rows]
    for b in range(1, 4):
        chosen = jnp.where(block == b, every[rows * b : rows * b + rows], chosen)
    return chosen


def add_up(slab, places):
    low, block = places & 255, lax.shift_right_logical(places, 8)
    rows = slab.shape[0]
    masked = [slab * (block == b).astype(F32).astype(BF) for b in range(4)]
    every = lax.dot_general(
        jnp.concatenate(masked, axis=0),
        one_hot(low, 256),
        (((1,), (1,)), ((), ())),
        preferred_element_type=F32,
    )
    return jnp.concatenate([every[rows * b : rows * b + rows] for b in range(4)], axis=1)


def reduce_kernel(units, gathered, *refs):
    lefts, rights = refs[:units], refs[units : 2 * units]
    rows_hbm, inv_ref, arr_ref, part_ref = refs[2 * units : 2 * units + 4]
    whole_out, pieces, table_hbm, small_out = refs[2 * units + 4 : 2 * units + 8]
    (
        rows_ref, rows_in, whole, table_out, leave, grads, left, right, load, small, rc, sa1, ra1, sb1, rb1, sa2, ra2, sb2, rb2, sz, rz, sf, rf, packed, back, summed,
        stc, rtc, st, rt, sm, rm, send, recv, row_send, row_recv, table_send, table_recv,
    ) = refs[2 * units + 8 :]
    pairs, count = rows_hbm.shape[0], rows_hbm.shape[2]
    section, dp = lax.axis_index("section"), lax.axis_index("dp")
    y, c = section // 2, section % 2
    z, x = dp // 2, dp % 2
    zh, zl = z // 2, z % 2
    core_peer = (y * 2 + 1 - c, dp)
    y_peer = ((1 - y) * 2 + c, dp)
    x_peer = (section, z * 2 + 1 - x)
    half = 512
    lo, hi = pl.ds(0, half), pl.ds(half, half)

    near_peer = (section, zh * 4 + (1 - zl) * 2 + x)
    far_peer = (section, (1 - zh) * 4 + zl * 2 + x)

    def dp_peer(j):
        return (section, lax.rem(dp + j, 8))

    peers = [core_peer, y_peer] + [dp_peer(j) for j in range(1, 8)]
    barrier = pltpu.get_barrier_semaphore()
    for peer in peers:
        pl.semaphore_signal(barrier, inc=1, device_id=peer, device_id_type=pl.DeviceIdType.MESH)

    flying, entered, loaded = [], [], []

    def enter():
        if not entered:
            pl.semaphore_wait(barrier, len(peers))
            entered.append(True)

    def start(src, dst, m, k, peer, sems=(send, recv)):
        enter()
        copy = pltpu.make_async_remote_copy(
            src_ref=src,
            dst_ref=dst,
            send_sem=sems[0].at[m, k],
            recv_sem=sems[1].at[m, k],
            device_id=peer,
            device_id_type=pl.DeviceIdType.MESH,
        )
        copy.start()
        flying.append(copy)
        return copy

    def wide(value):
        return value.astype(F32)

    copies = {}
    gone = []

    def leave_with(src, dst, k):
        copy = pltpu.make_async_copy(src, dst, leave.at[k])
        copy.start()
        gone.append(copy)

    def acc(m, stage, cols, yy, hh, ll, xx):
        zz = 2 * hh + ll
        total = wide(grads[m, yy, c, hh, ll, xx, :, cols]) + wide(rc[m, yy, hh, ll, xx, :, cols])
        if cols is lo:
            if stage >= 2:
                total += wide(ra1[m, yy, zz])
            if stage >= 3:
                total += wide(ra2[m, zz])
        else:
            if stage >= 2:
                total += wide(rb1[m, zz, xx])
            if stage >= 3:
                total += wide(rb2[m, zz])
        return total

    tokens = " ".join(ORDER).split()
    made = [int(t[1]) for t in tokens if t[0] == "C"]

    def height(m):
        return min(lefts[m].shape[0], left.shape[1])

    def loads(turn):
        m, slot = made[turn], turn % 2
        return [
            pltpu.make_async_copy(ref.at[:rows], buf.at[slot, :rows], load.at[slot, k])
            for k, (ref, buf, rows) in enumerate(
                ((lefts[m], left, height(m)), (rights[m], right, rights[m].shape[0]))
            )
        ]

    def make(m):
        turn = made.index(m)
        slot = turn % 2
        for copy in loads(turn):
            copy.wait()
        tall = height(m) - 1024
        across = rights[m].shape[0]
        for r in range(2):
            total = lax.dot_general(
                left[slot, 512 * r : 512 * r + 512 + r * tall],
                right[slot, :across],
                (((1,), (1,)), ((), ())),
                preferred_element_type=F32,
            )
            grads[m, r] = total[:512, :1024].astype(BF).reshape(2, 2, 2, 2, 32, 1024)
            if across > 1024:
                side = total[:512, 1024:].T
                group, at = m // 2, m % 2 * 8
                if tall:
                    small[group, at + 4 : at + 7, 512 * r : 512 * r + 512] = side[0:3]
                else:
                    small[group, at : at + 4, 512 * r : 512 * r + 512] = side[0:4]
                if tall and r:
                    small[group, at : at + 4] = total[512:516, :1024]
                    small[group, at + 7 : at + 8, 512:] = jnp.zeros((1, 512), F32)
                    for k in range(4):
                        small[group, at + 7 : at + 8, 128 * k : 128 * k + 128] = total[
                            512 + k : 513 + k, 1024:
                        ]
        if turn + 2 < units:
            for copy in loads(turn + 2):
                copy.start()

    def step0(m):
        make(m)
        copies[m, 0] = start(grads.at[m, :, 1 - c], rc.at[m], m, 0, core_peer)

    def step1(m):
        copies[m, 0].wait_recv()

        @pl.loop(0, 2)
        def _(hh):
            for ll in range(2):
                for i in range(2):
                    sa1[m, i, 2 * hh + ll] = acc(m, 1, lo, i, hh, ll, 1 - x).astype(BF)
                    sb1[m, 2 * hh + ll, i] = acc(m, 1, hi, 1 - y, hh, ll, i).astype(BF)

        copies[m, 1] = start(sa1.at[m], ra1.at[m], m, 1, x_peer)
        copies[m, 2] = start(sb1.at[m], rb1.at[m], m, 2, y_peer)

    def step2(m):
        copies[m, 1].wait_recv()
        copies[m, 2].wait_recv()

        @pl.loop(0, 2)
        def _(hh):
            for ll in range(2):
                sa2[m, 2 * hh + ll] = acc(m, 2, lo, 1 - y, hh, ll, x).astype(BF)
                sb2[m, 2 * hh + ll] = acc(m, 2, hi, y, hh, ll, 1 - x).astype(BF)

        copies[m, 3] = start(sa2.at[m], ra2.at[m], m, 3, y_peer)
        copies[m, 4] = start(sb2.at[m], rb2.at[m], m, 4, x_peer)

    def step3(m):
        copies[m, 3].wait_recv()
        copies[m, 4].wait_recv()
        for hh in range(2):
            for cols in (lo, hi):
                sz[m, hh, :, cols] = acc(m, 3, cols, y, hh, 1 - zl, x).astype(BF)
        copies[m, 5] = start(sz.at[m], rz.at[m], m, 5, near_peer)

    def step4(m):
        copies[m, 5].wait_recv()
        for cols in (lo, hi):
            total = acc(m, 3, cols, y, 1 - zh, zl, x) + wide(rz[m, 1 - zh, :, cols])
            sf[m, :, cols] = total.astype(BF)
        copies[m, 6] = start(sf.at[m], rf.at[m], m, 6, far_peer)

    def step5(m):
        copies[m, 6].wait_recv()
        for cols in (lo, hi):
            total = acc(m, 3, cols, y, zh, zl, x) + wide(rz[m, zh, :, cols]) + wide(rf[m, :, cols])
            if m < gathered:
                whole[m, y, c, zh, zl, x, :, cols] = total.astype(BF)
            else:
                pieces[m - gathered, :, cols] = total
        if m < gathered:
            ours = whole.at[m, y, c, zh, zl, x]
            copies[m, 7] = start(ours, ours, m, 7, far_peer)

    def step6(m):
        copies[m, 7].wait_recv()
        ours = whole.at[m, y, c, :, zl, x]
        copies[m, 8] = start(ours, ours, m, 8, near_peer)

    def step7(m):
        copies[m, 8].wait_recv()
        ours = whole.at[m, y, c, :, :, x, :, lo]
        copies[m, 11] = start(ours, ours, m, 11, y_peer)
        ours = whole.at[m, y, c, :, :, x, :, hi]
        copies[m, 12] = start(ours, ours, m, 12, x_peer)

    def step8(m):
        copies[m, 11].wait_recv()
        copies[m, 12].wait_recv()
        ours = whole.at[m, :, c, :, :, x, :, lo]
        copies[m, 13] = start(ours, ours, m, 13, x_peer)
        ours = whole.at[m, y, c, :, :, :, :, hi]
        copies[m, 14] = start(ours, ours, m, 14, y_peer)

    def step9(m):
        copies[m, 13].wait_recv()
        copies[m, 14].wait_recv()
        ours = whole.at[m, :, c]
        copies[m, 15] = start(ours, ours, m, 15, core_peer)

    def step10(m):
        copies[m, 15].wait_recv()
        leave_with(whole.at[m], whole_out.at[m], m)

    def lanes(place, size):
        return pl.ds(pl.multiple_of(place * size, size), size)

    cuts = [pairs * q // PARTS for q in range(PARTS + 1)]

    def row_copy(q, j):
        part = pl.ds(cuts[q], cuts[q + 1] - cuts[q])
        return pltpu.make_async_remote_copy(
            src_ref=packed.at[part, :, lanes(lax.rem(dp + j, 8), 128)],
            dst_ref=back.at[part, :, lanes(dp, 128)],
            send_sem=row_send.at[q, j],
            recv_sem=row_recv.at[q, j],
            device_id=dp_peer(j),
            device_id_type=pl.DeviceIdType.MESH,
        )

    rows_copy = pltpu.make_async_copy(rows_hbm, rows_ref, rows_in)

    def pack(q):
        if not loaded:
            rows_copy.wait()
            loaded.append(True)

        @pl.loop(cuts[q], cuts[q + 1])
        def _(i):
            first = pick(rows_ref[i, 0:48], inv_ref[pl.ds(2 * i, 1)])
            second = pick(rows_ref[i, 32:80], inv_ref[pl.ds(2 * i + 1, 1)])
            packed[i] = jnp.concatenate([first[0:40], second[8:48]], axis=0).astype(BF)
            back[i, :, lanes(dp, 128)] = packed[i, :, lanes(dp, 128)]

        enter()
        for j in range(1, 8):
            row_copy(q, j).start()

    def scatter(q):
        for j in range(1, 8):
            row_copy(q, j).wait_recv()

        @pl.loop(cuts[q], cuts[q + 1])
        def _(i):
            for h, (low, at) in enumerate(((0, 0), (32, 8))):
                total = add_up(back[i, low : low + 48], arr_ref[pl.ds(2 * i + h, 1)])
                summed[i, 40 * h : 40 * h + 40] = total[at : at + 40]
            stc[i] = summed[i, :, lanes(1 - c, half)].astype(BF)

        part = pl.ds(cuts[q], cuts[q + 1] - cuts[q])
        copies["t", q, 0] = start(stc.at[part], rtc.at[part], q, 0, core_peer, (table_send, table_recv))

    quarter = half // 2

    def quarter_of(yy):
        return lanes(2 * c + yy, quarter)

    def table1(q):
        copies["t", q, 0].wait_recv()

        @pl.loop(cuts[q], cuts[q + 1])
        def _(i):
            st[i] = (summed[i, :, quarter_of(1 - y)] + wide(rtc[i, :, lanes(1 - y, quarter)])).astype(BF)

        part = pl.ds(cuts[q], cuts[q + 1] - cuts[q])
        copies["t", q, 1] = start(st.at[part], rt.at[part], q, 1, y_peer, (table_send, table_recv))

    def table2(q):
        copies["t", q, 1].wait_recv()

        @pl.loop(cuts[q], cuts[q + 1])
        def _(i):
            total = summed[i, :, quarter_of(y)] + wide(rtc[i, :, lanes(y, quarter)]) + wide(rt[i])
            table_out[i, :, quarter_of(y)] = total.astype(BF)

        part = pl.ds(cuts[q], cuts[q + 1] - cuts[q])
        ours = table_out.at[part, :, quarter_of(y)]
        copies["t", q, 2] = start(ours, ours, q, 2, y_peer, (table_send, table_recv))

    def table3(q):
        copies["t", q, 2].wait_recv()
        part = pl.ds(cuts[q], cuts[q + 1] - cuts[q])
        ours = table_out.at[part, :, lanes(c, half)]
        copies["t", q, 3] = start(ours, ours, q, 3, core_peer, (table_send, table_recv))

    def table4(q):
        copies["t", q, 3].wait_recv()
        part = pl.ds(cuts[q], cuts[q + 1] - cuts[q])
        leave_with(table_out.at[part], table_hbm.at[part], gathered + q)

    s = units

    def small0():
        small[1, 12:16] = part_ref[0:4]
        copies[s, 0] = start(small.at[1 - c], rm.at[0], s, 0, core_peer)

    def small1():
        copies[s, 0].wait_recv()
        sm[0] = small[c] + rm[0]
        copies[s, 1] = start(sm.at[0], rm.at[1], s, 1, x_peer)

    def small2():
        copies[s, 1].wait_recv()
        sm[1] = sm[0] + rm[1]
        copies[s, 2] = start(sm.at[1], rm.at[2], s, 2, y_peer)

    def small3():
        copies[s, 2].wait_recv()
        sm[2] = sm[1] + rm[2]
        copies[s, 3] = start(sm.at[2], rm.at[3], s, 3, near_peer)

    def small4():
        copies[s, 3].wait_recv()
        sm[3] = sm[2] + rm[3]
        copies[s, 4] = start(sm.at[3], rm.at[4], s, 4, far_peer)

    def small5():
        copies[s, 4].wait_recv()
        small_out[c] = sm[3] + rm[4]
        ours = small_out.at[c]
        copies[s, 6] = start(ours, ours, s, 6, core_peer)

    def small6():
        copies[s, 6].wait_recv()

    steps = [step1, step2, step3, step4, step5, step6, step7, step8, step9, step10]
    smalls = [small0, small1, small2, small3, small4, small5, small6]
    tables = [table1, table2, table3, table4]
    rows_copy.start()
    for copy in loads(0) + loads(1):
        copy.start()
    for token in tokens:
        kind, numbers = token[0], [int(n, 16) for n in token[1:]]
        if kind == "C":
            step0(*numbers)
        elif kind == "P":
            pack(*numbers)
        elif kind == "S":
            scatter(*numbers)
        elif kind == "n":
            smalls[numbers[0]]()
        else:
            {"u": steps, "T": tables}[kind][numbers[0] - 1](numbers[1])
    for copy in flying:
        copy.wait_send()
    for copy in gone:
        copy.wait()

    for q in range(PARTS):
        for j in range(1, 8):
            row_copy(q, j).wait_send()


def reduce_all(lefts, rights, gathered, rows, source, arrived, small):
    units = len(lefts)
    pairs, _, count = rows.shape
    piece = (32, 1024)
    vmem = pl.BlockSpec(memory_space=pltpu.VMEM)
    hbm = pl.BlockSpec(memory_space=pl.ANY)
    whole, pieces, table_sum, small_sum = pl.pallas_call(
        lambda *refs: reduce_kernel(units, gathered, *refs),
        out_shape=[
            jax.ShapeDtypeStruct((gathered,) + VIEW + piece, BF),
            jax.ShapeDtypeStruct((units - gathered,) + piece, F32),
            jax.ShapeDtypeStruct((pairs, 80, count), BF),
            jax.ShapeDtypeStruct((2, 16, 1024), F32),
        ],
        in_specs=[hbm] * (2 * units + 1) + [vmem] * 3,
        out_specs=[hbm, vmem, hbm, vmem],
        scratch_shapes=[
            pltpu.VMEM((pairs, 80, count), BF),
            pltpu.SemaphoreType.DMA,
            pltpu.VMEM((gathered,) + VIEW + piece, BF),
            pltpu.VMEM((pairs, 80, count), BF),
            pltpu.SemaphoreType.DMA((gathered + PARTS,)),
            pltpu.VMEM((units,) + VIEW + piece, BF),
            pltpu.VMEM((2, 1040, count), BF),
            pltpu.VMEM((2, 1152, count), BF),
            pltpu.SemaphoreType.DMA((2, 2)),
            pltpu.VMEM((2, 16, 1024), F32),
            pltpu.VMEM((units, 2, 2, 2, 2) + piece, BF),
            pltpu.VMEM((units, 2, 4, 32, 512), BF),
            pltpu.VMEM((units, 2, 4, 32, 512), BF),
            pltpu.VMEM((units, 4, 2, 32, 512), BF),
            pltpu.VMEM((units, 4, 2, 32, 512), BF),
            pltpu.VMEM((units, 4, 32, 512), BF),
            pltpu.VMEM((units, 4, 32, 512), BF),
            pltpu.VMEM((units, 4, 32, 512), BF),
            pltpu.VMEM((units, 4, 32, 512), BF),
            pltpu.VMEM((units, 2) + piece, BF),
            pltpu.VMEM((units, 2) + piece, BF),
            pltpu.VMEM((units,) + piece, BF),
            pltpu.VMEM((units,) + piece, BF),
            pltpu.VMEM((pairs, 80, count), BF),
            pltpu.VMEM((pairs, 80, count), BF),
            pltpu.VMEM((pairs, 80, count), F32),
            pltpu.VMEM((pairs, 80, count // 2), BF),
            pltpu.VMEM((pairs, 80, count // 2), BF),
            pltpu.VMEM((pairs, 80, count // 4), BF),
            pltpu.VMEM((pairs, 80, count // 4), BF),
            pltpu.VMEM((4, 16, 1024), F32),
            pltpu.VMEM((5, 16, 1024), F32),
            pltpu.SemaphoreType.DMA((units + 1, 16)),
            pltpu.SemaphoreType.DMA((units + 1, 16)),
            pltpu.SemaphoreType.DMA((PARTS, 8)),
            pltpu.SemaphoreType.DMA((PARTS, 8)),
            pltpu.SemaphoreType.DMA((PARTS, 4)),
            pltpu.SemaphoreType.DMA((PARTS, 4)),
        ],
        compiler_params=pltpu.CompilerParams(
            collective_id=0, has_side_effects=True, vmem_limit_bytes=63 * 2**20
        ),
        name="reduce_all",
    )(
        *lefts,
        *rights,
        rows,
        source,
        arrived,
        small,
    )
    return whole.reshape(gathered, 1024, 1024), pieces, table_sum, small_sum.reshape(-1)


def lookup_kernel(
    fields, edim, ids_ref, table_hbm, dense_ref, x0_ref, arr_ref, inv_ref,
    table_ref, table_in, ids, slots, req, found, rep, held, pair, wide_rows, x0f, far, arr_far,
    id_send, id_recv, send, recv, far_send, far_recv, far_id_send, far_id_recv, half_send, half_recv,
):
    section, me = lax.axis_index("section"), lax.axis_index("dp")
    direct = fields // 2 - far.shape[0] // 2
    half, spot = me // 4, lax.rem(me, 4)
    twin = lax.rem(me + 4, 8)
    y, core = section // 2, lax.rem(section, 2)
    core_peer = (y * 2 + 1 - core, me)
    y_peer = ((1 - y) * 2 + core, me)
    dot = functools.partial(jnp.dot, preferred_element_type=F32)
    count = ids.shape[1]

    table_copy = pltpu.make_async_copy(table_hbm, table_ref, table_in)
    table_copy.start()

    def peer(j):
        return lax.rem(me + j, 8)

    def near(j):
        return lax.rem(spot + j, 4)

    def lanes(place, size=128):
        return pl.ds(pl.multiple_of(place * size, size), size)

    barrier = pltpu.get_barrier_semaphore()
    for j in range(1, 8):
        pl.semaphore_signal(
            barrier, inc=1, device_id=(section, peer(j)), device_id_type=pl.DeviceIdType.MESH
        )
    for other in (core_peer, y_peer):
        pl.semaphore_signal(barrier, inc=1, device_id=other, device_id_type=pl.DeviceIdType.MESH)

    def far_copy(k):
        quarter = section if k < 3 else (1 - y) * 2 + core
        window = far.at[:, :, lanes(quarter, count // 4)]
        return pltpu.make_async_remote_copy(
            src_ref=window if k else table_ref.at[2 * direct :, :, lanes(quarter, count // 4)],
            dst_ref=window,
            send_sem=far_send.at[k],
            recv_sem=far_recv.at[k],
            device_id=((section, twin), core_peer, y_peer, core_peer)[k],
            device_id_type=pl.DeviceIdType.MESH,
        )

    ids[...] = jnp.zeros_like(ids)
    ids[:fields] = ids_ref[...]
    every = ids[...]
    owner = lax.shift_right_logical(every, 10)
    hot = jnp.concatenate([(owner == o).astype(F32) for o in range(8)], axis=0).astype(BF)
    before = (
        lax.broadcasted_iota(jnp.int32, (count, count), 0)
        < lax.broadcasted_iota(jnp.int32, (count, count), 1)
    )
    ranks = dot(hot, before.astype(F32).astype(BF))
    rank = jnp.zeros((32, count), F32)
    for o in range(8):
        rank = jnp.where(owner == o, ranks[32 * o : 32 * o + 32], rank)
    slots[...] = owner * 128 + rank.astype(jnp.int32)
    pl.semaphore_wait(barrier, 9)
    table_copy.wait()
    far_copy(0).start()
    ids[...] = every & 1023
    def id_copy(group, j):
        eight = pl.ds(pl.multiple_of(8 * group, 8), 8)
        return pltpu.make_async_remote_copy(
            src_ref=req.at[eight, lanes(peer(j))],
            dst_ref=arr_ref.at[eight, lanes(me)],
            send_sem=id_send.at[group, j],
            recv_sem=id_recv.at[group, j],
            device_id=(section, peer(j)),
            device_id_type=pl.DeviceIdType.MESH,
        )

    def far_id_copy(group, j):
        eight = pl.ds(pl.multiple_of(8 * group, 8), 8)
        return pltpu.make_async_remote_copy(
            src_ref=req.at[eight, lanes(4 * (1 - half) + near(j))],
            dst_ref=arr_far.at[eight, lanes(spot)],
            send_sem=far_id_send.at[group, j],
            recv_sem=far_id_recv.at[group, j],
            device_id=(section, 4 * half + near(j)),
            device_id_type=pl.DeviceIdType.MESH,
        )

    @pl.loop(0, 4)
    def _(group):
        eight = pl.ds(pl.multiple_of(8 * group, 8), 8)
        slot8, local8 = slots[eight], ids[eight]
        place = lax.broadcasted_iota(jnp.int32, (1, count), 1)
        column = lax.broadcasted_iota(jnp.int32, (8, count), 0)
        wanted, source = [], []
        for k in range(8):
            slot, local = slot8[k : k + 1], local8[k : k + 1]
            owners = column == lax.shift_right_logical(slot, 7)
            parts = [local >> 5, local & 31, place >> 5, place & 31]
            left = jnp.concatenate(
                [jnp.where(owners, p.astype(F32), 0.0) for p in parts], axis=0
            ).astype(BF)
            right = one_hot(slot & 127, 128)
            sent = lax.dot_general(
                left, right, (((1,), (1,)), ((), ())), preferred_element_type=F32
            )
            rows = [
                (sent[n : n + 8] * 32 + sent[n + 8 : n + 16]).astype(jnp.int32) for n in (0, 16)
            ]
            for taken, r in zip((wanted, source), rows):
                taken.append(jnp.concatenate([r[o : o + 1] for o in range(8)], axis=1))
        req[eight] = jnp.concatenate(wanted, axis=0)
        inv_ref[eight] = jnp.concatenate(source, axis=0)
        for j in range(1, 8):
            id_copy(group, j).start()
        for j in range(1, 4):
            far_id_copy(group, j).start()
        arr_ref[eight, lanes(me)] = req[eight, lanes(me)]
        arr_far[eight, lanes(spot)] = req[eight, lanes(4 * (1 - half) + spot)]

    def ids_of(group):
        for j in range(1, 8):
            id_copy(group, j).wait_recv()


    def row_copy(i, j):
        return pltpu.make_async_remote_copy(
            src_ref=found.at[i, :, lanes(peer(j))],
            dst_ref=rep.at[i, :, lanes(me)],
            send_sem=send.at[i, j],
            recv_sem=recv.at[i, j],
            device_id=(section, peer(j)),
            device_id_type=pl.DeviceIdType.MESH,
        )

    pair[...] = jnp.zeros_like(pair)
    held[...] = jnp.zeros_like(held)

    def half_copy(i, j, far_side):
        owner_place = 4 * (1 - half) + spot if far_side else me
        return pltpu.make_async_remote_copy(
            src_ref=found.at[i, :, lanes(4 * far_side + near(j))],
            dst_ref=rep.at[i, :, lanes(owner_place)],
            send_sem=half_send.at[far_side, i - direct, j],
            recv_sem=half_recv.at[far_side, i - direct, j],
            device_id=(section, 4 * half + near(j)),
            device_id_type=pl.DeviceIdType.MESH,
        )

    assert direct % 4 == 0

    @pl.loop(0, direct)
    def _(i):
        @pl.when(lax.rem(i, 4) == 0)
        def _():
            ids_of(i // 4)

        for h in range(2):
            held[h, :edim] = table_ref[2 * i + h]
            chosen = pick(held[h], arr_ref[pl.ds(2 * i + h, 1)])
            pair[40 * h : 40 * h + edim] = chosen[:edim]
        found[i] = pair[...].astype(BF)
        for j in range(1, 8):
            row_copy(i, j).start()
        rep[i, :, lanes(me)] = found[i, :, lanes(me)]

    for group in range(direct // 4, 4):
        ids_of(group)

    @pl.loop(direct, fields // 2)
    def _(i):
        for h in range(2):
            held[h, :edim] = table_ref[2 * i + h]
            places = arr_ref[pl.ds(2 * i + h, 1), lanes(half, count // 2)]
            pair[40 * h : 40 * h + edim, : count // 2] = pick(held[h], places)[:edim]
        found[i, :, : count // 2] = pair[:, : count // 2].astype(BF)
        for j in range(1, 4):
            half_copy(i, j, 0).start()
        rep[i, :, lanes(me)] = found[i, :, lanes(spot)]

    far_copy(0).wait_recv()
    far_copy(2).start()
    far_copy(1).start()
    for group in range(4):
        for j in range(1, 4):
            far_id_copy(group, j).wait_recv()
    far_copy(2).wait_recv()
    far_copy(3).start()
    far_copy(1).wait_recv()
    far_copy(3).wait_recv()

    @pl.loop(direct, fields // 2)
    def _(i):
        for h in range(2):
            held[h, :edim] = far[2 * (i - direct) + h]
            places = arr_far[pl.ds(2 * i + h, 1)]
            pair[40 * h : 40 * h + edim, count // 2 :] = pick(held[h], places)[:edim]
        found[i, :, count // 2 :] = pair[:, count // 2 :].astype(BF)
        for j in range(1, 4):
            half_copy(i, j, 1).start()
        rep[i, :, lanes(4 * (1 - half) + spot)] = found[i, :, lanes(4 + spot)]

    def unpack(i):
        wide_rows[2 * i] = pick(rep[i, 0:48], slots[pl.ds(2 * i, 1)])[0:40]
        wide_rows[2 * i + 1] = pick(rep[i, 32:80], slots[pl.ds(2 * i + 1, 1)])[8:48]

    @pl.loop(0, direct)
    def _(i):
        for j in range(1, 8):
            row_copy(i, j).wait_recv()
        unpack(i)

    @pl.loop(direct, fields // 2)
    def _(i):
        for j in range(1, 4):
            half_copy(i, j, 0).wait_recv()
            half_copy(i, j, 1).wait_recv()
        unpack(i)

    sparse, extra = fields * edim, dense_ref.shape[0]
    x0f[sparse // 8 * 8 :] = jnp.zeros_like(x0f[sparse // 8 * 8 :])
    for f in range(fields):
        x0f[f * edim : f * edim + edim] = wide_rows[f, :edim]
    x0f[sparse : sparse + extra] = dense_ref[...].astype(F32)
    x0f[sparse + extra : sparse + extra + 1] = jnp.ones_like(x0f[:1])
    x0_ref[...] = x0f[...].astype(BF)

    @pl.loop(0, direct)
    def _(i):
        for j in range(1, 8):
            row_copy(i, j).wait_send()

    @pl.loop(direct, fields // 2)
    def _(i):
        for j in range(1, 4):
            half_copy(i, j, 0).wait_send()
            half_copy(i, j, 1).wait_send()

    for group in range(4):
        for j in range(1, 8):
            id_copy(group, j).wait_send()
        for j in range(1, 4):
            far_id_copy(group, j).wait_send()
    for n in range(4):
        far_copy(n).wait_send()


def look_up(ids_t, table_t, dense_t):
    fields, count = ids_t.shape
    edim = table_t.shape[1]
    tall = (fields * edim + dense_t.shape[0]) // 128 * 128 + 128
    mirrored = fields // 4 - 1
    vmem = pl.BlockSpec(memory_space=pltpu.VMEM)
    return pl.pallas_call(
        functools.partial(lookup_kernel, fields, edim),
        out_shape=[
            jax.ShapeDtypeStruct((tall, count), BF),
            jax.ShapeDtypeStruct((32, count), jnp.int32),
            jax.ShapeDtypeStruct((32, count), jnp.int32),
        ],
        in_specs=[vmem, pl.BlockSpec(memory_space=pl.ANY), vmem],
        out_specs=[vmem] * 3,
        scratch_shapes=[
            pltpu.VMEM(table_t.shape, BF),
            pltpu.SemaphoreType.DMA,
            pltpu.VMEM((32, count), jnp.int32),
            pltpu.VMEM((32, count), jnp.int32),
            pltpu.VMEM((32, count), jnp.int32),
            pltpu.VMEM((fields // 2, 80, count), BF),
            pltpu.VMEM((fields // 2, 80, count), BF),
            pltpu.VMEM((2, 48, count), BF),
            pltpu.VMEM((80, count), F32),
            pltpu.VMEM((fields, 40, count), F32),
            pltpu.VMEM((tall, count), F32),
            pltpu.VMEM((2 * mirrored, edim, count), BF),
            pltpu.VMEM((32, count // 2), jnp.int32),
            pltpu.SemaphoreType.DMA((4, 8)),
            pltpu.SemaphoreType.DMA((4, 8)),
            pltpu.SemaphoreType.DMA((fields // 2, 8)),
            pltpu.SemaphoreType.DMA((fields // 2, 8)),
            pltpu.SemaphoreType.DMA((4,)),
            pltpu.SemaphoreType.DMA((4,)),
            pltpu.SemaphoreType.DMA((4, 4)),
            pltpu.SemaphoreType.DMA((4, 4)),
            pltpu.SemaphoreType.DMA((2, mirrored, 4)),
            pltpu.SemaphoreType.DMA((2, mirrored, 4)),
        ],
        compiler_params=pltpu.CompilerParams(
            collective_id=1, has_side_effects=True, vmem_limit_bytes=63 * 2**20
        ),
        name="look_up",
    )(ids_t, table_t, dense_t)


def gelu_and_slope(pre):
    root = (2.0 / math.pi) ** 0.5
    square = pre * pre
    tanh = jnp.tanh(root * pre * (1.0 + 0.044715 * square))
    cdf = 0.5 + 0.5 * tanh
    bend = 0.5 * root * (1.0 - tanh * tanh) * (1.0 + 3 * 0.044715 * square)
    return pre * cdf, cdf + pre * bend


def network_kernel(
    width, edim, x0_hbm, labels_ref, weight_hbm, in_hbm, out_hbm, bias_ref, in_bias_ref, out_bias_ref, head_ref, hb_ref,
    probs_ref, rows_ref, dense_ref, small_ref, *rest,
):
    layers = weight_hbm.shape[0]
    kept = 2 * layers + 2
    outs = rest[:kept]
    (
        x0_ref, weight_ref, in_ref, out_ref, xs, vs, h1s, q1s, q2s, gs, us, d1s, d2s, dxs, accx, acch, accq, accs,
        lines, cols, enter, leave,
    ) = rest[kept:]
    main = in_hbm.shape[1]
    edge = slice(main, main + 16)
    count = x0_hbm.shape[1]
    block = us.shape[2]
    pairs = rows_ref.shape[0]

    entering = [
        pltpu.make_async_copy(src, dst, enter.at[k])
        for k, (src, dst) in enumerate(
            [(x0_hbm, x0_ref)]
            + [(weight_hbm.at[i], weight_ref.at[i]) for i in range(layers)]
            + [(in_hbm, in_ref), (out_hbm, out_ref)]
        )
    ]
    for copy in entering:
        copy.start()

    def leaving(k, n):
        at = pl.ds(pl.multiple_of(n * block, block), block)
        here = [xs.at[i, :, at] for i in range(layers - 1)] + [vs.at[i] for i in range(layers)]
        here += [h1s.at[:, at], q1s, q2s]
        return pltpu.make_async_copy(here[k], outs[k].at[:, at], leave.at[n, k])

    def dot(a, b, ca, cb):
        return lax.dot_general(a, b, (((ca,), (cb,)), ((), ())), preferred_element_type=F32)

    def fold(value):
        return functools.reduce(
            lambda a, b: a + b, [value[:, n : n + 128] for n in range(0, value.shape[1], 128)]
        )

    for layer in range(layers):
        vs[layer, main:] = jnp.zeros_like(vs[layer, main:])
    accx[...] = jnp.zeros_like(accx)
    acch[...] = jnp.zeros_like(acch)
    accq[...] = jnp.zeros_like(accq)
    accs[...] = jnp.zeros_like(accs)
    lines[...] = jnp.zeros_like(lines)
    lines[0:layers, :width] = bias_ref[...]
    lines[layers : layers + 1, :main] = in_bias_ref[...]
    lines[layers + 1 : layers + 2, :main] = out_bias_ref[...]
    head = head_ref[...].reshape(1, width + main)
    lines[layers + 2 : layers + 3, :width] = head[:, :width]
    lines[layers + 3 : layers + 4, :main] = head[:, width:]
    cols[...] = lines[...].T
    entering[0].wait()
    for layer in range(1, layers):
        xs[layer - 1, edge] = x0_ref[edge]

    blocks = count // block

    def one_block(n):
        at = slice(n * block, n * block + block)

        def before(*which):
            if n:
                for k in which:
                    leaving(k, n - 1).wait()

        def arrived(k):
            if n == 0:
                entering[k].wait()

        def complete(k):
            leaving(k, n).start()

        def x_of(layer):
            return x0_ref[:width, at] if layer == 0 else xs[layer - 1, :width, at]

        def col(k, size):
            return cols[:size, k : k + 1]

        for layer in range(layers):
            arrived(1 + layer)
            u = dot(weight_ref[layer], x_of(layer), 0, 0) + col(layer, width)
            us[layer, :width] = u
            x = (x_of(0).astype(F32) * u + x_of(layer).astype(F32)).astype(BF)
            if layer + 1 < layers:
                xs[layer, :width, at] = x
                complete(layer)
        last = x.astype(F32)
        arrived(layers + 1)
        h1, d1 = gelu_and_slope(dot(in_ref[...], x_of(0), 0, 0) + col(layers, main))
        d1s[...] = d1
        h1s[:, at] = h1.astype(BF)
        complete(2 * layers - 1)
        arrived(layers + 2)
        h2, d2 = gelu_and_slope(dot(out_ref[...], h1s[:, at], 0, 0) + col(layers + 1, main))
        d2s[...] = d2
        head_cross, head_tower = col(layers + 2, width), col(layers + 3, main)
        z = (
            jnp.sum(last * head_cross, axis=0, keepdims=True)
            + jnp.sum(h2 * head_tower, axis=0, keepdims=True)
            + hb_ref[0]
        )
        probs = jax.nn.sigmoid(z)
        target = labels_ref[:, at].astype(F32)
        probs_ref[:, at] = probs
        s = probs - target
        loss = jnp.maximum(z, 0.0) + jnp.log1p(jnp.exp(-jnp.abs(z))) - target * z
        accs[0:1] += fold(s)
        accs[1:2] += fold(loss)
        accx[:width] += fold(s * last)
        acch[...] += fold(s * h2)

        q2 = ((s * head_tower) * d2s[...]).astype(BF)
        before(2 * layers + 1)
        q2s[...] = q2
        complete(2 * layers + 1)
        acc = fold(q2.astype(F32))
        accq[...] += acc
        q1 = (dot(out_ref[...], q2, 1, 0) * d1s[...]).astype(BF)
        before(2 * layers)
        q1s[...] = q1
        complete(2 * layers)
        g = (s * head_cross).astype(BF)
        before(*range(layers - 1, 2 * layers - 1))
        for layer in reversed(range(layers)):
            gs[layer, :width] = g
            v = (g.astype(F32) * x_of(0).astype(F32)).astype(BF)
            vs[layer, :width] = v
            complete(layers - 1 + layer)
            g = g.astype(F32) + dot(weight_ref[layer], v, 1, 0)
            if layer:
                g = g.astype(BF)
        g += dot(in_ref[...], q1, 1, 0)
        for layer in range(layers):
            g += gs[layer, :width].astype(F32) * us[layer, :width]
        dxs[:width] = g
        for i in range(pairs):
            low = 2 * i * edim
            both = [dxs[low : low + 40], dxs[low + edim : low + edim + 40]]
            rows_ref[i, :, at] = jnp.concatenate(both, axis=0).astype(BF)
        dense_ref[:, at] = dxs[2 * pairs * edim : width]

    for n in range(blocks):
        one_block(n)
    for n in range(blocks):
        for k in range(kept):
            if n == blocks - 1 or k < layers - 1 or k == 2 * layers - 1:
                leaving(k, n).wait()

    head_x = jnp.sum(accx[...].T, axis=0, keepdims=True)
    head_h = jnp.sum(acch[...].T, axis=0, keepdims=True)
    sums = [
        jnp.broadcast_to(jnp.sum(accs[k : k + 1], axis=1, keepdims=True), (1, 128)) for k in (0, 1)
    ]
    misc = jnp.concatenate([head_x[:, main:]] + sums + [jnp.zeros((1, main - 384), F32)], axis=1)
    bias = jnp.sum(accq[...].T, axis=0, keepdims=True)
    small_ref[0:4] = jnp.concatenate([bias, head_x[:, :main], head_h, misc], axis=0)
    small_ref[4:] = jnp.zeros_like(small_ref[4:])


def network(
    x0, labels, cross_weight, tower_in, tower_out, cross_bias, in_bias, out_bias, head, head_bias, edim, pairs
):
    layers, width = cross_weight.shape[:2]
    main = tower_out.shape[0]
    count = x0.shape[1]
    block = 512
    tall = main + 16
    vmem = pl.BlockSpec(memory_space=pltpu.VMEM)
    hbm = pl.BlockSpec(memory_space=pl.ANY)
    return pl.pallas_call(
        functools.partial(network_kernel, width, edim),
        out_shape=[
            jax.ShapeDtypeStruct((1, count), F32),
            jax.ShapeDtypeStruct((pairs, 80, count), BF),
            jax.ShapeDtypeStruct((width - 2 * pairs * edim, count), F32),
            jax.ShapeDtypeStruct((8, main), F32),
        ]
        + [jax.ShapeDtypeStruct((tall, count), BF)] * (layers - 1)
        + [jax.ShapeDtypeStruct((main + 128, count), BF)] * layers
        + [jax.ShapeDtypeStruct((main, count), BF)] * 3,
        in_specs=[hbm, vmem, hbm, hbm, hbm] + [vmem] * 4 + [pl.BlockSpec(memory_space=pltpu.SMEM)],
        out_specs=[vmem] * 4 + [pl.BlockSpec(memory_space=pl.ANY)] * (2 * layers + 2),
        scratch_shapes=[
            pltpu.VMEM(x0.shape, BF),
            pltpu.VMEM(cross_weight.shape, BF),
            pltpu.VMEM(tower_in.shape, BF),
            pltpu.VMEM(tower_out.shape, BF),
            pltpu.VMEM((layers - 1, tall, count), BF),
            pltpu.VMEM((layers, main + 128, block), BF),
            pltpu.VMEM((main, count), BF),
            pltpu.VMEM((main, block), BF),
            pltpu.VMEM((main, block), BF),
            pltpu.VMEM((layers, tall, block), BF),
            pltpu.VMEM((layers, tall, block), F32),
            pltpu.VMEM((main, block), F32),
            pltpu.VMEM((main, block), F32),
            pltpu.VMEM((tall, block), F32),
            pltpu.VMEM((main + 128, 128), F32),
            pltpu.VMEM((main, 128), F32),
            pltpu.VMEM((main, 128), F32),
            pltpu.VMEM((8, 128), F32),
            pltpu.VMEM((128, main + 128), F32),
            pltpu.VMEM((main + 128, 128), F32),
            pltpu.SemaphoreType.DMA((layers + 3,)),
            pltpu.SemaphoreType.DMA((count // block, 2 * layers + 2)),
        ],
        compiler_params=pltpu.CompilerParams(vmem_limit_bytes=63 * 2**20),
        name="network",
    )(x0, labels, cross_weight, tower_in, tower_out, cross_bias, in_bias, out_bias, head, head_bias)


def finish_kernel(
    examples, whole_ref, small_ref, rows_ref, pieces_ref, out_ref, table_ref, bias_ref, in_ref, in_bias_ref,
    out_bias_ref, out_piece_ref, head_ref, slope_ref, loss_ref, turned,
):
    layers, main = small_ref.shape[0] - 1, small_ref.shape[2]
    rest = out_ref.shape[2] - main
    width = main + rest
    layer = pl.program_id(0)
    edim = table_ref.shape[1]

    edge = small_ref[layer]
    out_ref[0, :main, :main] = whole_ref[0].astype(F32)
    out_ref[0, :main, main:] = edge.T[:, 4 : 4 + rest]
    out_ref[0, main:, :main] = edge[:rest]
    for r in range(rest):
        out_ref[0, main + r : main + r + 1, main:] = edge[7:8, 128 * r : 128 * r + rest]
    for f in range(table_ref.shape[0]):
        table_ref[f] = rows_ref[f // 2, 40 * (f % 2) : 40 * (f % 2) + 40].astype(F32)[:edim]

    @pl.when(layer == 0)
    def _():
        for k in range(layers):
            bias_ref[k : k + 1, :main] = small_ref[k, 3:4]
            bias_ref[k : k + 1, main:] = small_ref[k, 7:8, 384 : 384 + rest]
        last = small_ref[layers]
        turned[...] = last.T
        share = in_ref.shape[0]
        me = lax.axis_index("section") * lax.axis_size("dp") + lax.axis_index("dp")
        mine = turned[pl.ds(pl.multiple_of(me * share, share), share)]
        rolled = pltpu.roll(last, lax.rem(main - me * share, main), 1)
        in_bias_ref[...] = rolled[3:4, :share]
        out_bias_ref[...] = rolled[4:5, :share]
        in_ref[:, :main] = pieces_ref[0]
        in_ref[:, main:] = mine[:, :rest]
        out_piece_ref[...] = pieces_ref[1]
        head = jnp.concatenate([last[5:6], last[7:8, :rest], last[6:7]], axis=1)
        head_ref[...] = head.reshape(width + main)
        slope_ref[...] = last[7:8, 128:129]
        loss_ref[...] = last[7:8, 256:257] / examples


def finish(whole, small, rows, pieces, width, fields, edim, examples):
    layers, main = whole.shape[:2]
    share = pieces.shape[1]
    pairs, _, count = rows.shape
    parts = 3
    step = -(-pairs // parts)

    def all_of(*shape):
        return pl.BlockSpec(shape, lambda i: (0,) * len(shape))

    return pl.pallas_call(
        functools.partial(finish_kernel, examples),
        out_shape=[
            jax.ShapeDtypeStruct((layers, width, width), F32),
            jax.ShapeDtypeStruct((fields, edim, count), F32),
            jax.ShapeDtypeStruct((layers, width), F32),
            jax.ShapeDtypeStruct((share, width), F32),
            jax.ShapeDtypeStruct((1, share), F32),
            jax.ShapeDtypeStruct((1, share), F32),
            jax.ShapeDtypeStruct((share, main), F32),
            jax.ShapeDtypeStruct((width + main,), F32),
            jax.ShapeDtypeStruct((1, 1), F32),
            jax.ShapeDtypeStruct((1, 1), F32),
        ],
        grid=(layers,),
        in_specs=[
            pl.BlockSpec((1, main, main), lambda i: (i, 0, 0)),
            all_of(layers + 1, 8, main),
            pl.BlockSpec((step, 80, count), lambda i: (i, 0, 0)),
            all_of(2, share, main),
        ],
        out_specs=[
            pl.BlockSpec((1, width, width), lambda i: (i, 0, 0)),
            pl.BlockSpec((2 * step, edim, count), lambda i: (i, 0, 0)),
            all_of(layers, width),
            all_of(share, width),
            all_of(1, share),
            all_of(1, share),
            all_of(share, main),
            all_of(width + main),
            all_of(1, 1),
            all_of(1, 1),
        ],
        scratch_shapes=[pltpu.VMEM((main, 8), F32)],
        compiler_params=pltpu.CompilerParams(vmem_limit_bytes=63 * 2**20),
        name="finish",
    )(whole, small, rows, pieces)


def general_body(
    ids,
    dense,
    labels,
    table,
    cross_weight,
    cross_bias,
    tower_in,
    tower_in_bias,
    tower_out,
    tower_out_bias,
    head_weight,
    head_bias,
):
    groups = lax.axis_size("dp")
    sections = lax.axis_size("section")
    device_count = groups * sections
    examples, fields = ids.shape
    table_rows, edim = table.shape[1:]
    layers, width = cross_weight.shape[:2]
    hidden = tower_out.shape[0]
    capacity = examples // groups
    sparse = fields * edim
    me = lax.axis_index("section") * groups + lax.axis_index("dp")

    idt = ids.T
    owner = idt // table_rows
    local = idt % table_rows
    owner_hot = owner[:, None, :] == jnp.arange(groups, dtype=jnp.int32)[None, :, None]
    lane = jnp.arange(examples, dtype=jnp.int32)
    before = (lane[:, None] < lane[None, :]).astype(BF)
    counts = mm(owner_hot.reshape(fields * groups, examples).astype(BF), before, (1, 0))
    rank = jnp.sum(jnp.where(owner_hot, counts.reshape(fields, groups, examples), 0.0), axis=1)
    slot = owner * capacity + rank.astype(jnp.int32)
    slot_hot = (slot[:, None, :] == lane[None, :, None]).astype(BF)
    halves = jnp.stack([local // 32, local % 32], axis=1).astype(BF)
    sent = lax.dot_general(
        halves, slot_hot, (((2,), (2,)), ((0,), (0,))), preferred_element_type=F32
    )
    requests = (sent[:, 0] * 32 + sent[:, 1]).astype(jnp.int32)
    requests = requests.reshape(fields, groups, capacity).transpose(1, 0, 2)
    arrived = lax.all_to_all(requests, "dp", 0, 0, tiled=True)
    arrived = arrived.transpose(1, 0, 2).reshape(fields, examples)
    row_hot = (
        arrived[:, None, :] == jnp.arange(table_rows, dtype=jnp.int32)[None, :, None]
    ).astype(BF)
    table_t = table.transpose(0, 2, 1)
    found = lax.dot_general(
        table_t, row_hot, (((2,), (1,)), ((0,), (0,))), preferred_element_type=F32
    ).astype(BF)
    found = found.reshape(sparse, groups, capacity).transpose(1, 0, 2)
    replies = lax.all_to_all(found, "dp", 0, 0, tiled=True)
    replies = replies.transpose(1, 0, 2).reshape(fields, edim, examples)
    embedded = lax.dot_general(
        replies, slot_hot, (((2,), (1,)), ((0,), (0,))), preferred_element_type=F32
    ).astype(BF)
    x0 = jnp.concatenate([embedded.reshape(sparse, examples), dense.T], axis=0)

    x0w = x0.astype(F32)
    xs, us = [x0], []
    for layer in range(layers):
        u = mm(cross_weight[layer], xs[-1], (0, 0)) + cross_bias[layer][:, None]
        us.append(u)
        xs.append((x0w * u + xs[-1].astype(F32)).astype(BF))
    p1 = mm(tower_in, x0, (0, 0)) + tower_in_bias[:, None]
    a1, d1 = gelu_parts(p1)
    h1 = a1.astype(BF)
    p2 = mm(tower_out, h1, (0, 0)) + tower_out_bias[:, None]
    h2, d2 = gelu_parts(p2)
    head_cross, head_tower = head_weight[:width], head_weight[width:]
    last = xs[-1].astype(F32)
    z = (
        jnp.sum(last * head_cross[:, None], axis=0)
        + jnp.sum(h2 * head_tower[:, None], axis=0)
        + head_bias[0]
    )
    probs = jax.nn.sigmoid(z)
    target = labels.astype(F32)
    loss = jnp.sum(jnp.logaddexp(0.0, z) - target * z)
    s = probs - target
    head_grad = jnp.concatenate([jnp.sum(s * last, axis=1), jnp.sum(s * h2, axis=1)])

    q2 = (s[None, :] * head_tower[:, None] * d2).astype(BF)
    tower_out_g = mm(q2, h1, (1, 1))
    q1 = (mm(tower_out, q2, (1, 0)) * d1).astype(BF)
    tower_in_g = mm(q1, x0, (1, 1))
    tower_biases = [jnp.sum(q1.astype(F32), axis=1), jnp.sum(q2.astype(F32), axis=1)]
    dx0 = mm(tower_in, q1, (1, 0))
    g = (s[None, :] * head_cross[:, None]).astype(BF)
    cross_g, cross_b = [None] * layers, [None] * layers
    for layer in reversed(range(layers)):
        gw = g.astype(F32)
        v = (gw * x0w).astype(BF)
        cross_g[layer] = mm(xs[layer], v, (1, 1))
        cross_b[layer] = jnp.sum(v.astype(F32), axis=1)
        dx0 = dx0 + gw * us[layer]
        g = gw + mm(cross_weight[layer], v, (1, 0))
        if layer:
            g = g.astype(BF)
    dx0 = dx0 + g

    packed = lax.dot_general(
        dx0[:sparse].astype(BF).reshape(fields, edim, examples),
        slot_hot,
        (((2,), (2,)), ((0,), (0,))),
        preferred_element_type=F32,
    ).astype(BF)
    packed = packed.reshape(sparse, groups, capacity).transpose(1, 0, 2)
    delivered = lax.all_to_all(packed, "dp", 0, 0, tiled=True)
    delivered = delivered.transpose(1, 0, 2).reshape(fields, edim, examples)
    table_g = lax.dot_general(
        delivered, row_hot, (((2,), (2,)), ((0,), (0,))), preferred_element_type=F32
    )
    table_g = lax.psum(table_g, "section").transpose(0, 2, 1)

    small = jnp.concatenate(
        cross_b + [head_grad, jnp.sum(s).reshape(1), loss.reshape(1)] + tower_biases
    )
    small = lax.psum(small, ("section", "dp"))
    sizes = [layers * width, width + hidden, 1, 1, hidden, hidden]
    ends = [sum(sizes[: i + 1]) for i in range(len(sizes))]
    pieces = [small[e - n : e] for e, n in zip(ends, sizes)]
    cross_b_out = pieces[0].reshape(layers, width)
    share = hidden // device_count
    bias_in, bias_out = (lax.dynamic_slice(p, (me * share,), (share,)) for p in pieces[4:])
    cross_out = lax.psum(jnp.stack(cross_g), ("section", "dp"))
    tower_in_out = lax.psum_scatter(
        tower_in_g, ("section", "dp"), scatter_dimension=0, tiled=True
    )
    tower_out_out = lax.psum_scatter(
        tower_out_g, ("section", "dp"), scatter_dimension=0, tiled=True
    )
    return (
        probs,
        pieces[3] / (examples * device_count),
        dx0[sparse:].T,
        table_g,
        cross_out,
        cross_b_out,
        tower_in_out.T,
        bias_in,
        tower_out_out.T,
        bias_out,
        pieces[1],
        pieces[2],
    )


def body(
    ids,
    dense,
    labels,
    table,
    cross_weight,
    cross_bias,
    tower_in,
    tower_in_bias,
    tower_out,
    tower_out_bias,
    head_weight,
    head_bias,
):
    groups = lax.axis_size("dp")
    sections = lax.axis_size("section")
    device_count = groups * sections
    examples, fields = ids.shape
    table_rows, edim = table.shape[1:]
    layers, width = cross_weight.shape[:2]
    hidden = tower_out.shape[0]
    capacity = examples // groups
    me = lax.axis_index("section") * groups + lax.axis_index("dp")
    idt = ids.T
    table_t = table.transpose(0, 2, 1)
    here = (sections, groups, capacity, table_rows) == (4, 8, 128, 1024)
    if here:
        x0, arrived, source = look_up(idt, table_t, dense.T)
        probs, rows, dense_g, small, *kept = network(
            x0,
            labels.reshape(1, examples),
            cross_weight,
            tower_in,
            tower_out,
            cross_bias,
            tower_in_bias.reshape(1, hidden),
            tower_out_bias.reshape(1, hidden),
            head_weight,
            head_bias,
            edim,
            fields // 2,
        )
        xs, vs = [x0] + kept[: layers - 1], kept[layers - 1 : 2 * layers - 1]
        h1, q1, q2 = kept[2 * layers - 1 :]
        whole, pieces, table_sum, small = reduce_all(
            xs + [q1, q2], vs + [x0, h1], layers, rows, source, arrived, small
        )
        small = small.reshape(layers + 1, 8, hidden)
        cross_out, table_g, cross_b_out, in_out, in_b, out_b, out_out, head_out, slopes, loss = finish(
            whole, small, table_sum, pieces, width, fields, edim, examples * device_count
        )
        return (
            probs.reshape(examples),
            loss.reshape(1),
            dense_g.T,
            table_g.transpose(0, 2, 1),
            cross_out,
            cross_b_out,
            in_out.T,
            in_b.reshape(in_b.shape[1]),
            out_out.T,
            out_b.reshape(out_b.shape[1]),
            head_out,
            slopes.reshape(1),
        )
    return general_body(
        ids, dense, labels, table, cross_weight, cross_bias, tower_in, tower_in_bias, tower_out,
        tower_out_bias, head_weight, head_bias,
    )


def solution(mesh):
    both = ("section", "dp")
    return jax.shard_map(
        body,
        mesh=mesh,
        in_specs=(P(both, None), P(both, None), P(both), P(None, "dp", None)) + (P(),) * 8,
        out_specs=(
            P(both),
            P(),
            P(both, None),
            P(None, "dp", None),
            P(),
            P(),
            P(None, both),
            P(both),
            P(None, both),
            P(both),
            P(),
            P(),
        ),
        check_vma=False,
    )
```
